128 devices in a mesh: gy: 8 (over x_lo, z), gz: 16 (over y, x_hi, core).
Axes of the slice: x: 4 (x_hi: 2, x_lo: 2; x = x_hi * 2 + x_lo), y: 4, z: 4, core: 2. Of those that a mesh axis runs over, the one named last changes fastest.
Arguments:
- universe: bfloat16 [4, 64, 128, 128], P(None, 'gy', 'gz'), may hold values from -6 to 6
- kernel1: bfloat16 [27, 32, 4], replicated, may hold values from -0.625 to 0.625
- bias1: float32 [32], replicated, may hold values from -3 to 3
- kernel2: bfloat16 [27, 64, 32], replicated, may hold values from -0.21875 to 0.21875
- bias2: float32 [64], replicated, may hold values from -3 to 3
- kernel3: bfloat16 [27, 128, 64], replicated, may hold values from -0.15625 to 0.15625
- bias3: float32 [128], replicated, may hold values from -3 to 3
- cotangent: bfloat16 [128, 8, 16, 16], P('gz', 'gy'), may hold values from -10 to 10
Outputs:
- features: bfloat16 [128, 8, 16, 16], P('gz', 'gy')
- grad_kernel1: float32 [27, 32, 4], replicated
- grad_bias1: float32 [32], replicated
- grad_kernel2: float32 [27, 64, 32], replicated
- grad_bias2: float32 [64], replicated
- grad_kernel3: float32 [27, 128, 64], P(None, 'gz')
- grad_bias3: float32 [128], P('gz')
The draws below stay inside these ranges and needn't reach their ends.
All inputs are finite; a program needn't handle non-finite values.
Results may differ from the reference program's by a relative error of at most 0.018.
The reference program's roundings to bfloat16 on the way count: a program that leaves them out, or rounds other values in their place, can miss the bound.
Values may be sent and summed in bfloat16 or wider, within the bound.
No kernel may reach another device: no remote copies, remote signals or barrier semaphores. Data moves between devices by JAX's collectives and lax.ppermute only.
A program may use at most 64 MiB of HBM per device.

```python
import math
import jax
import jax.numpy as jnp
from jax import lax

C0 = 4
C1 = 32
C2 = 64
C3 = 128
XS = 128
NY = 64
NZ = 128


def draw_cotangent(key, part):
    key = jax.random.fold_in(key, 7)
    first = jax.random.fold_in(key, 0)
    shape = (C3, NY // 8, NZ // 8, XS // 8)
    rows_y = jnp.arange(NY // 8, dtype=jnp.float32) / max(NY // 8 - 1, 1)
    cols_z = jnp.arange(NZ // 8, dtype=jnp.float32) / max(NZ // 8 - 1, 1)
    ramp = jnp.exp(0.5 * math.log(3.0) * (rows_y[:, None] + cols_z[None, :]))[:, :, None]
    values = jnp.clip(jax.random.normal(first, shape, jnp.float32), -2.5, 2.5)
    return (values * ramp).astype(jnp.bfloat16)


def block_levels(stream_key, dims, pieces, least, top_value):
    loudness, own = 1.0, jax.random.fold_in(stream_key, 6)
    for position, parts in pieces:
        steps = jnp.exp(jax.random.uniform(jax.random.fold_in(own, position), (parts,), jnp.float32, least / len(pieces), top_value / len(pieces)))
        loudness = loudness * jnp.repeat(steps, dims[position] // parts).reshape([-1 if axis == position else 1 for axis in range(len(dims))])
    return loudness


def scatter_about(key, dims, scale, limit, shards=(), kind=jnp.bfloat16):
    values = scale * jax.random.normal(key, dims, jnp.float32)
    if shards:
        values = values * block_levels(key, dims, shards, -0.22, 0.18)
    return jnp.clip(values, -limit, limit).astype(kind)


def setup_inputs(seed: int = 0) -> dict:
    seeds = jax.random.split(jax.random.key(seed), 9)
    return {
        "universe": scatter_about(seeds[0], (C0, NY, NZ, XS), 1.0, 6.0, ((1, 8), (2, 16))),
        "kernel1": scatter_about(seeds[1], (27, C1, C0), (27 * C0) ** -0.5, 0.625),
        "bias1": scatter_about(seeds[2], (C1,), 0.5, 3.0, (), jnp.float32),
        "kernel2": scatter_about(seeds[3], (27, C2, C1), (27 * C1) ** -0.5, 0.21875),
        "bias2": scatter_about(seeds[4], (C2,), 0.5, 3.0, (), jnp.float32),
        "kernel3": scatter_about(seeds[5], (27, C3, C2), (27 * C2) ** -0.5, 0.15625),
        "bias3": scatter_about(seeds[6], (C3,), 0.5, 3.0, (), jnp.float32),
        "cotangent": draw_cotangent(jax.random.fold_in(seeds[8], 71), 0),
    }


SHARPNESS = 2.0
LEAK_SLOPE = 0.3

def convf(field, kernel):
    out_chans = kernel.shape[1]
    in_chans = kernel.shape[2]
    filters = jnp.transpose(kernel.reshape(3, 3, 3, out_chans, in_chans), (3, 4, 1, 2, 0))
    result = lax.conv_general_dilated(field[None], filters, (1, 1, 1), 'SAME', dimension_numbers=('NCDHW', 'OIDHW', 'NCDHW'), precision=lax.Precision.HIGHEST)
    return result[0]

def pool_forward(pre):
    chans, rows_y, cols_z, depth = pre.shape
    active = jnp.where(pre > 0, pre, LEAK_SLOPE * pre)
    exponent = jnp.exp(SHARPNESS * active).reshape(chans, rows_y // 2, 2, cols_z // 2, 2, depth // 2, 2)
    total = exponent.sum(axis=(2, 4, 6))
    return (jnp.log(total * 0.125) / SHARPNESS).astype(jnp.bfloat16)

def pool_backward(pre, grad):
    chans, rows_y, cols_z, depth = pre.shape
    active = jnp.where(pre > 0, pre, LEAK_SLOPE * pre)
    exponent = jnp.exp(SHARPNESS * active).reshape(chans, rows_y // 2, 2, cols_z // 2, 2, depth // 2, 2)
    total = exponent.sum(axis=(2, 4, 6), keepdims=True)
    spread = grad.astype(jnp.float32)[:, :, None, :, None, :, None] * exponent / total
    spread = spread.reshape(pre.shape)
    return jnp.where(pre > 0, spread, LEAK_SLOPE * spread).astype(jnp.bfloat16)

def block_forward(hidden, kernel, bias):
    pre = convf(hidden.astype(jnp.float32), kernel.astype(jnp.float32)) + bias[:, None, None, None]
    return (pre, pool_forward(pre))

def reference(universe, kernel1, bias1, kernel2, bias2, kernel3, bias3, cotangent):
    pre1, hidden1 = block_forward(universe, kernel1, bias1)
    pre2, hidden2 = block_forward(hidden1, kernel2, bias2)
    pre3, features = block_forward(hidden2, kernel3, bias3)
    delta3 = pool_backward(pre3, cotangent)
    _, back3 = jax.vjp(convf, hidden2.astype(jnp.float32), kernel3.astype(jnp.float32))
    grad2, weight3 = back3(delta3.astype(jnp.float32))
    grad2 = grad2.astype(jnp.bfloat16)
    delta2 = pool_backward(pre2, grad2)
    _, back2 = jax.vjp(convf, hidden1.astype(jnp.float32), kernel2.astype(jnp.float32))
    grad1, weight2 = back2(delta2.astype(jnp.float32))
    grad1 = grad1.astype(jnp.bfloat16)
    delta1 = pool_backward(pre1, grad1)
    field0 = universe.astype(jnp.float32)
    _, back1 = jax.vjp(lambda kernel: convf(field0, kernel), kernel1.astype(jnp.float32))
    weight1, = back1(delta1.astype(jnp.float32))
    shift1 = delta1.astype(jnp.float32).sum(axis=(1, 2, 3))
    shift2 = delta2.astype(jnp.float32).sum(axis=(1, 2, 3))
    shift3 = delta3.astype(jnp.float32).sum(axis=(1, 2, 3))
    return (features, weight1, shift1, weight2, shift2, weight3, shift3)
```

```python
import functools

import jax
import jax.numpy as jnp
import numpy as np
from jax import lax
from jax.experimental import pallas as pl
from jax.experimental.pallas import tpu as pltpu
from jax.sharding import PartitionSpec as P

F32 = jnp.float32
BF16 = jnp.bfloat16
SLOPE = 0.3
PAIRS = ((0, 1), (2, 3), (-3, -2), (4, 5), (-1, 6))
VMEM = pl.BlockSpec(memory_space=pltpu.VMEM)
SMEM = pl.BlockSpec(memory_space=pltpu.SMEM)
LIMIT = 48 * 1024 * 1024


def dot(a, b):
    return jnp.dot(a, b, preferred_element_type=F32)


def dot_tn(a, b):
    return lax.dot_general(a, b, (((0,), (0,)), ((), ())), preferred_element_type=F32)


def dot_nt(a, b):
    return lax.dot_general(a, b, (((1,), (1,)), ((), ())), preferred_element_type=F32)


def lane(shape):
    return lax.broadcasted_iota(jnp.int32, shape, len(shape) - 1)


def exps(pre):
    return jnp.exp(2.0 * jnp.maximum(pre, SLOPE * pre))


def rounded(value):
    return value.astype(BF16).astype(F32)


def roll(value, amount, axis):
    return pltpu.roll(value, amount, axis)


def down(value):
    rows = lax.broadcasted_iota(jnp.int32, value.shape, 0)
    return jnp.where(rows == 0, 0.0, roll(value, 1, 0))


def up(value):
    count = value.shape[0]
    rows = lax.broadcasted_iota(jnp.int32, value.shape, 0)
    return jnp.where(rows == count - 1, 0.0, roll(value, count - 1, 0))


def forward_kernel(
    place, top, mid, bot, pick, w1, b1, w2, b2,
    hidden2, ratio2, patches1, ratio1, fields,
    left, field, first, spread, pre2, second,
):
    base_y, base_z, size_y, size_z = place[0], place[1], place[2], place[3]

    def inside(offset_y, offset_z, scale):
        row = base_y * (4 // scale) + offset_y
        col = base_z * (4 // scale) + offset_z
        ok_y = (row >= 0) & (row < size_y * (4 // scale))
        ok_z = (col >= 0) & (col < size_z * (4 // scale))
        return jnp.where(ok_y & ok_z, 1.0, 0.0)

    def lay(source, index, target):
        rows = source[index].astype(F32)
        pieces = []
        for one, two in PAIRS:
            a, b = 8 * (one + 3), 8 * (two + 3)
            pieces.append(jnp.concatenate([rows[a : a + 16], rows[b : b + 16]], axis=1))
        left[target] = jnp.concatenate(pieces, axis=0).astype(BF16)

    def lay_top(step, carry):
        lay(top, step + 1, step)
        return carry

    def lay_mid(step, carry):
        lay(mid, step, step + 7)
        return carry

    def lay_bot(step, carry):
        lay(bot, step, step + 15)
        return carry

    lax.fori_loop(0, 7, lay_top, 0)
    lax.fori_loop(0, 8, lay_mid, 0)
    lax.fori_loop(0, 7, lay_bot, 0)

    def sift(step, carry):
        block = left[pl.ds(2 * step, 2)].reshape(160, 256)
        out = dot(block, pick[...]).astype(BF16).reshape(2, 5, 16, 512)
        for px in range(4):
            for k in range(5):
                field[pl.ds(2 * step, 2), px * 16 : px * 16 + 16, k * 128 : k * 128 + 128] = out[
                    :, k, :, px * 128 : px * 128 + 128
                ]
        return carry

    lax.fori_loop(0, 11, sift, 0)
    fields[...] = field[6:16, :, :256]
    first[:, :, 0:8] = jnp.zeros((10, 10, 8, 128), F32)
    first[:, :, 72:80] = jnp.zeros((10, 10, 8, 128), F32)

    def block1(yw, carry):
        stack = field[pl.ds(2 * yw, 4)].reshape(256, 640)
        pre = dot_tn(stack, w1[...]) + b1[...]
        e = exps(pre)
        total = e[:, :128] + e[:, 128:]
        total = total + roll(total, 64, 1)
        total = total + roll(total, 32, 1)
        mean = total * 0.125
        pooled = rounded(jnp.log(mean) * 0.5)
        for k, pair in enumerate(PAIRS):
            for h, zw in enumerate(pair):
                at = k * 128 + h * 64
                first[yw, zw + 3, 8:72] = pooled[at : at + 64] * inside(yw - 3, zw, 1)

        @pl.when((yw >= 3) & (yw < 7))
        def _():
            share = 0.125 / mean[:256]
            share = jnp.concatenate([share, share], axis=1)
            ratio1[yw - 3] = jnp.where(pre[:256] > 0, 1.0, SLOPE) * (e[:256] * share)

        return carry

    lax.fori_loop(0, 10, block1, 0)

    group1 = lane((32, 128)) // 32

    def frame(yi, carry):
        for zi in range(10):
            part = first[yi, zi, pl.ds(7, 32, stride=2), :]
            for px in range(1, 4):
                part = jnp.where(group1 == px, first[yi, zi, pl.ds(7 + px, 32, stride=2), :], part)
            spread[yi, zi] = part.astype(BF16)
        return carry

    lax.fori_loop(0, 10, frame, 0)
    patches1[...] = spread[2:8, 2:8]

    for dy in range(3):
        block = jnp.concatenate(
            [
                jnp.concatenate([spread[dy : dy + 8, 2 * zo + pz] for pz in range(4)], axis=2)[:, None]
                for zo in range(4)
            ],
            axis=1,
        ).reshape(1024, 512)
        term = dot(block, w2[dy]).reshape(8, 4, 32, 256)
        pre2[...] = term + b2[...] if dy == 0 else pre2[...] + term

    half = lane((16, 128)) < 64

    def block2(yp, carry):
        pre = pre2[pl.ds(2 * yp, 2)]
        e = exps(pre)
        both = e[0] + e[1]
        total = (both[:, :, :128] + both[:, :, 128:]).reshape(128, 128)
        total = total + roll(total, 64, 1)
        mean = total * 0.125
        pooled = rounded(jnp.log(mean) * 0.5).reshape(4, 32, 128)
        share = (0.125 / mean).reshape(4, 32, 128)
        share = jnp.concatenate([share, share], axis=2)
        scaled = jnp.where(pre > 0, 1.0, SLOPE) * (e * share[None])
        for zo in range(4):
            ok = inside(yp - 1, zo - 1, 2)
            ratio2[pl.ds(2 * yp, 2), zo] = scaled[:, zo] * ok
            second[zo] = pooled[zo] * ok
            even = second[zo, pl.ds(0, 16, stride=2), :]
            odd = second[zo, pl.ds(1, 16, stride=2), :]
            hidden2[yp, zo] = jnp.where(half, even, odd).astype(BF16)
        return carry

    lax.fori_loop(0, 4, block2, 0)


def run_forward(place, pieces, pick, w1, b1, w2, b2):
    return pl.pallas_call(
        forward_kernel,
        name="forward",
        out_shape=(
            jax.ShapeDtypeStruct((4, 4, 16, 128), BF16),
            jax.ShapeDtypeStruct((8, 4, 32, 256), F32),
            jax.ShapeDtypeStruct((6, 6, 32, 128), BF16),
            jax.ShapeDtypeStruct((4, 256, 256), F32),
            jax.ShapeDtypeStruct((10, 64, 256), BF16),
        ),
        in_specs=[SMEM] + [VMEM] * 8,
        out_specs=(VMEM,) * 5,
        scratch_shapes=[
            pltpu.VMEM((22, 80, 256), BF16),
            pltpu.VMEM((22, 64, 640), BF16),
            pltpu.VMEM((10, 10, 80, 128), F32),
            pltpu.VMEM((10, 10, 32, 128), BF16),
            pltpu.VMEM((8, 4, 32, 256), F32),
            pltpu.VMEM((4, 32, 128), F32),
        ],
        compiler_params=pltpu.CompilerParams(vmem_limit_bytes=LIMIT),
    )(place, *pieces, pick, w1, b1, w2, b2)


def backward_kernel(
    groups,
    before, middle, after, own_cot, w3, b3, w2, ratio2, patches1, ratio1, fields,
    packed,
    patches2, pre3, delta3, patch2, grad2, delta2, patch1, grad1, delta1,
):
    wide = 128 // groups
    half = lane((16, 128)) < 64

    def lay(y, source):
        for z in range(8):
            swapped = roll(source(z).astype(F32), 64, 1)
            patches2[y, z] = jnp.concatenate(
                [jnp.where(half, down(swapped), swapped), jnp.where(half, swapped, up(swapped))], axis=1
            ).astype(BF16)

    for y in range(2):
        lay(y, lambda z: before[(y * 8 + z) * 16 : (y * 8 + z + 1) * 16])
        lay(y + 6, lambda z: after[(y * 8 + z) * 16 : (y * 8 + z + 1) * 16])

    def lay_middle(y, carry):
        lay(y + 2, lambda z: middle[y, z])
        return carry

    lax.fori_loop(0, 4, lay_middle, 0)

    for tap in range(9):
        dy, dz = tap // 3, tap % 3
        block = patches2[dy : dy + 6, dz : dz + 6].reshape(576, 256)
        term = dot(block, w3[tap]).reshape(6, 6, 16, 256)
        pre3[...] = term + b3[...] if tap == 0 else pre3[...] + term

    for wy in range(3):
        for wz in range(3):
            pre = pre3[2 * wy : 2 * wy + 2, 2 * wz : 2 * wz + 2]
            e = exps(pre)
            total = e[0, 0] + e[0, 1] + e[1, 0] + e[1, 1]
            total = total[:, :128] + total[:, 128:]
            mean = total * 0.125
            if wy == 1:
                cot = own_cot[wz * 16 : wz * 16 + 16]
            else:
                cot = (before if wy == 0 else after)[256 + wz * 16 : 272 + wz * 16]
            share = cot.astype(F32) * (0.125 / mean)
            share = jnp.concatenate([share, share], axis=1)
            delta3[2 * wy : 2 * wy + 2, 2 * wz : 2 * wz + 2] = (
                jnp.where(pre > 0, 1.0, SLOPE) * (e * share)
            ).astype(BF16)
            if wy == 1 and wz == 1:
                features = rounded(jnp.log(mean) * 0.5)

    own3 = delta3[2:4, 2:4].reshape(64, 256)
    bias3 = own3.astype(F32).sum(axis=0, keepdims=True)
    bias3 = bias3[:, :128] + bias3[:, 128:]
    low, high = [], []
    for tap in range(9):
        dy, dz = tap // 3, tap % 3
        block = patches2[dy + 2 : dy + 4, dz + 2 : dz + 4].reshape(64, 256)
        full = dot_tn(own3, block)
        one = full[:128]
        low_lanes, high_lanes = roll(full[128:, :128], 64, 1), roll(full[128:, 128:], 64, 1)
        tile0 = jnp.where(lane((128, 128)) < 64, low_lanes, high_lanes)
        tile1 = high_lanes
        low.append(one[:, :128] + tile0)
        high.append(one[:, 128:] + tile1)
    first_half = lane((128, 128)) < 64
    paired = []
    for m in range(5):
        other = roll(high[2 * m + 1], 64, 1) if 2 * m + 1 < 9 else jnp.zeros((128, 128), F32)
        paired.append(jnp.where(first_half, high[2 * m], other))
    kernel3 = [piece.reshape(groups, wide, 128) for piece in low + paired]

    for tap in range(9):
        dy, dz = tap // 3, tap % 3
        block = delta3[2 - dy : 6 - dy, 2 - dz : 6 - dz].reshape(256, 256)
        term = dot_nt(block, w3[tap]).reshape(4, 4, 16, 256)
        patch2[...] = term if tap == 0 else patch2[...] + term

    for y in range(4):
        for z in range(4):
            a, b = patch2[y, z, :, :128], patch2[y, z, :, 128:]
            x = rounded(jnp.where(half, b + up(a), a + down(b)))
            swapped = roll(x, 64, 1)
            grad2[y, z, pl.ds(0, 16, stride=2), :] = jnp.where(half, swapped, x)
            grad2[y, z, pl.ds(1, 16, stride=2), :] = jnp.where(half, x, swapped)

    for y in range(6):
        value = grad2[(y + 1) // 2]
        value = jnp.concatenate([value, value], axis=2)
        delta2[y] = (value * ratio2[y + 1]).astype(BF16)

    own2 = delta2[1:5, 1:3].reshape(256, 256)
    bias2 = own2.astype(F32).sum(axis=0, keepdims=True)
    bias2 = bias2[:, :128] + bias2[:, 128:]
    bias2 = bias2 + roll(bias2, 64, 1)
    kernel2 = []
    for dy in range(3):
        block = jnp.concatenate(
            [
                jnp.concatenate([patches1[dy : dy + 4, 2 * zo + pz] for pz in range(4)], axis=2)[:, None]
                for zo in range(2)
            ],
            axis=1,
        ).reshape(256, 512)
        full = dot_tn(own2, block)
        for dz in range(3):
            lanes0 = full[:, dz * 128 : dz * 128 + 128]
            lanes1 = full[:, dz * 128 + 128 : dz * 128 + 256]
            one = lanes0[:64] + lanes1[128:192]
            two = lanes0[64:128] + lanes1[192:256]
            kernel2.append(one + roll(two, 96, 1))
    kernel2 = jnp.concatenate(kernel2, axis=0).reshape(groups, 576 // groups, 128)

    for dy in range(3):
        block = delta2[2 - dy : 6 - dy].reshape(512, 256)
        term = dot_nt(block, w2[dy]).reshape(4, 4, 32, 512)
        patch1[...] = term if dy == 0 else patch1[...] + term

    low_half = lane((32, 128)) < 64
    group = lane((32, 128)) // 32

    def widen(value, which):
        value = jnp.where(group == which, value, 0.0)
        value = value + roll(value, 32, 1)
        return value + roll(value, 64, 1)

    def gather1(y, carry):
        for z, (zo_a, pz_a, zo_b, pz_b) in enumerate(((0, 3, 1, 1), (1, 2, 2, 0), (1, 3, 2, 1), (2, 2, 3, 0))):
            value = (
                patch1[y, zo_a, :, pz_a * 128 : pz_a * 128 + 128]
                + patch1[y, zo_b, :, pz_b * 128 : pz_b * 128 + 128]
            )
            value = rounded(value + roll(jnp.where(low_half, up(value), down(value)), 64, 1))
            grad1[z, pl.ds(0, 32, stride=2), :] = widen(value, 1)
            grad1[z, pl.ds(1, 32, stride=2), :] = widen(value, 2)
        value = grad1[...].reshape(256, 128)
        value = jnp.concatenate([value, value], axis=1)
        delta1[y] = (value * ratio1[y]).astype(BF16)
        return carry

    lax.fori_loop(0, 4, gather1, 0)

    bias1 = delta1[...].astype(F32).sum(axis=0).sum(axis=0, keepdims=True)
    bias1 = bias1[:, :128] + bias1[:, 128:]
    bias1 = bias1 + roll(bias1, 64, 1)
    bias1 = bias1 + roll(bias1, 32, 1)
    full = None
    for yw in range(4):
        term = dot(fields[2 * yw : 2 * yw + 4].reshape(256, 256), delta1[yw])
        full = term if full is None else full + term
    full = full.reshape(4, 4, 16, 256)
    kernel1 = []
    for dy in range(3):
        rows = full[dy, :, :, :128] + full[dy + 1, :, :, 128:]
        for dx in range(3):
            value = rows[dx] + roll(rows[dx + 1], 96, 1)
            kernel1.append(value + roll(roll(value, 12, 0), 64, 1))
    kernel1 = jnp.concatenate(kernel1, axis=0).reshape(groups, 144 // groups, 128)

    feature_rows = jnp.concatenate([features, jnp.zeros((112, 128), F32)], axis=0).T
    feature_rows = feature_rows.reshape(groups, wide, 128)
    low_lane = lane((1, 128)) < 64
    biases = jnp.concatenate([bias3, jnp.where(low_lane, bias2, bias1)], axis=0)
    biases = jnp.broadcast_to(biases[None], (groups, 2, 128))
    rows = 14 * wide + 720 // groups + wide + 2
    fill = packed.shape[1] - rows
    pieces = kernel3 + [feature_rows, kernel2, kernel1, biases, jnp.zeros((groups, fill, 128), F32)]
    packed[...] = jnp.concatenate(pieces, axis=1).astype(BF16)


def run_backward(groups, *operands):
    rows = 14 * (128 // groups) + 720 // groups + 128 // groups + 2
    rows = -(-rows // 16) * 16
    return pl.pallas_call(
        functools.partial(backward_kernel, groups),
        name="backward",
        out_shape=jax.ShapeDtypeStruct((groups, rows, 128), BF16),
        in_specs=[VMEM] * len(operands),
        out_specs=VMEM,
        scratch_shapes=[
            pltpu.VMEM((8, 8, 16, 256), BF16),
            pltpu.VMEM((6, 6, 16, 256), F32),
            pltpu.VMEM((6, 6, 16, 256), BF16),
            pltpu.VMEM((4, 4, 16, 256), F32),
            pltpu.VMEM((4, 4, 32, 128), F32),
            pltpu.VMEM((6, 4, 32, 256), BF16),
            pltpu.VMEM((4, 4, 32, 512), F32),
            pltpu.VMEM((4, 64, 128), F32),
            pltpu.VMEM((4, 256, 256), BF16),
        ],
        compiler_params=pltpu.CompilerParams(vmem_limit_bytes=LIMIT),
    )(*operands)


def pick_matrix():
    out = np.zeros((2, 128, 4, 2, 64), np.float32)
    for px in range(4):
        for w in range(64):
            x = 2 * w - 1 + px
            if 0 <= x < 128:
                for h in range(2):
                    out[h, x, px, h, w] = 1
    return out.reshape(256, 512).astype(jnp.bfloat16)


def spread_taps(taps, axis, out_axis):
    pads = [[(0, 0)] * taps.ndim for _ in range(2)]
    pads[0][axis] = (0, 1)
    pads[1][axis] = (1, 0)
    return jnp.stack([jnp.pad(taps, pads[0]), jnp.pad(taps, pads[1])], axis=out_axis)


def weights(kernel1, kernel2, kernel3):
    k1 = kernel1.reshape(3, 3, 3, 32, 4).transpose(1, 0, 2, 4, 3)
    k1 = spread_taps(k1, 1, 4)
    k1 = spread_taps(k1, 2, 4)
    k1 = spread_taps(k1, 0, 4)
    k2 = kernel2.reshape(3, 3, 3, 64, 32).transpose(1, 2, 0, 4, 3)
    k2 = spread_taps(k2, 2, 4)
    k2 = spread_taps(k2, 1, 4)
    k3 = kernel3.reshape(3, 3, 3, 128, 64).transpose(1, 2, 0, 4, 3)
    k3 = spread_taps(k3, 2, 4)
    return k1.reshape(256, 256), k2.reshape(3, 512, 256), k3.reshape(9, 256, 256)


def both_ways(to_next, to_previous, axis):
    devices = lax.axis_size(axis)
    forth = [(i, i + 1) for i in range(devices - 1)]
    back = [(i + 1, i) for i in range(devices - 1)]
    return lax.ppermute(to_next, axis, forth), lax.ppermute(to_previous, axis, back)


def shards(universe, kernel1, bias1, kernel2, bias2, kernel3, bias3, cotangent):
    size_y, size_z = lax.axis_size("gy"), lax.axis_size("gz")
    place_y, place_z = lax.axis_index("gy"), lax.axis_index("gz")
    wide = 128 // size_z
    place = jnp.stack([place_y, place_z, jnp.int32(size_y), jnp.int32(size_z)]).astype(jnp.int32)

    tile = universe.transpose(1, 2, 0, 3).reshape(8, 32, 128)
    lower, upper = both_ways(tile, tile, "gz")
    strip = jnp.concatenate([lower[:, 4:], tile, upper[:, :28], jnp.zeros((8, 8, 128), BF16)], axis=1)
    top, bottom = both_ways(strip, strip, "gy")

    w1, w2, w3 = weights(kernel1, kernel2, kernel3)
    cot = jnp.pad(cotangent[:, 0], ((0, 0), (1, 1), (0, 0)))
    cot = jnp.stack([cot[:, d : d + size_z] for d in range(3)], axis=2)
    cot = lax.all_to_all(cot.transpose(1, 0, 2, 3), "gz", 0, 0, tiled=True)
    cot = cot.reshape(128, 3, 16).transpose(1, 2, 0).reshape(48, 128)

    hidden2, ratio2, patches1, ratio1, fields = run_forward(
        place, (top, strip, bottom), jnp.asarray(pick_matrix()), w1,
        jnp.tile(bias1, 8)[None], w2, jnp.tile(bias2, 4)[None],
    )
    lower, upper = both_ways(hidden2[:, 0:2], hidden2[:, 2:4], "gz")
    middle = jnp.concatenate([lower, hidden2, upper], axis=1)
    before, after = both_ways(
        jnp.concatenate([middle[0:2].reshape(256, 128), cot], axis=0),
        jnp.concatenate([middle[2:4].reshape(256, 128), cot], axis=0),
        "gy",
    )
    packed = run_backward(
        size_z, before, middle, after, cot, w3, jnp.tile(bias3, 2)[None], w2, ratio2, patches1, ratio1, fields
    )
    packed = lax.all_to_all(packed, "gz", 0, 0, tiled=True)
    at = 14 * wide
    features = packed[:, at : at + wide, :16].transpose(1, 0, 2)[:, None]
    partial = packed.astype(F32).sum(axis=0).astype(BF16)
    total = lax.all_gather(partial, "gy", axis=0).astype(F32).sum(axis=0)
    rows2, rows1 = 576 // size_z, 144 // size_z
    low = total[: 9 * wide].reshape(3, 3, wide, 2, 64)
    high = total[9 * wide : 14 * wide].reshape(5, wide, 2, 64).transpose(0, 2, 1, 3)
    high = high.reshape(10, wide, 64)[:9].reshape(3, 3, wide, 1, 64)
    grad3 = jnp.concatenate([low, high], axis=3).transpose(3, 0, 1, 2, 4).reshape(27, wide, 64)
    at = at + wide
    rest = lax.all_gather(total[at : at + rows2 + rows1].astype(BF16), "gz", axis=0).astype(F32)
    grad2 = rest[:, :rows2].reshape(3, 3, 64, 4, 32)[:, :, :, :3]
    grad2 = grad2.transpose(3, 0, 1, 2, 4).reshape(27, 64, 32)
    grad1 = rest[:, rows2:].reshape(3, 3, 4, 4, 128)[:, :, :3, :, :32]
    grad1 = grad1.transpose(1, 0, 2, 4, 3).reshape(27, 32, 4)
    at = at + rows2 + rows1
    shift3 = lax.dynamic_slice_in_dim(total[at], place_z * wide, wide, 0)
    return features, grad1, total[at + 1, 64:96], grad2, total[at + 1, :64], grad3, shift3


def solution(mesh):
    in_specs = (P(None, "gy", "gz", None), P(), P(), P(), P(), P(), P(), P("gz", "gy", None, None))
    out_specs = (P("gz", "gy", None, None), P(), P(), P(), P(), P(None, "gz", None), P("gz"))
    return jax.shard_map(shards, mesh=mesh, in_specs=in_specs, out_specs=out_specs, check_vma=False)
```

```python
import functools

import jax
import jax.numpy as jnp
import numpy as np
from jax import lax
from jax.experimental import pallas as pl
from jax.experimental.pallas import tpu as pltpu
from jax.sharding import PartitionSpec as P

F32 = jnp.float32
BF16 = jnp.bfloat16
SLOPE = 0.3
PAIRS = ((0, 1), (2, 3), (-3, -2), (4, 5), (-1, 6))
VMEM = pl.BlockSpec(memory_space=pltpu.VMEM)
SMEM = pl.BlockSpec(memory_space=pltpu.SMEM)
LIMIT = 24 * 1024 * 1024


def dot(a, b):
    return jnp.dot(a, b, preferred_element_type=F32)


def dot_tn(a, b):
    return lax.dot_general(a, b, (((0,), (0,)), ((), ())), preferred_element_type=F32)


def dot_nt(a, b):
    return lax.dot_general(a, b, (((1,), (1,)), ((), ())), preferred_element_type=F32)


def lane(shape):
    return lax.broadcasted_iota(jnp.int32, shape, len(shape) - 1)


def exps(pre):
    return jnp.exp(2.0 * jnp.maximum(pre, SLOPE * pre))


def rounded(value):
    return value.astype(BF16).astype(F32)


def roll(value, amount, axis):
    return pltpu.roll(value, amount, axis)


def down(value):
    rows = lax.broadcasted_iota(jnp.int32, value.shape, 0)
    return jnp.where(rows == 0, 0.0, roll(value, 1, 0))


def up(value):
    count = value.shape[0]
    rows = lax.broadcasted_iota(jnp.int32, value.shape, 0)
    return jnp.where(rows == count - 1, 0.0, roll(value, count - 1, 0))


def forward_kernel(
    place, top, mid, bot, cot, pick, k1, b1, k2, b2,
    hidden2, to_next, to_previous, ratio2, patches1, ratio1, fields, w2,
    w1, left, field, first, spread, pre2, second,
):
    lay_weights1(k1, w1)
    lay_weights2(k2, w2)
    bias1 = jnp.concatenate([b1[...]] * 8, axis=1)
    bias2 = jnp.concatenate([b2[...]] * 4, axis=1)
    base_y, base_z, size_y, size_z = place[0], place[1], place[2], place[3]

    def inside(offset_y, offset_z, scale):
        row = base_y * (4 // scale) + offset_y
        col = base_z * (4 // scale) + offset_z
        ok_y = (row >= 0) & (row < size_y * (4 // scale))
        ok_z = (col >= 0) & (col < size_z * (4 // scale))
        return jnp.where(ok_y & ok_z, 1.0, 0.0)

    def lay(source, index, target):
        rows = source[index].astype(F32)
        pieces = []
        for one, two in PAIRS:
            a, b = 8 * (one + 3), 8 * (two + 3)
            pieces.append(jnp.concatenate([rows[a : a + 16], rows[b : b + 16]], axis=1))
        left[target] = jnp.concatenate(pieces, axis=0).astype(BF16)

    def lay_top(step, carry):
        lay(top, step + 1, step)
        return carry

    def lay_mid(step, carry):
        lay(mid, step, step + 7)
        return carry

    def lay_bot(step, carry):
        lay(bot, step, step + 15)
        return carry

    lax.fori_loop(0, 7, lay_top, 0)
    lax.fori_loop(0, 8, lay_mid, 0)
    lax.fori_loop(0, 7, lay_bot, 0)

    def sift(step, carry):
        block = left[pl.ds(2 * step, 2)].reshape(160, 256)
        out = dot(block, pick[...]).astype(BF16).reshape(2, 5, 16, 512)
        for px in range(4):
            for k in range(5):
                field[pl.ds(2 * step, 2), px * 16 : px * 16 + 16, k * 128 : k * 128 + 128] = out[
                    :, k, :, px * 128 : px * 128 + 128
                ]
        return carry

    lax.fori_loop(0, 11, sift, 0)
    fields[...] = field[6:16, :, :256]
    first[:, :, 0:8] = jnp.zeros((10, 10, 8, 128), F32)
    first[:, :, 72:80] = jnp.zeros((10, 10, 8, 128), F32)

    def block1(yw, carry):
        stack = field[pl.ds(2 * yw, 4)].reshape(256, 640)
        pre = dot_tn(stack, w1[...]) + bias1
        e = exps(pre)
        total = e[:, :128] + e[:, 128:]
        total = total + roll(total, 64, 1)
        total = total + roll(total, 32, 1)
        mean = total * 0.125
        pooled = rounded(jnp.log(mean) * 0.5)
        for k, pair in enumerate(PAIRS):
            for h, zw in enumerate(pair):
                at = k * 128 + h * 64
                first[yw, zw + 3, 8:72] = pooled[at : at + 64] * inside(yw - 3, zw, 1)

        @pl.when((yw >= 3) & (yw < 7))
        def _():
            share = 0.125 / mean[:256]
            share = jnp.concatenate([share, share], axis=1)
            ratio1[yw - 3] = jnp.where(pre[:256] > 0, 1.0, SLOPE) * (e[:256] * share)

        return carry

    lax.fori_loop(0, 10, block1, 0)

    group1 = lane((32, 128)) // 32

    def frame(yi, carry):
        for zi in range(10):
            part = first[yi, zi, pl.ds(7, 32, stride=2), :]
            for px in range(1, 4):
                part = jnp.where(group1 == px, first[yi, zi, pl.ds(7 + px, 32, stride=2), :], part)
            spread[yi, zi] = part.astype(BF16)
        return carry

    lax.fori_loop(0, 10, frame, 0)
    patches1[...] = spread[2:8, 2:8]

    for dy in range(3):
        block = jnp.concatenate(
            [
                jnp.concatenate([spread[dy : dy + 8, 2 * zo + pz] for pz in range(4)], axis=2)[:, None]
                for zo in range(4)
            ],
            axis=1,
        ).reshape(1024, 512)
        term = dot(block, w2[dy]).reshape(8, 4, 32, 256)
        pre2[...] = term + bias2 if dy == 0 else pre2[...] + term

    half = lane((16, 128)) < 64

    def block2(yp, carry):
        pre = pre2[pl.ds(2 * yp, 2)]
        e = exps(pre)
        both = e[0] + e[1]
        total = (both[:, :, :128] + both[:, :, 128:]).reshape(128, 128)
        total = total + roll(total, 64, 1)
        mean = total * 0.125
        pooled = rounded(jnp.log(mean) * 0.5).reshape(4, 32, 128)
        share = (0.125 / mean).reshape(4, 32, 128)
        share = jnp.concatenate([share, share], axis=2)
        scaled = jnp.where(pre > 0, 1.0, SLOPE) * (e * share[None])
        for zo in range(4):
            ok = inside(yp - 1, zo - 1, 2)
            ratio2[pl.ds(2 * yp, 2), zo] = scaled[:, zo] * ok
            second[zo] = pooled[zo] * ok
            even = second[zo, pl.ds(0, 16, stride=2), :]
            odd = second[zo, pl.ds(1, 16, stride=2), :]
            hidden2[yp, zo] = jnp.where(half, even, odd).astype(BF16)
        return carry

    lax.fori_loop(0, 4, block2, 0)
    to_next[0:128] = hidden2[:, 0:2].reshape(128, 128)
    to_previous[0:128] = hidden2[:, 2:4].reshape(128, 128)
    own = cot[...].astype(F32).T.astype(BF16)
    to_next[128:144] = own
    to_previous[128:144] = own


def lay_weights1(taps, out):
    group = lane((16, 128)) // 32
    zero = jnp.zeros((16, 128), F32)
    for py in range(4):
        for px in range(4):
            at = (py * 4 + px) * 16
            for qy in range(2):
                dy = py - qy
                sides = [
                    taps[(px - qx) * 3 + dy] if 0 <= dy < 3 and 0 <= px - qx < 3 else zero for qx in range(2)
                ]
                value = jnp.where(group == 0, sides[0], sides[1])
                shifted = jnp.where(group == 2, roll(sides[0], 4, 0), roll(sides[1], 4, 0))
                out[at : at + 16, qy * 128 : qy * 128 + 128] = jnp.where(group < 2, value, shifted).astype(BF16)


def lay_weights2(taps, out):
    zero = jnp.zeros((32, 64), BF16)
    for dy in range(3):
        out[dy, 384:512, 0:128] = jnp.zeros((128, 128), BF16)
        out[dy, 0:128, 128:256] = jnp.zeros((128, 128), BF16)
        for dz in range(3):
            for px in range(4):
                sides = [taps[(px - qx) * 9 + dy * 3 + dz] if 0 <= px - qx < 3 else zero for qx in range(2)]
                tile = jnp.concatenate(sides, axis=1)
                for qz in range(2):
                    at = (dz + qz) * 128 + px * 32
                    out[dy, at : at + 32, qz * 128 : qz * 128 + 128] = tile


def lay_weights3(taps, out):
    zero = jnp.zeros((64, 128), BF16)
    for tap in range(9):
        out[tap, 192:256, 0:128] = zero
        out[tap, 0:64, 128:256] = zero
        for dx in range(3):
            value = taps[dx * 9 + tap]
            out[tap, dx * 64 : dx * 64 + 64, 0:128] = value
            out[tap, dx * 64 + 64 : dx * 64 + 128, 128:256] = value


def run_forward(*operands):
    return pl.pallas_call(
        forward_kernel,
        name="forward",
        out_shape=(
            jax.ShapeDtypeStruct((4, 4, 16, 128), BF16),
            jax.ShapeDtypeStruct((144, 128), BF16),
            jax.ShapeDtypeStruct((144, 128), BF16),
            jax.ShapeDtypeStruct((8, 4, 32, 256), F32),
            jax.ShapeDtypeStruct((6, 6, 32, 128), BF16),
            jax.ShapeDtypeStruct((4, 256, 256), F32),
            jax.ShapeDtypeStruct((10, 64, 256), BF16),
            jax.ShapeDtypeStruct((3, 512, 256), BF16),
        ),
        in_specs=[SMEM] + [VMEM] * (len(operands) - 1),
        out_specs=(VMEM,) * 8,
        scratch_shapes=[
            pltpu.VMEM((256, 256), BF16),
            pltpu.VMEM((22, 80, 256), BF16),
            pltpu.VMEM((22, 64, 640), BF16),
            pltpu.VMEM((10, 10, 80, 128), F32),
            pltpu.VMEM((10, 10, 32, 128), BF16),
            pltpu.VMEM((8, 4, 32, 256), F32),
            pltpu.VMEM((4, 32, 128), F32),
        ],
        compiler_params=pltpu.CompilerParams(vmem_limit_bytes=LIMIT),
    )(*operands)


def weave_kernel(lower, hidden2, upper, to_next, to_previous):
    for target, first_row in ((to_next, 0), (to_previous, 2)):
        for y in range(2):
            row, at = first_row + y, y * 128
            target[at : at + 32] = lower[row * 32 : row * 32 + 32]
            target[at + 32 : at + 96] = hidden2[row].reshape(64, 128)
            target[at + 96 : at + 128] = upper[row * 32 : row * 32 + 32]
        target[256:272] = lower[128:144]
        target[288:304] = upper[128:144]


def run_weave(lower, hidden2, upper, own_cot):
    def kernel(lower, hidden2, upper, own_cot, to_next, to_previous):
        weave_kernel(lower, hidden2, upper, to_next, to_previous)
        to_next[272:288] = own_cot[128:144]
        to_previous[272:288] = own_cot[128:144]

    return pl.pallas_call(
        kernel,
        name="weave",
        out_shape=(jax.ShapeDtypeStruct((304, 128), BF16),) * 2,
        in_specs=[VMEM] * 4,
        out_specs=(VMEM,) * 2,
    )(lower, hidden2, upper, own_cot)


def backward_kernel(
    groups,
    before, lower, middle, upper, after, own_cot, k3, b3, w2, ratio2, patches1, ratio1, fields,
    packed,
    w3, patches2, pre3, delta3, patch2, grad2, delta2, patch1, grad1, delta1,
):
    wide = 128 // groups
    lay_weights3(k3, w3)
    bias3_in = jnp.concatenate([b3[...]] * 2, axis=1)
    half = lane((16, 128)) < 64

    def lay(y, source):
        for z in range(8):
            swapped = roll(source(z).astype(F32), 64, 1)
            patches2[y, z] = jnp.concatenate(
                [jnp.where(half, down(swapped), swapped), jnp.where(half, swapped, up(swapped))], axis=1
            ).astype(BF16)

    for y in range(2):
        lay(y, lambda z: before[(y * 8 + z) * 16 : (y * 8 + z + 1) * 16])
        lay(y + 6, lambda z: after[(y * 8 + z) * 16 : (y * 8 + z + 1) * 16])

    def pick_middle(y, z):
        if z < 2:
            return lower[(y * 2 + z) * 16 : (y * 2 + z + 1) * 16]
        if z < 6:
            return middle[y, z - 2]
        return upper[(y * 2 + z - 6) * 16 : (y * 2 + z - 5) * 16]

    for y in range(4):
        lay(y + 2, functools.partial(pick_middle, y))

    for tap in range(9):
        dy, dz = tap // 3, tap % 3
        block = patches2[dy : dy + 6, dz : dz + 6].reshape(576, 256)
        term = dot(block, w3[tap]).reshape(6, 6, 16, 256)
        pre3[...] = term + bias3_in if tap == 0 else pre3[...] + term

    for wy in range(3):
        for wz in range(3):
            pre = pre3[2 * wy : 2 * wy + 2, 2 * wz : 2 * wz + 2]
            e = exps(pre)
            total = e[0, 0] + e[0, 1] + e[1, 0] + e[1, 1]
            total = total[:, :128] + total[:, 128:]
            mean = total * 0.125
            if wy == 1:
                cot = (lower, own_cot, upper)[wz][128:144]
            else:
                cot = (before if wy == 0 else after)[256 + wz * 16 : 272 + wz * 16]
            share = cot.astype(F32) * (0.125 / mean)
            share = jnp.concatenate([share, share], axis=1)
            delta3[2 * wy : 2 * wy + 2, 2 * wz : 2 * wz + 2] = (
                jnp.where(pre > 0, 1.0, SLOPE) * (e * share)
            ).astype(BF16)
            if wy == 1 and wz == 1:
                features = rounded(jnp.log(mean) * 0.5)

    own3 = delta3[2:4, 2:4].reshape(64, 256)
    bias3 = own3.astype(F32).sum(axis=0, keepdims=True)
    bias3 = bias3[:, :128] + bias3[:, 128:]
    low, high = [], []
    for tap in range(9):
        dy, dz = tap // 3, tap % 3
        block = patches2[dy + 2 : dy + 4, dz + 2 : dz + 4].reshape(64, 256)
        full = dot_tn(own3, block)
        one = full[:128]
        low_lanes, high_lanes = roll(full[128:, :128], 64, 1), roll(full[128:, 128:], 64, 1)
        tile0 = jnp.where(lane((128, 128)) < 64, low_lanes, high_lanes)
        tile1 = high_lanes
        low.append(one[:, :128] + tile0)
        high.append(one[:, 128:] + tile1)
    first_half = lane((128, 128)) < 64
    paired = []
    for m in range(5):
        other = roll(high[2 * m + 1], 64, 1) if 2 * m + 1 < 9 else jnp.zeros((128, 128), F32)
        paired.append(jnp.where(first_half, high[2 * m], other))
    kernel3 = [piece.reshape(groups, wide, 128) for piece in low + paired]

    for tap in range(9):
        dy, dz = tap // 3, tap % 3
        block = delta3[2 - dy : 6 - dy, 2 - dz : 6 - dz].reshape(256, 256)
        term = dot_nt(block, w3[tap]).reshape(4, 4, 16, 256)
        patch2[...] = term if tap == 0 else patch2[...] + term

    for y in range(4):
        for z in range(4):
            a, b = patch2[y, z, :, :128], patch2[y, z, :, 128:]
            x = rounded(jnp.where(half, b + up(a), a + down(b)))
            swapped = roll(x, 64, 1)
            grad2[y, z, pl.ds(0, 16, stride=2), :] = jnp.where(half, swapped, x)
            grad2[y, z, pl.ds(1, 16, stride=2), :] = jnp.where(half, x, swapped)

    for y in range(6):
        value = grad2[(y + 1) // 2]
        value = jnp.concatenate([value, value], axis=2)
        delta2[y] = (value * ratio2[y + 1]).astype(BF16)

    own2 = delta2[1:5, 1:3].reshape(256, 256)
    bias2 = own2.astype(F32).sum(axis=0, keepdims=True)
    bias2 = bias2[:, :128] + bias2[:, 128:]
    bias2 = bias2 + roll(bias2, 64, 1)
    low_lane = lane((32, 128)) < 64
    taps = [None] * 27
    for dy in range(3):
        block = jnp.concatenate(
            [
                jnp.concatenate([patches1[dy : dy + 4, 2 * zo + pz] for pz in range(4)], axis=2)[:, None]
                for zo in range(2)
            ],
            axis=1,
        ).reshape(256, 512)
        full = dot_tn(block, own2)
        for dz in range(3):
            rows = full[dz * 128 : dz * 128 + 128, :128] + full[dz * 128 + 128 : dz * 128 + 256, 128:]
            for dx in range(3):
                taps[dx * 9 + dy * 3 + dz] = rows[dx * 32 : dx * 32 + 32] + roll(
                    rows[dx * 32 + 32 : dx * 32 + 64], 64, 1
                )
    kernel2 = [
        jnp.where(low_lane, taps[2 * m], roll(taps[2 * m + 1], 64, 1) if 2 * m + 1 < 27 else 0.0)
        for m in range(14)
    ]
    kernel2 = jnp.concatenate(kernel2, axis=0).reshape(groups, 448 // groups, 128)

    for dy in range(3):
        block = delta2[2 - dy : 6 - dy].reshape(512, 256)
        term = dot_nt(block, w2[dy]).reshape(4, 4, 32, 512)
        patch1[...] = term if dy == 0 else patch1[...] + term

    low_half = lane((32, 128)) < 64
    group = lane((32, 128)) // 32

    def widen(value, which):
        value = jnp.where(group == which, value, 0.0)
        value = value + roll(value, 32, 1)
        return value + roll(value, 64, 1)

    def gather1(y, carry):
        for z, (zo_a, pz_a, zo_b, pz_b) in enumerate(((0, 3, 1, 1), (1, 2, 2, 0), (1, 3, 2, 1), (2, 2, 3, 0))):
            value = (
                patch1[y, zo_a, :, pz_a * 128 : pz_a * 128 + 128]
                + patch1[y, zo_b, :, pz_b * 128 : pz_b * 128 + 128]
            )
            value = rounded(value + roll(jnp.where(low_half, up(value), down(value)), 64, 1))
            grad1[z, pl.ds(0, 32, stride=2), :] = widen(value, 1)
            grad1[z, pl.ds(1, 32, stride=2), :] = widen(value, 2)
        value = grad1[...].reshape(256, 128)
        value = jnp.concatenate([value, value], axis=1)
        delta1[y] = (value * ratio1[y]).astype(BF16)
        return carry

    lax.fori_loop(0, 4, gather1, 0)

    bias1 = delta1[...].astype(F32).sum(axis=0).sum(axis=0, keepdims=True)
    bias1 = bias1[:, :128] + bias1[:, 128:]
    bias1 = bias1 + roll(bias1, 64, 1)
    bias1 = bias1 + roll(bias1, 32, 1)
    full = None
    for yw in range(4):
        term = dot(fields[2 * yw : 2 * yw + 4].reshape(256, 256), delta1[yw])
        full = term if full is None else full + term
    full = full.reshape(4, 4, 16, 256)
    kernel1 = []
    group1 = lane((16, 128)) // 32
    for dy in range(3):
        rows = full[dy, :, :, :128] + full[dy + 1, :, :, 128:]
        pieces = []
        for dx in range(3):
            value = rows[dx] + roll(rows[dx + 1], 96, 1)
            value = value + roll(roll(value, 12, 0), 64, 1)
            pieces.append(roll(value, 32 * dx, 1) if dx else value)
        kernel1.append(jnp.where(group1 == 0, pieces[0], jnp.where(group1 == 1, pieces[1], pieces[2])))
    kernel1 = jnp.concatenate(kernel1, axis=0).reshape(groups, 48 // groups, 128)

    feature_rows = jnp.concatenate([features, jnp.zeros((112, 128), F32)], axis=0).T
    feature_rows = feature_rows.reshape(groups, wide, 128)
    biases = jnp.concatenate([bias3, jnp.where(lane((1, 128)) < 64, bias2, bias1)], axis=0)
    biases = jnp.broadcast_to(biases[None], (groups, 2, 128))
    rows = 15 * wide + 496 // groups + 2
    fill = packed.shape[1] - rows
    pieces = kernel3 + [feature_rows, kernel2, kernel1, biases, jnp.zeros((groups, fill, 128), F32)]
    packed[...] = jnp.concatenate(pieces, axis=1).astype(BF16)


def run_backward(groups, *operands):
    rows = 15 * (128 // groups) + 496 // groups + 2
    rows = -(-rows // 16) * 16
    return pl.pallas_call(
        functools.partial(backward_kernel, groups),
        name="backward",
        out_shape=jax.ShapeDtypeStruct((groups, rows, 128), BF16),
        in_specs=[VMEM] * len(operands),
        out_specs=VMEM,
        scratch_shapes=[
            pltpu.VMEM((9, 256, 256), BF16),
            pltpu.VMEM((8, 8, 16, 256), BF16),
            pltpu.VMEM((6, 6, 16, 256), F32),
            pltpu.VMEM((6, 6, 16, 256), BF16),
            pltpu.VMEM((4, 4, 16, 256), F32),
            pltpu.VMEM((4, 4, 32, 128), F32),
            pltpu.VMEM((6, 4, 32, 256), BF16),
            pltpu.VMEM((4, 4, 32, 512), F32),
            pltpu.VMEM((4, 64, 128), F32),
            pltpu.VMEM((4, 256, 256), BF16),
        ],
        compiler_params=pltpu.CompilerParams(vmem_limit_bytes=LIMIT),
    )(*operands)


def pick_matrix():
    out = np.zeros((2, 128, 4, 2, 64), np.float32)
    for px in range(4):
        for w in range(64):
            x = 2 * w - 1 + px
            if 0 <= x < 128:
                for h in range(2):
                    out[h, x, px, h, w] = 1
    return out.reshape(256, 512).astype(jnp.bfloat16)


def unpack_kernel(rest, grad1, grad2):
    groups, rows = rest.shape[0], rest.shape[1]
    rows2 = 448 // groups
    whole = rest[...].astype(F32)
    grad = whole[:, :rows2].reshape(14, 32, 128)
    for tap in range(27):
        grad2[tap] = grad[tap // 2, :, (tap % 2) * 64 : (tap % 2) * 64 + 64]
    grad = whole[:, rows2:].reshape(3, 16, 128)
    for dy in range(3):
        for dz in range(3):
            for dx in range(3):
                grad1[dx * 9 + dy * 3 + dz] = grad[dy, dz * 4 : dz * 4 + 4, dx * 32 : dx * 32 + 32]


def run_unpack(rest):
    return pl.pallas_call(
        unpack_kernel,
        name="unpack",
        out_shape=(jax.ShapeDtypeStruct((27, 4, 32), F32), jax.ShapeDtypeStruct((27, 32, 64), F32)),
        in_specs=[VMEM],
        out_specs=(VMEM, VMEM),
    )(rest)


def spread_to_all(value, axis):
    return lax.all_to_all(jnp.broadcast_to(value[None], (lax.axis_size(axis),) + value.shape), axis, 0, 0, tiled=True)


def both_ways(to_next, to_previous, axis):
    devices = lax.axis_size(axis)
    forth = [(i, i + 1) for i in range(devices - 1)]
    back = [(i + 1, i) for i in range(devices - 1)]
    return lax.ppermute(to_next, axis, forth), lax.ppermute(to_previous, axis, back)


def shards(universe, kernel1, bias1, kernel2, bias2, kernel3, bias3, cotangent):
    size_y, size_z = lax.axis_size("gy"), lax.axis_size("gz")
    place_y, place_z = lax.axis_index("gy"), lax.axis_index("gz")
    wide = 128 // size_z
    place = jnp.stack([place_y, place_z, jnp.int32(size_y), jnp.int32(size_z)]).astype(jnp.int32)

    tile = universe.transpose(1, 2, 0, 3).reshape(8, 32, 128)
    lower, upper = both_ways(tile, tile, "gz")
    strip = jnp.concatenate([lower[:, 4:], tile, upper[:, :28], jnp.zeros((8, 8, 128), BF16)], axis=1)
    top, bottom = both_ways(strip, strip, "gy")

    cot = lax.all_to_all(cotangent[:, 0].transpose(1, 0, 2), "gz", 0, 0, tiled=True).reshape(128, 16)
    k1 = kernel1.transpose(0, 2, 1).reshape(9, 12, 32).astype(F32)
    k1 = jnp.tile(jnp.pad(k1, ((0, 0), (0, 4), (0, 0))), (1, 1, 4))
    k2, k3 = kernel2.transpose(0, 2, 1), kernel3.transpose(0, 2, 1)

    hidden2, to_next, to_previous, ratio2, patches1, ratio1, fields, w2 = run_forward(
        place, top, strip, bottom, cot, jnp.asarray(pick_matrix()), k1, bias1[None], k2, bias2[None]
    )
    lower, upper = both_ways(to_next, to_previous, "gz")
    row_next, row_previous = run_weave(lower, hidden2, upper, to_next)
    before, after = both_ways(row_next, row_previous, "gy")
    packed = run_backward(
        size_z, before, lower, hidden2, upper, after, to_next, k3, bias3[None], w2, ratio2, patches1, ratio1, fields
    )
    packed = lax.all_to_all(packed, "gz", 0, 0, tiled=True)
    at = 14 * wide
    features = packed[:, at : at + wide, :16].transpose(1, 0, 2)[:, None]
    partial = packed.astype(F32).sum(axis=0).astype(BF16)
    total = spread_to_all(partial, "gy").astype(F32).sum(axis=0)
    at = at + wide
    last = at + 496 // size_z
    grad1, grad2 = run_unpack(spread_to_all(total[at:last].astype(BF16), "gz"))
    low = total[: 9 * wide].reshape(3, 3, wide, 2, 64)
    high = total[9 * wide : 14 * wide].reshape(5, wide, 2, 64).transpose(0, 2, 1, 3)
    high = high.reshape(10, wide, 64)[:9].reshape(3, 3, wide, 1, 64)
    grad3 = jnp.concatenate([low, high], axis=3).transpose(3, 0, 1, 2, 4).reshape(27, wide, 64)
    shift3 = lax.dynamic_slice_in_dim(total[last], place_z * wide, wide, 0)
    return (
        features, grad1.transpose(0, 2, 1), total[last + 1, 64:96], grad2.transpose(0, 2, 1),
        total[last + 1, :64], grad3, shift3,
    )


def solution(mesh):
    in_specs = (P(None, "gy", "gz", None), P(), P(), P(), P(), P(), P(), P("gz", "gy", None, None))
    out_specs = (P("gz", "gy", None, None), P(), P(), P(), P(), P(None, "gz", None), P("gz"))
    return jax.shard_map(shards, mesh=mesh, in_specs=in_specs, out_specs=out_specs, check_vma=False)
```

```python
import functools

import jax
import jax.numpy as jnp
import numpy as np
from jax import lax
from jax.experimental import pallas as pl
from jax.experimental.pallas import tpu as pltpu
from jax.sharding import PartitionSpec as P

F32 = jnp.float32
BF16 = jnp.bfloat16
SLOPE = 0.3
PAIRS = ((0, 1), (2, 3), (-3, -2), (4, 5), (-1, 6))
VMEM = pl.BlockSpec(memory_space=pltpu.VMEM)
HBM = pl.BlockSpec(memory_space=pltpu.HBM)
LIMIT = 24 * 1024 * 1024


def dot(a, b):
    return jnp.dot(a, b, preferred_element_type=F32)


def dot_tn(a, b):
    return lax.dot_general(a, b, (((0,), (0,)), ((), ())), preferred_element_type=F32)


def dot_nt(a, b):
    return lax.dot_general(a, b, (((1,), (1,)), ((), ())), preferred_element_type=F32)


def lane(shape):
    return lax.broadcasted_iota(jnp.int32, shape, len(shape) - 1)


def exps(pre):
    return jnp.exp(2.0 * jnp.maximum(pre, SLOPE * pre))


def rounded(value):
    return value.astype(BF16).astype(F32)


def roll(value, amount, axis):
    return pltpu.roll(value, amount, axis)


def down(value):
    rows = lax.broadcasted_iota(jnp.int32, value.shape, 0)
    return jnp.where(rows == 0, 0.0, roll(value, 1, 0))


def up(value):
    count = value.shape[0]
    rows = lax.broadcasted_iota(jnp.int32, value.shape, 0)
    return jnp.where(rows == count - 1, 0.0, roll(value, count - 1, 0))


def fetch(sources, targets, sems):
    copies = [
        pltpu.make_async_copy(source, target, sems.at[k])
        for k, (source, target) in enumerate(zip(sources, targets))
    ]
    for copy in copies:
        copy.start()
    return copies


def landing(operands):
    return [pltpu.VMEM(x.shape, x.dtype) for x in operands]


def forward_kernel(*refs):
    sources, refs = refs[:9], refs[9:]
    (to_next, to_previous, *kept_out), refs = refs[:9], refs[9:]
    (top, mid, bot, cot, pick, k1, b1, k2, b2), refs = refs[:9], refs[9:]
    kept, refs = refs[:7], refs[7:]
    hidden2, own_cot, ratio2, patches1, ratio1, fields, w2 = kept
    w1, left, field, first, spread, pre2, second, in_sems, out_sems = refs
    copies = fetch(sources, (top, mid, bot, cot, pick, k1, b1, k2, b2), in_sems)
    leaving = [pltpu.make_async_copy(kept[k], kept_out[k], out_sems.at[k]) for k in range(7)]
    for k in range(5, 9):
        copies[k].wait()
    lay_weights1(k1, w1)
    lay_weights2(k2, w2)
    leaving[6].start()
    for k in range(5):
        copies[k].wait()
    bias1 = jnp.concatenate([b1[...]] * 8, axis=1)
    bias2 = jnp.concatenate([b2[...]] * 4, axis=1)
    base_y, base_z = lax.axis_index("gy"), lax.axis_index("gz")
    size_y, size_z = lax.axis_size("gy"), lax.axis_size("gz")

    def inside(offset_y, offset_z, scale):
        row = base_y * (4 // scale) + offset_y
        col = base_z * (4 // scale) + offset_z
        ok_y = (row >= 0) & (row < size_y * (4 // scale))
        ok_z = (col >= 0) & (col < size_z * (4 // scale))
        return jnp.where(ok_y & ok_z, 1.0, 0.0)

    def lay(source, index, target):
        rows = source[index].astype(F32)
        pieces = []
        for one, two in PAIRS:
            a, b = 8 * (one + 3), 8 * (two + 3)
            pieces.append(jnp.concatenate([rows[a : a + 16], rows[b : b + 16]], axis=1))
        left[target] = jnp.concatenate(pieces, axis=0).astype(BF16)

    def lay_top(step, carry):
        lay(top, step + 1, step)
        return carry

    def lay_mid(step, carry):
        lay(mid, step, step + 7)
        return carry

    def lay_bot(step, carry):
        lay(bot, step, step + 15)
        return carry

    lax.fori_loop(0, 7, lay_top, 0)
    lax.fori_loop(0, 8, lay_mid, 0)
    lax.fori_loop(0, 7, lay_bot, 0)

    def sift(step, carry):
        block = left[pl.ds(2 * step, 2)].reshape(160, 256)
        out = dot(block, pick[...]).astype(BF16).reshape(2, 5, 16, 512)
        for px in range(4):
            for k in range(5):
                field[pl.ds(2 * step, 2), px * 16 : px * 16 + 16, k * 128 : k * 128 + 128] = out[
                    :, k, :, px * 128 : px * 128 + 128
                ]
        return carry

    lax.fori_loop(0, 11, sift, 0)
    fields[...] = field[6:16, :, :256]
    leaving[5].start()
    first[:, :, 0:8] = jnp.zeros((10, 10, 8, 128), F32)
    first[:, :, 72:80] = jnp.zeros((10, 10, 8, 128), F32)

    def block1(yw, carry):
        stack = field[pl.ds(2 * yw, 4)].reshape(256, 640)
        pre = dot_tn(stack, w1[...]) + bias1
        e = exps(pre)
        total = e[:, :128] + e[:, 128:]
        total = total + roll(total, 64, 1)
        total = total + roll(total, 32, 1)
        mean = total * 0.125
        pooled = rounded(jnp.log(mean) * 0.5)
        for k, pair in enumerate(PAIRS):
            for h, zw in enumerate(pair):
                at = k * 128 + h * 64
                first[yw, zw + 3, 8:72] = pooled[at : at + 64] * inside(yw - 3, zw, 1)

        @pl.when((yw >= 3) & (yw < 7))
        def _():
            share = 0.125 / mean[:256]
            share = jnp.concatenate([share, share], axis=1)
            ratio1[yw - 3] = jnp.where(pre[:256] > 0, 1.0, SLOPE) * (e[:256] * share)

        return carry

    lax.fori_loop(0, 10, block1, 0)
    leaving[4].start()

    group1 = lane((32, 128)) // 32

    def frame(yi, carry):
        for zi in range(10):
            part = first[yi, zi, pl.ds(7, 32, stride=2), :]
            for px in range(1, 4):
                part = jnp.where(group1 == px, first[yi, zi, pl.ds(7 + px, 32, stride=2), :], part)
            spread[yi, zi] = part.astype(BF16)
        return carry

    lax.fori_loop(0, 10, frame, 0)
    patches1[...] = spread[2:8, 2:8]
    leaving[3].start()

    for dy in range(3):
        block = jnp.concatenate(
            [
                jnp.concatenate([spread[dy : dy + 8, 2 * zo + pz] for pz in range(4)], axis=2)[:, None]
                for zo in range(4)
            ],
            axis=1,
        ).reshape(1024, 512)
        term = dot(block, w2[dy]).reshape(8, 4, 32, 256)
        pre2[...] = term + bias2 if dy == 0 else pre2[...] + term

    half = lane((16, 128)) < 64

    def block2(yp, carry):
        pre = pre2[pl.ds(2 * yp, 2)]
        e = exps(pre)
        both = e[0] + e[1]
        total = (both[:, :, :128] + both[:, :, 128:]).reshape(128, 128)
        total = total + roll(total, 64, 1)
        mean = total * 0.125
        pooled = rounded(jnp.log(mean) * 0.5).reshape(4, 32, 128)
        share = (0.125 / mean).reshape(4, 32, 128)
        share = jnp.concatenate([share, share], axis=2)
        scaled = jnp.where(pre > 0, 1.0, SLOPE) * (e * share[None])
        for zo in range(4):
            ok = inside(yp - 1, zo - 1, 2)
            ratio2[pl.ds(2 * yp, 2), zo] = scaled[:, zo] * ok
            second[zo] = pooled[zo] * ok
            even = second[zo, pl.ds(0, 16, stride=2), :]
            odd = second[zo, pl.ds(1, 16, stride=2), :]
            hidden2[yp, zo] = jnp.where(half, even, odd).astype(BF16)
        return carry

    lax.fori_loop(0, 4, block2, 0)
    leaving[0].start()
    leaving[2].start()
    to_next[0:128] = hidden2[:, 0:2].reshape(128, 128)
    to_previous[0:128] = hidden2[:, 2:4].reshape(128, 128)
    own = cot[...].astype(F32).T.astype(BF16)
    to_next[128:144] = own
    to_previous[128:144] = own
    own_cot[...] = own
    leaving[1].start()
    for copy in leaving:
        copy.wait()


def lay_weights1(taps, out):
    group = lane((16, 128)) // 32
    zero = jnp.zeros((16, 128), F32)
    for py in range(4):
        for px in range(4):
            at = (py * 4 + px) * 16
            for qy in range(2):
                dy = py - qy
                sides = [
                    taps[(px - qx) * 3 + dy] if 0 <= dy < 3 and 0 <= px - qx < 3 else zero for qx in range(2)
                ]
                value = jnp.where(group == 0, sides[0], sides[1])
                shifted = jnp.where(group == 2, roll(sides[0], 4, 0), roll(sides[1], 4, 0))
                out[at : at + 16, qy * 128 : qy * 128 + 128] = jnp.where(group < 2, value, shifted).astype(BF16)


def lay_weights2(taps, out):
    zero = jnp.zeros((32, 64), BF16)
    for dy in range(3):
        out[dy, 384:512, 0:128] = jnp.zeros((128, 128), BF16)
        out[dy, 0:128, 128:256] = jnp.zeros((128, 128), BF16)
        for dz in range(3):
            for px in range(4):
                sides = [taps[(px - qx) * 9 + dy * 3 + dz] if 0 <= px - qx < 3 else zero for qx in range(2)]
                tile = jnp.concatenate(sides, axis=1)
                for qz in range(2):
                    at = (dz + qz) * 128 + px * 32
                    out[dy, at : at + 32, qz * 128 : qz * 128 + 128] = tile


def lay_weights3(taps, out):
    zero = jnp.zeros((64, 128), BF16)
    for tap in range(9):
        out[tap, 192:256, 0:128] = zero
        out[tap, 0:64, 128:256] = zero
        for dx in range(3):
            value = taps[dx * 9 + tap]
            out[tap, dx * 64 : dx * 64 + 64, 0:128] = value
            out[tap, dx * 64 + 64 : dx * 64 + 128, 128:256] = value


def run_forward(*operands):
    kept = (
        jax.ShapeDtypeStruct((4, 4, 16, 128), BF16),
        jax.ShapeDtypeStruct((16, 128), BF16),
        jax.ShapeDtypeStruct((8, 4, 32, 256), F32),
        jax.ShapeDtypeStruct((6, 6, 32, 128), BF16),
        jax.ShapeDtypeStruct((4, 256, 256), F32),
        jax.ShapeDtypeStruct((10, 64, 256), BF16),
        jax.ShapeDtypeStruct((3, 512, 256), BF16),
    )
    return pl.pallas_call(
        forward_kernel,
        name="forward",
        out_shape=(jax.ShapeDtypeStruct((144, 128), BF16),) * 2 + kept,
        in_specs=[HBM] * len(operands),
        out_specs=(VMEM,) * 2 + (HBM,) * 7,
        scratch_shapes=landing(operands)
        + landing(kept)
        + [
            pltpu.VMEM((256, 256), BF16),
            pltpu.VMEM((22, 80, 256), BF16),
            pltpu.VMEM((22, 64, 640), BF16),
            pltpu.VMEM((10, 10, 80, 128), F32),
            pltpu.VMEM((10, 10, 32, 128), BF16),
            pltpu.VMEM((8, 4, 32, 256), F32),
            pltpu.VMEM((4, 32, 128), F32),
            pltpu.SemaphoreType.DMA((9,)),
            pltpu.SemaphoreType.DMA((7,)),
        ],
        compiler_params=pltpu.CompilerParams(vmem_limit_bytes=LIMIT),
    )(*operands)


def weave_kernel(lower, hidden2, upper, own_cot, to_next, to_previous, sems):
    pairs = []
    for target, first_row in ((to_next, 0), (to_previous, 2)):
        for y in range(2):
            row, at = first_row + y, y * 128
            pairs.append((lower.at[pl.ds(row * 32, 32)], target.at[pl.ds(at, 32)]))
            for z in range(4):
                pairs.append((hidden2.at[row, z], target.at[pl.ds(at + 32 + 16 * z, 16)]))
            pairs.append((upper.at[pl.ds(row * 32, 32)], target.at[pl.ds(at + 96, 32)]))
        pairs.append((lower.at[pl.ds(128, 16)], target.at[pl.ds(256, 16)]))
        pairs.append((own_cot, target.at[pl.ds(272, 16)]))
        pairs.append((upper.at[pl.ds(128, 16)], target.at[pl.ds(288, 16)]))
    for copy in fetch(*zip(*pairs), sems):
        copy.wait()


def run_weave(*operands):
    return pl.pallas_call(
        weave_kernel,
        name="weave",
        out_shape=(jax.ShapeDtypeStruct((304, 128), BF16),) * 2,
        in_specs=[HBM] * 4,
        out_specs=(HBM,) * 2,
        scratch_shapes=[pltpu.SemaphoreType.DMA((30,))],
    )(*operands)


def backward_kernel(*refs):
    sources, packed, refs = refs[:13], refs[13], refs[14:]
    landed, refs = refs[:13], refs[13:]
    k3, b3, lower, middle, upper, own_cot, before, after, ratio2, w2, patches1, ratio1, fields = landed
    w3, patches2, pre3, delta3, patch2, grad2, delta2, patch1, grad1, delta1, turned, in_sems = refs
    copies = fetch(sources, landed, in_sems)
    rows_y, groups = packed.shape[0], packed.shape[1]
    wide = 128 // groups
    for k in range(2):
        copies[k].wait()
    lay_weights3(k3, w3)
    for k in range(2, 8):
        copies[k].wait()
    bias3_in = jnp.concatenate([b3[...]] * 2, axis=1)
    half = lane((16, 128)) < 64

    def lay(y, source):
        for z in range(8):
            swapped = roll(source(z).astype(F32), 64, 1)
            patches2[y, z] = jnp.concatenate(
                [jnp.where(half, down(swapped), swapped), jnp.where(half, swapped, up(swapped))], axis=1
            ).astype(BF16)

    for y in range(2):
        lay(y, lambda z: before[(y * 8 + z) * 16 : (y * 8 + z + 1) * 16])
        lay(y + 6, lambda z: after[(y * 8 + z) * 16 : (y * 8 + z + 1) * 16])

    def pick_middle(y, z):
        if z < 2:
            return lower[(y * 2 + z) * 16 : (y * 2 + z + 1) * 16]
        if z < 6:
            return middle[y, z - 2]
        return upper[(y * 2 + z - 6) * 16 : (y * 2 + z - 5) * 16]

    for y in range(4):
        lay(y + 2, functools.partial(pick_middle, y))

    for tap in range(9):
        dy, dz = tap // 3, tap % 3
        block = patches2[dy : dy + 6, dz : dz + 6].reshape(576, 256)
        term = dot(block, w3[tap]).reshape(6, 6, 16, 256)
        pre3[...] = term + bias3_in if tap == 0 else pre3[...] + term

    for wy in range(3):
        for wz in range(3):
            pre = pre3[2 * wy : 2 * wy + 2, 2 * wz : 2 * wz + 2]
            e = exps(pre)
            total = e[0, 0] + e[0, 1] + e[1, 0] + e[1, 1]
            total = total[:, :128] + total[:, 128:]
            mean = total * 0.125
            if wy == 1:
                cot = own_cot[...] if wz == 1 else (lower if wz == 0 else upper)[128:144]
            else:
                cot = (before if wy == 0 else after)[256 + wz * 16 : 272 + wz * 16]
            share = cot.astype(F32) * (0.125 / mean)
            share = jnp.concatenate([share, share], axis=1)
            delta3[2 * wy : 2 * wy + 2, 2 * wz : 2 * wz + 2] = (
                jnp.where(pre > 0, 1.0, SLOPE) * (e * share)
            ).astype(BF16)
            if wy == 1 and wz == 1:
                features = rounded(jnp.log(mean) * 0.5)

    own3 = delta3[2:4, 2:4].reshape(64, 256)
    bias3 = own3.astype(F32).sum(axis=0, keepdims=True)
    bias3 = bias3[:, :128] + bias3[:, 128:]
    low, high = [], []
    for tap in range(9):
        dy, dz = tap // 3, tap % 3
        block = patches2[dy + 2 : dy + 4, dz + 2 : dz + 4].reshape(64, 256)
        full = dot_tn(own3, block)
        one = full[:128]
        low_lanes, high_lanes = roll(full[128:, :128], 64, 1), roll(full[128:, 128:], 64, 1)
        tile0 = jnp.where(lane((128, 128)) < 64, low_lanes, high_lanes)
        tile1 = high_lanes
        low.append(one[:, :128] + tile0)
        high.append(one[:, 128:] + tile1)
    first_half = lane((128, 128)) < 64
    paired = []
    for m in range(5):
        other = roll(high[2 * m + 1], 64, 1) if 2 * m + 1 < 9 else jnp.zeros((128, 128), F32)
        paired.append(jnp.where(first_half, high[2 * m], other))
    kernel3 = [piece.reshape(groups, wide, 128) for piece in low + paired]

    for tap in range(9):
        dy, dz = tap // 3, tap % 3
        block = delta3[2 - dy : 6 - dy, 2 - dz : 6 - dz].reshape(256, 256)
        term = dot_nt(block, w3[tap]).reshape(4, 4, 16, 256)
        patch2[...] = term if tap == 0 else patch2[...] + term

    for y in range(4):
        for z in range(4):
            a, b = patch2[y, z, :, :128], patch2[y, z, :, 128:]
            x = rounded(jnp.where(half, b + up(a), a + down(b)))
            swapped = roll(x, 64, 1)
            grad2[y, z, pl.ds(0, 16, stride=2), :] = jnp.where(half, swapped, x)
            grad2[y, z, pl.ds(1, 16, stride=2), :] = jnp.where(half, x, swapped)

    copies[8].wait()
    for y in range(6):
        value = grad2[(y + 1) // 2]
        value = jnp.concatenate([value, value], axis=2)
        delta2[y] = (value * ratio2[y + 1]).astype(BF16)

    own2 = delta2[1:5, 1:3].reshape(256, 256)
    bias2 = own2.astype(F32).sum(axis=0, keepdims=True)
    bias2 = bias2[:, :128] + bias2[:, 128:]
    bias2 = bias2 + roll(bias2, 64, 1)
    copies[9].wait()
    copies[10].wait()
    taps = [None] * 27
    for dy in range(3):
        block = jnp.concatenate(
            [
                jnp.concatenate([patches1[dy : dy + 4, 2 * zo + pz] for pz in range(4)], axis=2)[:, None]
                for zo in range(2)
            ],
            axis=1,
        ).reshape(256, 512)
        full = dot_tn(block, own2)
        for dz in range(3):
            rows = full[dz * 128 : dz * 128 + 128, :128] + full[dz * 128 + 128 : dz * 128 + 256, 128:]
            for dx in range(3):
                taps[dx * 9 + dy * 3 + dz] = rows[dx * 32 : dx * 32 + 32] + roll(
                    rows[dx * 32 + 32 : dx * 32 + 64], 64, 1
                )
    for dy in range(3):
        block = delta2[2 - dy : 6 - dy].reshape(512, 256)
        term = dot_nt(block, w2[dy]).reshape(4, 4, 32, 512)
        patch1[...] = term if dy == 0 else patch1[...] + term

    low_half = lane((32, 128)) < 64
    group = lane((32, 128)) // 32

    def widen(value, which):
        value = jnp.where(group == which, value, 0.0)
        value = value + roll(value, 32, 1)
        return value + roll(value, 64, 1)

    copies[11].wait()
    copies[12].wait()

    def gather1(y, carry):
        for z, (zo_a, pz_a, zo_b, pz_b) in enumerate(((0, 3, 1, 1), (1, 2, 2, 0), (1, 3, 2, 1), (2, 2, 3, 0))):
            value = (
                patch1[y, zo_a, :, pz_a * 128 : pz_a * 128 + 128]
                + patch1[y, zo_b, :, pz_b * 128 : pz_b * 128 + 128]
            )
            value = rounded(value + roll(jnp.where(low_half, up(value), down(value)), 64, 1))
            grad1[z, pl.ds(0, 32, stride=2), :] = widen(value, 1)
            grad1[z, pl.ds(1, 32, stride=2), :] = widen(value, 2)
        value = grad1[...].reshape(256, 128)
        value = jnp.concatenate([value, value], axis=1)
        delta1[y] = (value * ratio1[y]).astype(BF16)
        return carry

    lax.fori_loop(0, 4, gather1, 0)

    bias1 = delta1[...].astype(F32).sum(axis=0).sum(axis=0, keepdims=True)
    bias1 = bias1[:, :128] + bias1[:, 128:]
    bias1 = bias1 + roll(bias1, 64, 1)
    bias1 = bias1 + roll(bias1, 32, 1)
    full = None
    for yw in range(4):
        term = dot(fields[2 * yw : 2 * yw + 4].reshape(256, 256), delta1[yw])
        full = term if full is None else full + term
    full = full.reshape(4, 4, 16, 256)
    kernel1 = []
    for dy in range(3):
        rows = full[dy, :, :, :128] + full[dy + 1, :, :, 128:]
        for dx in range(3):
            value = rows[dx] + roll(rows[dx + 1], 96, 1)
            kernel1.append(value + roll(roll(value, 12, 0), 64, 1))

    biases = jnp.concatenate(
        [bias3, jnp.where(lane((1, 128)) < 64, bias2, bias1), jnp.zeros((14, 128), F32)], axis=0
    )
    shared = jnp.concatenate(taps + kernel1 + [biases], axis=0)
    count = rows_y * groups
    shared = shared.reshape(rows_y, groups, 1024 // count, 128)

    turned[...] = jnp.concatenate([features, jnp.zeros((112, 128), F32)], axis=0).T
    feature_rows = turned[pl.ds(0, 16, stride=8), :]
    for c in range(1, 8):
        feature_rows = feature_rows + roll(turned[pl.ds(c, 16, stride=8), :], 16 * c, 1)
    feature_rows = feature_rows.reshape(groups, wide // 8, 128)

    kernel3 = jnp.concatenate(kernel3, axis=1)
    share = 14 * wide // rows_y
    used = 1024 // count + share + wide // 8
    fill = jnp.zeros((groups, packed.shape[2] - used, 128), F32)
    for a in range(rows_y):
        own = kernel3[:, a * share : a * share + share]
        packed[a] = jnp.concatenate([shared[a], own, feature_rows, fill], axis=1).astype(BF16)


def packed_rows(rows_y, groups):
    wide = 128 // groups
    used = 1024 // (rows_y * groups) + 14 * wide // rows_y + wide // 8
    return -(-used // 8) * 8


def run_backward(rows_y, groups, *operands):
    return pl.pallas_call(
        backward_kernel,
        name="backward",
        out_shape=jax.ShapeDtypeStruct((rows_y, groups, packed_rows(rows_y, groups), 128), BF16),
        in_specs=[HBM] * len(operands),
        out_specs=VMEM,
        scratch_shapes=landing(operands)
        + [
            pltpu.VMEM((9, 256, 256), BF16),
            pltpu.VMEM((8, 8, 16, 256), BF16),
            pltpu.VMEM((6, 6, 16, 256), F32),
            pltpu.VMEM((6, 6, 16, 256), BF16),
            pltpu.VMEM((4, 4, 16, 256), F32),
            pltpu.VMEM((4, 4, 32, 128), F32),
            pltpu.VMEM((6, 4, 32, 256), BF16),
            pltpu.VMEM((4, 4, 32, 512), F32),
            pltpu.VMEM((4, 64, 128), F32),
            pltpu.VMEM((4, 256, 256), BF16),
            pltpu.VMEM((128, 128), F32),
            pltpu.SemaphoreType.DMA((13,)),
        ],
        compiler_params=pltpu.CompilerParams(vmem_limit_bytes=LIMIT),
    )(*operands)


def sum_kernel(source, to_column, to_all, features, landed, shown, sems):
    rows_y = to_column.shape[0]
    count, shared = to_all.shape[0], to_all.shape[1]
    groups = count // rows_y
    wide = 128 // groups
    share = 14 * wide // rows_y
    parts = sems.shape[0] - 1
    size = count // parts
    copies = fetch(
        [source.at[pl.ds(k * size, size)] for k in range(parts)],
        [landed.at[pl.ds(k * size, size)] for k in range(parts)],
        sems,
    )
    total = None
    for k in range(parts):
        copies[k].wait()
        term = landed[k * size : k * size + size].astype(F32).sum(axis=0)
        total = term if total is None else total + term
    total = total.astype(BF16).astype(F32)
    to_all[...] = jnp.broadcast_to(total[None, :shared], to_all.shape).astype(BF16)
    fill = jnp.zeros((to_column.shape[1] - share, 128), F32)
    column = jnp.concatenate([total[shared : shared + share], fill], axis=0)
    to_column[...] = jnp.broadcast_to(column[None], to_column.shape).astype(BF16)
    own = landed[pl.ds(lax.axis_index("gy") * groups, groups)].astype(F32)
    for c in range(wide):
        shown[c] = own[:, shared + share + c // 8, (c % 8) * 16 : (c % 8) * 16 + 16].astype(BF16)
    last = pltpu.make_async_copy(shown, features, sems.at[parts])
    last.start()
    last.wait()


def run_sum(received, rows_y, groups):
    count, wide = rows_y * groups, 128 // groups
    share = -(-(14 * wide // rows_y) // 16) * 16
    return pl.pallas_call(
        sum_kernel,
        name="sum",
        out_shape=(
            jax.ShapeDtypeStruct((rows_y, share, 128), BF16),
            jax.ShapeDtypeStruct((count, 1024 // count, 128), BF16),
            jax.ShapeDtypeStruct((wide, groups, 16), BF16),
        ),
        in_specs=[HBM],
        out_specs=(VMEM, VMEM, HBM),
        scratch_shapes=[
            pltpu.VMEM(received.shape, BF16),
            pltpu.VMEM((wide, groups, 16), BF16),
            pltpu.SemaphoreType.DMA((5,)),
        ],
    )(received)


def unpack_kernel(column_in, shared_in, grad1, grad2, grad3, shift1, shift2, shift3, column, shared, lines, sems):
    copies = fetch((column_in, shared_in), (column, shared), sems)
    rows_y, count = column.shape[0], shared.shape[0]
    wide = grad3.shape[1]
    share = 14 * wide // rows_y
    copies[0].wait()
    for a in range(rows_y):
        lines[a * share : a * share + share] = column[a].astype(F32)[:share]
    for tap in range(9):
        low = lines[tap * wide : tap * wide + wide]
        grad3[tap] = low[:, :64]
        grad3[9 + tap] = low[:, 64:]
        at = (9 + tap // 2) * wide
        grad3[18 + tap] = lines[at : at + wide][:, (tap % 2) * 64 : (tap % 2) * 64 + 64]
    copies[1].wait()
    rows = shared[...].astype(F32).reshape(1024, 128)
    for tap in range(27):
        grad2[tap] = rows[tap * 32 : tap * 32 + 32, :64]
    for dy in range(3):
        for dx in range(3):
            at = 864 + (dy * 3 + dx) * 16
            for dz in range(3):
                grad1[dx * 9 + dy * 3 + dz] = rows[at + dz * 4 : at + dz * 4 + 4, :32]
    biases = rows[1008:1016]
    shift1[...] = biases[1:2, 64:96]
    shift2[...] = biases[1:2, :64]
    place = lax.axis_index("gz")
    shift3[...] = roll(biases, lax.rem(128 - place * wide, 128), 1)[0:1, :wide]


def run_unpack(column, shared, wide):
    return pl.pallas_call(
        unpack_kernel,
        name="unpack",
        out_shape=(
            jax.ShapeDtypeStruct((27, 4, 32), F32),
            jax.ShapeDtypeStruct((27, 32, 64), F32),
            jax.ShapeDtypeStruct((27, wide, 64), F32),
            jax.ShapeDtypeStruct((1, 32), F32),
            jax.ShapeDtypeStruct((1, 64), F32),
            jax.ShapeDtypeStruct((1, wide), F32),
        ),
        in_specs=[HBM] * 2,
        out_specs=(VMEM,) * 6,
        scratch_shapes=[
            pltpu.VMEM(column.shape, BF16),
            pltpu.VMEM(shared.shape, BF16),
            pltpu.VMEM((14 * wide, 128), F32),
            pltpu.SemaphoreType.DMA((2,)),
        ],
    )(column, shared)


def pick_matrix():
    out = np.zeros((2, 128, 4, 2, 64), np.float32)
    for px in range(4):
        for w in range(64):
            x = 2 * w - 1 + px
            if 0 <= x < 128:
                for h in range(2):
                    out[h, x, px, h, w] = 1
    return out.reshape(256, 512).astype(jnp.bfloat16)


def both_ways(to_next, to_previous, axis):
    devices = lax.axis_size(axis)
    forth = [(i, i + 1) for i in range(devices - 1)]
    back = [(i + 1, i) for i in range(devices - 1)]
    return lax.ppermute(to_next, axis, forth), lax.ppermute(to_previous, axis, back)


def shards(universe, kernel1, bias1, kernel2, bias2, kernel3, bias3, cotangent):
    size_y, size_z = lax.axis_size("gy"), lax.axis_size("gz")
    wide = 128 // size_z

    tile = universe.transpose(1, 2, 0, 3).reshape(8, 32, 128)
    lower, upper = both_ways(tile, tile, "gz")
    strip = jnp.concatenate([lower[:, 4:], tile, upper[:, :28], jnp.zeros((8, 8, 128), BF16)], axis=1)
    top, bottom = both_ways(strip, strip, "gy")

    cotangent, strip = lax.optimization_barrier((cotangent, strip))
    cot = lax.all_to_all(cotangent[:, 0].transpose(1, 0, 2), "gz", 0, 0, tiled=True).reshape(128, 16)
    k1 = kernel1.transpose(0, 2, 1).reshape(9, 12, 32).astype(F32)
    k1 = jnp.tile(jnp.pad(k1, ((0, 0), (0, 4), (0, 0))), (1, 1, 4))
    k2, k3 = kernel2.transpose(0, 2, 1), kernel3.transpose(0, 2, 1)

    to_next, to_previous, hidden2, own_cot, ratio2, patches1, ratio1, fields, w2 = run_forward(
        top, strip, bottom, cot, jnp.asarray(pick_matrix()), k1, bias1[None], k2, bias2[None]
    )
    lower, upper = both_ways(to_next, to_previous, "gz")
    row_next, row_previous = run_weave(lower, hidden2, upper, own_cot)
    before, after = both_ways(row_next, row_previous, "gy")
    packed = run_backward(
        size_y, size_z,
        k3, bias3[None], lower, hidden2, upper, own_cot, before, after, ratio2, w2, patches1, ratio1, fields,
    )
    packed = packed.reshape((size_y * size_z,) + packed.shape[2:])
    packed = lax.all_to_all(packed, ("gy", "gz"), 0, 0, tiled=True)
    to_column, to_all, features = run_sum(packed, size_y, size_z)
    to_column = lax.all_to_all(to_column, "gy", 0, 0, tiled=True)
    to_all = lax.all_to_all(to_all, ("gy", "gz"), 0, 0, tiled=True)
    grad1, grad2, grad3, shift1, shift2, shift3 = run_unpack(to_column, to_all, wide)
    return (
        features[:, None], grad1.transpose(0, 2, 1), shift1[0], grad2.transpose(0, 2, 1), shift2[0], grad3, shift3[0]
    )


def solution(mesh):
    in_specs = (P(None, "gy", "gz", None), P(), P(), P(), P(), P(), P(), P("gz", "gy", None, None))
    out_specs = (P("gz", "gy", None, None), P(), P(), P(), P(), P(None, "gz", None), P("gz"))
    return jax.shard_map(shards, mesh=mesh, in_specs=in_specs, out_specs=out_specs, check_vma=False)
```

```python
import functools

import jax
import jax.numpy as jnp
import numpy as np
from jax import lax
from jax.experimental import pallas as pl
from jax.experimental.pallas import tpu as pltpu
from jax.sharding import PartitionSpec as P

F32 = jnp.float32
BF16 = jnp.bfloat16
SLOPE = 0.3
PAIRS = ((0, 1), (2, 3), (-3, -2), (4, 5), (-1, 6))
VMEM = pl.BlockSpec(memory_space=pltpu.VMEM)
LIMIT = 24 * 1024 * 1024


def dot(a, b):
    return jnp.dot(a, b, preferred_element_type=F32)


def dot_tn(a, b):
    return lax.dot_general(a, b, (((0,), (0,)), ((), ())), preferred_element_type=F32)


def dot_nt(a, b):
    return lax.dot_general(a, b, (((1,), (1,)), ((), ())), preferred_element_type=F32)


def lane(shape):
    return lax.broadcasted_iota(jnp.int32, shape, len(shape) - 1)


def exps(pre):
    return jnp.exp(2.0 * jnp.maximum(pre, SLOPE * pre))


def rounded(value):
    return value.astype(BF16).astype(F32)


def roll(value, amount, axis):
    return pltpu.roll(value, amount, axis)


def down(value):
    rows = lax.broadcasted_iota(jnp.int32, value.shape, 0)
    return jnp.where(rows == 0, 0.0, roll(value, 1, 0))


def up(value):
    count = value.shape[0]
    rows = lax.broadcasted_iota(jnp.int32, value.shape, 0)
    return jnp.where(rows == count - 1, 0.0, roll(value, count - 1, 0))


def forward_kernel(*refs):
    (top, mid, bot, cot, pick, k1, b1, k2, b2), refs = refs[:9], refs[9:]
    (to_next, to_previous, hidden2, own_cot, ratio2, patches1, ratio1, fields, w2), refs = refs[:9], refs[9:]
    w1, left, field, first, spread, pre2, second = refs
    lay_weights1(k1, w1)
    lay_weights2(k2, w2)
    bias1 = jnp.concatenate([b1[...]] * 8, axis=1)
    bias2 = jnp.concatenate([b2[...]] * 4, axis=1)
    base_y, base_z = lax.axis_index("gy"), lax.axis_index("gz")
    size_y, size_z = lax.axis_size("gy"), lax.axis_size("gz")

    def inside(offset_y, offset_z, scale):
        row = base_y * (4 // scale) + offset_y
        col = base_z * (4 // scale) + offset_z
        ok_y = (row >= 0) & (row < size_y * (4 // scale))
        ok_z = (col >= 0) & (col < size_z * (4 // scale))
        return jnp.where(ok_y & ok_z, 1.0, 0.0)

    def lay(source, index, target):
        rows = source[index].astype(F32)
        pieces = []
        for one, two in PAIRS:
            a, b = 8 * (one + 3), 8 * (two + 3)
            pieces.append(jnp.concatenate([rows[a : a + 16], rows[b : b + 16]], axis=1))
        left[target] = jnp.concatenate(pieces, axis=0).astype(BF16)

    def lay_top(step, carry):
        lay(top, step + 1, step)
        return carry

    def lay_mid(step, carry):
        lay(mid, step, step + 7)
        return carry

    def lay_bot(step, carry):
        lay(bot, step, step + 15)
        return carry

    lax.fori_loop(0, 7, lay_top, 0)
    lax.fori_loop(0, 8, lay_mid, 0)
    lax.fori_loop(0, 7, lay_bot, 0)

    def sift(step, carry):
        block = left[pl.ds(2 * step, 2)].reshape(160, 256)
        out = dot(block, pick[...]).astype(BF16).reshape(2, 5, 16, 512)
        for px in range(4):
            for k in range(5):
                field[pl.ds(2 * step, 2), px * 16 : px * 16 + 16, k * 128 : k * 128 + 128] = out[
                    :, k, :, px * 128 : px * 128 + 128
                ]
        return carry

    lax.fori_loop(0, 11, sift, 0)
    fields[...] = field[6:16, :, :256]
    first[:, :, 0:8] = jnp.zeros((10, 10, 8, 128), F32)
    first[:, :, 72:80] = jnp.zeros((10, 10, 8, 128), F32)

    def block1(yw, carry):
        stack = field[pl.ds(2 * yw, 4)].reshape(256, 640)
        pre = dot_tn(stack, w1[...]) + bias1
        e = exps(pre)
        total = e[:, :128] + e[:, 128:]
        total = total + roll(total, 64, 1)
        total = total + roll(total, 32, 1)
        mean = total * 0.125
        pooled = rounded(jnp.log(mean) * 0.5)
        for k, pair in enumerate(PAIRS):
            for h, zw in enumerate(pair):
                at = k * 128 + h * 64
                first[yw, zw + 3, 8:72] = pooled[at : at + 64] * inside(yw - 3, zw, 1)

        @pl.when((yw >= 3) & (yw < 7))
        def _():
            share = 0.125 / mean[:256]
            share = jnp.concatenate([share, share], axis=1)
            ratio1[yw - 3] = jnp.where(pre[:256] > 0, 1.0, SLOPE) * (e[:256] * share)

        return carry

    lax.fori_loop(0, 10, block1, 0)

    group1 = lane((32, 128)) // 32

    def frame(yi, carry):
        for zi in range(10):
            part = first[yi, zi, pl.ds(7, 32, stride=2), :]
            for px in range(1, 4):
                part = jnp.where(group1 == px, first[yi, zi, pl.ds(7 + px, 32, stride=2), :], part)
            spread[yi, zi] = part.astype(BF16)
        return carry

    lax.fori_loop(0, 10, frame, 0)
    patches1[...] = spread[2:8, 2:8]

    for dy in range(3):
        block = jnp.concatenate(
            [
                jnp.concatenate([spread[dy : dy + 8, 2 * zo + pz] for pz in range(4)], axis=2)[:, None]
                for zo in range(4)
            ],
            axis=1,
        ).reshape(1024, 512)
        term = dot(block, w2[dy]).reshape(8, 4, 32, 256)
        pre2[...] = term + bias2 if dy == 0 else pre2[...] + term

    half = lane((16, 128)) < 64

    def block2(yp, carry):
        pre = pre2[pl.ds(2 * yp, 2)]
        e = exps(pre)
        both = e[0] + e[1]
        total = (both[:, :, :128] + both[:, :, 128:]).reshape(128, 128)
        total = total + roll(total, 64, 1)
        mean = total * 0.125
        pooled = rounded(jnp.log(mean) * 0.5).reshape(4, 32, 128)
        share = (0.125 / mean).reshape(4, 32, 128)
        share = jnp.concatenate([share, share], axis=2)
        scaled = jnp.where(pre > 0, 1.0, SLOPE) * (e * share[None])
        for zo in range(4):
            ok = inside(yp - 1, zo - 1, 2)
            ratio2[pl.ds(2 * yp, 2), zo] = scaled[:, zo] * ok
            second[zo] = pooled[zo] * ok
            even = second[zo, pl.ds(0, 16, stride=2), :]
            odd = second[zo, pl.ds(1, 16, stride=2), :]
            hidden2[yp, zo] = jnp.where(half, even, odd).astype(BF16)
        return carry

    lax.fori_loop(0, 4, block2, 0)
    to_next[0:128] = hidden2[:, 0:2].reshape(128, 128)
    to_previous[0:128] = hidden2[:, 2:4].reshape(128, 128)
    own = cot[...].astype(F32).T.astype(BF16)
    to_next[128:144] = own
    to_previous[128:144] = own
    own_cot[...] = own


def lay_weights1(taps, out):
    group = lane((16, 128)) // 32
    zero = jnp.zeros((16, 128), F32)
    wide = []
    for k in range(9):
        pieces = [taps[3 * k + dz].astype(F32) for dz in range(3)] + [jnp.zeros((4, 32), F32)]
        rows = jnp.concatenate(pieces, axis=0)
        wide.append(jnp.concatenate([rows] * 4, axis=1))
    for py in range(4):
        for px in range(4):
            at = (py * 4 + px) * 16
            for qy in range(2):
                dy = py - qy
                sides = [
                    wide[(px - qx) * 3 + dy] if 0 <= dy < 3 and 0 <= px - qx < 3 else zero for qx in range(2)
                ]
                value = jnp.where(group == 0, sides[0], sides[1])
                shifted = jnp.where(group == 2, roll(sides[0], 4, 0), roll(sides[1], 4, 0))
                out[at : at + 16, qy * 128 : qy * 128 + 128] = jnp.where(group < 2, value, shifted).astype(BF16)


def lay_weights2(taps, out):
    zero = jnp.zeros((32, 64), BF16)
    for dy in range(3):
        out[dy, 384:512, 0:128] = jnp.zeros((128, 128), BF16)
        out[dy, 0:128, 128:256] = jnp.zeros((128, 128), BF16)
        for dz in range(3):
            for px in range(4):
                sides = [taps[(px - qx) * 9 + dy * 3 + dz] if 0 <= px - qx < 3 else zero for qx in range(2)]
                tile = jnp.concatenate(sides, axis=1)
                for qz in range(2):
                    at = (dz + qz) * 128 + px * 32
                    out[dy, at : at + 32, qz * 128 : qz * 128 + 128] = tile


def lay_weights3(taps, out):
    zero = jnp.zeros((64, 128), BF16)
    for tap in range(9):
        out[tap, 192:256, 0:128] = zero
        out[tap, 0:64, 128:256] = zero
        for dx in range(3):
            value = taps[dx * 9 + tap]
            out[tap, dx * 64 : dx * 64 + 64, 0:128] = value
            out[tap, dx * 64 + 64 : dx * 64 + 128, 128:256] = value


def run_forward(*operands):
    kept = (
        jax.ShapeDtypeStruct((4, 4, 16, 128), BF16),
        jax.ShapeDtypeStruct((16, 128), BF16),
        jax.ShapeDtypeStruct((8, 4, 32, 256), F32),
        jax.ShapeDtypeStruct((6, 6, 32, 128), BF16),
        jax.ShapeDtypeStruct((4, 256, 256), F32),
        jax.ShapeDtypeStruct((10, 64, 256), BF16),
        jax.ShapeDtypeStruct((3, 512, 256), BF16),
    )
    return pl.pallas_call(
        forward_kernel,
        name="forward",
        out_shape=(jax.ShapeDtypeStruct((144, 128), BF16),) * 2 + kept,
        in_specs=[VMEM] * len(operands),
        out_specs=(VMEM,) * 9,
        scratch_shapes=[
            pltpu.VMEM((256, 256), BF16),
            pltpu.VMEM((22, 80, 256), BF16),
            pltpu.VMEM((22, 64, 640), BF16),
            pltpu.VMEM((10, 10, 80, 128), F32),
            pltpu.VMEM((10, 10, 32, 128), BF16),
            pltpu.VMEM((8, 4, 32, 256), F32),
            pltpu.VMEM((4, 32, 128), F32),
        ],
        compiler_params=pltpu.CompilerParams(vmem_limit_bytes=LIMIT),
    )(*operands)


def weave_kernel(lower, hidden2, upper, own_cot, to_next, to_previous):
    for target, first_row in ((to_next, 0), (to_previous, 2)):
        for y in range(2):
            row, at = first_row + y, y * 128
            target[at : at + 32] = lower[row * 32 : row * 32 + 32]
            target[at + 32 : at + 96] = hidden2[row].reshape(64, 128)
            target[at + 96 : at + 128] = upper[row * 32 : row * 32 + 32]
        target[256:272] = lower[128:144]
        target[272:288] = own_cot[...]
        target[288:304] = upper[128:144]


def run_weave(*operands):
    return pl.pallas_call(
        weave_kernel,
        name="weave",
        out_shape=(jax.ShapeDtypeStruct((304, 128), BF16),) * 2,
        in_specs=[VMEM] * 4,
        out_specs=(VMEM,) * 2,
        compiler_params=pltpu.CompilerParams(vmem_limit_bytes=LIMIT),
    )(*operands)


def backward_kernel(*refs):
    (k3, b3, lower, middle, upper, own_cot, before, after, ratio2, w2, patches1, ratio1, fields), refs = (
        refs[:13], refs[13:],
    )
    packed, w3, patches2, pre3, delta3, patch2, grad2, delta2, patch1, grad1, delta1, turned = refs
    groups = packed.shape[0]
    wide = 128 // groups
    lay_weights3(k3, w3)
    bias3_in = jnp.concatenate([b3[...]] * 2, axis=1)
    half = lane((16, 128)) < 64

    def lay(y, source):
        for z in range(8):
            swapped = roll(source(z).astype(F32), 64, 1)
            patches2[y, z] = jnp.concatenate(
                [jnp.where(half, down(swapped), swapped), jnp.where(half, swapped, up(swapped))], axis=1
            ).astype(BF16)

    for y in range(2):
        lay(y, lambda z: before[(y * 8 + z) * 16 : (y * 8 + z + 1) * 16])
        lay(y + 6, lambda z: after[(y * 8 + z) * 16 : (y * 8 + z + 1) * 16])

    def pick_middle(y, z):
        if z < 2:
            return lower[(y * 2 + z) * 16 : (y * 2 + z + 1) * 16]
        if z < 6:
            return middle[y, z - 2]
        return upper[(y * 2 + z - 6) * 16 : (y * 2 + z - 5) * 16]

    for y in range(4):
        lay(y + 2, functools.partial(pick_middle, y))

    for tap in range(9):
        dy, dz = tap // 3, tap % 3
        block = patches2[dy : dy + 6, dz : dz + 6].reshape(576, 256)
        term = dot(block, w3[tap]).reshape(6, 6, 16, 256)
        pre3[...] = term + bias3_in if tap == 0 else pre3[...] + term

    for wy in range(3):
        for wz in range(3):
            pre = pre3[2 * wy : 2 * wy + 2, 2 * wz : 2 * wz + 2]
            e = exps(pre)
            total = e[0, 0] + e[0, 1] + e[1, 0] + e[1, 1]
            total = total[:, :128] + total[:, 128:]
            mean = total * 0.125
            if wy == 1:
                cot = own_cot[...] if wz == 1 else (lower if wz == 0 else upper)[128:144]
            else:
                cot = (before if wy == 0 else after)[256 + wz * 16 : 272 + wz * 16]
            share = cot.astype(F32) * (0.125 / mean)
            share = jnp.concatenate([share, share], axis=1)
            delta3[2 * wy : 2 * wy + 2, 2 * wz : 2 * wz + 2] = (
                jnp.where(pre > 0, 1.0, SLOPE) * (e * share)
            ).astype(BF16)
            if wy == 1 and wz == 1:
                features = rounded(jnp.log(mean) * 0.5)

    own3 = delta3[2:4, 2:4].reshape(64, 256)
    bias3 = own3.astype(F32).sum(axis=0, keepdims=True)
    bias3 = bias3[:, :128] + bias3[:, 128:]
    low, high = [], []
    for tap in range(9):
        dy, dz = tap // 3, tap % 3
        block = patches2[dy + 2 : dy + 4, dz + 2 : dz + 4].reshape(64, 256)
        full = dot_tn(own3, block)
        one = full[:128]
        low_lanes, high_lanes = roll(full[128:, :128], 64, 1), roll(full[128:, 128:], 64, 1)
        tile0 = jnp.where(lane((128, 128)) < 64, low_lanes, high_lanes)
        tile1 = high_lanes
        low.append(one[:, :128] + tile0)
        high.append(one[:, 128:] + tile1)
    first_half = lane((128, 128)) < 64
    paired = []
    for m in range(5):
        other = roll(high[2 * m + 1], 64, 1) if 2 * m + 1 < 9 else jnp.zeros((128, 128), F32)
        paired.append(jnp.where(first_half, high[2 * m], other))
    kernel3 = [piece.reshape(groups, wide, 128) for piece in low + paired]

    for tap in range(9):
        dy, dz = tap // 3, tap % 3
        block = delta3[2 - dy : 6 - dy, 2 - dz : 6 - dz].reshape(256, 256)
        term = dot_nt(block, w3[tap]).reshape(4, 4, 16, 256)
        patch2[...] = term if tap == 0 else patch2[...] + term

    for y in range(4):
        for z in range(4):
            a, b = patch2[y, z, :, :128], patch2[y, z, :, 128:]
            x = rounded(jnp.where(half, b + up(a), a + down(b)))
            swapped = roll(x, 64, 1)
            grad2[y, z, pl.ds(0, 16, stride=2), :] = jnp.where(half, swapped, x)
            grad2[y, z, pl.ds(1, 16, stride=2), :] = jnp.where(half, x, swapped)

    for y in range(6):
        value = grad2[(y + 1) // 2]
        value = jnp.concatenate([value, value], axis=2)
        delta2[y] = (value * ratio2[y + 1]).astype(BF16)

    own2 = delta2[1:5, 1:3].reshape(256, 256)
    bias2 = own2.astype(F32).sum(axis=0, keepdims=True)
    bias2 = bias2[:, :128] + bias2[:, 128:]
    bias2 = bias2 + roll(bias2, 64, 1)
    taps = [None] * 27
    for dy in range(3):
        block = jnp.concatenate(
            [
                jnp.concatenate([patches1[dy : dy + 4, 2 * zo + pz] for pz in range(4)], axis=2)[:, None]
                for zo in range(2)
            ],
            axis=1,
        ).reshape(256, 512)
        full = dot_tn(block, own2)
        for dz in range(3):
            rows = full[dz * 128 : dz * 128 + 128, :128] + full[dz * 128 + 128 : dz * 128 + 256, 128:]
            for dx in range(3):
                taps[dx * 9 + dy * 3 + dz] = rows[dx * 32 : dx * 32 + 32] + roll(
                    rows[dx * 32 + 32 : dx * 32 + 64], 64, 1
                )
    for dy in range(3):
        block = delta2[2 - dy : 6 - dy].reshape(512, 256)
        term = dot_nt(block, w2[dy]).reshape(4, 4, 32, 512)
        patch1[...] = term if dy == 0 else patch1[...] + term

    low_half = lane((32, 128)) < 64
    group = lane((32, 128)) // 32

    def widen(value, which):
        value = jnp.where(group == which, value, 0.0)
        value = value + roll(value, 32, 1)
        return value + roll(value, 64, 1)


    def gather1(y, carry):
        for z, (zo_a, pz_a, zo_b, pz_b) in enumerate(((0, 3, 1, 1), (1, 2, 2, 0), (1, 3, 2, 1), (2, 2, 3, 0))):
            value = (
                patch1[y, zo_a, :, pz_a * 128 : pz_a * 128 + 128]
                + patch1[y, zo_b, :, pz_b * 128 : pz_b * 128 + 128]
            )
            value = rounded(value + roll(jnp.where(low_half, up(value), down(value)), 64, 1))
            grad1[z, pl.ds(0, 32, stride=2), :] = widen(value, 1)
            grad1[z, pl.ds(1, 32, stride=2), :] = widen(value, 2)
        value = grad1[...].reshape(256, 128)
        value = jnp.concatenate([value, value], axis=1)
        delta1[y] = (value * ratio1[y]).astype(BF16)
        return carry

    lax.fori_loop(0, 4, gather1, 0)

    bias1 = delta1[...].astype(F32).sum(axis=0).sum(axis=0, keepdims=True)
    bias1 = bias1[:, :128] + bias1[:, 128:]
    bias1 = bias1 + roll(bias1, 64, 1)
    bias1 = bias1 + roll(bias1, 32, 1)
    full = None
    for yw in range(4):
        term = dot(fields[2 * yw : 2 * yw + 4].reshape(256, 256), delta1[yw])
        full = term if full is None else full + term
    full = full.reshape(4, 4, 16, 256)
    kernel1 = []
    group1 = lane((16, 128)) // 32
    for dy in range(3):
        rows = full[dy, :, :, :128] + full[dy + 1, :, :, 128:]
        pieces = []
        for dx in range(3):
            value = rows[dx] + roll(rows[dx + 1], 96, 1)
            value = value + roll(roll(value, 12, 0), 64, 1)
            pieces.append(roll(value, 32 * dx, 1) if dx else value)
        kernel1.append(jnp.where(group1 == 0, pieces[0], jnp.where(group1 == 1, pieces[1], pieces[2])))

    low_lane = lane((32, 128)) < 64
    kernel2 = [
        jnp.where(low_lane, taps[2 * m], roll(taps[2 * m + 1], 64, 1) if 2 * m + 1 < 27 else 0.0)
        for m in range(14)
    ]
    biases = jnp.concatenate(
        [bias3, jnp.where(lane((1, 128)) < 64, bias2, bias1), jnp.zeros((14, 128), F32)], axis=0
    )
    shared = jnp.concatenate(kernel2 + kernel1 + [biases], axis=0).reshape(groups, 512 // groups, 128)

    turned[...] = jnp.concatenate([features, jnp.zeros((112, 128), F32)], axis=0).T
    feature_rows = turned[pl.ds(0, 16, stride=8), :]
    for c in range(1, 8):
        feature_rows = feature_rows + roll(turned[pl.ds(c, 16, stride=8), :], 16 * c, 1)
    feature_rows = feature_rows.reshape(groups, wide // 8, 128)

    fill = jnp.zeros((groups, packed.shape[1] - 512 // groups - 14 * wide - wide // 8, 128), F32)
    packed[...] = jnp.concatenate([shared] + kernel3 + [feature_rows, fill], axis=1).astype(BF16)


def packed_rows(groups):
    wide = 128 // groups
    return -(-(512 // groups + 14 * wide + wide // 8) // 8) * 8


def run_backward(groups, *operands):
    return pl.pallas_call(
        backward_kernel,
        name="backward",
        out_shape=jax.ShapeDtypeStruct((groups, packed_rows(groups), 128), BF16),
        in_specs=[VMEM] * len(operands),
        out_specs=VMEM,
        scratch_shapes=[
            pltpu.VMEM((9, 256, 256), BF16),
            pltpu.VMEM((8, 8, 16, 256), BF16),
            pltpu.VMEM((6, 6, 16, 256), F32),
            pltpu.VMEM((6, 6, 16, 256), BF16),
            pltpu.VMEM((4, 4, 16, 256), F32),
            pltpu.VMEM((4, 4, 32, 128), F32),
            pltpu.VMEM((6, 4, 32, 256), BF16),
            pltpu.VMEM((4, 4, 32, 512), F32),
            pltpu.VMEM((4, 64, 128), F32),
            pltpu.VMEM((4, 256, 256), BF16),
            pltpu.VMEM((128, 128), F32),
        ],
        compiler_params=pltpu.CompilerParams(vmem_limit_bytes=LIMIT),
    )(*operands)


def sum_kernel(received, to_column, features):
    groups, rows = received.shape[0], to_column.shape[1]
    wide = 128 // groups
    own = received[:, rows : rows + wide // 8].astype(F32)
    for c in range(wide):
        features[c] = own[:, c // 8, (c % 8) * 16 : (c % 8) * 16 + 16].astype(BF16)
    total = received[:, :rows].astype(F32).sum(axis=0)
    to_column[...] = jnp.broadcast_to(total[None], to_column.shape).astype(BF16)


def run_sum(received, rows_y):
    groups = received.shape[0]
    wide = 128 // groups
    return pl.pallas_call(
        sum_kernel,
        name="sum",
        out_shape=(
            jax.ShapeDtypeStruct((rows_y, 512 // groups + 14 * wide, 128), BF16),
            jax.ShapeDtypeStruct((wide, groups, 16), BF16),
        ),
        in_specs=[VMEM],
        out_specs=(VMEM, VMEM),
        compiler_params=pltpu.CompilerParams(vmem_limit_bytes=LIMIT),
    )(received)


def share_kernel(column, to_all):
    total = column[:, : to_all.shape[1]].astype(F32).sum(axis=0)
    to_all[...] = jnp.broadcast_to(total[None], to_all.shape).astype(BF16)


def run_share(column, groups):
    return pl.pallas_call(
        share_kernel,
        name="share",
        out_shape=jax.ShapeDtypeStruct((groups, 512 // groups, 128), BF16),
        in_specs=[VMEM],
        out_specs=VMEM,
        compiler_params=pltpu.CompilerParams(vmem_limit_bytes=LIMIT),
    )(column)


def third_kernel(column, grad3):
    wide = grad3.shape[1]
    first = column.shape[1] - 14 * wide
    lines = column[:, first:].astype(F32).sum(axis=0)
    for tap in range(9):
        low = lines[tap * wide : tap * wide + wide]
        grad3[tap] = low[:, :64]
        grad3[9 + tap] = low[:, 64:]
        at = (9 + tap // 2) * wide
        grad3[18 + tap] = lines[at : at + wide][:, (tap % 2) * 64 : (tap % 2) * 64 + 64]


def run_third(column, wide):
    return pl.pallas_call(
        third_kernel,
        name="third",
        out_shape=jax.ShapeDtypeStruct((27, wide, 64), F32),
        in_specs=[VMEM],
        out_specs=VMEM,
        compiler_params=pltpu.CompilerParams(vmem_limit_bytes=LIMIT),
    )(column)


def unpack_kernel(shared, grad1, grad2, shift1, shift2, shift3):
    wide = shift3.shape[1]
    rows = shared[...].astype(F32).reshape(512, 128)
    for tap in range(27):
        at = (tap // 2) * 32
        grad2[tap] = rows[at : at + 32, (tap % 2) * 64 : (tap % 2) * 64 + 64]
    for dy in range(3):
        for dz in range(3):
            at = 448 + dy * 16 + dz * 4
            for dx in range(3):
                grad1[dx * 9 + dy * 3 + dz] = rows[at : at + 4, dx * 32 : dx * 32 + 32]
    biases = rows[496:504]
    shift1[...] = biases[1:2, 64:96]
    shift2[...] = biases[1:2, :64]
    place = lax.axis_index("gz")
    shift3[...] = roll(biases, lax.rem(128 - place * wide, 128), 1)[0:1, :wide]


def run_unpack(shared):
    wide = 128 // shared.shape[0]
    return pl.pallas_call(
        unpack_kernel,
        name="unpack",
        out_shape=(
            jax.ShapeDtypeStruct((27, 4, 32), F32),
            jax.ShapeDtypeStruct((27, 32, 64), F32),
            jax.ShapeDtypeStruct((1, 32), F32),
            jax.ShapeDtypeStruct((1, 64), F32),
            jax.ShapeDtypeStruct((1, wide), F32),
        ),
        in_specs=[VMEM],
        out_specs=(VMEM,) * 5,
        compiler_params=pltpu.CompilerParams(vmem_limit_bytes=LIMIT),
    )(shared)


def pick_matrix():
    out = np.zeros((2, 128, 4, 2, 64), np.float32)
    for px in range(4):
        for w in range(64):
            x = 2 * w - 1 + px
            if 0 <= x < 128:
                for h in range(2):
                    out[h, x, px, h, w] = 1
    return out.reshape(256, 512).astype(jnp.bfloat16)


def both_ways(to_next, to_previous, axis):
    devices = lax.axis_size(axis)
    forth = [(i, i + 1) for i in range(devices - 1)]
    back = [(i + 1, i) for i in range(devices - 1)]
    return lax.ppermute(to_next, axis, forth), lax.ppermute(to_previous, axis, back)


def shards(universe, kernel1, bias1, kernel2, bias2, kernel3, bias3, cotangent):
    size_y, size_z = lax.axis_size("gy"), lax.axis_size("gz")
    wide = 128 // size_z

    tile = universe.transpose(1, 2, 0, 3).reshape(8, 32, 128)
    lower, upper = both_ways(tile, tile, "gz")
    strip = jnp.concatenate([lower[:, 4:], tile, upper[:, :28], jnp.zeros((8, 8, 128), BF16)], axis=1)
    top, bottom = both_ways(strip, strip, "gy")

    cot = lax.all_to_all(cotangent[:, 0].transpose(1, 0, 2), "gz", 0, 0, tiled=True).reshape(128, 16)
    k1 = kernel1.transpose(0, 2, 1)
    k2, k3 = kernel2.transpose(0, 2, 1), kernel3.transpose(0, 2, 1)

    to_next, to_previous, hidden2, own_cot, ratio2, patches1, ratio1, fields, w2 = run_forward(
        top, strip, bottom, cot, jnp.asarray(pick_matrix()), k1, bias1[None], k2, bias2[None]
    )
    lower, upper = both_ways(to_next, to_previous, "gz")
    row_next, row_previous = run_weave(lower, hidden2, upper, own_cot)
    before, after = both_ways(row_next, row_previous, "gy")
    packed = run_backward(
        size_z,
        k3, bias3[None], lower, hidden2, upper, own_cot, before, after, ratio2, w2, patches1, ratio1, fields,
    )
    packed = lax.all_to_all(packed, "gz", 0, 0, tiled=True)
    column, features = run_sum(packed, size_y)
    column = lax.all_to_all(column, "gy", 0, 0, tiled=True)
    shared = lax.all_to_all(run_share(column, size_z), "gz", 0, 0, tiled=True)
    grad3 = run_third(column, wide)
    grad1, grad2, shift1, shift2, shift3 = run_unpack(shared)
    return (
        features[:, None], grad1.transpose(0, 2, 1), shift1[0], grad2.transpose(0, 2, 1), shift2[0], grad3, shift3[0]
    )


def solution(mesh):
    in_specs = (P(None, "gy", "gz", None), P(), P(), P(), P(), P(), P(), P("gz", "gy", None, None))
    out_specs = (P("gz", "gy", None, None), P(), P(), P(), P(), P(None, "gz", None), P("gz"))
    return jax.shard_map(shards, mesh=mesh, in_specs=in_specs, out_specs=out_specs, check_vma=False)
```

```python
import functools

import jax
import jax.numpy as jnp
import numpy as np
from jax import lax
from jax.experimental import pallas as pl
from jax.experimental.pallas import tpu as pltpu
from jax.sharding import PartitionSpec as P

F32 = jnp.float32
BF16 = jnp.bfloat16
SLOPE = 0.3
PAIRS = ((0, 1), (2, 3), (-3, -2), (4, 5), (-1, 6))
VMEM = pl.BlockSpec(memory_space=pltpu.VMEM)
LIMIT = 24 * 1024 * 1024


def dot(a, b):
    return jnp.dot(a, b, preferred_element_type=F32)


def dot_tn(a, b):
    return lax.dot_general(a, b, (((0,), (0,)), ((), ())), preferred_element_type=F32)


def dot_nt(a, b):
    return lax.dot_general(a, b, (((1,), (1,)), ((), ())), preferred_element_type=F32)


def lane(shape):
    return lax.broadcasted_iota(jnp.int32, shape, len(shape) - 1)


def exps(pre):
    return jnp.exp(2.0 * jnp.maximum(pre, SLOPE * pre))


def rounded(value):
    return value.astype(BF16).astype(F32)


def roll(value, amount, axis):
    return pltpu.roll(value, amount, axis)


def down(value):
    rows = lax.broadcasted_iota(jnp.int32, value.shape, 0)
    return jnp.where(rows == 0, 0.0, roll(value, 1, 0))


def up(value):
    count = value.shape[0]
    rows = lax.broadcasted_iota(jnp.int32, value.shape, 0)
    return jnp.where(rows == count - 1, 0.0, roll(value, count - 1, 0))


def forward_kernel(*refs):
    (top, mid, bot, cot, pick, k1, b1, k2, b2), refs = refs[:9], refs[9:]
    (to_next, to_previous, hidden2, own_cot, ratio2, patches1, ratio1, fields, w2), refs = refs[:9], refs[9:]
    w1, left, field, first, spread, pre2, second = refs
    lay_weights1(k1, w1)
    lay_weights2(k2, w2)
    bias1 = jnp.concatenate([b1[...]] * 8, axis=1)
    bias2 = jnp.concatenate([b2[...]] * 4, axis=1)
    base_y, base_z = lax.axis_index("gy"), lax.axis_index("gz")
    size_y, size_z = lax.axis_size("gy"), lax.axis_size("gz")

    def inside(offset_y, offset_z, scale):
        row = base_y * (4 // scale) + offset_y
        col = base_z * (4 // scale) + offset_z
        ok_y = (row >= 0) & (row < size_y * (4 // scale))
        ok_z = (col >= 0) & (col < size_z * (4 // scale))
        return jnp.where(ok_y & ok_z, 1.0, 0.0)

    def lay(source, index, target):
        rows = source[index].astype(F32)
        pieces = []
        for one, two in PAIRS:
            a, b = 8 * (one + 3), 8 * (two + 3)
            pieces.append(jnp.concatenate([rows[a : a + 16], rows[b : b + 16]], axis=1))
        left[target] = jnp.concatenate(pieces, axis=0).astype(BF16)

    def lay_top(step, carry):
        lay(top, step + 1, step)
        return carry

    def lay_mid(step, carry):
        lay(mid, step, step + 7)
        return carry

    def lay_bot(step, carry):
        lay(bot, step, step + 15)
        return carry

    lax.fori_loop(0, 7, lay_top, 0)
    lax.fori_loop(0, 8, lay_mid, 0)
    lax.fori_loop(0, 7, lay_bot, 0)

    def sift(step, carry):
        block = left[pl.ds(2 * step, 2)].reshape(160, 256)
        out = dot(block, pick[...]).astype(BF16).reshape(2, 5, 16, 512)
        for px in range(4):
            for k in range(5):
                field[pl.ds(2 * step, 2), px * 16 : px * 16 + 16, k * 128 : k * 128 + 128] = out[
                    :, k, :, px * 128 : px * 128 + 128
                ]
        return carry

    lax.fori_loop(0, 11, sift, 0)
    fields[...] = field[6:16, :, :256]
    first[:, :, 0:8] = jnp.zeros((10, 10, 8, 128), F32)
    first[:, :, 72:80] = jnp.zeros((10, 10, 8, 128), F32)

    def block1(yw, carry):
        stack = field[pl.ds(2 * yw, 4)].reshape(256, 640)
        pre = dot_tn(stack, w1[...]) + bias1
        e = exps(pre)
        total = e[:, :128] + e[:, 128:]
        total = total + roll(total, 64, 1)
        total = total + roll(total, 32, 1)
        mean = total * 0.125
        pooled = rounded(jnp.log(mean) * 0.5)
        for k, pair in enumerate(PAIRS):
            for h, zw in enumerate(pair):
                at = k * 128 + h * 64
                first[yw, zw + 3, 8:72] = pooled[at : at + 64] * inside(yw - 3, zw, 1)

        @pl.when((yw >= 3) & (yw < 7))
        def _():
            share = 0.125 / mean[:256]
            share = jnp.concatenate([share, share], axis=1)
            ratio1[yw - 3] = jnp.where(pre[:256] > 0, 1.0, SLOPE) * (e[:256] * share)

        return carry

    lax.fori_loop(0, 10, block1, 0)

    group1 = lane((32, 128)) // 32

    def frame(yi, carry):
        for zi in range(10):
            part = first[yi, zi, pl.ds(7, 32, stride=2), :]
            for px in range(1, 4):
                part = jnp.where(group1 == px, first[yi, zi, pl.ds(7 + px, 32, stride=2), :], part)
            spread[yi, zi] = part.astype(BF16)
        return carry

    lax.fori_loop(0, 10, frame, 0)
    patches1[...] = spread[2:8, 2:8]

    for dy in range(3):
        block = jnp.concatenate(
            [
                jnp.concatenate([spread[dy : dy + 8, 2 * zo + pz] for pz in range(4)], axis=2)[:, None]
                for zo in range(4)
            ],
            axis=1,
        ).reshape(1024, 512)
        term = dot(block, w2[dy]).reshape(8, 4, 32, 256)
        pre2[...] = term + bias2 if dy == 0 else pre2[...] + term

    half = lane((16, 128)) < 64

    def block2(yp, carry):
        pre = pre2[pl.ds(2 * yp, 2)]
        e = exps(pre)
        both = e[0] + e[1]
        total = (both[:, :, :128] + both[:, :, 128:]).reshape(128, 128)
        total = total + roll(total, 64, 1)
        mean = total * 0.125
        pooled = rounded(jnp.log(mean) * 0.5).reshape(4, 32, 128)
        share = (0.125 / mean).reshape(4, 32, 128)
        share = jnp.concatenate([share, share], axis=2)
        scaled = jnp.where(pre > 0, 1.0, SLOPE) * (e * share[None])
        for zo in range(4):
            ok = inside(yp - 1, zo - 1, 2)
            ratio2[pl.ds(2 * yp, 2), zo] = scaled[:, zo] * ok
            second[zo] = pooled[zo] * ok
            even = second[zo, pl.ds(0, 16, stride=2), :]
            odd = second[zo, pl.ds(1, 16, stride=2), :]
            hidden2[yp, zo] = jnp.where(half, even, odd).astype(BF16)
        return carry

    lax.fori_loop(0, 4, block2, 0)
    to_next[0:128] = hidden2[:, 0:2].reshape(128, 128)
    to_previous[0:128] = hidden2[:, 2:4].reshape(128, 128)
    own = cot[...].astype(F32).T.astype(BF16)
    to_next[128:144] = own
    to_previous[128:144] = own
    own_cot[...] = own


def lay_weights1(taps, out):
    group = lane((16, 128)) // 32
    zero = jnp.zeros((16, 128), F32)
    wide = []
    for k in range(9):
        pieces = [taps[3 * k + dz].astype(F32) for dz in range(3)] + [jnp.zeros((4, 32), F32)]
        rows = jnp.concatenate(pieces, axis=0)
        wide.append(jnp.concatenate([rows] * 4, axis=1))
    for py in range(4):
        for px in range(4):
            at = (py * 4 + px) * 16
            for qy in range(2):
                dy = py - qy
                sides = [
                    wide[(px - qx) * 3 + dy] if 0 <= dy < 3 and 0 <= px - qx < 3 else zero for qx in range(2)
                ]
                value = jnp.where(group == 0, sides[0], sides[1])
                shifted = jnp.where(group == 2, roll(sides[0], 4, 0), roll(sides[1], 4, 0))
                out[at : at + 16, qy * 128 : qy * 128 + 128] = jnp.where(group < 2, value, shifted).astype(BF16)


def lay_weights2(taps, out):
    zero = jnp.zeros((32, 64), BF16)
    for dy in range(3):
        out[dy, 384:512, 0:128] = jnp.zeros((128, 128), BF16)
        out[dy, 0:128, 128:256] = jnp.zeros((128, 128), BF16)
        for dz in range(3):
            for px in range(4):
                sides = [taps[(px - qx) * 9 + dy * 3 + dz] if 0 <= px - qx < 3 else zero for qx in range(2)]
                tile = jnp.concatenate(sides, axis=1)
                for qz in range(2):
                    at = (dz + qz) * 128 + px * 32
                    out[dy, at : at + 32, qz * 128 : qz * 128 + 128] = tile


def lay_weights3(taps, out):
    zero = jnp.zeros((64, 128), BF16)
    for tap in range(9):
        out[tap, 192:256, 0:128] = zero
        out[tap, 0:64, 128:256] = zero
        for dx in range(3):
            value = taps[dx * 9 + tap]
            out[tap, dx * 64 : dx * 64 + 64, 0:128] = value
            out[tap, dx * 64 + 64 : dx * 64 + 128, 128:256] = value


def run_forward(*operands):
    kept = (
        jax.ShapeDtypeStruct((4, 4, 16, 128), BF16),
        jax.ShapeDtypeStruct((16, 128), BF16),
        jax.ShapeDtypeStruct((8, 4, 32, 256), F32),
        jax.ShapeDtypeStruct((6, 6, 32, 128), BF16),
        jax.ShapeDtypeStruct((4, 256, 256), F32),
        jax.ShapeDtypeStruct((10, 64, 256), BF16),
        jax.ShapeDtypeStruct((3, 512, 256), BF16),
    )
    return pl.pallas_call(
        forward_kernel,
        name="forward",
        out_shape=(jax.ShapeDtypeStruct((144, 128), BF16),) * 2 + kept,
        in_specs=[VMEM] * len(operands),
        out_specs=(VMEM,) * 9,
        scratch_shapes=[
            pltpu.VMEM((256, 256), BF16),
            pltpu.VMEM((22, 80, 256), BF16),
            pltpu.VMEM((22, 64, 640), BF16),
            pltpu.VMEM((10, 10, 80, 128), F32),
            pltpu.VMEM((10, 10, 32, 128), BF16),
            pltpu.VMEM((8, 4, 32, 256), F32),
            pltpu.VMEM((4, 32, 128), F32),
        ],
        compiler_params=pltpu.CompilerParams(vmem_limit_bytes=LIMIT),
    )(*operands)


def weave_kernel(lower, hidden2, upper, own_cot, to_next, to_previous):
    for target, first_row in ((to_next, 0), (to_previous, 2)):
        for y in range(2):
            row, at = first_row + y, y * 128
            target[at : at + 32] = lower[row * 32 : row * 32 + 32]
            target[at + 32 : at + 96] = hidden2[row].reshape(64, 128)
            target[at + 96 : at + 128] = upper[row * 32 : row * 32 + 32]
        target[256:272] = lower[128:144]
        target[272:288] = own_cot[...]
        target[288:304] = upper[128:144]


def run_weave(*operands):
    return pl.pallas_call(
        weave_kernel,
        name="weave",
        out_shape=(jax.ShapeDtypeStruct((304, 128), BF16),) * 2,
        in_specs=[VMEM] * 4,
        out_specs=(VMEM,) * 2,
        compiler_params=pltpu.CompilerParams(vmem_limit_bytes=LIMIT),
    )(*operands)


def backward_kernel(*refs):
    (k3, b3, lower, middle, upper, own_cot, before, after, ratio2, w2, patches1, ratio1, fields), refs = (
        refs[:13], refs[13:],
    )
    packed3, packed, w3, patches2, pre3, delta3, patch2, grad2, delta2, patch1, grad1, delta1, turned = refs
    groups = packed.shape[0]
    wide = 128 // groups
    lay_weights3(k3, w3)
    bias3_in = jnp.concatenate([b3[...]] * 2, axis=1)
    half = lane((16, 128)) < 64

    def lay(y, source):
        for z in range(8):
            swapped = roll(source(z).astype(F32), 64, 1)
            patches2[y, z] = jnp.concatenate(
                [jnp.where(half, down(swapped), swapped), jnp.where(half, swapped, up(swapped))], axis=1
            ).astype(BF16)

    for y in range(2):
        lay(y, lambda z: before[(y * 8 + z) * 16 : (y * 8 + z + 1) * 16])
        lay(y + 6, lambda z: after[(y * 8 + z) * 16 : (y * 8 + z + 1) * 16])

    def pick_middle(y, z):
        if z < 2:
            return lower[(y * 2 + z) * 16 : (y * 2 + z + 1) * 16]
        if z < 6:
            return middle[y, z - 2]
        return upper[(y * 2 + z - 6) * 16 : (y * 2 + z - 5) * 16]

    for y in range(4):
        lay(y + 2, functools.partial(pick_middle, y))

    for tap in range(9):
        dy, dz = tap // 3, tap % 3
        block = patches2[dy : dy + 6, dz : dz + 6].reshape(576, 256)
        term = dot(block, w3[tap]).reshape(6, 6, 16, 256)
        pre3[...] = term + bias3_in if tap == 0 else pre3[...] + term

    for wy in range(3):
        for wz in range(3):
            pre = pre3[2 * wy : 2 * wy + 2, 2 * wz : 2 * wz + 2]
            e = exps(pre)
            total = e[0, 0] + e[0, 1] + e[1, 0] + e[1, 1]
            total = total[:, :128] + total[:, 128:]
            mean = total * 0.125
            if wy == 1:
                cot = own_cot[...] if wz == 1 else (lower if wz == 0 else upper)[128:144]
            else:
                cot = (before if wy == 0 else after)[256 + wz * 16 : 272 + wz * 16]
            share = cot.astype(F32) * (0.125 / mean)
            share = jnp.concatenate([share, share], axis=1)
            delta3[2 * wy : 2 * wy + 2, 2 * wz : 2 * wz + 2] = (
                jnp.where(pre > 0, 1.0, SLOPE) * (e * share)
            ).astype(BF16)
            if wy == 1 and wz == 1:
                features = rounded(jnp.log(mean) * 0.5)

    own3 = delta3[2:4, 2:4].reshape(64, 256)
    bias3 = own3.astype(F32).sum(axis=0, keepdims=True)
    bias3 = bias3[:, :128] + bias3[:, 128:]
    low, high = [], []
    for tap in range(9):
        dy, dz = tap // 3, tap % 3
        block = patches2[dy + 2 : dy + 4, dz + 2 : dz + 4].reshape(64, 256)
        full = dot_tn(own3, block)
        one = full[:128]
        low_lanes, high_lanes = roll(full[128:, :128], 64, 1), roll(full[128:, 128:], 64, 1)
        tile0 = jnp.where(lane((128, 128)) < 64, low_lanes, high_lanes)
        tile1 = high_lanes
        low.append(one[:, :128] + tile0)
        high.append(one[:, 128:] + tile1)
    first_half = lane((128, 128)) < 64
    paired = []
    for m in range(5):
        other = roll(high[2 * m + 1], 64, 1) if 2 * m + 1 < 9 else jnp.zeros((128, 128), F32)
        paired.append(jnp.where(first_half, high[2 * m], other))
    kernel3 = [piece.reshape(groups, wide, 128) for piece in low + paired]

    turned[...] = jnp.concatenate([features, jnp.zeros((112, 128), F32)], axis=0).T
    feature_rows = turned[pl.ds(0, 16, stride=8), :]
    for c in range(1, 8):
        feature_rows = feature_rows + roll(turned[pl.ds(c, 16, stride=8), :], 16 * c, 1)
    feature_rows = feature_rows.reshape(groups, wide // 8, 128)
    fill = jnp.zeros((groups, packed3.shape[1] - 14 * wide - wide // 8, 128), F32)
    packed3[...] = jnp.concatenate(kernel3 + [feature_rows, fill], axis=1).astype(BF16)

    for tap in range(9):
        dy, dz = tap // 3, tap % 3
        block = delta3[2 - dy : 6 - dy, 2 - dz : 6 - dz].reshape(256, 256)
        term = dot_nt(block, w3[tap]).reshape(4, 4, 16, 256)
        patch2[...] = term if tap == 0 else patch2[...] + term

    for y in range(4):
        for z in range(4):
            a, b = patch2[y, z, :, :128], patch2[y, z, :, 128:]
            x = rounded(jnp.where(half, b + up(a), a + down(b)))
            swapped = roll(x, 64, 1)
            grad2[y, z, pl.ds(0, 16, stride=2), :] = jnp.where(half, swapped, x)
            grad2[y, z, pl.ds(1, 16, stride=2), :] = jnp.where(half, x, swapped)

    for y in range(6):
        value = grad2[(y + 1) // 2]
        value = jnp.concatenate([value, value], axis=2)
        delta2[y] = (value * ratio2[y + 1]).astype(BF16)

    own2 = delta2[1:5, 1:3].reshape(256, 256)
    bias2 = own2.astype(F32).sum(axis=0, keepdims=True)
    bias2 = bias2[:, :128] + bias2[:, 128:]
    bias2 = bias2 + roll(bias2, 64, 1)
    taps = [None] * 27
    for dy in range(3):
        block = jnp.concatenate(
            [
                jnp.concatenate([patches1[dy : dy + 4, 2 * zo + pz] for pz in range(4)], axis=2)[:, None]
                for zo in range(2)
            ],
            axis=1,
        ).reshape(256, 512)
        full = dot_tn(block, own2)
        for dz in range(3):
            rows = full[dz * 128 : dz * 128 + 128, :128] + full[dz * 128 + 128 : dz * 128 + 256, 128:]
            for dx in range(3):
                taps[dx * 9 + dy * 3 + dz] = rows[dx * 32 : dx * 32 + 32] + roll(
                    rows[dx * 32 + 32 : dx * 32 + 64], 64, 1
                )
    for dy in range(3):
        block = delta2[2 - dy : 6 - dy].reshape(512, 256)
        term = dot_nt(block, w2[dy]).reshape(4, 4, 32, 512)
        patch1[...] = term if dy == 0 else patch1[...] + term

    low_half = lane((32, 128)) < 64
    group = lane((32, 128)) // 32

    def widen(value, which):
        value = jnp.where(group == which, value, 0.0)
        value = value + roll(value, 32, 1)
        return value + roll(value, 64, 1)


    def gather1(y, carry):
        for z, (zo_a, pz_a, zo_b, pz_b) in enumerate(((0, 3, 1, 1), (1, 2, 2, 0), (1, 3, 2, 1), (2, 2, 3, 0))):
            value = (
                patch1[y, zo_a, :, pz_a * 128 : pz_a * 128 + 128]
                + patch1[y, zo_b, :, pz_b * 128 : pz_b * 128 + 128]
            )
            value = rounded(value + roll(jnp.where(low_half, up(value), down(value)), 64, 1))
            grad1[z, pl.ds(0, 32, stride=2), :] = widen(value, 1)
            grad1[z, pl.ds(1, 32, stride=2), :] = widen(value, 2)
        value = grad1[...].reshape(256, 128)
        value = jnp.concatenate([value, value], axis=1)
        delta1[y] = (value * ratio1[y]).astype(BF16)
        return carry

    lax.fori_loop(0, 4, gather1, 0)

    bias1 = delta1[...].astype(F32).sum(axis=0).sum(axis=0, keepdims=True)
    bias1 = bias1[:, :128] + bias1[:, 128:]
    bias1 = bias1 + roll(bias1, 64, 1)
    bias1 = bias1 + roll(bias1, 32, 1)
    full = None
    for yw in range(4):
        term = dot(fields[2 * yw : 2 * yw + 4].reshape(256, 256), delta1[yw])
        full = term if full is None else full + term
    full = full.reshape(4, 4, 16, 256)
    kernel1 = []
    group1 = lane((16, 128)) // 32
    for dy in range(3):
        rows = full[dy, :, :, :128] + full[dy + 1, :, :, 128:]
        pieces = []
        for dx in range(3):
            value = rows[dx] + roll(rows[dx + 1], 96, 1)
            value = value + roll(roll(value, 12, 0), 64, 1)
            pieces.append(roll(value, 32 * dx, 1) if dx else value)
        kernel1.append(jnp.where(group1 == 0, pieces[0], jnp.where(group1 == 1, pieces[1], pieces[2])))

    low_lane = lane((32, 128)) < 64
    kernel2 = [
        jnp.where(low_lane, taps[2 * m], roll(taps[2 * m + 1], 64, 1) if 2 * m + 1 < 27 else 0.0)
        for m in range(14)
    ]
    biases = jnp.concatenate(
        [bias3, jnp.where(lane((1, 128)) < 64, bias2, bias1), jnp.zeros((14, 128), F32)], axis=0
    )
    shared = jnp.concatenate(kernel2 + kernel1 + [biases], axis=0)
    packed[...] = shared.reshape(groups, 512 // groups, 128).astype(BF16)


def run_backward(groups, *operands):
    wide = 128 // groups
    return pl.pallas_call(
        backward_kernel,
        name="backward",
        out_shape=(
            jax.ShapeDtypeStruct((groups, -(-(14 * wide + wide // 8) // 8) * 8, 128), BF16),
            jax.ShapeDtypeStruct((groups, 512 // groups, 128), BF16),
        ),
        in_specs=[VMEM] * len(operands),
        out_specs=(VMEM, VMEM),
        scratch_shapes=[
            pltpu.VMEM((9, 256, 256), BF16),
            pltpu.VMEM((8, 8, 16, 256), BF16),
            pltpu.VMEM((6, 6, 16, 256), F32),
            pltpu.VMEM((6, 6, 16, 256), BF16),
            pltpu.VMEM((4, 4, 16, 256), F32),
            pltpu.VMEM((4, 4, 32, 128), F32),
            pltpu.VMEM((6, 4, 32, 256), BF16),
            pltpu.VMEM((4, 4, 32, 512), F32),
            pltpu.VMEM((4, 64, 128), F32),
            pltpu.VMEM((4, 256, 256), BF16),
            pltpu.VMEM((128, 128), F32),
        ],
        compiler_params=pltpu.CompilerParams(vmem_limit_bytes=LIMIT),
    )(*operands)


def sum_kernel(received, to_column, features):
    groups, rows = received.shape[0], to_column.shape[1]
    wide = 128 // groups
    own = received[:, rows : rows + wide // 8].astype(F32)
    for c in range(wide):
        features[c] = own[:, c // 8, (c % 8) * 16 : (c % 8) * 16 + 16].astype(BF16)
    total = received[:, :rows].astype(F32).sum(axis=0)
    to_column[...] = jnp.broadcast_to(total[None], to_column.shape).astype(BF16)


def run_sum(received, rows_y):
    groups = received.shape[0]
    wide = 128 // groups
    return pl.pallas_call(
        sum_kernel,
        name="sum",
        out_shape=(
            jax.ShapeDtypeStruct((rows_y, 14 * wide, 128), BF16),
            jax.ShapeDtypeStruct((wide, groups, 16), BF16),
        ),
        in_specs=[VMEM],
        out_specs=(VMEM, VMEM),
        compiler_params=pltpu.CompilerParams(vmem_limit_bytes=LIMIT),
    )(received)


def share_kernel(parts, to_each):
    total = parts[...].astype(F32).sum(axis=0)
    to_each[...] = jnp.broadcast_to(total[None], to_each.shape).astype(BF16)


def run_share(parts, count):
    return pl.pallas_call(
        share_kernel,
        name="share",
        out_shape=jax.ShapeDtypeStruct((count,) + parts.shape[1:], BF16),
        in_specs=[VMEM],
        out_specs=VMEM,
        compiler_params=pltpu.CompilerParams(vmem_limit_bytes=LIMIT),
    )(parts)


def third_kernel(column, grad3):
    wide = grad3.shape[1]
    lines = column[...].astype(F32).sum(axis=0)
    for tap in range(9):
        low = lines[tap * wide : tap * wide + wide]
        grad3[tap] = low[:, :64]
        grad3[9 + tap] = low[:, 64:]
        at = (9 + tap // 2) * wide
        grad3[18 + tap] = lines[at : at + wide][:, (tap % 2) * 64 : (tap % 2) * 64 + 64]


def run_third(column, wide):
    return pl.pallas_call(
        third_kernel,
        name="third",
        out_shape=jax.ShapeDtypeStruct((27, wide, 64), F32),
        in_specs=[VMEM],
        out_specs=VMEM,
        compiler_params=pltpu.CompilerParams(vmem_limit_bytes=LIMIT),
    )(column)


def unpack_kernel(shared, grad1, grad2, shift1, shift2, shift3):
    wide = shift3.shape[1]
    rows = shared[...].astype(F32).reshape(512, 128)
    for tap in range(27):
        at = (tap // 2) * 32
        grad2[tap] = rows[at : at + 32, (tap % 2) * 64 : (tap % 2) * 64 + 64]
    for dy in range(3):
        for dz in range(3):
            at = 448 + dy * 16 + dz * 4
            for dx in range(3):
                grad1[dx * 9 + dy * 3 + dz] = rows[at : at + 4, dx * 32 : dx * 32 + 32]
    biases = rows[496:504]
    shift1[...] = biases[1:2, 64:96]
    shift2[...] = biases[1:2, :64]
    place = lax.axis_index("gz")
    shift3[...] = roll(biases, lax.rem(128 - place * wide, 128), 1)[0:1, :wide]


def run_unpack(shared):
    wide = 128 // shared.shape[0]
    return pl.pallas_call(
        unpack_kernel,
        name="unpack",
        out_shape=(
            jax.ShapeDtypeStruct((27, 4, 32), F32),
            jax.ShapeDtypeStruct((27, 32, 64), F32),
            jax.ShapeDtypeStruct((1, 32), F32),
            jax.ShapeDtypeStruct((1, 64), F32),
            jax.ShapeDtypeStruct((1, wide), F32),
        ),
        in_specs=[VMEM],
        out_specs=(VMEM,) * 5,
        compiler_params=pltpu.CompilerParams(vmem_limit_bytes=LIMIT),
    )(shared)


def pick_matrix():
    out = np.zeros((2, 128, 4, 2, 64), np.float32)
    for px in range(4):
        for w in range(64):
            x = 2 * w - 1 + px
            if 0 <= x < 128:
                for h in range(2):
                    out[h, x, px, h, w] = 1
    return out.reshape(256, 512).astype(jnp.bfloat16)


def both_ways(to_next, to_previous, axis):
    devices = lax.axis_size(axis)
    forth = [(i, i + 1) for i in range(devices - 1)]
    back = [(i + 1, i) for i in range(devices - 1)]
    return lax.ppermute(to_next, axis, forth), lax.ppermute(to_previous, axis, back)


def shards(universe, kernel1, bias1, kernel2, bias2, kernel3, bias3, cotangent):
    size_y, size_z = lax.axis_size("gy"), lax.axis_size("gz")
    wide = 128 // size_z

    tile = universe.transpose(1, 2, 0, 3).reshape(8, 32, 128)
    lower, upper = both_ways(tile, tile, "gz")
    strip = jnp.concatenate([lower[:, 4:], tile, upper[:, :28], jnp.zeros((8, 8, 128), BF16)], axis=1)
    cot = lax.all_to_all(cotangent[:, 0].transpose(1, 0, 2), "gz", 0, 0, tiled=True).reshape(128, 16)
    strip, cot = lax.optimization_barrier((strip, cot))
    top, bottom = both_ways(strip, strip, "gy")

    k1 = kernel1.transpose(0, 2, 1)
    k2, k3 = kernel2.transpose(0, 2, 1), kernel3.transpose(0, 2, 1)

    to_next, to_previous, hidden2, own_cot, ratio2, patches1, ratio1, fields, w2 = run_forward(
        top, strip, bottom, cot, jnp.asarray(pick_matrix()), k1, bias1[None], k2, bias2[None]
    )
    lower, upper = both_ways(to_next, to_previous, "gz")
    row_next, row_previous = run_weave(lower, hidden2, upper, own_cot)
    before, after = both_ways(row_next, row_previous, "gy")
    packed3, packed = run_backward(
        size_z,
        k3, bias3[None], lower, hidden2, upper, own_cot, before, after, ratio2, w2, patches1, ratio1, fields,
    )
    packed = lax.all_to_all(packed, "gz", 0, 0, tiled=True)
    packed3 = lax.all_to_all(packed3, "gz", 0, 0, tiled=True)
    shared = lax.all_to_all(run_share(packed, size_y), "gy", 0, 0, tiled=True)
    column, features = run_sum(packed3, size_y)
    shared, column = lax.optimization_barrier((shared, column))
    shared = lax.all_to_all(run_share(shared, size_z), "gz", 0, 0, tiled=True)
    grad3 = run_third(lax.all_to_all(column, "gy", 0, 0, tiled=True), wide)
    grad1, grad2, shift1, shift2, shift3 = run_unpack(shared)
    return (
        features[:, None], grad1.transpose(0, 2, 1), shift1[0], grad2.transpose(0, 2, 1), shift2[0], grad3, shift3[0]
    )


def solution(mesh):
    in_specs = (P(None, "gy", "gz", None), P(), P(), P(), P(), P(), P(), P("gz", "gy", None, None))
    out_specs = (P("gz", "gy", None, None), P(), P(), P(), P(), P(None, "gz", None), P("gz"))
    return jax.shard_map(shards, mesh=mesh, in_specs=in_specs, out_specs=out_specs, check_vma=False)
```

```python
import functools
import math

import jax
import jax.numpy as jnp
from jax import lax
from jax.experimental import pallas as pl
from jax.experimental.pallas import tpu as pltpu
from jax.sharding import PartitionSpec as P

F32 = jnp.float32
BF16 = jnp.bfloat16
SLOPE = 0.3
TWO_LOG2_E = 2.0 / math.log(2.0)
PAIRS = ((0, 1), (2, 3), (-3, -2), (4, 5), (-1, 6))
VMEM = pl.BlockSpec(memory_space=pltpu.VMEM)
LIMIT = 24 * 1024 * 1024


def dot(a, b):
    return jnp.dot(a, b, preferred_element_type=F32)


def dot_tn(a, b):
    return lax.dot_general(a, b, (((0,), (0,)), ((), ())), preferred_element_type=F32)


def dot_nt(a, b):
    return lax.dot_general(a, b, (((1,), (1,)), ((), ())), preferred_element_type=F32)


def lane(shape):
    return lax.broadcasted_iota(jnp.int32, shape, len(shape) - 1)


def exps(pre):
    scaled = pre * TWO_LOG2_E
    return jnp.exp2(jnp.maximum(scaled, SLOPE * scaled))


def rounded(value):
    return value.astype(BF16).astype(F32)


def roll(value, amount, axis):
    return pltpu.roll(value, amount, axis)


def down(value):
    rows = lax.broadcasted_iota(jnp.int32, value.shape, 0)
    return jnp.where(rows == 0, 0.0, roll(value, 1, 0))


def up(value):
    count = value.shape[0]
    rows = lax.broadcasted_iota(jnp.int32, value.shape, 0)
    return jnp.where(rows == count - 1, 0.0, roll(value, count - 1, 0))


def weights_kernel(k1, b1, k2, b2, k3, b3, w1, w2, w3, biases, pick):
    lay_weights1(k1, w1)
    lay_weights2(k2, w2)
    lay_weights3(k3, w3)
    rows = [
        jnp.concatenate([b1[...]] * 8, axis=1),
        jnp.concatenate([b2[...]] * 4, axis=1),
        jnp.concatenate([b3[...]] * 2, axis=1),
    ]
    biases[...] = jnp.concatenate(rows + [jnp.zeros((5, 256), F32)], axis=0)
    for px in range(4):
        row = lax.broadcasted_iota(jnp.int32, (256, 128), 0)
        col = lax.broadcasted_iota(jnp.int32, (256, 128), 1)
        same = row // 128 == col // 64
        hit = (row % 128) == 2 * (col % 64) - 1 + px
        pick[:, px * 128 : px * 128 + 128] = jnp.where(same & hit, 1.0, 0.0).astype(BF16)


def run_weights(*operands):
    return pl.pallas_call(
        weights_kernel,
        name="weights",
        out_shape=(
            jax.ShapeDtypeStruct((256, 256), BF16),
            jax.ShapeDtypeStruct((3, 512, 256), BF16),
            jax.ShapeDtypeStruct((9, 256, 256), BF16),
            jax.ShapeDtypeStruct((8, 256), F32),
            jax.ShapeDtypeStruct((256, 512), BF16),
        ),
        in_specs=[VMEM] * 6,
        out_specs=(VMEM,) * 5,
        compiler_params=pltpu.CompilerParams(vmem_limit_bytes=LIMIT),
    )(*operands)


def forward_kernel(
    top, mid, bot, cot, w1, w2, biases, pick,
    to_next, to_previous, hidden2, own_cot, ratio2, patches1, ratio1, fields,
    left, field, turned, first, spread, pre2, second,
):
    bias1, bias2 = biases[0:1], biases[1:2]
    base_y, base_z = lax.axis_index("gy"), lax.axis_index("gz")
    size_y, size_z = lax.axis_size("gy"), lax.axis_size("gz")

    def inside(offset_y, offset_z, scale):
        row = base_y * (4 // scale) + offset_y
        col = base_z * (4 // scale) + offset_z
        ok_y = (row >= 0) & (row < size_y * (4 // scale))
        ok_z = (col >= 0) & (col < size_z * (4 // scale))
        return jnp.where(ok_y & ok_z, 1.0, 0.0)

    def lay(source, index, target):
        rows = source[index].astype(F32)
        pieces = []
        for one, two in PAIRS:
            a, b = 8 * (one + 3), 8 * (two + 3)
            pieces.append(jnp.concatenate([rows[a : a + 16], rows[b : b + 16]], axis=1))
        left[target] = jnp.concatenate(pieces, axis=0).astype(BF16)

    def lay_top(step, carry):
        lay(top, step + 1, step)
        return carry

    def lay_mid(step, carry):
        lay(mid, step, step + 7)
        return carry

    def lay_bot(step, carry):
        lay(bot, step, step + 15)
        return carry

    lax.fori_loop(0, 7, lay_top, 0)
    lax.fori_loop(0, 8, lay_mid, 0)
    lax.fori_loop(0, 7, lay_bot, 0)

    def sift(step, carry):
        block = left[pl.ds(2 * step, 2)].reshape(160, 256)
        out = dot(block, pick[...]).astype(BF16).reshape(2, 5, 16, 512)
        for parity in range(2):
            for px in range(4):
                at = (parity * 4 + px) * 16
                for k in range(5):
                    field[step, at : at + 16, k * 128 : k * 128 + 128] = out[
                        parity, k, :, px * 128 : px * 128 + 128
                    ]
        turned[step] = field[step].T
        return carry

    lax.fori_loop(0, 11, sift, 0)
    fields[...] = field[3:8, :, :256]
    first[:, :, 0:8] = jnp.zeros((10, 10, 8, 128), F32)
    first[:, :, 72:80] = jnp.zeros((10, 10, 8, 128), F32)

    def block1(yw, carry):
        stack = jnp.concatenate([turned[yw], turned[yw + 1]], axis=1)
        pre = dot(stack, w1[...]) + bias1
        e = exps(pre)
        total = e[:, :128] + e[:, 128:]
        total = total + roll(total, 64, 1)
        total = total + roll(total, 32, 1)
        mean = total * 0.125
        pooled = rounded(jnp.log(mean) * 0.5)
        for k, pair in enumerate(PAIRS):
            for h, zw in enumerate(pair):
                at = k * 128 + h * 64
                first[yw, zw + 3, 8:72] = pooled[at : at + 64] * inside(yw - 3, zw, 1)

        @pl.when((yw >= 3) & (yw < 7))
        def _():
            share = 0.125 / mean[:256]
            share = jnp.concatenate([share, share], axis=1)
            ratio1[yw - 3] = jnp.where(pre[:256] > 0, 1.0, SLOPE) * (e[:256] * share)

        return carry

    lax.fori_loop(0, 10, block1, 0)

    group1 = lane((32, 128)) // 32

    def frame(yi, carry):
        for zi in range(10):
            part = first[yi, zi, pl.ds(7, 32, stride=2), :]
            for px in range(1, 4):
                part = jnp.where(group1 == px, first[yi, zi, pl.ds(7 + px, 32, stride=2), :], part)
            spread[yi, zi] = part.astype(BF16)
        return carry

    lax.fori_loop(0, 10, frame, 0)
    patches1[...] = spread[2:8, 2:8]

    for dy in range(3):
        block = jnp.concatenate(
            [
                jnp.concatenate([spread[dy : dy + 8, 2 * zo + pz] for pz in range(4)], axis=2)[:, None]
                for zo in range(4)
            ],
            axis=1,
        ).reshape(1024, 512)
        term = dot(block, w2[dy]).reshape(8, 4, 32, 256)
        pre2[...] = term + bias2 if dy == 0 else pre2[...] + term

    half = lane((16, 128)) < 64

    def block2(yp, carry):
        pre = pre2[pl.ds(2 * yp, 2)]
        e = exps(pre)
        both = e[0] + e[1]
        total = (both[:, :, :128] + both[:, :, 128:]).reshape(128, 128)
        total = total + roll(total, 64, 1)
        mean = total * 0.125
        pooled = rounded(jnp.log(mean) * 0.5).reshape(4, 32, 128)
        share = (0.125 / mean).reshape(4, 32, 128)
        share = jnp.concatenate([share, share], axis=2)
        scaled = jnp.where(pre > 0, 1.0, SLOPE) * (e * share[None])
        for zo in range(4):
            ok = inside(yp - 1, zo - 1, 2)
            ratio2[pl.ds(2 * yp, 2), zo] = scaled[:, zo] * ok
            second[zo] = pooled[zo] * ok
            even = second[zo, pl.ds(0, 16, stride=2), :]
            odd = second[zo, pl.ds(1, 16, stride=2), :]
            hidden2[yp, zo] = jnp.where(half, even, odd).astype(BF16)
        return carry

    lax.fori_loop(0, 4, block2, 0)
    to_next[0:128] = hidden2[:, 0:2].reshape(128, 128)
    to_previous[0:128] = hidden2[:, 2:4].reshape(128, 128)
    own = cot[...].astype(F32).T.astype(BF16)
    to_next[128:144] = own
    to_previous[128:144] = own
    own_cot[...] = own


def lay_weights1(taps, out):
    group = lane((16, 128)) // 32
    zero = jnp.zeros((16, 128), F32)
    wide = []
    for k in range(9):
        pieces = [taps[3 * k + dz].astype(F32) for dz in range(3)] + [jnp.zeros((4, 32), F32)]
        rows = jnp.concatenate(pieces, axis=0)
        wide.append(jnp.concatenate([rows] * 4, axis=1))
    for py in range(4):
        for px in range(4):
            at = (py * 4 + px) * 16
            for qy in range(2):
                dy = py - qy
                sides = [
                    wide[(px - qx) * 3 + dy] if 0 <= dy < 3 and 0 <= px - qx < 3 else zero for qx in range(2)
                ]
                value = jnp.where(group == 0, sides[0], sides[1])
                shifted = jnp.where(group == 2, roll(sides[0], 4, 0), roll(sides[1], 4, 0))
                out[at : at + 16, qy * 128 : qy * 128 + 128] = jnp.where(group < 2, value, shifted).astype(BF16)


def lay_weights2(taps, out):
    zero = jnp.zeros((32, 64), BF16)
    for dy in range(3):
        out[dy, 384:512, 0:128] = jnp.zeros((128, 128), BF16)
        out[dy, 0:128, 128:256] = jnp.zeros((128, 128), BF16)
        for dz in range(3):
            for px in range(4):
                sides = [taps[(px - qx) * 9 + dy * 3 + dz] if 0 <= px - qx < 3 else zero for qx in range(2)]
                tile = jnp.concatenate(sides, axis=1)
                for qz in range(2):
                    at = (dz + qz) * 128 + px * 32
                    out[dy, at : at + 32, qz * 128 : qz * 128 + 128] = tile


def lay_weights3(taps, out):
    zero = jnp.zeros((64, 128), BF16)
    for tap in range(9):
        out[tap, 192:256, 0:128] = zero
        out[tap, 0:64, 128:256] = zero
        for dx in range(3):
            value = taps[dx * 9 + tap]
            out[tap, dx * 64 : dx * 64 + 64, 0:128] = value
            out[tap, dx * 64 + 64 : dx * 64 + 128, 128:256] = value


def run_forward(*operands):
    return pl.pallas_call(
        forward_kernel,
        name="forward",
        out_shape=(
            jax.ShapeDtypeStruct((144, 128), BF16),
            jax.ShapeDtypeStruct((144, 128), BF16),
            jax.ShapeDtypeStruct((4, 4, 16, 128), BF16),
            jax.ShapeDtypeStruct((16, 128), BF16),
            jax.ShapeDtypeStruct((8, 4, 32, 256), F32),
            jax.ShapeDtypeStruct((6, 6, 32, 128), BF16),
            jax.ShapeDtypeStruct((4, 256, 256), F32),
            jax.ShapeDtypeStruct((5, 128, 256), BF16),
        ),
        in_specs=[VMEM] * len(operands),
        out_specs=(VMEM,) * 8,
        scratch_shapes=[
            pltpu.VMEM((22, 80, 256), BF16),
            pltpu.VMEM((11, 128, 640), BF16),
            pltpu.VMEM((11, 640, 128), BF16),
            pltpu.VMEM((10, 10, 80, 128), F32),
            pltpu.VMEM((10, 10, 32, 128), BF16),
            pltpu.VMEM((8, 4, 32, 256), F32),
            pltpu.VMEM((4, 32, 128), F32),
        ],
        compiler_params=pltpu.CompilerParams(vmem_limit_bytes=LIMIT),
    )(*operands)


def weave_kernel(lower, hidden2, upper, own_cot, to_next, to_previous):
    for target, first_row in ((to_next, 0), (to_previous, 2)):
        for y in range(2):
            row, at = first_row + y, y * 128
            target[at : at + 32] = lower[row * 32 : row * 32 + 32]
            target[at + 32 : at + 96] = hidden2[row].reshape(64, 128)
            target[at + 96 : at + 128] = upper[row * 32 : row * 32 + 32]
        target[256:272] = lower[128:144]
        target[272:288] = own_cot[...]
        target[288:304] = upper[128:144]


def run_weave(*operands):
    return pl.pallas_call(
        weave_kernel,
        name="weave",
        out_shape=(jax.ShapeDtypeStruct((304, 128), BF16),) * 2,
        in_specs=[VMEM] * 4,
        out_specs=(VMEM,) * 2,
        compiler_params=pltpu.CompilerParams(vmem_limit_bytes=LIMIT),
    )(*operands)


def lay_patches2(rows, target):
    half = lane((16, 128)) < 64
    swapped = roll(rows.astype(F32), 64, 1)
    target[...] = jnp.concatenate(
        [jnp.where(half, down(swapped), swapped), jnp.where(half, swapped, up(swapped))], axis=1
    ).astype(BF16)


def pool3(pre, cot):
    e = exps(pre)
    total = e[0, 0] + e[0, 1] + e[1, 0] + e[1, 1]
    total = total[:, :128] + total[:, 128:]
    mean = total * 0.125
    share = cot.astype(F32) * (0.125 / mean)
    share = jnp.concatenate([share, share], axis=1)
    return mean, (jnp.where(pre > 0, 1.0, SLOPE) * (e * share)).astype(BF16)


def own_kernel(hidden2, own_cot, w3, biases, packed, shift3, patches2, pre3, turned):
    groups = packed.shape[0]
    wide = 128 // groups
    for y in range(4):
        for z in range(4):
            lay_patches2(hidden2[y, z], patches2.at[y, z])
    for tap in range(9):
        dy, dz = tap // 3, tap % 3
        block = patches2[dy : dy + 2, dz : dz + 2].reshape(64, 256)
        term = dot(block, w3[tap])
        pre3[...] = term + biases[2:3] if tap == 0 else pre3[...] + term
    mean, delta = pool3(pre3[...].reshape(2, 2, 16, 256), own_cot[...])
    features = rounded(jnp.log(mean) * 0.5)
    own3 = delta.reshape(64, 256)
    bias3 = own3.astype(F32).sum(axis=0, keepdims=True)
    shift3[...] = bias3[:, :128] + bias3[:, 128:]
    low, high = [], []
    for tap in range(9):
        dy, dz = tap // 3, tap % 3
        block = patches2[dy : dy + 2, dz : dz + 2].reshape(64, 256)
        full = dot_tn(own3, block)
        one = full[:128]
        low_lanes, high_lanes = roll(full[128:, :128], 64, 1), roll(full[128:, 128:], 64, 1)
        tile0 = jnp.where(lane((128, 128)) < 64, low_lanes, high_lanes)
        tile1 = high_lanes
        low.append(one[:, :128] + tile0)
        high.append(one[:, 128:] + tile1)
    first_half = lane((128, 128)) < 64
    paired = []
    for m in range(5):
        other = roll(high[2 * m + 1], 64, 1) if 2 * m + 1 < 9 else jnp.zeros((128, 128), F32)
        paired.append(jnp.where(first_half, high[2 * m], other))
    kernel3 = [piece.reshape(groups, wide, 128) for piece in low + paired]

    turned[...] = jnp.concatenate([features, jnp.zeros((112, 128), F32)], axis=0).T
    feature_rows = turned[pl.ds(0, 16, stride=8), :]
    for c in range(1, 8):
        feature_rows = feature_rows + roll(turned[pl.ds(c, 16, stride=8), :], 16 * c, 1)
    feature_rows = feature_rows.reshape(groups, wide // 8, 128)
    fill = jnp.zeros((groups, packed.shape[1] - 14 * wide - wide // 8, 128), F32)
    packed[...] = jnp.concatenate(kernel3 + [feature_rows, fill], axis=1).astype(BF16)


def run_own(groups, *operands):
    wide = 128 // groups
    return pl.pallas_call(
        own_kernel,
        name="own",
        out_shape=(
            jax.ShapeDtypeStruct((groups, -(-(14 * wide + wide // 8) // 8) * 8, 128), BF16),
            jax.ShapeDtypeStruct((1, 128), F32),
        ),
        in_specs=[VMEM] * len(operands),
        out_specs=(VMEM,) * 2,
        scratch_shapes=[
            pltpu.VMEM((4, 4, 16, 256), BF16),
            pltpu.VMEM((64, 256), F32),
            pltpu.VMEM((128, 128), F32),
        ],
        compiler_params=pltpu.CompilerParams(vmem_limit_bytes=LIMIT),
        cost_estimate=pl.CostEstimate(flops=150000000, bytes_accessed=4000000, transcendentals=20000),
    )(*operands)


def backward_kernel(
    before, lower, middle, upper, after, own_cot, w3, biases, w2, ratio2, patches1, ratio1, fields, packed3, shift3,
    packed, patches2, pre3, delta3, patch2, grad2, delta2, patch1, grad1, delta1,
):
    groups = packed.shape[0]
    half = lane((16, 128)) < 64

    def lay(y, source):
        for z in range(8):
            lay_patches2(source(z), patches2.at[y, z])

    for y in range(2):
        lay(y, lambda z: before[(y * 8 + z) * 16 : (y * 8 + z + 1) * 16])
        lay(y + 6, lambda z: after[(y * 8 + z) * 16 : (y * 8 + z + 1) * 16])

    def pick_middle(y, z):
        if z < 2:
            return lower[(y * 2 + z) * 16 : (y * 2 + z + 1) * 16]
        if z < 6:
            return middle[y, z - 2]
        return upper[(y * 2 + z - 6) * 16 : (y * 2 + z - 5) * 16]

    for y in range(4):
        lay(y + 2, functools.partial(pick_middle, y))

    for tap in range(9):
        dy, dz = tap // 3, tap % 3
        block = patches2[dy : dy + 6, dz : dz + 6].reshape(576, 256)
        term = dot(block, w3[tap]).reshape(6, 6, 16, 256)
        pre3[...] = term + biases[2:3] if tap == 0 else pre3[...] + term

    for wy in range(3):
        for wz in range(3):
            pre = pre3[2 * wy : 2 * wy + 2, 2 * wz : 2 * wz + 2]
            if wy == 1:
                cot = own_cot[...] if wz == 1 else (lower if wz == 0 else upper)[128:144]
            else:
                cot = (before if wy == 0 else after)[256 + wz * 16 : 272 + wz * 16]
            delta3[2 * wy : 2 * wy + 2, 2 * wz : 2 * wz + 2] = pool3(pre, cot)[1]

    for tap in range(9):
        dy, dz = tap // 3, tap % 3
        block = delta3[2 - dy : 6 - dy, 2 - dz : 6 - dz].reshape(256, 256)
        term = dot_nt(block, w3[tap]).reshape(4, 4, 16, 256)
        patch2[...] = term if tap == 0 else patch2[...] + term

    for y in range(4):
        for z in range(4):
            a, b = patch2[y, z, :, :128], patch2[y, z, :, 128:]
            x = rounded(jnp.where(half, b + up(a), a + down(b)))
            swapped = roll(x, 64, 1)
            grad2[y, z, pl.ds(0, 16, stride=2), :] = jnp.where(half, swapped, x)
            grad2[y, z, pl.ds(1, 16, stride=2), :] = jnp.where(half, x, swapped)

    for y in range(6):
        value = grad2[(y + 1) // 2]
        value = jnp.concatenate([value, value], axis=2)
        delta2[y] = (value * ratio2[y + 1]).astype(BF16)

    own2 = delta2[1:5, 1:3].reshape(256, 256)
    bias2 = own2.astype(F32).sum(axis=0, keepdims=True)
    bias2 = bias2[:, :128] + bias2[:, 128:]
    bias2 = bias2 + roll(bias2, 64, 1)
    taps = [None] * 27
    for dy in range(3):
        block = jnp.concatenate(
            [
                jnp.concatenate([patches1[dy : dy + 4, 2 * zo + pz] for pz in range(4)], axis=2)[:, None]
                for zo in range(2)
            ],
            axis=1,
        ).reshape(256, 512)
        full = dot_tn(block, own2)
        for dz in range(3):
            rows = full[dz * 128 : dz * 128 + 128, :128] + full[dz * 128 + 128 : dz * 128 + 256, 128:]
            for dx in range(3):
                taps[dx * 9 + dy * 3 + dz] = rows[dx * 32 : dx * 32 + 32] + roll(
                    rows[dx * 32 + 32 : dx * 32 + 64], 64, 1
                )
    for dy in range(3):
        block = delta2[2 - dy : 6 - dy].reshape(512, 256)
        term = dot_nt(block, w2[dy]).reshape(4, 4, 32, 512)
        patch1[...] = term if dy == 0 else patch1[...] + term

    low_half = lane((32, 128)) < 64
    group = lane((32, 128)) // 32

    def widen(value, which):
        value = jnp.where(group == which, value, 0.0)
        value = value + roll(value, 32, 1)
        return value + roll(value, 64, 1)


    def gather1(y, carry):
        for z, (zo_a, pz_a, zo_b, pz_b) in enumerate(((0, 3, 1, 1), (1, 2, 2, 0), (1, 3, 2, 1), (2, 2, 3, 0))):
            value = (
                patch1[y, zo_a, :, pz_a * 128 : pz_a * 128 + 128]
                + patch1[y, zo_b, :, pz_b * 128 : pz_b * 128 + 128]
            )
            value = rounded(value + roll(jnp.where(low_half, up(value), down(value)), 64, 1))
            grad1[z, pl.ds(0, 32, stride=2), :] = widen(value, 1)
            grad1[z, pl.ds(1, 32, stride=2), :] = widen(value, 2)
        value = grad1[...].reshape(256, 128)
        value = jnp.concatenate([value, value], axis=1)
        delta1[y] = (value * ratio1[y]).astype(BF16)
        return carry

    lax.fori_loop(0, 4, gather1, 0)

    bias1 = delta1[...].astype(F32).sum(axis=0).sum(axis=0, keepdims=True)
    bias1 = bias1[:, :128] + bias1[:, 128:]
    bias1 = bias1 + roll(bias1, 64, 1)
    bias1 = bias1 + roll(bias1, 32, 1)
    full = None
    for yw in range(4):
        term = dot(fields[yw : yw + 2].reshape(256, 256), delta1[yw])
        full = term if full is None else full + term
    full = full.reshape(4, 4, 16, 256)
    kernel1 = []
    group1 = lane((16, 128)) // 32
    for dy in range(3):
        rows = full[dy, :, :, :128] + full[dy + 1, :, :, 128:]
        pieces = []
        for dx in range(3):
            value = rows[dx] + roll(rows[dx + 1], 96, 1)
            value = value + roll(roll(value, 12, 0), 64, 1)
            pieces.append(roll(value, 32 * dx, 1) if dx else value)
        kernel1.append(jnp.where(group1 == 0, pieces[0], jnp.where(group1 == 1, pieces[1], pieces[2])))

    low_lane = lane((32, 128)) < 64
    kernel2 = [
        jnp.where(low_lane, taps[2 * m], roll(taps[2 * m + 1], 64, 1) if 2 * m + 1 < 27 else 0.0)
        for m in range(14)
    ]
    shifts = jnp.concatenate(
        [shift3[...], jnp.where(lane((1, 128)) < 64, bias2, bias1), jnp.zeros((14, 128), F32)], axis=0
    )
    shared = jnp.concatenate(kernel2 + kernel1 + [shifts], axis=0)
    rows = 512 // groups
    packed[:, :rows] = shared.reshape(groups, rows, 128).astype(BF16)
    packed[:, rows:] = packed3[...]


def run_backward(groups, *operands):
    return pl.pallas_call(
        backward_kernel,
        name="backward",
        out_shape=jax.ShapeDtypeStruct((groups, 512 // groups + operands[-2].shape[1], 128), BF16),
        in_specs=[VMEM] * len(operands),
        out_specs=VMEM,
        scratch_shapes=[
            pltpu.VMEM((8, 8, 16, 256), BF16),
            pltpu.VMEM((6, 6, 16, 256), F32),
            pltpu.VMEM((6, 6, 16, 256), BF16),
            pltpu.VMEM((4, 4, 16, 256), F32),
            pltpu.VMEM((4, 4, 32, 128), F32),
            pltpu.VMEM((6, 4, 32, 256), BF16),
            pltpu.VMEM((4, 4, 32, 512), F32),
            pltpu.VMEM((4, 64, 128), F32),
            pltpu.VMEM((4, 256, 256), BF16),
        ],
        compiler_params=pltpu.CompilerParams(vmem_limit_bytes=LIMIT),
    )(*operands)


def sum_kernel(received, to_column, features):
    groups, rows = received.shape[0], to_column.shape[1]
    wide = 128 // groups
    own = received[:, rows : rows + wide // 8].astype(F32)
    for c in range(wide):
        features[c] = own[:, c // 8, (c % 8) * 16 : (c % 8) * 16 + 16].astype(BF16)
    total = received[:, :rows].astype(F32).sum(axis=0)
    to_column[...] = jnp.broadcast_to(total[None], to_column.shape).astype(BF16)


def run_sum(received, rows_y):
    groups = received.shape[0]
    wide = 128 // groups
    return pl.pallas_call(
        sum_kernel,
        name="sum",
        out_shape=(
            jax.ShapeDtypeStruct((rows_y, 512 // groups + 14 * wide, 128), BF16),
            jax.ShapeDtypeStruct((wide, groups, 16), BF16),
        ),
        in_specs=[VMEM],
        out_specs=(VMEM, VMEM),
        compiler_params=pltpu.CompilerParams(vmem_limit_bytes=LIMIT),
    )(received)


def share_kernel(column, to_all):
    total = column[:, : to_all.shape[1]].astype(F32).sum(axis=0)
    to_all[...] = jnp.broadcast_to(total[None], to_all.shape).astype(BF16)


def run_share(column, groups):
    return pl.pallas_call(
        share_kernel,
        name="share",
        out_shape=jax.ShapeDtypeStruct((groups, 512 // groups, 128), BF16),
        in_specs=[VMEM],
        out_specs=VMEM,
        compiler_params=pltpu.CompilerParams(vmem_limit_bytes=LIMIT),
    )(column)


def third_kernel(column, grad3):
    wide = grad3.shape[1]
    first = column.shape[1] - 14 * wide
    lines = column[:, first:].astype(F32).sum(axis=0)
    for tap in range(9):
        low = lines[tap * wide : tap * wide + wide]
        grad3[tap] = low[:, :64]
        grad3[9 + tap] = low[:, 64:]
        at = (9 + tap // 2) * wide
        grad3[18 + tap] = lines[at : at + wide][:, (tap % 2) * 64 : (tap % 2) * 64 + 64]


def run_third(column, wide):
    return pl.pallas_call(
        third_kernel,
        name="third",
        out_shape=jax.ShapeDtypeStruct((27, wide, 64), F32),
        in_specs=[VMEM],
        out_specs=VMEM,
        compiler_params=pltpu.CompilerParams(vmem_limit_bytes=LIMIT),
    )(column)


def unpack_kernel(shared, grad1, grad2, shift1, shift2, shift3):
    wide = shift3.shape[1]
    rows = shared[...].astype(F32).reshape(512, 128)
    for tap in range(27):
        at = (tap // 2) * 32
        grad2[tap] = rows[at : at + 32, (tap % 2) * 64 : (tap % 2) * 64 + 64]
    for dy in range(3):
        for dz in range(3):
            at = 448 + dy * 16 + dz * 4
            for dx in range(3):
                grad1[dx * 9 + dy * 3 + dz] = rows[at : at + 4, dx * 32 : dx * 32 + 32]
    biases = rows[496:504]
    shift1[...] = biases[1:2, 64:96]
    shift2[...] = biases[1:2, :64]
    place = lax.axis_index("gz")
    shift3[...] = roll(biases, lax.rem(128 - place * wide, 128), 1)[0:1, :wide]


def run_unpack(shared):
    wide = 128 // shared.shape[0]
    return pl.pallas_call(
        unpack_kernel,
        name="unpack",
        out_shape=(
            jax.ShapeDtypeStruct((27, 4, 32), F32),
            jax.ShapeDtypeStruct((27, 32, 64), F32),
            jax.ShapeDtypeStruct((1, 32), F32),
            jax.ShapeDtypeStruct((1, 64), F32),
            jax.ShapeDtypeStruct((1, wide), F32),
        ),
        in_specs=[VMEM],
        out_specs=(VMEM,) * 5,
        compiler_params=pltpu.CompilerParams(vmem_limit_bytes=LIMIT),
    )(shared)


def both_ways(to_next, to_previous, axis):
    devices = lax.axis_size(axis)
    forth = [(i, i + 1) for i in range(devices - 1)]
    back = [(i + 1, i) for i in range(devices - 1)]
    return lax.ppermute(to_next, axis, forth), lax.ppermute(to_previous, axis, back)


def shards(universe, kernel1, bias1, kernel2, bias2, kernel3, bias3, cotangent):
    size_y, size_z = lax.axis_size("gy"), lax.axis_size("gz")
    wide = 128 // size_z

    tile = universe.transpose(1, 2, 0, 3).reshape(8, 32, 128)
    cot = lax.all_to_all(cotangent[:, 0].transpose(1, 0, 2), "gz", 0, 0, tiled=True).reshape(128, 16)
    tile, cot = lax.optimization_barrier((tile, cot))
    lower, upper = both_ways(tile, tile, "gz")
    strip = jnp.concatenate([lower[:, 4:], tile, upper[:, :28], jnp.zeros((8, 8, 128), BF16)], axis=1)
    top, bottom = both_ways(strip, strip, "gy")

    k1, k2, k3 = kernel1.transpose(0, 2, 1), kernel2.transpose(0, 2, 1), kernel3.transpose(0, 2, 1)
    w1, w2, w3, biases, pick = run_weights(k1, bias1[None], k2, bias2[None], k3, bias3[None])
    to_next, to_previous, hidden2, own_cot, ratio2, patches1, ratio1, fields = run_forward(
        top, strip, bottom, cot, w1, w2, biases, pick
    )
    lower, upper = both_ways(to_next, to_previous, "gz")
    packed3, shift3 = run_own(size_z, hidden2, own_cot, w3, biases)
    row_next, row_previous = run_weave(lower, hidden2, upper, own_cot)
    before, after = both_ways(row_next, row_previous, "gy")
    packed = run_backward(
        size_z,
        before, lower, hidden2, upper, after, own_cot, w3, biases, w2, ratio2, patches1, ratio1, fields,
        packed3, shift3,
    )
    packed = lax.all_to_all(packed, "gz", 0, 0, tiled=True)
    column, features = run_sum(packed, size_y)
    column = lax.all_to_all(column, "gy", 0, 0, tiled=True)
    shared = lax.all_to_all(run_share(column, size_z), "gz", 0, 0, tiled=True)
    grad3 = run_third(column, wide)
    grad1, grad2, shift1, shift2, shift3 = run_unpack(shared)
    return (
        features[:, None], grad1.transpose(0, 2, 1), shift1[0], grad2.transpose(0, 2, 1), shift2[0], grad3, shift3[0]
    )


def solution(mesh):
    in_specs = (P(None, "gy", "gz", None), P(), P(), P(), P(), P(), P(), P("gz", "gy", None, None))
    out_specs = (P("gz", "gy", None, None), P(), P(), P(), P(), P(None, "gz", None), P("gz"))
    return jax.shard_map(shards, mesh=mesh, in_specs=in_specs, out_specs=out_specs, check_vma=False)
```

```python
import functools
import math

import jax
import jax.numpy as jnp
from jax import lax
from jax.experimental import pallas as pl
from jax.experimental.pallas import tpu as pltpu
from jax.sharding import PartitionSpec as P

F32 = jnp.float32
BF16 = jnp.bfloat16
SLOPE = 0.3
TWO_LOG2_E = 2.0 / math.log(2.0)
PAIRS = ((0, 1), (2, 3), (-3, -2), (4, 5), (-1, 6))
VMEM = pl.BlockSpec(memory_space=pltpu.VMEM)
LIMIT = 24 * 1024 * 1024


def dot(a, b):
    return jnp.dot(a, b, preferred_element_type=F32)


def dot_tn(a, b):
    return lax.dot_general(a, b, (((0,), (0,)), ((), ())), preferred_element_type=F32)


def dot_nt(a, b):
    return lax.dot_general(a, b, (((1,), (1,)), ((), ())), preferred_element_type=F32)


def lane(shape):
    return lax.broadcasted_iota(jnp.int32, shape, len(shape) - 1)


def exps(pre):
    scaled = pre * TWO_LOG2_E
    return jnp.exp2(jnp.maximum(scaled, SLOPE * scaled))


def rounded(value):
    return value.astype(BF16).astype(F32)


def roll(value, amount, axis):
    return pltpu.roll(value, amount, axis)


def down(value):
    rows = lax.broadcasted_iota(jnp.int32, value.shape, 0)
    return jnp.where(rows == 0, 0.0, roll(value, 1, 0))


def up(value):
    count = value.shape[0]
    rows = lax.broadcasted_iota(jnp.int32, value.shape, 0)
    return jnp.where(rows == count - 1, 0.0, roll(value, count - 1, 0))


def lay_pick(pick):
    for px in range(4):
        row = lax.broadcasted_iota(jnp.int32, (256, 128), 0)
        col = lax.broadcasted_iota(jnp.int32, (256, 128), 1)
        same = row // 128 == col // 64
        hit = (row % 128) == 2 * (col % 64) - 1 + px
        pick[:, px * 128 : px * 128 + 128] = jnp.where(same & hit, 1.0, 0.0).astype(BF16)


def forward_kernel(
    top, mid, bot, cot, k1, b1, k2, b2,
    to_next, to_previous, hidden2, own_cot, ratio2, patches1, ratio1, fields, w2,
    w1, pick, left, field, turned, pre1, first, spread, pre2, second,
):
    lay_weights1(k1, w1)
    lay_weights2(k2, w2)
    lay_pick(pick)
    bias1 = jnp.concatenate([b1[...]] * 8, axis=1)
    bias2 = jnp.concatenate([b2[...]] * 4, axis=1)
    base_y, base_z = lax.axis_index("gy"), lax.axis_index("gz")
    size_y, size_z = lax.axis_size("gy"), lax.axis_size("gz")

    def inside(offset_y, offset_z, scale):
        row = base_y * (4 // scale) + offset_y
        col = base_z * (4 // scale) + offset_z
        ok_y = (row >= 0) & (row < size_y * (4 // scale))
        ok_z = (col >= 0) & (col < size_z * (4 // scale))
        return jnp.where(ok_y & ok_z, 1.0, 0.0)

    def lay(source, index, target):
        rows = source[index].astype(F32)
        pieces = []
        for one, two in PAIRS:
            a, b = 8 * (one + 3), 8 * (two + 3)
            pieces.append(jnp.concatenate([rows[a : a + 16], rows[b : b + 16]], axis=1))
        left[target] = jnp.concatenate(pieces, axis=0).astype(BF16)

    def lay_top(step, carry):
        lay(top, step + 1, step)
        return carry

    def lay_mid(step, carry):
        lay(mid, step, step + 7)
        return carry

    def lay_bot(step, carry):
        lay(bot, step, step + 15)
        return carry

    lax.fori_loop(0, 7, lay_top, 0)
    lax.fori_loop(0, 8, lay_mid, 0)
    lax.fori_loop(0, 7, lay_bot, 0)

    def sift(step, carry):
        block = left[pl.ds(2 * step, 2)].reshape(160, 256)
        out = dot(block, pick[...]).astype(BF16).reshape(2, 5, 16, 512)
        for parity in range(2):
            for px in range(4):
                at = (parity * 4 + px) * 16
                for k in range(5):
                    field[step, at : at + 16, k * 128 : k * 128 + 128] = out[
                        parity, k, :, px * 128 : px * 128 + 128
                    ]
        turned[step] = field[step].T
        return carry

    lax.fori_loop(0, 11, sift, 0)
    fields[...] = field[3:8, :, :256]
    first[:, :, 0:8] = jnp.zeros((10, 10, 8, 128), F32)
    first[:, :, 72:80] = jnp.zeros((10, 10, 8, 128), F32)

    def block1(yw, carry):
        stack = jnp.concatenate([turned[yw], turned[yw + 1]], axis=1)
        pre1[...] = dot(stack, w1[...])
        place = jnp.where((yw >= 3) & (yw < 7), yw - 3, 4)
        for k, pair in enumerate(PAIRS):
            for h, zw in enumerate(pair):
                at = k * 128 + h * 64
                pre = pre1[at : at + 64] + bias1
                e = exps(pre)
                total = e[:, :128] + e[:, 128:]
                total = total + roll(total, 64, 1)
                total = total + roll(total, 32, 1)
                mean = total * 0.125
                pooled = rounded(jnp.log(mean) * 0.5)
                first[yw, zw + 3, 8:72] = pooled * inside(yw - 3, zw, 1)
                if k < 2:
                    share = 0.125 / mean
                    share = jnp.concatenate([share, share], axis=1)
                    ratio1[place, at : at + 64] = jnp.where(pre > 0, 1.0, SLOPE) * (e * share)
        return carry

    lax.fori_loop(0, 10, block1, 0)

    group1 = lane((32, 128)) // 32

    def frame(yi, carry):
        for zi in range(10):
            part = first[yi, zi, pl.ds(7, 32, stride=2), :]
            for px in range(1, 4):
                part = jnp.where(group1 == px, first[yi, zi, pl.ds(7 + px, 32, stride=2), :], part)
            spread[yi, zi] = part.astype(BF16)
        return carry

    lax.fori_loop(0, 10, frame, 0)
    patches1[...] = spread[2:8, 2:8]

    half = lane((16, 128)) < 64

    def block2(yp, carry):
        columns = []
        for zo in range(4):
            tiles = [spread[pl.ds(2 * yp + dy, 2), 2 * zo + pz] for dy in range(3) for pz in range(4)]
            columns.append(jnp.concatenate(tiles, axis=2)[:, None])
        block = jnp.concatenate(columns, axis=1).reshape(256, 1536)
        pre2[...] = dot(block, w2[...].reshape(1536, 256)).reshape(2, 4, 32, 256)
        for zo in range(4):
            pre = pre2[:, zo] + bias2
            e = exps(pre)
            both = e[0] + e[1]
            total = both[:, :128] + both[:, 128:]
            total = total + roll(total, 64, 1)
            mean = total * 0.125
            ok = inside(yp - 1, zo - 1, 2)
            share = (0.125 * ok) / mean
            share = jnp.concatenate([share, share], axis=1)
            ratio2[pl.ds(2 * yp, 2), zo] = jnp.where(pre > 0, 1.0, SLOPE) * (e * share[None])
            second[zo] = rounded(jnp.log(mean) * 0.5) * ok
            even = second[zo, pl.ds(0, 16, stride=2), :]
            odd = second[zo, pl.ds(1, 16, stride=2), :]
            hidden2[yp, zo] = jnp.where(half, even, odd).astype(BF16)
        return carry

    lax.fori_loop(0, 4, block2, 0)
    to_next[0:128] = hidden2[:, 0:2].reshape(128, 128)
    to_previous[0:128] = hidden2[:, 2:4].reshape(128, 128)
    own = cot[...].astype(F32).T.astype(BF16)
    to_next[128:144] = own
    to_previous[128:144] = own
    own_cot[...] = own


def lay_weights1(taps, out):
    group = lane((16, 128)) // 32
    zero = jnp.zeros((16, 128), F32)
    wide = []
    for k in range(9):
        pieces = [taps[3 * k + dz].astype(F32) for dz in range(3)] + [jnp.zeros((4, 32), F32)]
        rows = jnp.concatenate(pieces, axis=0)
        wide.append(jnp.concatenate([rows] * 4, axis=1))
    for py in range(4):
        for px in range(4):
            at = (py * 4 + px) * 16
            for qy in range(2):
                dy = py - qy
                sides = [
                    wide[(px - qx) * 3 + dy] if 0 <= dy < 3 and 0 <= px - qx < 3 else zero for qx in range(2)
                ]
                value = jnp.where(group == 0, sides[0], sides[1])
                shifted = jnp.where(group == 2, roll(sides[0], 4, 0), roll(sides[1], 4, 0))
                out[at : at + 16, qy * 128 : qy * 128 + 128] = jnp.where(group < 2, value, shifted).astype(BF16)


def lay_weights2(taps, out):
    zero = jnp.zeros((32, 64), BF16)
    for dy in range(3):
        out[dy, 384:512, 0:128] = jnp.zeros((128, 128), BF16)
        out[dy, 0:128, 128:256] = jnp.zeros((128, 128), BF16)
        for dz in range(3):
            for px in range(4):
                sides = [taps[(px - qx) * 9 + dy * 3 + dz] if 0 <= px - qx < 3 else zero for qx in range(2)]
                tile = jnp.concatenate(sides, axis=1)
                for qz in range(2):
                    at = (dz + qz) * 128 + px * 32
                    out[dy, at : at + 32, qz * 128 : qz * 128 + 128] = tile


def lay_weights3(taps, out):
    zero = jnp.zeros((64, 128), BF16)
    for tap in range(9):
        out[tap, 192:256, 0:128] = zero
        out[tap, 0:64, 128:256] = zero
        for dx in range(3):
            value = taps[dx * 9 + tap]
            out[tap, dx * 64 : dx * 64 + 64, 0:128] = value
            out[tap, dx * 64 + 64 : dx * 64 + 128, 128:256] = value


def run_forward(*operands):
    return pl.pallas_call(
        forward_kernel,
        name="forward",
        out_shape=(
            jax.ShapeDtypeStruct((144, 128), BF16),
            jax.ShapeDtypeStruct((144, 128), BF16),
            jax.ShapeDtypeStruct((4, 4, 16, 128), BF16),
            jax.ShapeDtypeStruct((16, 128), BF16),
            jax.ShapeDtypeStruct((8, 4, 32, 256), F32),
            jax.ShapeDtypeStruct((6, 6, 32, 128), BF16),
            jax.ShapeDtypeStruct((5, 256, 256), F32),
            jax.ShapeDtypeStruct((5, 128, 256), BF16),
            jax.ShapeDtypeStruct((3, 512, 256), BF16),
        ),
        in_specs=[VMEM] * len(operands),
        out_specs=(VMEM,) * 9,
        scratch_shapes=[
            pltpu.VMEM((256, 256), BF16),
            pltpu.VMEM((256, 512), BF16),
            pltpu.VMEM((22, 80, 256), BF16),
            pltpu.VMEM((11, 128, 640), BF16),
            pltpu.VMEM((11, 640, 128), BF16),
            pltpu.VMEM((640, 256), F32),
            pltpu.VMEM((10, 10, 80, 128), F32),
            pltpu.VMEM((10, 10, 32, 128), BF16),
            pltpu.VMEM((2, 4, 32, 256), F32),
            pltpu.VMEM((4, 32, 128), F32),
        ],
        compiler_params=pltpu.CompilerParams(vmem_limit_bytes=LIMIT),
    )(*operands)


def weave_kernel(lower, hidden2, upper, own_cot, to_next, to_previous):
    for target, first_row in ((to_next, 0), (to_previous, 2)):
        for y in range(2):
            row, at = first_row + y, y * 128
            target[at : at + 32] = lower[row * 32 : row * 32 + 32]
            target[at + 32 : at + 96] = hidden2[row].reshape(64, 128)
            target[at + 96 : at + 128] = upper[row * 32 : row * 32 + 32]
        target[256:272] = lower[128:144]
        target[272:288] = own_cot[...]
        target[288:304] = upper[128:144]


def run_weave(*operands):
    return pl.pallas_call(
        weave_kernel,
        name="weave",
        out_shape=(jax.ShapeDtypeStruct((304, 128), BF16),) * 2,
        in_specs=[VMEM] * 4,
        out_specs=(VMEM,) * 2,
        compiler_params=pltpu.CompilerParams(vmem_limit_bytes=LIMIT),
    )(*operands)


def lay_patches2(rows, target):
    half = lane((16, 128)) < 64
    swapped = roll(rows.astype(F32), 64, 1)
    target[...] = jnp.concatenate(
        [jnp.where(half, down(swapped), swapped), jnp.where(half, swapped, up(swapped))], axis=1
    ).astype(BF16)


def pool3(pre, cot):
    e = exps(pre)
    total = e[0, 0] + e[0, 1] + e[1, 0] + e[1, 1]
    total = total[:, :128] + total[:, 128:]
    mean = total * 0.125
    share = cot.astype(F32) * (0.125 / mean)
    share = jnp.concatenate([share, share], axis=1)
    return mean, (jnp.where(pre > 0, 1.0, SLOPE) * (e * share)).astype(BF16)


def own_kernel(hidden2, own_cot, k3, b3, packed, shift3, w3, wide3, patches2, pre3, turned):
    groups = packed.shape[0]
    wide = 128 // groups
    lay_weights3(k3, w3)
    wide3[...] = jnp.concatenate([b3[...]] * 2, axis=1)
    for y in range(4):
        for z in range(4):
            lay_patches2(hidden2[y, z], patches2.at[y, z])
    for tap in range(9):
        dy, dz = tap // 3, tap % 3
        block = patches2[dy : dy + 2, dz : dz + 2].reshape(64, 256)
        term = dot(block, w3[tap])
        pre3[...] = term + wide3[...] if tap == 0 else pre3[...] + term
    mean, delta = pool3(pre3[...].reshape(2, 2, 16, 256), own_cot[...])
    features = rounded(jnp.log(mean) * 0.5)
    own3 = delta.reshape(64, 256)
    bias3 = own3.astype(F32).sum(axis=0, keepdims=True)
    shift3[...] = bias3[:, :128] + bias3[:, 128:]
    low, high = [], []
    for tap in range(9):
        dy, dz = tap // 3, tap % 3
        block = patches2[dy : dy + 2, dz : dz + 2].reshape(64, 256)
        full = dot_tn(own3, block)
        one = full[:128]
        low_lanes, high_lanes = roll(full[128:, :128], 64, 1), roll(full[128:, 128:], 64, 1)
        tile0 = jnp.where(lane((128, 128)) < 64, low_lanes, high_lanes)
        tile1 = high_lanes
        low.append(one[:, :128] + tile0)
        high.append(one[:, 128:] + tile1)
    first_half = lane((128, 128)) < 64
    paired = []
    for m in range(5):
        other = roll(high[2 * m + 1], 64, 1) if 2 * m + 1 < 9 else jnp.zeros((128, 128), F32)
        paired.append(jnp.where(first_half, high[2 * m], other))
    kernel3 = [piece.reshape(groups, wide, 128) for piece in low + paired]

    turned[...] = jnp.concatenate([features, jnp.zeros((112, 128), F32)], axis=0).T
    feature_rows = turned[pl.ds(0, 16, stride=8), :]
    for c in range(1, 8):
        feature_rows = feature_rows + roll(turned[pl.ds(c, 16, stride=8), :], 16 * c, 1)
    feature_rows = feature_rows.reshape(groups, wide // 8, 128)
    fill = jnp.zeros((groups, packed.shape[1] - 14 * wide - wide // 8, 128), F32)
    packed[...] = jnp.concatenate(kernel3 + [feature_rows, fill], axis=1).astype(BF16)


def run_own(groups, *operands):
    wide = 128 // groups
    return pl.pallas_call(
        own_kernel,
        name="own",
        out_shape=(
            jax.ShapeDtypeStruct((groups, -(-(14 * wide + wide // 8) // 8) * 8, 128), BF16),
            jax.ShapeDtypeStruct((1, 128), F32),
            jax.ShapeDtypeStruct((9, 256, 256), BF16),
            jax.ShapeDtypeStruct((1, 256), F32),
        ),
        in_specs=[VMEM] * len(operands),
        out_specs=(VMEM,) * 4,
        scratch_shapes=[
            pltpu.VMEM((4, 4, 16, 256), BF16),
            pltpu.VMEM((64, 256), F32),
            pltpu.VMEM((128, 128), F32),
        ],
        compiler_params=pltpu.CompilerParams(vmem_limit_bytes=LIMIT),
        cost_estimate=pl.CostEstimate(flops=150000000, bytes_accessed=4000000, transcendentals=20000),
    )(*operands)


def backward_kernel(
    before, lower, middle, upper, after, own_cot, w3, bias3, w2, ratio2, patches1, ratio1, fields, packed3, shift3,
    packed, patches2, pre3, delta3, patch2, grad2, delta2, patch1, beside, grad1, delta1,
):
    groups = packed.shape[0]
    half = lane((16, 128)) < 64

    def lay(y, source):
        for z in range(8):
            lay_patches2(source(z), patches2.at[y, z])

    for y in range(2):
        lay(y, lambda z: before[(y * 8 + z) * 16 : (y * 8 + z + 1) * 16])
        lay(y + 6, lambda z: after[(y * 8 + z) * 16 : (y * 8 + z + 1) * 16])

    def pick_middle(y, z):
        if z < 2:
            return lower[(y * 2 + z) * 16 : (y * 2 + z + 1) * 16]
        if z < 6:
            return middle[y, z - 2]
        return upper[(y * 2 + z - 6) * 16 : (y * 2 + z - 5) * 16]

    for y in range(4):
        lay(y + 2, functools.partial(pick_middle, y))

    for dy in range(3):
        blocks = [patches2[dy : dy + 6, dz : dz + 6].reshape(576, 256) for dz in range(3)]
        weights = w3[3 * dy : 3 * dy + 3].reshape(768, 256)
        term = dot(jnp.concatenate(blocks, axis=1), weights).reshape(6, 6, 16, 256)
        pre3[...] = term + bias3[...] if dy == 0 else pre3[...] + term

    for wy in range(3):
        for wz in range(3):
            pre = pre3[2 * wy : 2 * wy + 2, 2 * wz : 2 * wz + 2]
            if wy == 1:
                cot = own_cot[...] if wz == 1 else (lower if wz == 0 else upper)[128:144]
            else:
                cot = (before if wy == 0 else after)[256 + wz * 16 : 272 + wz * 16]
            delta3[2 * wy : 2 * wy + 2, 2 * wz : 2 * wz + 2] = pool3(pre, cot)[1]

    for dy in range(3):
        blocks = [delta3[2 - dy : 6 - dy, 2 - dz : 6 - dz].reshape(256, 256) for dz in range(3)]
        weights = jnp.concatenate([w3[3 * dy + dz] for dz in range(3)], axis=1)
        term = dot_nt(jnp.concatenate(blocks, axis=1), weights).reshape(4, 4, 16, 256)
        patch2[...] = term if dy == 0 else patch2[...] + term

    for y in range(4):
        for z in range(4):
            a, b = patch2[y, z, :, :128], patch2[y, z, :, 128:]
            x = rounded(jnp.where(half, b + up(a), a + down(b)))
            swapped = roll(x, 64, 1)
            grad2[y, z, pl.ds(0, 16, stride=2), :] = jnp.where(half, swapped, x)
            grad2[y, z, pl.ds(1, 16, stride=2), :] = jnp.where(half, x, swapped)

    for y in range(6):
        value = grad2[(y + 1) // 2]
        value = jnp.concatenate([value, value], axis=2)
        delta2[y] = (value * ratio2[y + 1]).astype(BF16)

    own2 = delta2[1:5, 1:3].reshape(256, 256)
    bias2 = own2.astype(F32).sum(axis=0, keepdims=True)
    bias2 = bias2[:, :128] + bias2[:, 128:]
    bias2 = bias2 + roll(bias2, 64, 1)
    taps = [None] * 27
    for dy in range(3):
        block = jnp.concatenate(
            [
                jnp.concatenate([patches1[dy : dy + 4, 2 * zo + pz] for pz in range(4)], axis=2)[:, None]
                for zo in range(2)
            ],
            axis=1,
        ).reshape(256, 512)
        full = dot_tn(block, own2)
        for dz in range(3):
            rows = full[dz * 128 : dz * 128 + 128, :128] + full[dz * 128 + 128 : dz * 128 + 256, 128:]
            for dx in range(3):
                taps[dx * 9 + dy * 3 + dz] = rows[dx * 32 : dx * 32 + 32] + roll(
                    rows[dx * 32 + 32 : dx * 32 + 64], 64, 1
                )
    def g1(columns, lanes, rows):
        blocks = [delta2[2 - dy : 6 - dy, columns, :, lanes].reshape(-1, lanes.stop - lanes.start) for dy in range(3)]
        weights = jnp.concatenate([w2[dy, rows, lanes] for dy in range(3)], axis=1)
        return dot_nt(jnp.concatenate(blocks, axis=1), weights)

    patch1[...] = g1(slice(1, 3), slice(0, 256), slice(0, 512)).reshape(4, 2, 32, 512)
    below = g1(slice(0, 1), slice(128, 256), slice(384, 512)).reshape(4, 32, 128)
    above = g1(slice(3, 4), slice(0, 128), slice(0, 128)).reshape(4, 32, 128)
    beside[0] = below
    beside[1] = above

    low_half = lane((32, 128)) < 64
    group = lane((32, 128)) // 32

    def widen(value, which):
        value = jnp.where(group == which, value, 0.0)
        value = value + roll(value, 32, 1)
        return value + roll(value, 64, 1)


    def gather1(y, carry):
        def part(zo, pz):
            return patch1[y, zo, :, pz * 128 : pz * 128 + 128]

        sums = (
            beside[0, y] + part(0, 1), part(0, 2) + part(1, 0), part(0, 3) + part(1, 1), part(1, 2) + beside[1, y],
        )
        for z, value in enumerate(sums):
            value = rounded(value + roll(jnp.where(low_half, up(value), down(value)), 64, 1))
            grad1[z, pl.ds(0, 32, stride=2), :] = widen(value, 1)
            grad1[z, pl.ds(1, 32, stride=2), :] = widen(value, 2)
        value = grad1[...].reshape(256, 128)
        value = jnp.concatenate([value, value], axis=1)
        delta1[y] = (value * ratio1[y]).astype(BF16)
        return carry

    lax.fori_loop(0, 4, gather1, 0)

    bias1 = delta1[...].astype(F32).sum(axis=0).sum(axis=0, keepdims=True)
    bias1 = bias1[:, :128] + bias1[:, 128:]
    bias1 = bias1 + roll(bias1, 64, 1)
    bias1 = bias1 + roll(bias1, 32, 1)
    full = None
    for yw in range(4):
        term = dot(fields[yw : yw + 2].reshape(256, 256), delta1[yw])
        full = term if full is None else full + term
    full = full.reshape(4, 4, 16, 256)
    kernel1 = []
    group1 = lane((16, 128)) // 32
    for dy in range(3):
        rows = full[dy, :, :, :128] + full[dy + 1, :, :, 128:]
        pieces = []
        for dx in range(3):
            value = rows[dx] + roll(rows[dx + 1], 96, 1)
            value = value + roll(roll(value, 12, 0), 64, 1)
            pieces.append(roll(value, 32 * dx, 1) if dx else value)
        kernel1.append(jnp.where(group1 == 0, pieces[0], jnp.where(group1 == 1, pieces[1], pieces[2])))

    low_lane = lane((32, 128)) < 64
    kernel2 = [
        jnp.where(low_lane, taps[2 * m], roll(taps[2 * m + 1], 64, 1) if 2 * m + 1 < 27 else 0.0)
        for m in range(14)
    ]
    shifts = jnp.concatenate(
        [shift3[...], jnp.where(lane((1, 128)) < 64, bias2, bias1), jnp.zeros((14, 128), F32)], axis=0
    )
    shared = jnp.concatenate(kernel2 + kernel1 + [shifts], axis=0)
    rows = 512 // groups
    packed[:, :rows] = shared.reshape(groups, rows, 128).astype(BF16)
    packed[:, rows:] = packed3[...]


def run_backward(groups, *operands):
    return pl.pallas_call(
        backward_kernel,
        name="backward",
        out_shape=jax.ShapeDtypeStruct((groups, 512 // groups + operands[-2].shape[1], 128), BF16),
        in_specs=[VMEM] * len(operands),
        out_specs=VMEM,
        scratch_shapes=[
            pltpu.VMEM((8, 8, 16, 256), BF16),
            pltpu.VMEM((6, 6, 16, 256), F32),
            pltpu.VMEM((6, 6, 16, 256), BF16),
            pltpu.VMEM((4, 4, 16, 256), F32),
            pltpu.VMEM((4, 4, 32, 128), F32),
            pltpu.VMEM((6, 4, 32, 256), BF16),
            pltpu.VMEM((4, 2, 32, 512), F32),
            pltpu.VMEM((2, 4, 32, 128), F32),
            pltpu.VMEM((4, 64, 128), F32),
            pltpu.VMEM((4, 256, 256), BF16),
        ],
        compiler_params=pltpu.CompilerParams(vmem_limit_bytes=LIMIT),
    )(*operands)


def sum_kernel(received, to_column, features):
    groups, rows = received.shape[0], to_column.shape[1]
    wide = 128 // groups
    own = received[:, rows : rows + wide // 8].astype(F32)
    for c in range(wide):
        features[c] = own[:, c // 8, (c % 8) * 16 : (c % 8) * 16 + 16].astype(BF16)
    total = received[:, :rows].astype(F32).sum(axis=0)
    to_column[...] = jnp.broadcast_to(total[None], to_column.shape).astype(BF16)


def run_sum(received, rows_y):
    groups = received.shape[0]
    wide = 128 // groups
    return pl.pallas_call(
        sum_kernel,
        name="sum",
        out_shape=(
            jax.ShapeDtypeStruct((rows_y, 512 // groups + 14 * wide, 128), BF16),
            jax.ShapeDtypeStruct((wide, groups, 16), BF16),
        ),
        in_specs=[VMEM],
        out_specs=(VMEM, VMEM),
        compiler_params=pltpu.CompilerParams(vmem_limit_bytes=LIMIT),
    )(received)


def share_kernel(column, to_all):
    total = column[:, : to_all.shape[1]].astype(F32).sum(axis=0)
    to_all[...] = jnp.broadcast_to(total[None], to_all.shape).astype(BF16)


def run_share(column, groups):
    return pl.pallas_call(
        share_kernel,
        name="share",
        out_shape=jax.ShapeDtypeStruct((groups, 512 // groups, 128), BF16),
        in_specs=[VMEM],
        out_specs=VMEM,
        compiler_params=pltpu.CompilerParams(vmem_limit_bytes=LIMIT),
    )(column)


def third_kernel(column, grad3):
    wide = grad3.shape[1]
    first = column.shape[1] - 14 * wide
    lines = column[:, first:].astype(F32).sum(axis=0)
    for tap in range(9):
        low = lines[tap * wide : tap * wide + wide]
        grad3[tap] = low[:, :64]
        grad3[9 + tap] = low[:, 64:]
        at = (9 + tap // 2) * wide
        grad3[18 + tap] = lines[at : at + wide][:, (tap % 2) * 64 : (tap % 2) * 64 + 64]


def run_third(column, wide):
    return pl.pallas_call(
        third_kernel,
        name="third",
        out_shape=jax.ShapeDtypeStruct((27, wide, 64), F32),
        in_specs=[VMEM],
        out_specs=VMEM,
        compiler_params=pltpu.CompilerParams(vmem_limit_bytes=LIMIT),
    )(column)


def unpack_kernel(shared, grad1, grad2, shift1, shift2, shift3):
    wide = shift3.shape[1]
    rows = shared[...].astype(F32).reshape(512, 128)
    for tap in range(27):
        at = (tap // 2) * 32
        grad2[tap] = rows[at : at + 32, (tap % 2) * 64 : (tap % 2) * 64 + 64]
    for dy in range(3):
        for dz in range(3):
            at = 448 + dy * 16 + dz * 4
            for dx in range(3):
                grad1[dx * 9 + dy * 3 + dz] = rows[at : at + 4, dx * 32 : dx * 32 + 32]
    biases = rows[496:504]
    shift1[...] = biases[1:2, 64:96]
    shift2[...] = biases[1:2, :64]
    place = lax.axis_index("gz")
    shift3[...] = roll(biases, lax.rem(128 - place * wide, 128), 1)[0:1, :wide]


def run_unpack(shared):
    wide = 128 // shared.shape[0]
    return pl.pallas_call(
        unpack_kernel,
        name="unpack",
        out_shape=(
            jax.ShapeDtypeStruct((27, 4, 32), F32),
            jax.ShapeDtypeStruct((27, 32, 64), F32),
            jax.ShapeDtypeStruct((1, 32), F32),
            jax.ShapeDtypeStruct((1, 64), F32),
            jax.ShapeDtypeStruct((1, wide), F32),
        ),
        in_specs=[VMEM],
        out_specs=(VMEM,) * 5,
        compiler_params=pltpu.CompilerParams(vmem_limit_bytes=LIMIT),
    )(shared)


def both_ways(to_next, to_previous, axis):
    devices = lax.axis_size(axis)
    forth = [(i, i + 1) for i in range(devices - 1)]
    back = [(i + 1, i) for i in range(devices - 1)]
    return lax.ppermute(to_next, axis, forth), lax.ppermute(to_previous, axis, back)


def shards(universe, kernel1, bias1, kernel2, bias2, kernel3, bias3, cotangent):
    size_y, size_z = lax.axis_size("gy"), lax.axis_size("gz")
    wide = 128 // size_z

    tile = universe.transpose(1, 2, 0, 3).reshape(8, 32, 128)
    cot = lax.all_to_all(cotangent[:, 0].transpose(1, 0, 2), "gz", 0, 0, tiled=True).reshape(128, 16)
    lower, upper = both_ways(tile, tile, "gz")
    strip = jnp.concatenate([lower[:, 4:], tile, upper[:, :28], jnp.zeros((8, 8, 128), BF16)], axis=1)
    top, bottom = both_ways(strip, strip, "gy")

    k1, k2, k3 = kernel1.transpose(0, 2, 1), kernel2.transpose(0, 2, 1), kernel3.transpose(0, 2, 1)
    to_next, to_previous, hidden2, own_cot, ratio2, patches1, ratio1, fields, w2 = run_forward(
        top, strip, bottom, cot, k1, bias1[None], k2, bias2[None]
    )
    lower, upper = both_ways(to_next, to_previous, "gz")
    packed3, shift3, w3, wide3 = run_own(size_z, hidden2, own_cot, k3, bias3[None])
    row_next, row_previous = run_weave(lower, hidden2, upper, own_cot)
    before, after = both_ways(row_next, row_previous, "gy")
    packed = run_backward(
        size_z,
        before, lower, hidden2, upper, after, own_cot, w3, wide3, w2, ratio2, patches1, ratio1, fields,
        packed3, shift3,
    )
    packed = lax.all_to_all(packed, "gz", 0, 0, tiled=True)
    column, features = run_sum(packed, size_y)
    column = lax.all_to_all(column, "gy", 0, 0, tiled=True)
    shared = lax.all_to_all(run_share(column, size_z), "gz", 0, 0, tiled=True)
    grad3 = run_third(column, wide)
    grad1, grad2, shift1, shift2, shift3 = run_unpack(shared)
    return (
        features[:, None], grad1.transpose(0, 2, 1), shift1[0], grad2.transpose(0, 2, 1), shift2[0], grad3, shift3[0]
    )


def solution(mesh):
    in_specs = (P(None, "gy", "gz", None), P(), P(), P(), P(), P(), P(), P("gz", "gy", None, None))
    out_specs = (P("gz", "gy", None, None), P(), P(), P(), P(), P(None, "gz", None), P("gz"))
    return jax.shard_map(shards, mesh=mesh, in_specs=in_specs, out_specs=out_specs, check_vma=False)
```

```python
import functools
import math

import jax
import jax.numpy as jnp
from jax import lax
from jax.experimental import pallas as pl
from jax.experimental.pallas import tpu as pltpu
from jax.sharding import PartitionSpec as P

F32 = jnp.float32
BF16 = jnp.bfloat16
SLOPE = 0.3
TWO_LOG2_E = 2.0 / math.log(2.0)
PAIRS = ((0, 1), (2, 3), (-3, -2), (4, 5), (-1, 6))
VMEM = pl.BlockSpec(memory_space=pltpu.VMEM)
LIMIT = 24 * 1024 * 1024


def dot(a, b):
    return jnp.dot(a, b, preferred_element_type=F32)


def dot_tn(a, b):
    return lax.dot_general(a, b, (((0,), (0,)), ((), ())), preferred_element_type=F32)


def dot_nt(a, b):
    return lax.dot_general(a, b, (((1,), (1,)), ((), ())), preferred_element_type=F32)


def lane(shape):
    return lax.broadcasted_iota(jnp.int32, shape, len(shape) - 1)


def exps(pre):
    scaled = pre * TWO_LOG2_E
    return jnp.exp2(jnp.maximum(scaled, SLOPE * scaled))


def rounded(value):
    return value.astype(BF16).astype(F32)


def roll(value, amount, axis):
    return pltpu.roll(value, amount, axis)


def down(value):
    rows = lax.broadcasted_iota(jnp.int32, value.shape, 0)
    return jnp.where(rows == 0, 0.0, roll(value, 1, 0))


def up(value):
    count = value.shape[0]
    rows = lax.broadcasted_iota(jnp.int32, value.shape, 0)
    return jnp.where(rows == count - 1, 0.0, roll(value, count - 1, 0))


def lay_pick(pick):
    for px in range(4):
        row = lax.broadcasted_iota(jnp.int32, (256, 128), 0)
        col = lax.broadcasted_iota(jnp.int32, (256, 128), 1)
        same = row // 128 == col // 64
        hit = (row % 128) == 2 * (col % 64) - 1 + px
        pick[:, px * 128 : px * 128 + 128] = jnp.where(same & hit, 1.0, 0.0).astype(BF16)


def forward_kernel(
    top, mid, bot, k1, k2, biases,
    to_next, to_previous, hidden2, ratio2, patches1, ratio1, fields, w2,
    w1, pick, left, field, turned, pre1, first, spread, pre2, second,
):
    lay_weights1(k1, w1)
    lay_weights2(k2, w2)
    lay_pick(pick)
    bias1 = jnp.concatenate([biases[0:1, :32]] * 8, axis=1)
    bias2 = jnp.concatenate([biases[1:2, :64]] * 4, axis=1)
    base_y, base_z = lax.axis_index("gy"), lax.axis_index("gz")
    size_y, size_z = lax.axis_size("gy"), lax.axis_size("gz")

    def inside(offset_y, offset_z, scale):
        row = base_y * (4 // scale) + offset_y
        col = base_z * (4 // scale) + offset_z
        ok_y = (row >= 0) & (row < size_y * (4 // scale))
        ok_z = (col >= 0) & (col < size_z * (4 // scale))
        return jnp.where(ok_y & ok_z, 1.0, 0.0)

    def lay(source, index, target):
        rows = source[index].astype(F32)
        pieces = []
        for one, two in PAIRS:
            a, b = 8 * (one + 3), 8 * (two + 3)
            pieces.append(jnp.concatenate([rows[a : a + 16], rows[b : b + 16]], axis=1))
        left[target] = jnp.concatenate(pieces, axis=0).astype(BF16)

    def lay_both(step, carry):
        lay(mid, step, step + 7)
        lay(mid, step + 4, step + 11)
        return carry

    def lay_ends(step, carry):
        lay(top, step + 1, step)
        lay(bot, step, step + 15)
        return carry

    lax.fori_loop(0, 4, lay_both, 0)
    lax.fori_loop(0, 7, lay_ends, 0)

    for part in range(2):
        block = left[part * 11 : part * 11 + 11].reshape(880, 256)
        out = dot(block, pick[...]).astype(BF16).reshape(11, 5, 16, 512)
        for step in range(11):
            row = part * 11 + step
            for px in range(4):
                at = (row % 2 * 4 + px) * 16
                for k in range(5):
                    field[row // 2, at : at + 16, k * 128 : k * 128 + 128] = out[
                        step, k, :, px * 128 : px * 128 + 128
                    ]
    for pair in range(11):
        turned[pair] = field[pair].T
    fields[...] = field[3:8, :, :256]
    first[:, :, 0:8] = jnp.zeros((10, 10, 8, 128), F32)
    first[:, :, 72:80] = jnp.zeros((10, 10, 8, 128), F32)

    def block1(step, carry):
        for part in range(2):
            stack = jnp.concatenate([turned[2 * step + part], turned[2 * step + part + 1]], axis=1)
            pre1[part] = dot(stack, w1[...])
        for part in range(2):
            yw = 2 * step + part
            place = jnp.where((yw >= 3) & (yw < 7), yw - 3, 4)
            for k, pair in enumerate(PAIRS):
                for h, zw in enumerate(pair):
                    at = k * 128 + h * 64
                    pre = pre1[part, at : at + 64] + bias1
                    e = exps(pre)
                    total = e[:, :128] + e[:, 128:]
                    total = total + roll(total, 64, 1)
                    total = total + roll(total, 32, 1)
                    mean = total * 0.125
                    pooled = rounded(jnp.log(mean) * 0.5)
                    first[yw, zw + 3, 8:72] = pooled * inside(yw - 3, zw, 1)
                    if k < 2:
                        share = 0.125 / mean
                        share = jnp.concatenate([share, share], axis=1)
                        ratio1[place, at : at + 64] = jnp.where(pre > 0, 1.0, SLOPE) * (e * share)
        return carry

    lax.fori_loop(0, 5, block1, 0)

    group1 = lane((32, 128)) // 32

    def frame(yi, carry):
        for zi in range(10):
            part = first[yi, zi, pl.ds(7, 32, stride=2), :]
            for px in range(1, 4):
                part = jnp.where(group1 == px, first[yi, zi, pl.ds(7 + px, 32, stride=2), :], part)
            spread[yi, zi] = part.astype(BF16)
        return carry

    lax.fori_loop(0, 10, frame, 0)
    patches1[...] = spread[2:8, 2:8]

    half = lane((16, 128)) < 64

    def block2(step, carry):
        for part in range(2):
            yp = 2 * step + part
            columns = []
            for zo in range(4):
                tiles = [spread[pl.ds(2 * yp + dy, 2), 2 * zo + pz] for dy in range(3) for pz in range(4)]
                columns.append(jnp.concatenate(tiles, axis=2)[:, None])
            block = jnp.concatenate(columns, axis=1).reshape(256, 1536)
            pre2[part] = dot(block, w2[...].reshape(1536, 256)).reshape(2, 4, 32, 256)
        for part in range(2):
            yp = 2 * step + part
            for zo in range(4):
                pre = pre2[part, :, zo] + bias2
                e = exps(pre)
                both = e[0] + e[1]
                total = both[:, :128] + both[:, 128:]
                total = total + roll(total, 64, 1)
                mean = total * 0.125
                ok = inside(yp - 1, zo - 1, 2)
                share = (0.125 * ok) / mean
                share = jnp.concatenate([share, share], axis=1)
                ratio2[pl.ds(2 * yp, 2), zo] = jnp.where(pre > 0, 1.0, SLOPE) * (e * share[None])
                second[part, zo] = rounded(jnp.log(mean) * 0.5) * ok
        for part in range(2):
            for zo in range(4):
                even = second[part, zo, pl.ds(0, 16, stride=2), :]
                odd = second[part, zo, pl.ds(1, 16, stride=2), :]
                hidden2[2 * step + part, zo] = jnp.where(half, even, odd).astype(BF16)
        return carry

    lax.fori_loop(0, 2, block2, 0)
    to_next[...] = hidden2[:, 0:2].reshape(128, 128)
    to_previous[...] = hidden2[:, 2:4].reshape(128, 128)


def lay_weights1(taps, out):
    group = lane((16, 128)) // 32
    zero = jnp.zeros((16, 128), F32)
    wide = []
    for k in range(9):
        pieces = [taps[3 * k + dz].astype(F32) for dz in range(3)] + [jnp.zeros((4, 32), F32)]
        rows = jnp.concatenate(pieces, axis=0)
        wide.append(jnp.concatenate([rows] * 4, axis=1))
    for py in range(4):
        for px in range(4):
            at = (py * 4 + px) * 16
            for qy in range(2):
                dy = py - qy
                sides = [
                    wide[(px - qx) * 3 + dy] if 0 <= dy < 3 and 0 <= px - qx < 3 else zero for qx in range(2)
                ]
                value = jnp.where(group == 0, sides[0], sides[1])
                shifted = jnp.where(group == 2, roll(sides[0], 4, 0), roll(sides[1], 4, 0))
                out[at : at + 16, qy * 128 : qy * 128 + 128] = jnp.where(group < 2, value, shifted).astype(BF16)


def lay_weights2(taps, out):
    zero = jnp.zeros((32, 64), F32)
    for dy in range(3):
        out[dy, 384:512, 0:128] = jnp.zeros((128, 128), BF16)
        out[dy, 0:128, 128:256] = jnp.zeros((128, 128), BF16)
        for dz in range(3):
            for px in range(4):
                sides = [taps[(px - qx) * 9 + dy * 3 + dz] if 0 <= px - qx < 3 else zero for qx in range(2)]
                tile = jnp.concatenate(sides, axis=1).astype(BF16)
                for qz in range(2):
                    at = (dz + qz) * 128 + px * 32
                    out[dy, at : at + 32, qz * 128 : qz * 128 + 128] = tile


def lay_weights3(taps, out):
    zero = jnp.zeros((64, 128), BF16)
    for tap in range(9):
        out[tap, 192:256, 0:128] = zero
        out[tap, 0:64, 128:256] = zero
        for dx in range(3):
            value = taps[dx * 9 + tap]
            out[tap, dx * 64 : dx * 64 + 64, 0:128] = value
            out[tap, dx * 64 + 64 : dx * 64 + 128, 128:256] = value


def run_forward(*operands):
    return pl.pallas_call(
        forward_kernel,
        name="forward",
        out_shape=(
            jax.ShapeDtypeStruct((128, 128), BF16),
            jax.ShapeDtypeStruct((128, 128), BF16),
            jax.ShapeDtypeStruct((4, 4, 16, 128), BF16),
            jax.ShapeDtypeStruct((8, 4, 32, 256), F32),
            jax.ShapeDtypeStruct((6, 6, 32, 128), BF16),
            jax.ShapeDtypeStruct((5, 256, 256), F32),
            jax.ShapeDtypeStruct((5, 128, 256), BF16),
            jax.ShapeDtypeStruct((3, 512, 256), BF16),
        ),
        in_specs=[VMEM] * len(operands),
        out_specs=(VMEM,) * 8,
        cost_estimate=pl.CostEstimate(flops=5000000000, bytes_accessed=8000000, transcendentals=8000000),
        scratch_shapes=[
            pltpu.VMEM((256, 256), BF16),
            pltpu.VMEM((256, 512), BF16),
            pltpu.VMEM((22, 80, 256), BF16),
            pltpu.VMEM((11, 128, 640), BF16),
            pltpu.VMEM((11, 640, 128), BF16),
            pltpu.VMEM((2, 640, 256), F32),
            pltpu.VMEM((10, 10, 80, 128), F32),
            pltpu.VMEM((10, 10, 32, 128), BF16),
            pltpu.VMEM((2, 2, 4, 32, 256), F32),
            pltpu.VMEM((2, 4, 32, 128), F32),
        ],
        compiler_params=pltpu.CompilerParams(vmem_limit_bytes=LIMIT),
    )(*operands)


def deal_kernel(cot, dealt):
    groups, width = dealt.shape[0], dealt.shape[2]
    rows = jnp.concatenate([cot[c, 0].astype(F32) for c in range(width // 16)], axis=1)
    rows = jnp.concatenate([jnp.zeros((1, width), F32), rows, jnp.zeros((1, width), F32)], axis=0)
    for k in range(groups):
        dealt[k] = jnp.concatenate([rows[k : k + 3], jnp.zeros((5, width), F32)], axis=0).astype(BF16)


def run_deal(cot):
    wide, _, groups, depth = cot.shape
    return pl.pallas_call(
        deal_kernel,
        name="deal",
        out_shape=jax.ShapeDtypeStruct((groups, 8, wide * depth), BF16),
        in_specs=[VMEM],
        out_specs=VMEM,
        compiler_params=pltpu.CompilerParams(vmem_limit_bytes=LIMIT),
    )(cot)


def weave_kernel(lower, hidden2, upper, dealt, to_next, to_previous, own_cot):
    for target, first_row in ((to_next, 0), (to_previous, 2)):
        for y in range(2):
            row, at = first_row + y, y * 128
            target[at : at + 32] = lower[row * 32 : row * 32 + 32]
            target[at + 32 : at + 96] = hidden2[row].reshape(64, 128)
            target[at + 96 : at + 128] = upper[row * 32 : row * 32 + 32]
    groups = dealt.shape[0]
    wide = 128 // groups
    row = lax.broadcasted_iota(jnp.int32, (128, 128), 0)
    col = lax.broadcasted_iota(jnp.int32, (128, 128), 1)
    order = jnp.where(col == row % groups * wide + row // groups, 1.0, 0.0).astype(BF16)
    whole = dealt[...].astype(F32)
    for d in range(3):
        lines = whole[:, d]
        stack = jnp.concatenate([lines[:, c * 16 : c * 16 + 16] for c in range(wide)], axis=0).astype(BF16)
        rows = dot_tn(stack, order).astype(BF16)
        for target, at in ((to_next, 256), (to_previous, 256), (own_cot, 0)):
            target[at + 16 * d : at + 16 * d + 16] = rows


def run_weave(*operands):
    return pl.pallas_call(
        weave_kernel,
        name="weave",
        out_shape=(jax.ShapeDtypeStruct((304, 128), BF16),) * 2 + (jax.ShapeDtypeStruct((48, 128), BF16),),
        in_specs=[VMEM] * 4,
        out_specs=(VMEM,) * 3,
        compiler_params=pltpu.CompilerParams(vmem_limit_bytes=LIMIT),
    )(*operands)


def lay_patches2(rows, target):
    half = lane((16, 128)) < 64
    swapped = roll(rows.astype(F32), 64, 1)
    target[...] = jnp.concatenate(
        [jnp.where(half, down(swapped), swapped), jnp.where(half, swapped, up(swapped))], axis=1
    ).astype(BF16)


def pool3(pre, cot):
    e = exps(pre)
    total = e[0, 0] + e[0, 1] + e[1, 0] + e[1, 1]
    total = total[:, :128] + total[:, 128:]
    mean = total * 0.125
    share = cot.astype(F32) * (0.125 / mean)
    share = jnp.concatenate([share, share], axis=1)
    return mean, (jnp.where(pre > 0, 1.0, SLOPE) * (e * share)).astype(BF16)


def own_kernel(hidden2, own_cot, k3, biases, packed, shift3, w3, wide3, patches2, pre3, turned):
    groups = packed.shape[0]
    wide = 128 // groups
    lay_weights3(k3, w3)
    wide3[...] = jnp.concatenate([biases[2:3]] * 2, axis=1)
    for y in range(4):
        for z in range(4):
            lay_patches2(hidden2[y, z], patches2.at[y, z])
    for tap in range(9):
        dy, dz = tap // 3, tap % 3
        block = patches2[dy : dy + 2, dz : dz + 2].reshape(64, 256)
        term = dot(block, w3[tap])
        pre3[...] = term + wide3[...] if tap == 0 else pre3[...] + term
    mean, delta = pool3(pre3[...].reshape(2, 2, 16, 256), own_cot[16:32])
    features = rounded(jnp.log(mean) * 0.5)
    own3 = delta.reshape(64, 256)
    bias3 = own3.astype(F32).sum(axis=0, keepdims=True)
    shift3[...] = bias3[:, :128] + bias3[:, 128:]
    low, high = [], []
    for tap in range(9):
        dy, dz = tap // 3, tap % 3
        block = patches2[dy : dy + 2, dz : dz + 2].reshape(64, 256)
        full = dot_tn(own3, block)
        one = full[:128]
        low_lanes, high_lanes = roll(full[128:, :128], 64, 1), roll(full[128:, 128:], 64, 1)
        tile0 = jnp.where(lane((128, 128)) < 64, low_lanes, high_lanes)
        tile1 = high_lanes
        low.append(one[:, :128] + tile0)
        high.append(one[:, 128:] + tile1)
    first_half = lane((128, 128)) < 64
    paired = []
    for m in range(5):
        other = roll(high[2 * m + 1], 64, 1) if 2 * m + 1 < 9 else jnp.zeros((128, 128), F32)
        paired.append(jnp.where(first_half, high[2 * m], other))
    kernel3 = [piece.reshape(groups, wide, 128) for piece in low + paired]

    turned[...] = jnp.concatenate([features, jnp.zeros((112, 128), F32)], axis=0).T
    feature_rows = turned[pl.ds(0, 16, stride=8), :]
    for c in range(1, 8):
        feature_rows = feature_rows + roll(turned[pl.ds(c, 16, stride=8), :], 16 * c, 1)
    feature_rows = feature_rows.reshape(groups, wide // 8, 128)
    fill = jnp.zeros((groups, packed.shape[1] - 14 * wide - wide // 8, 128), F32)
    packed[...] = jnp.concatenate(kernel3 + [feature_rows, fill], axis=1).astype(BF16)


def run_own(groups, *operands):
    wide = 128 // groups
    return pl.pallas_call(
        own_kernel,
        name="own",
        out_shape=(
            jax.ShapeDtypeStruct((groups, -(-(14 * wide + wide // 8) // 8) * 8, 128), BF16),
            jax.ShapeDtypeStruct((1, 128), F32),
            jax.ShapeDtypeStruct((9, 256, 256), BF16),
            jax.ShapeDtypeStruct((1, 256), F32),
        ),
        in_specs=[VMEM] * len(operands),
        out_specs=(VMEM,) * 4,
        scratch_shapes=[
            pltpu.VMEM((4, 4, 16, 256), BF16),
            pltpu.VMEM((64, 256), F32),
            pltpu.VMEM((128, 128), F32),
        ],
        compiler_params=pltpu.CompilerParams(vmem_limit_bytes=LIMIT),
        cost_estimate=pl.CostEstimate(flops=150000000, bytes_accessed=4000000, transcendentals=20000),
    )(*operands)


def backward_kernel(
    before, lower, middle, upper, after, own_cot, w3, bias3, w2, ratio2, patches1, ratio1, fields, packed3, shift3,
    packed, patches2, pre3, delta3, patch2, grad2, delta2, patch1, beside, grad1, delta1,
):
    groups = packed.shape[0]
    half = lane((16, 128)) < 64

    def lay(y, source):
        for z in range(8):
            lay_patches2(source(z), patches2.at[y, z])

    for y in range(2):
        lay(y, lambda z: before[(y * 8 + z) * 16 : (y * 8 + z + 1) * 16])
        lay(y + 6, lambda z: after[(y * 8 + z) * 16 : (y * 8 + z + 1) * 16])

    def pick_middle(y, z):
        if z < 2:
            return lower[(y * 2 + z) * 16 : (y * 2 + z + 1) * 16]
        if z < 6:
            return middle[y, z - 2]
        return upper[(y * 2 + z - 6) * 16 : (y * 2 + z - 5) * 16]

    for y in range(4):
        lay(y + 2, functools.partial(pick_middle, y))

    for dy in range(3):
        blocks = [patches2[dy : dy + 6, dz : dz + 6].reshape(576, 256) for dz in range(3)]
        weights = w3[3 * dy : 3 * dy + 3].reshape(768, 256)
        term = dot(jnp.concatenate(blocks, axis=1), weights).reshape(6, 6, 16, 256)
        pre3[...] = term + bias3[...] if dy == 0 else pre3[...] + term

    for wy in range(3):
        for wz in range(3):
            pre = pre3[2 * wy : 2 * wy + 2, 2 * wz : 2 * wz + 2]
            if wy == 1:
                cot = own_cot[wz * 16 : wz * 16 + 16]
            else:
                cot = (before if wy == 0 else after)[256 + wz * 16 : 272 + wz * 16]
            delta3[2 * wy : 2 * wy + 2, 2 * wz : 2 * wz + 2] = pool3(pre, cot)[1]

    for dy in range(3):
        blocks = [delta3[2 - dy : 6 - dy, 2 - dz : 6 - dz].reshape(256, 256) for dz in range(3)]
        weights = jnp.concatenate([w3[3 * dy + dz] for dz in range(3)], axis=1)
        term = dot_nt(jnp.concatenate(blocks, axis=1), weights).reshape(4, 4, 16, 256)
        patch2[...] = term if dy == 0 else patch2[...] + term

    for y in range(4):
        for z in range(4):
            a, b = patch2[y, z, :, :128], patch2[y, z, :, 128:]
            x = rounded(jnp.where(half, b + up(a), a + down(b)))
            swapped = roll(x, 64, 1)
            grad2[y, z, pl.ds(0, 16, stride=2), :] = jnp.where(half, swapped, x)
            grad2[y, z, pl.ds(1, 16, stride=2), :] = jnp.where(half, x, swapped)

    for y in range(6):
        value = grad2[(y + 1) // 2]
        value = jnp.concatenate([value, value], axis=2)
        delta2[y] = (value * ratio2[y + 1]).astype(BF16)

    own2 = delta2[1:5, 1:3].reshape(256, 256)
    bias2 = own2.astype(F32).sum(axis=0, keepdims=True)
    bias2 = bias2[:, :128] + bias2[:, 128:]
    bias2 = bias2 + roll(bias2, 64, 1)
    taps = [None] * 27
    for dy in range(3):
        block = jnp.concatenate(
            [
                jnp.concatenate([patches1[dy : dy + 4, 2 * zo + pz] for pz in range(4)], axis=2)[:, None]
                for zo in range(2)
            ],
            axis=1,
        ).reshape(256, 512)
        full = dot_tn(block, own2)
        for dz in range(3):
            rows = full[dz * 128 : dz * 128 + 128, :128] + full[dz * 128 + 128 : dz * 128 + 256, 128:]
            for dx in range(3):
                taps[dx * 9 + dy * 3 + dz] = rows[dx * 32 : dx * 32 + 32] + roll(
                    rows[dx * 32 + 32 : dx * 32 + 64], 64, 1
                )
    def g1(columns, lanes, rows):
        blocks = [delta2[2 - dy : 6 - dy, columns, :, lanes].reshape(-1, lanes.stop - lanes.start) for dy in range(3)]
        weights = jnp.concatenate([w2[dy, rows, lanes] for dy in range(3)], axis=1)
        return dot_nt(jnp.concatenate(blocks, axis=1), weights)

    patch1[...] = g1(slice(1, 3), slice(0, 256), slice(0, 512)).reshape(4, 2, 32, 512)
    below = g1(slice(0, 1), slice(128, 256), slice(384, 512)).reshape(4, 32, 128)
    above = g1(slice(3, 4), slice(0, 128), slice(0, 128)).reshape(4, 32, 128)
    beside[0] = below
    beside[1] = above

    low_half = lane((32, 128)) < 64
    group = lane((32, 128)) // 32

    def widen(value, which):
        value = jnp.where(group == which, value, 0.0)
        value = value + roll(value, 32, 1)
        return value + roll(value, 64, 1)


    def gather1(y, carry):
        def part(zo, pz):
            return patch1[y, zo, :, pz * 128 : pz * 128 + 128]

        sums = (
            beside[0, y] + part(0, 1), part(0, 2) + part(1, 0), part(0, 3) + part(1, 1), part(1, 2) + beside[1, y],
        )
        for z, value in enumerate(sums):
            value = rounded(value + roll(jnp.where(low_half, up(value), down(value)), 64, 1))
            grad1[z, pl.ds(0, 32, stride=2), :] = widen(value, 1)
            grad1[z, pl.ds(1, 32, stride=2), :] = widen(value, 2)
        value = grad1[...].reshape(256, 128)
        value = jnp.concatenate([value, value], axis=1)
        delta1[y] = (value * ratio1[y]).astype(BF16)
        return carry

    lax.fori_loop(0, 4, gather1, 0)

    bias1 = delta1[...].astype(F32).sum(axis=0).sum(axis=0, keepdims=True)
    bias1 = bias1[:, :128] + bias1[:, 128:]
    bias1 = bias1 + roll(bias1, 64, 1)
    bias1 = bias1 + roll(bias1, 32, 1)
    full = None
    for yw in range(4):
        term = dot(fields[yw : yw + 2].reshape(256, 256), delta1[yw])
        full = term if full is None else full + term
    full = full.reshape(4, 4, 16, 256)
    kernel1 = []
    group1 = lane((16, 128)) // 32
    for dy in range(3):
        rows = full[dy, :, :, :128] + full[dy + 1, :, :, 128:]
        pieces = []
        for dx in range(3):
            value = rows[dx] + roll(rows[dx + 1], 96, 1)
            value = value + roll(roll(value, 12, 0), 64, 1)
            pieces.append(roll(value, 32 * dx, 1) if dx else value)
        kernel1.append(jnp.where(group1 == 0, pieces[0], jnp.where(group1 == 1, pieces[1], pieces[2])))

    low_lane = lane((32, 128)) < 64
    kernel2 = [
        jnp.where(low_lane, taps[2 * m], roll(taps[2 * m + 1], 64, 1) if 2 * m + 1 < 27 else 0.0)
        for m in range(14)
    ]
    shifts = jnp.concatenate(
        [shift3[...], jnp.where(lane((1, 128)) < 64, bias2, bias1), jnp.zeros((14, 128), F32)], axis=0
    )
    shared = jnp.concatenate(kernel2 + kernel1 + [shifts], axis=0)
    rows = 512 // groups
    packed[:, :rows] = shared.reshape(groups, rows, 128).astype(BF16)
    packed[:, rows:] = packed3[...]


def run_backward(groups, *operands):
    return pl.pallas_call(
        backward_kernel,
        name="backward",
        out_shape=jax.ShapeDtypeStruct((groups, 512 // groups + operands[-2].shape[1], 128), BF16),
        in_specs=[VMEM] * len(operands),
        out_specs=VMEM,
        scratch_shapes=[
            pltpu.VMEM((8, 8, 16, 256), BF16),
            pltpu.VMEM((6, 6, 16, 256), F32),
            pltpu.VMEM((6, 6, 16, 256), BF16),
            pltpu.VMEM((4, 4, 16, 256), F32),
            pltpu.VMEM((4, 4, 32, 128), F32),
            pltpu.VMEM((6, 4, 32, 256), BF16),
            pltpu.VMEM((4, 2, 32, 512), F32),
            pltpu.VMEM((2, 4, 32, 128), F32),
            pltpu.VMEM((4, 64, 128), F32),
            pltpu.VMEM((4, 256, 256), BF16),
        ],
        compiler_params=pltpu.CompilerParams(vmem_limit_bytes=LIMIT),
    )(*operands)


def sum_kernel(received, to_column, features):
    groups, rows = received.shape[0], to_column.shape[1]
    wide = 128 // groups
    own = received[:, rows : rows + wide // 8].astype(F32)
    for c in range(wide):
        features[c] = own[:, c // 8, (c % 8) * 16 : (c % 8) * 16 + 16].astype(BF16)
    total = received[:, :rows].astype(F32).sum(axis=0)
    to_column[...] = jnp.broadcast_to(total[None], to_column.shape).astype(BF16)


def run_sum(received, rows_y):
    groups = received.shape[0]
    wide = 128 // groups
    return pl.pallas_call(
        sum_kernel,
        name="sum",
        out_shape=(
            jax.ShapeDtypeStruct((rows_y, 512 // groups + 14 * wide, 128), BF16),
            jax.ShapeDtypeStruct((wide, groups, 16), BF16),
        ),
        in_specs=[VMEM],
        out_specs=(VMEM, VMEM),
        compiler_params=pltpu.CompilerParams(vmem_limit_bytes=LIMIT),
    )(received)


def share_kernel(column, to_all):
    total = column[:, : to_all.shape[1]].astype(F32).sum(axis=0)
    to_all[...] = jnp.broadcast_to(total[None], to_all.shape).astype(BF16)


def run_share(column, groups):
    return pl.pallas_call(
        share_kernel,
        name="share",
        out_shape=jax.ShapeDtypeStruct((groups, 512 // groups, 128), BF16),
        in_specs=[VMEM],
        out_specs=VMEM,
        compiler_params=pltpu.CompilerParams(vmem_limit_bytes=LIMIT),
    )(column)


def third_kernel(column, grad3):
    wide = grad3.shape[1]
    first = column.shape[1] - 14 * wide
    lines = column[:, first:].astype(F32).sum(axis=0)
    for tap in range(9):
        low = lines[tap * wide : tap * wide + wide]
        grad3[tap] = low[:, :64]
        grad3[9 + tap] = low[:, 64:]
        at = (9 + tap // 2) * wide
        grad3[18 + tap] = lines[at : at + wide][:, (tap % 2) * 64 : (tap % 2) * 64 + 64]


def run_third(column, wide):
    return pl.pallas_call(
        third_kernel,
        name="third",
        out_shape=jax.ShapeDtypeStruct((27, wide, 64), F32),
        in_specs=[VMEM],
        out_specs=VMEM,
        compiler_params=pltpu.CompilerParams(vmem_limit_bytes=LIMIT),
    )(column)


def unpack_kernel(shared, grad1, grad2, shift1, shift2, shift3):
    wide = shift3.shape[1]
    rows = shared[...].astype(F32).reshape(512, 128)
    for tap in range(27):
        at = (tap // 2) * 32
        grad2[tap] = rows[at : at + 32, (tap % 2) * 64 : (tap % 2) * 64 + 64]
    for dy in range(3):
        for dz in range(3):
            at = 448 + dy * 16 + dz * 4
            for dx in range(3):
                grad1[dx * 9 + dy * 3 + dz] = rows[at : at + 4, dx * 32 : dx * 32 + 32]
    biases = rows[496:504]
    shift1[...] = biases[1:2, 64:96]
    shift2[...] = biases[1:2, :64]
    place = lax.axis_index("gz")
    shift3[...] = roll(biases, lax.rem(128 - place * wide, 128), 1)[0:1, :wide]


def run_unpack(shared):
    wide = 128 // shared.shape[0]
    return pl.pallas_call(
        unpack_kernel,
        name="unpack",
        out_shape=(
            jax.ShapeDtypeStruct((27, 4, 32), F32),
            jax.ShapeDtypeStruct((27, 32, 64), F32),
            jax.ShapeDtypeStruct((1, 32), F32),
            jax.ShapeDtypeStruct((1, 64), F32),
            jax.ShapeDtypeStruct((1, wide), F32),
        ),
        in_specs=[VMEM],
        out_specs=(VMEM,) * 5,
        compiler_params=pltpu.CompilerParams(vmem_limit_bytes=LIMIT),
    )(shared)


def both_ways(to_next, to_previous, axis):
    devices = lax.axis_size(axis)
    forth = [(i, i + 1) for i in range(devices - 1)]
    back = [(i + 1, i) for i in range(devices - 1)]
    return lax.ppermute(to_next, axis, forth), lax.ppermute(to_previous, axis, back)


def shards(universe, kernel1, bias1, kernel2, bias2, kernel3, bias3, cotangent):
    size_y, size_z = lax.axis_size("gy"), lax.axis_size("gz")
    wide = 128 // size_z

    tile = universe.transpose(1, 2, 0, 3).reshape(8, 32, 128)
    dealt = lax.all_to_all(run_deal(cotangent), "gz", 0, 0, tiled=True)
    biases = jnp.stack([jnp.pad(bias1, (0, 96)), jnp.pad(bias2, (0, 64)), bias3])
    lower, upper = both_ways(tile, tile, "gz")
    strip = jnp.concatenate([lower[:, 4:], tile, upper[:, :28], jnp.zeros((8, 8, 128), BF16)], axis=1)
    top, bottom = both_ways(strip, strip, "gy")

    k1, k2 = kernel1.transpose(0, 2, 1).astype(F32), kernel2.transpose(0, 2, 1).astype(F32)
    k3 = kernel3.transpose(0, 2, 1)
    top, dealt = lax.optimization_barrier((top, dealt))
    to_next, to_previous, hidden2, ratio2, patches1, ratio1, fields, w2 = run_forward(
        top, strip, bottom, k1, k2, biases
    )
    lower, upper = both_ways(to_next, to_previous, "gz")
    row_next, row_previous, own_cot = run_weave(lower, hidden2, upper, dealt)
    packed3, shift3, w3, wide3 = run_own(size_z, hidden2, own_cot, k3, biases)
    before, after = both_ways(row_next, row_previous, "gy")
    packed = run_backward(
        size_z,
        before, lower, hidden2, upper, after, own_cot, w3, wide3, w2, ratio2, patches1, ratio1, fields,
        packed3, shift3,
    )
    packed = lax.all_to_all(packed, "gz", 0, 0, tiled=True)
    column, features = run_sum(packed, size_y)
    column = lax.all_to_all(column, "gy", 0, 0, tiled=True)
    shared = lax.all_to_all(run_share(column, size_z), "gz", 0, 0, tiled=True)
    grad3 = run_third(column, wide)
    grad1, grad2, shift1, shift2, shift3 = run_unpack(shared)
    return (
        features[:, None], grad1.transpose(0, 2, 1), shift1[0], grad2.transpose(0, 2, 1), shift2[0], grad3, shift3[0]
    )


def solution(mesh):
    in_specs = (P(None, "gy", "gz", None), P(), P(), P(), P(), P(), P(), P("gz", "gy", None, None))
    out_specs = (P("gz", "gy", None, None), P(), P(), P(), P(), P(None, "gz", None), P("gz"))
    return jax.shard_map(shards, mesh=mesh, in_specs=in_specs, out_specs=out_specs, check_vma=False)
```

```python
import functools
import math

import jax
import jax.numpy as jnp
from jax import lax
from jax.experimental import pallas as pl
from jax.experimental.pallas import tpu as pltpu
from jax.sharding import PartitionSpec as P

F32 = jnp.float32
BF16 = jnp.bfloat16
SLOPE = 0.3
TWO_LOG2_E = 2.0 / math.log(2.0)
PAIRS = ((0, 1), (2, 3), (-3, -2), (4, 5), (-1, 6))
VMEM = pl.BlockSpec(memory_space=pltpu.VMEM)
LIMIT = 24 * 1024 * 1024


def dot(a, b):
    return jnp.dot(a, b, preferred_element_type=F32)


def dot_tn(a, b):
    return lax.dot_general(a, b, (((0,), (0,)), ((), ())), preferred_element_type=F32)


def dot_nt(a, b):
    return lax.dot_general(a, b, (((1,), (1,)), ((), ())), preferred_element_type=F32)


def lane(shape):
    return lax.broadcasted_iota(jnp.int32, shape, len(shape) - 1)


def exps(pre):
    scaled = pre * TWO_LOG2_E
    return jnp.exp2(jnp.maximum(scaled, SLOPE * scaled))


def rounded(value):
    return value.astype(BF16).astype(F32)


def roll(value, amount, axis):
    return pltpu.roll(value, amount, axis)


def down(value):
    rows = lax.broadcasted_iota(jnp.int32, value.shape, 0)
    return jnp.where(rows == 0, 0.0, roll(value, 1, 0))


def up(value):
    count = value.shape[0]
    rows = lax.broadcasted_iota(jnp.int32, value.shape, 0)
    return jnp.where(rows == count - 1, 0.0, roll(value, count - 1, 0))


def lay_pick(pick):
    for px in range(4):
        row = lax.broadcasted_iota(jnp.int32, (256, 128), 0)
        col = lax.broadcasted_iota(jnp.int32, (256, 128), 1)
        same = row // 128 == col // 64
        hit = (row % 128) == 2 * (col % 64) - 1 + px
        pick[:, px * 128 : px * 128 + 128] = jnp.where(same & hit, 1.0, 0.0).astype(BF16)


def forward_kernel(
    top, mid, bot, cot, k1, k2, biases,
    to_next, to_previous, hidden2, own_cot, ratio2, patches1, ratio1, fields, w2,
    w1, pick, left, field, turned, pre1, first, spread, pre2, second,
):
    lay_weights1(k1, w1)
    lay_weights2(k2, w2)
    lay_pick(pick)
    bias1 = jnp.concatenate([biases[0:1, :32]] * 8, axis=1)
    bias2 = jnp.concatenate([biases[1:2, :64]] * 4, axis=1)
    base_y, base_z = lax.axis_index("gy"), lax.axis_index("gz")
    size_y, size_z = lax.axis_size("gy"), lax.axis_size("gz")

    def inside(offset_y, offset_z, scale):
        row = base_y * (4 // scale) + offset_y
        col = base_z * (4 // scale) + offset_z
        ok_y = (row >= 0) & (row < size_y * (4 // scale))
        ok_z = (col >= 0) & (col < size_z * (4 // scale))
        return jnp.where(ok_y & ok_z, 1.0, 0.0)

    def lay(source, index, target):
        rows = source[index].astype(F32)
        pieces = []
        for one, two in PAIRS:
            a, b = 8 * (one + 3), 8 * (two + 3)
            pieces.append(jnp.concatenate([rows[a : a + 16], rows[b : b + 16]], axis=1))
        left[target] = jnp.concatenate(pieces, axis=0).astype(BF16)

    for row in range(22):
        source, index = (top, row + 1) if row < 7 else ((mid, row - 7) if row < 15 else (bot, row - 15))
        lay(source, index, row)

    for part in range(2):
        block = left[part * 11 : part * 11 + 11].reshape(880, 256)
        out = dot(block, pick[...]).astype(BF16).reshape(11, 5, 16, 512)
        for step in range(11):
            row = part * 11 + step
            for px in range(4):
                at = (row % 2 * 4 + px) * 16
                for k in range(5):
                    field[row // 2, at : at + 16, k * 128 : k * 128 + 128] = out[
                        step, k, :, px * 128 : px * 128 + 128
                    ]
    for pair in range(11):
        turned[pair] = field[pair].T
    fields[...] = field[3:8, :, :256]
    first[:, :, 0:8] = jnp.zeros((10, 10, 8, 128), F32)
    first[:, :, 72:80] = jnp.zeros((10, 10, 8, 128), F32)

    def block1(step, carry):
        for part in range(5):
            stack = jnp.concatenate([turned[5 * step + part], turned[5 * step + part + 1]], axis=1)
            pre1[part] = dot(stack, w1[...])
        for part in range(5):
            yw = 5 * step + part
            place = jnp.where((yw >= 3) & (yw < 7), yw - 3, 4)
            for k, pair in enumerate(PAIRS):
                for h, zw in enumerate(pair):
                    at = k * 128 + h * 64
                    pre = pre1[part, at : at + 64] + bias1
                    e = exps(pre)
                    total = e[:, :128] + e[:, 128:]
                    total = total + roll(total, 64, 1)
                    total = total + roll(total, 32, 1)
                    mean = total * 0.125
                    pooled = rounded(jnp.log(mean) * 0.5)
                    first[yw, zw + 3, 8:72] = pooled * inside(yw - 3, zw, 1)
                    if k < 2:
                        share = 0.125 / mean
                        share = jnp.concatenate([share, share], axis=1)
                        ratio1[place, at : at + 64] = jnp.where(pre > 0, 1.0, SLOPE) * (e * share)
        return carry

    lax.fori_loop(0, 2, block1, 0)

    group1 = lane((32, 128)) // 32

    def frame(step, carry):
        for part in range(5):
            yi = 5 * step + part
            for zi in range(10):
                value = first[yi, zi, pl.ds(7, 32, stride=2), :]
                for px in range(1, 4):
                    value = jnp.where(group1 == px, first[yi, zi, pl.ds(7 + px, 32, stride=2), :], value)
                spread[yi, zi] = value.astype(BF16)
        return carry

    lax.fori_loop(0, 2, frame, 0)
    patches1[...] = spread[2:8, 2:8]

    half = lane((16, 128)) < 64

    for yp in range(4):
        columns = []
        for zo in range(4):
            tiles = [spread[2 * yp + dy : 2 * yp + dy + 2, 2 * zo + pz] for dy in range(3) for pz in range(4)]
            columns.append(jnp.concatenate(tiles, axis=2)[:, None])
        block = jnp.concatenate(columns, axis=1).reshape(256, 1536)
        pre2[yp] = dot(block, w2[...].reshape(1536, 256)).reshape(2, 4, 32, 256)
    for yp in range(4):
        for zo in range(4):
            pre = pre2[yp, :, zo] + bias2
            e = exps(pre)
            both = e[0] + e[1]
            total = both[:, :128] + both[:, 128:]
            total = total + roll(total, 64, 1)
            mean = total * 0.125
            ok = inside(yp - 1, zo - 1, 2)
            share = (0.125 * ok) / mean
            share = jnp.concatenate([share, share], axis=1)
            ratio2[2 * yp : 2 * yp + 2, zo] = jnp.where(pre > 0, 1.0, SLOPE) * (e * share[None])
            second[yp, zo] = rounded(jnp.log(mean) * 0.5) * ok
    for yp in range(4):
        for zo in range(4):
            even = second[yp, zo, pl.ds(0, 16, stride=2), :]
            odd = second[yp, zo, pl.ds(1, 16, stride=2), :]
            hidden2[yp, zo] = jnp.where(half, even, odd).astype(BF16)
    own = cot[...].astype(F32).T.astype(BF16)
    own_cot[...] = own
    to_next[:128] = hidden2[:, 0:2].reshape(128, 128)
    to_previous[:128] = hidden2[:, 2:4].reshape(128, 128)
    to_next[128:144] = own
    to_previous[128:144] = own


def lay_weights1(taps, out):
    group = lane((16, 128)) // 32
    zero = jnp.zeros((16, 128), F32)
    wide = []
    for k in range(9):
        pieces = [taps[3 * k + dz].astype(F32) for dz in range(3)] + [jnp.zeros((4, 32), F32)]
        rows = jnp.concatenate(pieces, axis=0)
        wide.append(jnp.concatenate([rows] * 4, axis=1))
    for py in range(4):
        for px in range(4):
            at = (py * 4 + px) * 16
            for qy in range(2):
                dy = py - qy
                sides = [
                    wide[(px - qx) * 3 + dy] if 0 <= dy < 3 and 0 <= px - qx < 3 else zero for qx in range(2)
                ]
                value = jnp.where(group == 0, sides[0], sides[1])
                shifted = jnp.where(group == 2, roll(sides[0], 4, 0), roll(sides[1], 4, 0))
                out[at : at + 16, qy * 128 : qy * 128 + 128] = jnp.where(group < 2, value, shifted).astype(BF16)


def lay_weights2(taps, out):
    zero = jnp.zeros((32, 64), F32)
    for dy in range(3):
        out[dy, 384:512, 0:128] = jnp.zeros((128, 128), BF16)
        out[dy, 0:128, 128:256] = jnp.zeros((128, 128), BF16)
        for dz in range(3):
            for px in range(4):
                sides = [taps[(px - qx) * 9 + dy * 3 + dz] if 0 <= px - qx < 3 else zero for qx in range(2)]
                tile = jnp.concatenate(sides, axis=1).astype(BF16)
                for qz in range(2):
                    at = (dz + qz) * 128 + px * 32
                    out[dy, at : at + 32, qz * 128 : qz * 128 + 128] = tile


def lay_weights3(taps, out):
    zero = jnp.zeros((64, 128), BF16)
    for tap in range(9):
        out[tap, 192:256, 0:128] = zero
        out[tap, 0:64, 128:256] = zero
        for dx in range(3):
            value = taps[dx * 9 + tap]
            out[tap, dx * 64 : dx * 64 + 64, 0:128] = value
            out[tap, dx * 64 + 64 : dx * 64 + 128, 128:256] = value


def run_forward(*operands):
    return pl.pallas_call(
        forward_kernel,
        name="forward",
        out_shape=(
            jax.ShapeDtypeStruct((144, 128), BF16),
            jax.ShapeDtypeStruct((144, 128), BF16),
            jax.ShapeDtypeStruct((4, 4, 16, 128), BF16),
            jax.ShapeDtypeStruct((16, 128), BF16),
            jax.ShapeDtypeStruct((8, 4, 32, 256), F32),
            jax.ShapeDtypeStruct((6, 6, 32, 128), BF16),
            jax.ShapeDtypeStruct((5, 256, 256), F32),
            jax.ShapeDtypeStruct((5, 128, 256), BF16),
            jax.ShapeDtypeStruct((3, 512, 256), BF16),
        ),
        in_specs=[VMEM] * len(operands),
        out_specs=(VMEM,) * 9,
        cost_estimate=pl.CostEstimate(flops=5000000000, bytes_accessed=8000000, transcendentals=8000000),
        scratch_shapes=[
            pltpu.VMEM((256, 256), BF16),
            pltpu.VMEM((256, 512), BF16),
            pltpu.VMEM((22, 80, 256), BF16),
            pltpu.VMEM((11, 128, 640), BF16),
            pltpu.VMEM((11, 640, 128), BF16),
            pltpu.VMEM((5, 640, 256), F32),
            pltpu.VMEM((10, 10, 80, 128), F32),
            pltpu.VMEM((10, 10, 32, 128), BF16),
            pltpu.VMEM((4, 2, 4, 32, 256), F32),
            pltpu.VMEM((4, 4, 32, 128), F32),
        ],
        compiler_params=pltpu.CompilerParams(vmem_limit_bytes=LIMIT),
    )(*operands)


def weave_kernel(lower, hidden2, upper, own_cot, to_next, to_previous):
    for target, first_row in ((to_next, 0), (to_previous, 2)):
        for y in range(2):
            row, at = first_row + y, y * 128
            target[at : at + 32] = lower[row * 32 : row * 32 + 32]
            target[at + 32 : at + 96] = hidden2[row].reshape(64, 128)
            target[at + 96 : at + 128] = upper[row * 32 : row * 32 + 32]
        target[256:272] = lower[128:144]
        target[272:288] = own_cot[...]
        target[288:304] = upper[128:144]


def run_weave(*operands):
    return pl.pallas_call(
        weave_kernel,
        name="weave",
        out_shape=(jax.ShapeDtypeStruct((304, 128), BF16),) * 2,
        in_specs=[VMEM] * 4,
        out_specs=(VMEM,) * 2,
        compiler_params=pltpu.CompilerParams(vmem_limit_bytes=LIMIT),
    )(*operands)


def lay_patches2(rows, target):
    half = lane((16, 128)) < 64
    swapped = roll(rows.astype(F32), 64, 1)
    target[...] = jnp.concatenate(
        [jnp.where(half, down(swapped), swapped), jnp.where(half, swapped, up(swapped))], axis=1
    ).astype(BF16)


def pool3(pre, cot):
    e = exps(pre)
    total = e[0, 0] + e[0, 1] + e[1, 0] + e[1, 1]
    total = total[:, :128] + total[:, 128:]
    mean = total * 0.125
    share = cot.astype(F32) * (0.125 / mean)
    share = jnp.concatenate([share, share], axis=1)
    return mean, (jnp.where(pre > 0, 1.0, SLOPE) * (e * share)).astype(BF16)


def own_kernel(hidden2, own_cot, k3, biases, packed, shift3, w3, wide3, patches2, pre3, turned):
    groups = packed.shape[0]
    wide = 128 // groups
    lay_weights3(k3, w3)
    wide3[...] = jnp.concatenate([biases[2:3]] * 2, axis=1)
    for y in range(4):
        for z in range(4):
            lay_patches2(hidden2[y, z], patches2.at[y, z])
    for tap in range(9):
        dy, dz = tap // 3, tap % 3
        block = patches2[dy : dy + 2, dz : dz + 2].reshape(64, 256)
        term = dot(block, w3[tap])
        pre3[...] = term + wide3[...] if tap == 0 else pre3[...] + term
    mean, delta = pool3(pre3[...].reshape(2, 2, 16, 256), own_cot[...])
    features = rounded(jnp.log(mean) * 0.5)
    own3 = delta.reshape(64, 256)
    bias3 = own3.astype(F32).sum(axis=0, keepdims=True)
    shift3[...] = bias3[:, :128] + bias3[:, 128:]
    low, high = [], []
    for tap in range(9):
        dy, dz = tap // 3, tap % 3
        block = patches2[dy : dy + 2, dz : dz + 2].reshape(64, 256)
        full = dot_tn(own3, block)
        one = full[:128]
        low_lanes, high_lanes = roll(full[128:, :128], 64, 1), roll(full[128:, 128:], 64, 1)
        tile0 = jnp.where(lane((128, 128)) < 64, low_lanes, high_lanes)
        tile1 = high_lanes
        low.append(one[:, :128] + tile0)
        high.append(one[:, 128:] + tile1)
    first_half = lane((128, 128)) < 64
    paired = []
    for m in range(5):
        other = roll(high[2 * m + 1], 64, 1) if 2 * m + 1 < 9 else jnp.zeros((128, 128), F32)
        paired.append(jnp.where(first_half, high[2 * m], other))
    kernel3 = [piece.reshape(groups, wide, 128) for piece in low + paired]

    turned[...] = jnp.concatenate([features, jnp.zeros((112, 128), F32)], axis=0).T
    feature_rows = turned[pl.ds(0, 16, stride=8), :]
    for c in range(1, 8):
        feature_rows = feature_rows + roll(turned[pl.ds(c, 16, stride=8), :], 16 * c, 1)
    feature_rows = feature_rows.reshape(groups, wide // 8, 128)
    fill = jnp.zeros((groups, packed.shape[1] - 14 * wide - wide // 8, 128), F32)
    packed[...] = jnp.concatenate(kernel3 + [feature_rows, fill], axis=1).astype(BF16)


def run_own(groups, *operands):
    wide = 128 // groups
    return pl.pallas_call(
        own_kernel,
        name="own",
        out_shape=(
            jax.ShapeDtypeStruct((groups, -(-(14 * wide + wide // 8) // 8) * 8, 128), BF16),
            jax.ShapeDtypeStruct((1, 128), F32),
            jax.ShapeDtypeStruct((9, 256, 256), BF16),
            jax.ShapeDtypeStruct((1, 256), F32),
        ),
        in_specs=[VMEM] * len(operands),
        out_specs=(VMEM,) * 4,
        scratch_shapes=[
            pltpu.VMEM((4, 4, 16, 256), BF16),
            pltpu.VMEM((64, 256), F32),
            pltpu.VMEM((128, 128), F32),
        ],
        compiler_params=pltpu.CompilerParams(vmem_limit_bytes=LIMIT),
        cost_estimate=pl.CostEstimate(flops=150000000, bytes_accessed=4000000, transcendentals=20000),
    )(*operands)


def backward_kernel(
    before, lower, middle, upper, after, own_cot, w3, bias3, w2, ratio2, patches1, ratio1, fields, packed3, shift3,
    packed, patches2, pre3, delta3, patch2, grad2, delta2, patch1, beside, grad1, delta1,
):
    groups = packed.shape[0]
    half = lane((16, 128)) < 64

    def lay(y, source):
        for z in range(8):
            lay_patches2(source(z), patches2.at[y, z])

    for y in range(2):
        lay(y, lambda z: before[(y * 8 + z) * 16 : (y * 8 + z + 1) * 16])
        lay(y + 6, lambda z: after[(y * 8 + z) * 16 : (y * 8 + z + 1) * 16])

    def pick_middle(y, z):
        if z < 2:
            return lower[(y * 2 + z) * 16 : (y * 2 + z + 1) * 16]
        if z < 6:
            return middle[y, z - 2]
        return upper[(y * 2 + z - 6) * 16 : (y * 2 + z - 5) * 16]

    for y in range(4):
        lay(y + 2, functools.partial(pick_middle, y))

    for dy in range(3):
        blocks = [patches2[dy : dy + 6, dz : dz + 6].reshape(576, 256) for dz in range(3)]
        weights = w3[3 * dy : 3 * dy + 3].reshape(768, 256)
        term = dot(jnp.concatenate(blocks, axis=1), weights).reshape(6, 6, 16, 256)
        pre3[...] = term + bias3[...] if dy == 0 else pre3[...] + term

    for wy in range(3):
        for wz in range(3):
            pre = pre3[2 * wy : 2 * wy + 2, 2 * wz : 2 * wz + 2]
            if wy == 1:
                cot = own_cot[...] if wz == 1 else (lower if wz == 0 else upper)[128:144]
            else:
                cot = (before if wy == 0 else after)[256 + wz * 16 : 272 + wz * 16]
            delta3[2 * wy : 2 * wy + 2, 2 * wz : 2 * wz + 2] = pool3(pre, cot)[1]

    for dy in range(3):
        blocks = [delta3[2 - dy : 6 - dy, 2 - dz : 6 - dz].reshape(256, 256) for dz in range(3)]
        weights = jnp.concatenate([w3[3 * dy + dz] for dz in range(3)], axis=1)
        term = dot_nt(jnp.concatenate(blocks, axis=1), weights).reshape(4, 4, 16, 256)
        patch2[...] = term if dy == 0 else patch2[...] + term

    for y in range(4):
        for z in range(4):
            a, b = patch2[y, z, :, :128], patch2[y, z, :, 128:]
            x = rounded(jnp.where(half, b + up(a), a + down(b)))
            swapped = roll(x, 64, 1)
            grad2[y, z, pl.ds(0, 16, stride=2), :] = jnp.where(half, swapped, x)
            grad2[y, z, pl.ds(1, 16, stride=2), :] = jnp.where(half, x, swapped)

    for y in range(6):
        value = grad2[(y + 1) // 2]
        value = jnp.concatenate([value, value], axis=2)
        delta2[y] = (value * ratio2[y + 1]).astype(BF16)

    own2 = delta2[1:5, 1:3].reshape(256, 256)
    bias2 = own2.astype(F32).sum(axis=0, keepdims=True)
    bias2 = bias2[:, :128] + bias2[:, 128:]
    bias2 = bias2 + roll(bias2, 64, 1)
    taps = [None] * 27
    for dy in range(3):
        block = jnp.concatenate(
            [
                jnp.concatenate([patches1[dy : dy + 4, 2 * zo + pz] for pz in range(4)], axis=2)[:, None]
                for zo in range(2)
            ],
            axis=1,
        ).reshape(256, 512)
        full = dot_tn(block, own2)
        for dz in range(3):
            rows = full[dz * 128 : dz * 128 + 128, :128] + full[dz * 128 + 128 : dz * 128 + 256, 128:]
            for dx in range(3):
                taps[dx * 9 + dy * 3 + dz] = rows[dx * 32 : dx * 32 + 32] + roll(
                    rows[dx * 32 + 32 : dx * 32 + 64], 64, 1
                )
    def g1(columns, lanes, rows):
        blocks = [delta2[2 - dy : 6 - dy, columns, :, lanes].reshape(-1, lanes.stop - lanes.start) for dy in range(3)]
        weights = jnp.concatenate([w2[dy, rows, lanes] for dy in range(3)], axis=1)
        return dot_nt(jnp.concatenate(blocks, axis=1), weights)

    patch1[...] = g1(slice(1, 3), slice(0, 256), slice(0, 512)).reshape(4, 2, 32, 512)
    below = g1(slice(0, 1), slice(128, 256), slice(384, 512)).reshape(4, 32, 128)
    above = g1(slice(3, 4), slice(0, 128), slice(0, 128)).reshape(4, 32, 128)
    beside[0] = below
    beside[1] = above

    low_half = lane((32, 128)) < 64
    group = lane((32, 128)) // 32

    def widen(value, which):
        value = jnp.where(group == which, value, 0.0)
        value = value + roll(value, 32, 1)
        return value + roll(value, 64, 1)


    for y in range(4):
        def part(zo, pz):
            return patch1[y, zo, :, pz * 128 : pz * 128 + 128]

        sums = (
            beside[0, y] + part(0, 1), part(0, 2) + part(1, 0), part(0, 3) + part(1, 1), part(1, 2) + beside[1, y],
        )
        for z, value in enumerate(sums):
            value = rounded(value + roll(jnp.where(low_half, up(value), down(value)), 64, 1))
            grad1[y, z, pl.ds(0, 32, stride=2), :] = widen(value, 1)
            grad1[y, z, pl.ds(1, 32, stride=2), :] = widen(value, 2)
        value = grad1[y].reshape(256, 128)
        value = jnp.concatenate([value, value], axis=1)
        delta1[y] = (value * ratio1[y]).astype(BF16)

    bias1 = delta1[...].astype(F32).sum(axis=0).sum(axis=0, keepdims=True)
    bias1 = bias1[:, :128] + bias1[:, 128:]
    bias1 = bias1 + roll(bias1, 64, 1)
    bias1 = bias1 + roll(bias1, 32, 1)
    full = None
    for yw in range(4):
        term = dot(fields[yw : yw + 2].reshape(256, 256), delta1[yw])
        full = term if full is None else full + term
    full = full.reshape(4, 4, 16, 256)
    kernel1 = []
    group1 = lane((16, 128)) // 32
    for dy in range(3):
        rows = full[dy, :, :, :128] + full[dy + 1, :, :, 128:]
        pieces = []
        for dx in range(3):
            value = rows[dx] + roll(rows[dx + 1], 96, 1)
            value = value + roll(roll(value, 12, 0), 64, 1)
            pieces.append(roll(value, 32 * dx, 1) if dx else value)
        kernel1.append(jnp.where(group1 == 0, pieces[0], jnp.where(group1 == 1, pieces[1], pieces[2])))

    low_lane = lane((32, 128)) < 64
    kernel2 = [
        jnp.where(low_lane, taps[2 * m], roll(taps[2 * m + 1], 64, 1) if 2 * m + 1 < 27 else 0.0)
        for m in range(14)
    ]
    shifts = jnp.concatenate(
        [shift3[...], jnp.where(lane((1, 128)) < 64, bias2, bias1), jnp.zeros((14, 128), F32)], axis=0
    )
    shared = jnp.concatenate(kernel2 + kernel1 + [shifts], axis=0)
    rows = 512 // groups
    packed[:, :rows] = shared.reshape(groups, rows, 128).astype(BF16)
    packed[:, rows:] = packed3[...]


def run_backward(groups, *operands):
    return pl.pallas_call(
        backward_kernel,
        name="backward",
        out_shape=jax.ShapeDtypeStruct((groups, 512 // groups + operands[-2].shape[1], 128), BF16),
        in_specs=[VMEM] * len(operands),
        out_specs=VMEM,
        scratch_shapes=[
            pltpu.VMEM((8, 8, 16, 256), BF16),
            pltpu.VMEM((6, 6, 16, 256), F32),
            pltpu.VMEM((6, 6, 16, 256), BF16),
            pltpu.VMEM((4, 4, 16, 256), F32),
            pltpu.VMEM((4, 4, 32, 128), F32),
            pltpu.VMEM((6, 4, 32, 256), BF16),
            pltpu.VMEM((4, 2, 32, 512), F32),
            pltpu.VMEM((2, 4, 32, 128), F32),
            pltpu.VMEM((4, 4, 64, 128), F32),
            pltpu.VMEM((4, 256, 256), BF16),
        ],
        compiler_params=pltpu.CompilerParams(vmem_limit_bytes=LIMIT),
    )(*operands)


def sum_kernel(received, to_column, features):
    groups, rows = received.shape[0], to_column.shape[1]
    wide = 128 // groups
    own = received[:, rows : rows + wide // 8].astype(F32)
    for c in range(wide):
        features[c] = own[:, c // 8, (c % 8) * 16 : (c % 8) * 16 + 16].astype(BF16)
    total = received[:, :rows].astype(F32).sum(axis=0)
    to_column[...] = jnp.broadcast_to(total[None], to_column.shape).astype(BF16)


def run_sum(received, rows_y):
    groups = received.shape[0]
    wide = 128 // groups
    return pl.pallas_call(
        sum_kernel,
        name="sum",
        out_shape=(
            jax.ShapeDtypeStruct((rows_y, 512 // groups + 14 * wide, 128), BF16),
            jax.ShapeDtypeStruct((wide, groups, 16), BF16),
        ),
        in_specs=[VMEM],
        out_specs=(VMEM, VMEM),
        compiler_params=pltpu.CompilerParams(vmem_limit_bytes=LIMIT),
    )(received)


def share_kernel(column, to_all):
    total = column[:, : to_all.shape[1]].astype(F32).sum(axis=0)
    to_all[...] = jnp.broadcast_to(total[None], to_all.shape).astype(BF16)


def run_share(column, groups):
    return pl.pallas_call(
        share_kernel,
        name="share",
        out_shape=jax.ShapeDtypeStruct((groups, 512 // groups, 128), BF16),
        in_specs=[VMEM],
        out_specs=VMEM,
        compiler_params=pltpu.CompilerParams(vmem_limit_bytes=LIMIT),
    )(column)


def third_kernel(column, grad3):
    wide = grad3.shape[1]
    first = column.shape[1] - 14 * wide
    lines = column[:, first:].astype(F32).sum(axis=0)
    for tap in range(9):
        low = lines[tap * wide : tap * wide + wide]
        grad3[tap] = low[:, :64]
        grad3[9 + tap] = low[:, 64:]
        at = (9 + tap // 2) * wide
        grad3[18 + tap] = lines[at : at + wide][:, (tap % 2) * 64 : (tap % 2) * 64 + 64]


def run_third(column, wide):
    return pl.pallas_call(
        third_kernel,
        name="third",
        out_shape=jax.ShapeDtypeStruct((27, wide, 64), F32),
        in_specs=[VMEM],
        out_specs=VMEM,
        compiler_params=pltpu.CompilerParams(vmem_limit_bytes=LIMIT),
    )(column)


def unpack_kernel(shared, grad1, grad2, shift1, shift2, shift3):
    wide = shift3.shape[1]
    rows = shared[...].astype(F32).reshape(512, 128)
    for tap in range(27):
        at = (tap // 2) * 32
        grad2[tap] = rows[at : at + 32, (tap % 2) * 64 : (tap % 2) * 64 + 64]
    for dy in range(3):
        for dz in range(3):
            at = 448 + dy * 16 + dz * 4
            for dx in range(3):
                grad1[dx * 9 + dy * 3 + dz] = rows[at : at + 4, dx * 32 : dx * 32 + 32]
    biases = rows[496:504]
    shift1[...] = biases[1:2, 64:96]
    shift2[...] = biases[1:2, :64]
    place = lax.axis_index("gz")
    shift3[...] = roll(biases, lax.rem(128 - place * wide, 128), 1)[0:1, :wide]


def run_unpack(shared):
    wide = 128 // shared.shape[0]
    return pl.pallas_call(
        unpack_kernel,
        name="unpack",
        out_shape=(
            jax.ShapeDtypeStruct((27, 4, 32), F32),
            jax.ShapeDtypeStruct((27, 32, 64), F32),
            jax.ShapeDtypeStruct((1, 32), F32),
            jax.ShapeDtypeStruct((1, 64), F32),
            jax.ShapeDtypeStruct((1, wide), F32),
        ),
        in_specs=[VMEM],
        out_specs=(VMEM,) * 5,
        compiler_params=pltpu.CompilerParams(vmem_limit_bytes=LIMIT),
    )(shared)


def both_ways(to_next, to_previous, axis):
    devices = lax.axis_size(axis)
    forth = [(i, i + 1) for i in range(devices - 1)]
    back = [(i + 1, i) for i in range(devices - 1)]
    return lax.ppermute(to_next, axis, forth), lax.ppermute(to_previous, axis, back)


def shards(universe, kernel1, bias1, kernel2, bias2, kernel3, bias3, cotangent):
    size_y, size_z = lax.axis_size("gy"), lax.axis_size("gz")
    wide = 128 // size_z

    tile = universe.transpose(1, 2, 0, 3).reshape(8, 32, 128)
    cot = lax.all_to_all(cotangent[:, 0].transpose(1, 0, 2), "gz", 0, 0, tiled=True).reshape(128, 16)
    biases = jnp.stack([jnp.pad(bias1, (0, 96)), jnp.pad(bias2, (0, 64)), bias3])
    lower, upper = both_ways(tile, tile, "gz")
    strip = jnp.concatenate([lower[:, 4:], tile, upper[:, :28], jnp.zeros((8, 8, 128), BF16)], axis=1)
    strip, kernel1, kernel2 = lax.optimization_barrier((strip, kernel1, kernel2))
    top, bottom = both_ways(strip, strip, "gy")

    k1, k2 = kernel1.transpose(0, 2, 1).astype(F32), kernel2.transpose(0, 2, 1).astype(F32)
    k3 = kernel3.transpose(0, 2, 1)
    to_next, to_previous, hidden2, own_cot, ratio2, patches1, ratio1, fields, w2 = run_forward(
        top, strip, bottom, cot, k1, k2, biases
    )
    lower, upper = both_ways(to_next, to_previous, "gz")
    row_next, row_previous = run_weave(lower, hidden2, upper, own_cot)
    packed3, shift3, w3, wide3 = run_own(size_z, hidden2, own_cot, k3, biases)
    before, after = both_ways(row_next, row_previous, "gy")
    packed = run_backward(
        size_z,
        before, lower, hidden2, upper, after, own_cot, w3, wide3, w2, ratio2, patches1, ratio1, fields,
        packed3, shift3,
    )
    packed = lax.all_to_all(packed, "gz", 0, 0, tiled=True)
    column, features = run_sum(packed, size_y)
    column = lax.all_to_all(column, "gy", 0, 0, tiled=True)
    shared = lax.all_to_all(run_share(column, size_z), "gz", 0, 0, tiled=True)
    grad3 = run_third(column, wide)
    grad1, grad2, shift1, shift2, shift3 = run_unpack(shared)
    return (
        features[:, None], grad1.transpose(0, 2, 1), shift1[0], grad2.transpose(0, 2, 1), shift2[0], grad3, shift3[0]
    )


def solution(mesh):
    in_specs = (P(None, "gy", "gz", None), P(), P(), P(), P(), P(), P(), P("gz", "gy", None, None))
    out_specs = (P("gz", "gy", None, None), P(), P(), P(), P(), P(None, "gz", None), P("gz"))
    return jax.shard_map(shards, mesh=mesh, in_specs=in_specs, out_specs=out_specs, check_vma=False)
```

```python
import functools
import math

import jax
import jax.numpy as jnp
from jax import lax
from jax.experimental import pallas as pl
from jax.experimental.pallas import tpu as pltpu
from jax.sharding import PartitionSpec as P

F32 = jnp.float32
BF16 = jnp.bfloat16
SLOPE = 0.3
TWO_LOG2_E = 2.0 / math.log(2.0)
PAIRS = ((0, 1), (2, 3), (-3, -2), (4, 5), (-1, 6))
VMEM = pl.BlockSpec(memory_space=pltpu.VMEM)
LIMIT = 24 * 1024 * 1024


def dot(a, b):
    return jnp.dot(a, b, preferred_element_type=F32)


def dot_tn(a, b):
    return lax.dot_general(a, b, (((0,), (0,)), ((), ())), preferred_element_type=F32)


def dot_nt(a, b):
    return lax.dot_general(a, b, (((1,), (1,)), ((), ())), preferred_element_type=F32)


def lane(shape):
    return lax.broadcasted_iota(jnp.int32, shape, len(shape) - 1)


def exps(pre):
    scaled = pre * TWO_LOG2_E
    return jnp.exp2(jnp.maximum(scaled, SLOPE * scaled))


def pool1(e):
    total = e[:, :128] + e[:, 128:]
    total = total + roll(total, 64, 1)
    total = total + roll(total, 32, 1)
    return total * 0.125


def rounded(value):
    return value.astype(BF16).astype(F32)


def roll(value, amount, axis):
    return pltpu.roll(value, amount, axis)


def down(value):
    rows = lax.broadcasted_iota(jnp.int32, value.shape, 0)
    return jnp.where(rows == 0, 0.0, roll(value, 1, 0))


def up(value):
    count = value.shape[0]
    rows = lax.broadcasted_iota(jnp.int32, value.shape, 0)
    return jnp.where(rows == count - 1, 0.0, roll(value, count - 1, 0))


def lay_pick(pick):
    for px in range(4):
        row = lax.broadcasted_iota(jnp.int32, (256, 128), 0)
        col = lax.broadcasted_iota(jnp.int32, (256, 128), 1)
        same = row // 128 == col // 64
        hit = (row % 128) == 2 * (col % 64) - 1 + px
        pick[:, px * 128 : px * 128 + 128] = jnp.where(same & hit, 1.0, 0.0).astype(BF16)


def forward_kernel(
    top, mid, bot, cot, k1, k2, biases,
    to_next, to_previous, hidden2, own_cot, ratio2, patches1, turned_own, fields, w2, w1,
    pick, left, field, turned, pre1, first, spread, pre2, second,
):
    lay_weights1(k1, w1)
    lay_weights2(k2, w2)
    lay_pick(pick)
    bias1 = jnp.concatenate([biases[0:1, :32]] * 8, axis=1)
    bias2 = jnp.concatenate([biases[1:2, :64]] * 4, axis=1)
    base_y, base_z = lax.axis_index("gy"), lax.axis_index("gz")
    size_y, size_z = lax.axis_size("gy"), lax.axis_size("gz")

    def inside(offset_y, offset_z, scale):
        row = base_y * (4 // scale) + offset_y
        col = base_z * (4 // scale) + offset_z
        ok_y = (row >= 0) & (row < size_y * (4 // scale))
        ok_z = (col >= 0) & (col < size_z * (4 // scale))
        return jnp.where(ok_y & ok_z, 1.0, 0.0)

    def lay(source, index, target):
        rows = source[index].astype(F32)
        pieces = []
        for one, two in PAIRS:
            a, b = 8 * (one + 3), 8 * (two + 3)
            pieces.append(jnp.concatenate([rows[a : a + 16], rows[b : b + 16]], axis=1))
        left[target] = jnp.concatenate(pieces, axis=0).astype(BF16)

    def lay_both(step, carry):
        lay(mid, step, step + 7)
        lay(mid, step + 4, step + 11)
        return carry

    def lay_ends(step, carry):
        lay(top, step + 1, step)
        lay(bot, step, step + 15)
        return carry

    lax.fori_loop(0, 4, lay_both, 0)
    lax.fori_loop(0, 7, lay_ends, 0)

    for part in range(2):
        block = left[part * 11 : part * 11 + 11].reshape(880, 256)
        out = dot(block, pick[...]).astype(BF16).reshape(11, 5, 16, 512)
        for step in range(11):
            row = part * 11 + step
            for px in range(4):
                at = (row % 2 * 4 + px) * 16
                for k in range(5):
                    field[row // 2, at : at + 16, k * 128 : k * 128 + 128] = out[
                        step, k, :, px * 128 : px * 128 + 128
                    ]
    for pair in range(11):
        turned[pair] = field[pair].T
    fields[...] = field[3:8, :, :256]
    first[:, :, 0:8] = jnp.zeros((10, 10, 8, 128), F32)
    first[:, :, 72:80] = jnp.zeros((10, 10, 8, 128), F32)

    def block1(step, carry):
        for part in range(2):
            stack = jnp.concatenate([turned[2 * step + part], turned[2 * step + part + 1]], axis=1)
            pre1[part] = dot(stack, w1[...])
        for part in range(2):
            yw = 2 * step + part
            for k, pair in enumerate(PAIRS):
                for h, zw in enumerate(pair):
                    at = k * 128 + h * 64
                    mean = pool1(exps(pre1[part, at : at + 64] + bias1))
                    pooled = rounded(jnp.log(mean) * 0.5)
                    first[yw, zw + 3, 8:72] = pooled * inside(yw - 3, zw, 1)
        return carry

    lax.fori_loop(0, 5, block1, 0)
    turned_own[...] = turned[3:8, :256]

    group1 = lane((32, 128)) // 32

    def frame(yi, carry):
        for zi in range(10):
            part = first[yi, zi, pl.ds(7, 32, stride=2), :]
            for px in range(1, 4):
                part = jnp.where(group1 == px, first[yi, zi, pl.ds(7 + px, 32, stride=2), :], part)
            spread[yi, zi] = part.astype(BF16)
        return carry

    lax.fori_loop(0, 10, frame, 0)
    patches1[...] = spread[2:8, 2:8]

    half = lane((16, 128)) < 64

    def block2(step, carry):
        for part in range(2):
            yp = 2 * step + part
            columns = []
            for zo in range(4):
                tiles = [spread[pl.ds(2 * yp + dy, 2), 2 * zo + pz] for dy in range(3) for pz in range(4)]
                columns.append(jnp.concatenate(tiles, axis=2)[:, None])
            block = jnp.concatenate(columns, axis=1).reshape(256, 1536)
            pre2[part] = dot(block, w2[...].reshape(1536, 256)).reshape(2, 4, 32, 256)
        for part in range(2):
            yp = 2 * step + part
            for zo in range(4):
                pre = pre2[part, :, zo] + bias2
                e = exps(pre)
                both = e[0] + e[1]
                total = both[:, :128] + both[:, 128:]
                total = total + roll(total, 64, 1)
                mean = total * 0.125
                ok = inside(yp - 1, zo - 1, 2)
                share = (0.125 * ok) / mean
                share = jnp.concatenate([share, share], axis=1)
                ratio2[pl.ds(2 * yp, 2), zo] = jnp.where(pre > 0, 1.0, SLOPE) * (e * share[None])
                second[part, zo] = rounded(jnp.log(mean) * 0.5) * ok
        for part in range(2):
            for zo in range(4):
                even = second[part, zo, pl.ds(0, 16, stride=2), :]
                odd = second[part, zo, pl.ds(1, 16, stride=2), :]
                hidden2[2 * step + part, zo] = jnp.where(half, even, odd).astype(BF16)
        return carry

    lax.fori_loop(0, 2, block2, 0)
    own = cot[...].astype(F32).T.astype(BF16)
    own_cot[...] = own
    to_next[:128] = hidden2[:, 0:2].reshape(128, 128)
    to_previous[:128] = hidden2[:, 2:4].reshape(128, 128)
    to_next[128:144] = own
    to_previous[128:144] = own


def lay_weights1(taps, out):
    group = lane((16, 128)) // 32
    zero = jnp.zeros((16, 128), F32)
    wide = []
    for k in range(9):
        pieces = [taps[3 * k + dz].astype(F32) for dz in range(3)] + [jnp.zeros((4, 32), F32)]
        rows = jnp.concatenate(pieces, axis=0)
        wide.append(jnp.concatenate([rows] * 4, axis=1))
    for py in range(4):
        for px in range(4):
            at = (py * 4 + px) * 16
            for qy in range(2):
                dy = py - qy
                sides = [
                    wide[(px - qx) * 3 + dy] if 0 <= dy < 3 and 0 <= px - qx < 3 else zero for qx in range(2)
                ]
                value = jnp.where(group == 0, sides[0], sides[1])
                shifted = jnp.where(group == 2, roll(sides[0], 4, 0), roll(sides[1], 4, 0))
                out[at : at + 16, qy * 128 : qy * 128 + 128] = jnp.where(group < 2, value, shifted).astype(BF16)


def lay_weights2(taps, out):
    zero = jnp.zeros((32, 64), F32)
    for dy in range(3):
        out[dy, 384:512, 0:128] = jnp.zeros((128, 128), BF16)
        out[dy, 0:128, 128:256] = jnp.zeros((128, 128), BF16)
        for dz in range(3):
            for px in range(4):
                sides = [taps[(px - qx) * 9 + dy * 3 + dz] if 0 <= px - qx < 3 else zero for qx in range(2)]
                tile = jnp.concatenate(sides, axis=1).astype(BF16)
                for qz in range(2):
                    at = (dz + qz) * 128 + px * 32
                    out[dy, at : at + 32, qz * 128 : qz * 128 + 128] = tile


def lay_weights3(taps, out):
    zero = jnp.zeros((64, 128), BF16)
    for tap in range(9):
        out[tap, 192:256, 0:128] = zero
        out[tap, 0:64, 128:256] = zero
        for dx in range(3):
            value = taps[dx * 9 + tap]
            out[tap, dx * 64 : dx * 64 + 64, 0:128] = value
            out[tap, dx * 64 + 64 : dx * 64 + 128, 128:256] = value


def run_forward(*operands):
    return pl.pallas_call(
        forward_kernel,
        name="forward",
        out_shape=(
            jax.ShapeDtypeStruct((144, 128), BF16),
            jax.ShapeDtypeStruct((144, 128), BF16),
            jax.ShapeDtypeStruct((4, 4, 16, 128), BF16),
            jax.ShapeDtypeStruct((16, 128), BF16),
            jax.ShapeDtypeStruct((8, 4, 32, 256), F32),
            jax.ShapeDtypeStruct((6, 6, 32, 128), BF16),
            jax.ShapeDtypeStruct((5, 256, 128), BF16),
            jax.ShapeDtypeStruct((5, 128, 256), BF16),
            jax.ShapeDtypeStruct((3, 512, 256), BF16),
            jax.ShapeDtypeStruct((256, 256), BF16),
        ),
        in_specs=[VMEM] * len(operands),
        out_specs=(VMEM,) * 10,
        cost_estimate=pl.CostEstimate(flops=5000000000, bytes_accessed=8000000, transcendentals=8000000),
        scratch_shapes=[
            pltpu.VMEM((256, 512), BF16),
            pltpu.VMEM((22, 80, 256), BF16),
            pltpu.VMEM((11, 128, 640), BF16),
            pltpu.VMEM((11, 640, 128), BF16),
            pltpu.VMEM((2, 640, 256), F32),
            pltpu.VMEM((10, 10, 80, 128), F32),
            pltpu.VMEM((10, 10, 32, 128), BF16),
            pltpu.VMEM((2, 2, 4, 32, 256), F32),
            pltpu.VMEM((2, 4, 32, 128), F32),
        ],
        compiler_params=pltpu.CompilerParams(vmem_limit_bytes=LIMIT),
    )(*operands)


def weave_kernel(lower, hidden2, upper, own_cot, to_next, to_previous):
    for target, first_row in ((to_next, 0), (to_previous, 2)):
        for y in range(2):
            row, at = first_row + y, y * 128
            target[at : at + 32] = lower[row * 32 : row * 32 + 32]
            target[at + 32 : at + 96] = hidden2[row].reshape(64, 128)
            target[at + 96 : at + 128] = upper[row * 32 : row * 32 + 32]
        target[256:272] = lower[128:144]
        target[272:288] = own_cot[...]
        target[288:304] = upper[128:144]


def run_weave(*operands):
    return pl.pallas_call(
        weave_kernel,
        name="weave",
        out_shape=(jax.ShapeDtypeStruct((304, 128), BF16),) * 2,
        in_specs=[VMEM] * 4,
        out_specs=(VMEM,) * 2,
        compiler_params=pltpu.CompilerParams(vmem_limit_bytes=LIMIT),
    )(*operands)


def lay_patches2(rows, target):
    half = lane((16, 128)) < 64
    swapped = roll(rows.astype(F32), 64, 1)
    target[...] = jnp.concatenate(
        [jnp.where(half, down(swapped), swapped), jnp.where(half, swapped, up(swapped))], axis=1
    ).astype(BF16)


def pool3(pre, cot):
    e = exps(pre)
    total = e[0, 0] + e[0, 1] + e[1, 0] + e[1, 1]
    total = total[:, :128] + total[:, 128:]
    mean = total * 0.125
    share = cot.astype(F32) * (0.125 / mean)
    share = jnp.concatenate([share, share], axis=1)
    return mean, (jnp.where(pre > 0, 1.0, SLOPE) * (e * share)).astype(BF16)


def own_kernel(
    hidden2, own_cot, k3, biases, turned_own, w1, packed, shift3, w3, wide3, ratio1, patches2, pre3, turned
):
    groups = packed.shape[0]
    wide = 128 // groups
    bias1 = jnp.concatenate([biases[0:1, :32]] * 8, axis=1)
    for yw in range(4):
        stack = jnp.concatenate([turned_own[yw], turned_own[yw + 1]], axis=1)
        ratio1[yw] = dot(stack, w1[...])
    for yw in range(4):
        for at in range(0, 256, 64):
            pre = ratio1[yw, at : at + 64] + bias1
            e = exps(pre)
            share = 0.125 / pool1(e)
            share = jnp.concatenate([share, share], axis=1)
            ratio1[yw, at : at + 64] = jnp.where(pre > 0, 1.0, SLOPE) * (e * share)
    lay_weights3(k3, w3)
    wide3[...] = jnp.concatenate([biases[2:3]] * 2, axis=1)
    for y in range(4):
        for z in range(4):
            lay_patches2(hidden2[y, z], patches2.at[y, z])
    for tap in range(9):
        dy, dz = tap // 3, tap % 3
        block = patches2[dy : dy + 2, dz : dz + 2].reshape(64, 256)
        term = dot(block, w3[tap])
        pre3[...] = term + wide3[...] if tap == 0 else pre3[...] + term
    mean, delta = pool3(pre3[...].reshape(2, 2, 16, 256), own_cot[...])
    features = rounded(jnp.log(mean) * 0.5)
    own3 = delta.reshape(64, 256)
    bias3 = own3.astype(F32).sum(axis=0, keepdims=True)
    shift3[...] = bias3[:, :128] + bias3[:, 128:]
    low, high = [], []
    for tap in range(9):
        dy, dz = tap // 3, tap % 3
        block = patches2[dy : dy + 2, dz : dz + 2].reshape(64, 256)
        full = dot_tn(own3, block)
        one = full[:128]
        low_lanes, high_lanes = roll(full[128:, :128], 64, 1), roll(full[128:, 128:], 64, 1)
        tile0 = jnp.where(lane((128, 128)) < 64, low_lanes, high_lanes)
        tile1 = high_lanes
        low.append(one[:, :128] + tile0)
        high.append(one[:, 128:] + tile1)
    first_half = lane((128, 128)) < 64
    paired = []
    for m in range(5):
        other = roll(high[2 * m + 1], 64, 1) if 2 * m + 1 < 9 else jnp.zeros((128, 128), F32)
        paired.append(jnp.where(first_half, high[2 * m], other))
    kernel3 = [piece.reshape(groups, wide, 128) for piece in low + paired]

    turned[...] = jnp.concatenate([features, jnp.zeros((112, 128), F32)], axis=0).T
    feature_rows = turned[pl.ds(0, 16, stride=8), :]
    for c in range(1, 8):
        feature_rows = feature_rows + roll(turned[pl.ds(c, 16, stride=8), :], 16 * c, 1)
    feature_rows = feature_rows.reshape(groups, wide // 8, 128)
    fill = jnp.zeros((groups, packed.shape[1] - 14 * wide - wide // 8, 128), F32)
    packed[...] = jnp.concatenate(kernel3 + [feature_rows, fill], axis=1).astype(BF16)


def run_own(groups, *operands):
    wide = 128 // groups
    return pl.pallas_call(
        own_kernel,
        name="own",
        out_shape=(
            jax.ShapeDtypeStruct((groups, -(-(14 * wide + wide // 8) // 8) * 8, 128), BF16),
            jax.ShapeDtypeStruct((1, 128), F32),
            jax.ShapeDtypeStruct((9, 256, 256), BF16),
            jax.ShapeDtypeStruct((1, 256), F32),
            jax.ShapeDtypeStruct((4, 256, 256), F32),
        ),
        in_specs=[VMEM] * len(operands),
        out_specs=(VMEM,) * 5,
        scratch_shapes=[
            pltpu.VMEM((4, 4, 16, 256), BF16),
            pltpu.VMEM((64, 256), F32),
            pltpu.VMEM((128, 128), F32),
        ],
        compiler_params=pltpu.CompilerParams(vmem_limit_bytes=LIMIT),
        cost_estimate=pl.CostEstimate(flops=150000000, bytes_accessed=4000000, transcendentals=20000),
    )(*operands)


def backward_kernel(
    before, lower, middle, upper, after, own_cot, w3, bias3, w2, ratio2, patches1, ratio1, fields, packed3, shift3,
    packed, patches2, pre3, delta3, patch2, grad2, delta2, patch1, beside, grad1, delta1,
):
    groups = packed.shape[0]
    half = lane((16, 128)) < 64

    def lay(y, source):
        for z in range(8):
            lay_patches2(source(z), patches2.at[y, z])

    for y in range(2):
        lay(y, lambda z: before[(y * 8 + z) * 16 : (y * 8 + z + 1) * 16])
        lay(y + 6, lambda z: after[(y * 8 + z) * 16 : (y * 8 + z + 1) * 16])

    def pick_middle(y, z):
        if z < 2:
            return lower[(y * 2 + z) * 16 : (y * 2 + z + 1) * 16]
        if z < 6:
            return middle[y, z - 2]
        return upper[(y * 2 + z - 6) * 16 : (y * 2 + z - 5) * 16]

    for y in range(4):
        lay(y + 2, functools.partial(pick_middle, y))

    for dy in range(3):
        blocks = [patches2[dy : dy + 6, dz : dz + 6].reshape(576, 256) for dz in range(3)]
        weights = w3[3 * dy : 3 * dy + 3].reshape(768, 256)
        term = dot(jnp.concatenate(blocks, axis=1), weights).reshape(6, 6, 16, 256)
        pre3[...] = term + bias3[...] if dy == 0 else pre3[...] + term

    for wy in range(3):
        for wz in range(3):
            pre = pre3[2 * wy : 2 * wy + 2, 2 * wz : 2 * wz + 2]
            if wy == 1:
                cot = own_cot[...] if wz == 1 else (lower if wz == 0 else upper)[128:144]
            else:
                cot = (before if wy == 0 else after)[256 + wz * 16 : 272 + wz * 16]
            delta3[2 * wy : 2 * wy + 2, 2 * wz : 2 * wz + 2] = pool3(pre, cot)[1]

    for dy in range(3):
        blocks = [delta3[2 - dy : 6 - dy, 2 - dz : 6 - dz].reshape(256, 256) for dz in range(3)]
        weights = jnp.concatenate([w3[3 * dy + dz] for dz in range(3)], axis=1)
        term = dot_nt(jnp.concatenate(blocks, axis=1), weights).reshape(4, 4, 16, 256)
        patch2[...] = term if dy == 0 else patch2[...] + term

    for y in range(4):
        for z in range(4):
            a, b = patch2[y, z, :, :128], patch2[y, z, :, 128:]
            x = rounded(jnp.where(half, b + up(a), a + down(b)))
            swapped = roll(x, 64, 1)
            grad2[y, z, pl.ds(0, 16, stride=2), :] = jnp.where(half, swapped, x)
            grad2[y, z, pl.ds(1, 16, stride=2), :] = jnp.where(half, x, swapped)

    for y in range(6):
        value = grad2[(y + 1) // 2]
        value = jnp.concatenate([value, value], axis=2)
        delta2[y] = (value * ratio2[y + 1]).astype(BF16)

    own2 = delta2[1:5, 1:3].reshape(256, 256)
    bias2 = own2.astype(F32).sum(axis=0, keepdims=True)
    bias2 = bias2[:, :128] + bias2[:, 128:]
    bias2 = bias2 + roll(bias2, 64, 1)
    taps = [None] * 27
    for dy in range(3):
        block = jnp.concatenate(
            [
                jnp.concatenate([patches1[dy : dy + 4, 2 * zo + pz] for pz in range(4)], axis=2)[:, None]
                for zo in range(2)
            ],
            axis=1,
        ).reshape(256, 512)
        full = dot_tn(block, own2)
        for dz in range(3):
            rows = full[dz * 128 : dz * 128 + 128, :128] + full[dz * 128 + 128 : dz * 128 + 256, 128:]
            for dx in range(3):
                taps[dx * 9 + dy * 3 + dz] = rows[dx * 32 : dx * 32 + 32] + roll(
                    rows[dx * 32 + 32 : dx * 32 + 64], 64, 1
                )
    def g1(columns, lanes, rows):
        blocks = [delta2[2 - dy : 6 - dy, columns, :, lanes].reshape(-1, lanes.stop - lanes.start) for dy in range(3)]
        weights = jnp.concatenate([w2[dy, rows, lanes] for dy in range(3)], axis=1)
        return dot_nt(jnp.concatenate(blocks, axis=1), weights)

    patch1[...] = g1(slice(1, 3), slice(0, 256), slice(0, 512)).reshape(4, 2, 32, 512)
    below = g1(slice(0, 1), slice(128, 256), slice(384, 512)).reshape(4, 32, 128)
    above = g1(slice(3, 4), slice(0, 128), slice(0, 128)).reshape(4, 32, 128)
    beside[0] = below
    beside[1] = above

    low_half = lane((32, 128)) < 64
    group = lane((32, 128)) // 32

    def widen(value, which):
        value = jnp.where(group == which, value, 0.0)
        value = value + roll(value, 32, 1)
        return value + roll(value, 64, 1)


    for y in range(4):
        def part(zo, pz):
            return patch1[y, zo, :, pz * 128 : pz * 128 + 128]

        sums = (
            beside[0, y] + part(0, 1), part(0, 2) + part(1, 0), part(0, 3) + part(1, 1), part(1, 2) + beside[1, y],
        )
        for z, value in enumerate(sums):
            value = rounded(value + roll(jnp.where(low_half, up(value), down(value)), 64, 1))
            grad1[y, z, pl.ds(0, 32, stride=2), :] = widen(value, 1)
            grad1[y, z, pl.ds(1, 32, stride=2), :] = widen(value, 2)
        value = grad1[y].reshape(256, 128)
        value = jnp.concatenate([value, value], axis=1)
        delta1[y] = (value * ratio1[y]).astype(BF16)

    bias1 = delta1[...].astype(F32).sum(axis=0).sum(axis=0, keepdims=True)
    bias1 = bias1[:, :128] + bias1[:, 128:]
    bias1 = bias1 + roll(bias1, 64, 1)
    bias1 = bias1 + roll(bias1, 32, 1)
    full = None
    for yw in range(4):
        term = dot(fields[yw : yw + 2].reshape(256, 256), delta1[yw])
        full = term if full is None else full + term
    full = full.reshape(4, 4, 16, 256)
    kernel1 = []
    group1 = lane((16, 128)) // 32
    for dy in range(3):
        rows = full[dy, :, :, :128] + full[dy + 1, :, :, 128:]
        pieces = []
        for dx in range(3):
            value = rows[dx] + roll(rows[dx + 1], 96, 1)
            value = value + roll(roll(value, 12, 0), 64, 1)
            pieces.append(roll(value, 32 * dx, 1) if dx else value)
        kernel1.append(jnp.where(group1 == 0, pieces[0], jnp.where(group1 == 1, pieces[1], pieces[2])))

    low_lane = lane((32, 128)) < 64
    kernel2 = [
        jnp.where(low_lane, taps[2 * m], roll(taps[2 * m + 1], 64, 1) if 2 * m + 1 < 27 else 0.0)
        for m in range(14)
    ]
    shifts = jnp.concatenate(
        [shift3[...], jnp.where(lane((1, 128)) < 64, bias2, bias1), jnp.zeros((14, 128), F32)], axis=0
    )
    shared = jnp.concatenate(kernel2 + kernel1 + [shifts], axis=0)
    rows = 512 // groups
    packed[:, :rows] = shared.reshape(groups, rows, 128).astype(BF16)
    packed[:, rows:] = packed3[...]


def run_backward(groups, *operands):
    return pl.pallas_call(
        backward_kernel,
        name="backward",
        out_shape=jax.ShapeDtypeStruct((groups, 512 // groups + operands[-2].shape[1], 128), BF16),
        in_specs=[VMEM] * len(operands),
        out_specs=VMEM,
        scratch_shapes=[
            pltpu.VMEM((8, 8, 16, 256), BF16),
            pltpu.VMEM((6, 6, 16, 256), F32),
            pltpu.VMEM((6, 6, 16, 256), BF16),
            pltpu.VMEM((4, 4, 16, 256), F32),
            pltpu.VMEM((4, 4, 32, 128), F32),
            pltpu.VMEM((6, 4, 32, 256), BF16),
            pltpu.VMEM((4, 2, 32, 512), F32),
            pltpu.VMEM((2, 4, 32, 128), F32),
            pltpu.VMEM((4, 4, 64, 128), F32),
            pltpu.VMEM((4, 256, 256), BF16),
        ],
        compiler_params=pltpu.CompilerParams(vmem_limit_bytes=LIMIT),
    )(*operands)


def sum_kernel(received, to_column, features):
    groups, rows = received.shape[0], to_column.shape[1]
    wide = 128 // groups
    own = received[:, rows : rows + wide // 8].astype(F32)
    for c in range(wide):
        features[c] = own[:, c // 8, (c % 8) * 16 : (c % 8) * 16 + 16].astype(BF16)
    total = received[:, :rows].astype(F32).sum(axis=0)
    to_column[...] = jnp.broadcast_to(total[None], to_column.shape).astype(BF16)


def run_sum(received, rows_y):
    groups = received.shape[0]
    wide = 128 // groups
    return pl.pallas_call(
        sum_kernel,
        name="sum",
        out_shape=(
            jax.ShapeDtypeStruct((rows_y, 512 // groups + 14 * wide, 128), BF16),
            jax.ShapeDtypeStruct((wide, groups, 16), BF16),
        ),
        in_specs=[VMEM],
        out_specs=(VMEM, VMEM),
        compiler_params=pltpu.CompilerParams(vmem_limit_bytes=LIMIT),
    )(received)


def share_kernel(column, to_all):
    total = column[:, : to_all.shape[1]].astype(F32).sum(axis=0)
    to_all[...] = jnp.broadcast_to(total[None], to_all.shape).astype(BF16)


def run_share(column, groups):
    return pl.pallas_call(
        share_kernel,
        name="share",
        out_shape=jax.ShapeDtypeStruct((groups, 512 // groups, 128), BF16),
        in_specs=[VMEM],
        out_specs=VMEM,
        compiler_params=pltpu.CompilerParams(vmem_limit_bytes=LIMIT),
    )(column)


def third_kernel(column, grad3):
    wide = grad3.shape[1]
    first = column.shape[1] - 14 * wide
    lines = column[:, first:].astype(F32).sum(axis=0)
    for tap in range(9):
        low = lines[tap * wide : tap * wide + wide]
        grad3[tap] = low[:, :64]
        grad3[9 + tap] = low[:, 64:]
        at = (9 + tap // 2) * wide
        grad3[18 + tap] = lines[at : at + wide][:, (tap % 2) * 64 : (tap % 2) * 64 + 64]


def run_third(column, wide):
    return pl.pallas_call(
        third_kernel,
        name="third",
        out_shape=jax.ShapeDtypeStruct((27, wide, 64), F32),
        in_specs=[VMEM],
        out_specs=VMEM,
        compiler_params=pltpu.CompilerParams(vmem_limit_bytes=LIMIT),
    )(column)


def unpack_kernel(shared, grad1, grad2, shift1, shift2, shift3):
    wide = shift3.shape[1]
    rows = shared[...].astype(F32).reshape(512, 128)
    for tap in range(27):
        at = (tap // 2) * 32
        grad2[tap] = rows[at : at + 32, (tap % 2) * 64 : (tap % 2) * 64 + 64]
    for dy in range(3):
        for dz in range(3):
            at = 448 + dy * 16 + dz * 4
            for dx in range(3):
                grad1[dx * 9 + dy * 3 + dz] = rows[at : at + 4, dx * 32 : dx * 32 + 32]
    biases = rows[496:504]
    shift1[...] = biases[1:2, 64:96]
    shift2[...] = biases[1:2, :64]
    place = lax.axis_index("gz")
    shift3[...] = roll(biases, lax.rem(128 - place * wide, 128), 1)[0:1, :wide]


def run_unpack(shared):
    wide = 128 // shared.shape[0]
    return pl.pallas_call(
        unpack_kernel,
        name="unpack",
        out_shape=(
            jax.ShapeDtypeStruct((27, 4, 32), F32),
            jax.ShapeDtypeStruct((27, 32, 64), F32),
            jax.ShapeDtypeStruct((1, 32), F32),
            jax.ShapeDtypeStruct((1, 64), F32),
            jax.ShapeDtypeStruct((1, wide), F32),
        ),
        in_specs=[VMEM],
        out_specs=(VMEM,) * 5,
        compiler_params=pltpu.CompilerParams(vmem_limit_bytes=LIMIT),
    )(shared)


def both_ways(to_next, to_previous, axis):
    devices = lax.axis_size(axis)
    forth = [(i, i + 1) for i in range(devices - 1)]
    back = [(i + 1, i) for i in range(devices - 1)]
    return lax.ppermute(to_next, axis, forth), lax.ppermute(to_previous, axis, back)


def shards(universe, kernel1, bias1, kernel2, bias2, kernel3, bias3, cotangent):
    size_y, size_z = lax.axis_size("gy"), lax.axis_size("gz")
    wide = 128 // size_z

    tile = universe.transpose(1, 2, 0, 3).reshape(8, 32, 128)
    cot = lax.all_to_all(cotangent[:, 0].transpose(1, 0, 2), "gz", 0, 0, tiled=True).reshape(128, 16)
    lower, upper = both_ways(tile, tile, "gz")
    strip = jnp.concatenate([lower[:, 4:], tile, upper[:, :28], jnp.zeros((8, 8, 128), BF16)], axis=1)
    strip, kernel1, kernel2, bias1, bias2, bias3 = lax.optimization_barrier(
        (strip, kernel1, kernel2, bias1, bias2, bias3)
    )
    top, bottom = both_ways(strip, strip, "gy")
    biases = jnp.stack([jnp.pad(bias1, (0, 96)), jnp.pad(bias2, (0, 64)), bias3])

    k1, k2 = kernel1.transpose(0, 2, 1).astype(F32), kernel2.transpose(0, 2, 1).astype(F32)
    k3 = kernel3.transpose(0, 2, 1)
    to_next, to_previous, hidden2, own_cot, ratio2, patches1, turned_own, fields, w2, w1 = run_forward(
        top, strip, bottom, cot, k1, k2, biases
    )
    lower, upper = both_ways(to_next, to_previous, "gz")
    row_next, row_previous = run_weave(lower, hidden2, upper, own_cot)
    packed3, shift3, w3, wide3, ratio1 = run_own(size_z, hidden2, own_cot, k3, biases, turned_own, w1)
    before, after = both_ways(row_next, row_previous, "gy")
    packed = run_backward(
        size_z,
        before, lower, hidden2, upper, after, own_cot, w3, wide3, w2, ratio2, patches1, ratio1, fields,
        packed3, shift3,
    )
    packed = lax.all_to_all(packed, "gz", 0, 0, tiled=True)
    column, features = run_sum(packed, size_y)
    column = lax.all_to_all(column, "gy", 0, 0, tiled=True)
    shared = lax.all_to_all(run_share(column, size_z), "gz", 0, 0, tiled=True)
    grad3 = run_third(column, wide)
    grad1, grad2, shift1, shift2, shift3 = run_unpack(shared)
    return (
        features[:, None], grad1.transpose(0, 2, 1), shift1[0], grad2.transpose(0, 2, 1), shift2[0], grad3, shift3[0]
    )


def solution(mesh):
    in_specs = (P(None, "gy", "gz", None), P(), P(), P(), P(), P(), P(), P("gz", "gy", None, None))
    out_specs = (P("gz", "gy", None, None), P(), P(), P(), P(), P(None, "gz", None), P("gz"))
    return jax.shard_map(shards, mesh=mesh, in_specs=in_specs, out_specs=out_specs, check_vma=False)
```

```python
import functools
import math

import jax
import jax.numpy as jnp
from jax import lax
from jax.experimental import pallas as pl
from jax.experimental.pallas import tpu as pltpu
from jax.sharding import PartitionSpec as P

F32 = jnp.float32
BF16 = jnp.bfloat16
SLOPE = 0.3
TWO_LOG2_E = 2.0 / math.log(2.0)
PAIRS = ((0, 1), (2, 3), (-3, -2), (4, 5), (-1, 6))
VMEM = pl.BlockSpec(memory_space=pltpu.VMEM)
LIMIT = 24 * 1024 * 1024


def dot(a, b):
    return jnp.dot(a, b, preferred_element_type=F32)


def dot_tn(a, b):
    return lax.dot_general(a, b, (((0,), (0,)), ((), ())), preferred_element_type=F32)


def dot_nt(a, b):
    return lax.dot_general(a, b, (((1,), (1,)), ((), ())), preferred_element_type=F32)


def lane(shape):
    return lax.broadcasted_iota(jnp.int32, shape, len(shape) - 1)


def exps(pre):
    scaled = pre * TWO_LOG2_E
    return jnp.exp2(jnp.maximum(scaled, SLOPE * scaled))


def pool1(e):
    total = e[:, :128] + e[:, 128:]
    total = total + roll(total, 64, 1)
    total = total + roll(total, 32, 1)
    return total * 0.125


def odd(axis):
    return lax.rem(lax.axis_index(axis), 2)


def sided(axis, far, near):
    flag = odd(axis).astype(F32)
    far, near = far.astype(F32), near.astype(F32)
    return (near * flag + far * (1.0 - flag)).astype(BF16), (far * flag + near * (1.0 - flag)).astype(BF16)


def rounded(value):
    return value.astype(BF16).astype(F32)


def roll(value, amount, axis):
    return pltpu.roll(value, amount, axis)


def down(value):
    rows = lax.broadcasted_iota(jnp.int32, value.shape, 0)
    return jnp.where(rows == 0, 0.0, roll(value, 1, 0))


def up(value):
    count = value.shape[0]
    rows = lax.broadcasted_iota(jnp.int32, value.shape, 0)
    return jnp.where(rows == count - 1, 0.0, roll(value, count - 1, 0))


def lay_pick(pick):
    for px in range(4):
        row = lax.broadcasted_iota(jnp.int32, (256, 128), 0)
        col = lax.broadcasted_iota(jnp.int32, (256, 128), 1)
        same = row // 128 == col // 64
        hit = (row % 128) == 2 * (col % 64) - 1 + px
        pick[:, px * 128 : px * 128 + 128] = jnp.where(same & hit, 1.0, 0.0).astype(BF16)


def forward_kernel(
    near, mid, far, cot, k1, k2, biases,
    to_far, to_near, hidden2, own_cot, ratio2, patches1, turned_own, fields, w2, w1,
    pick, left, field, turned, pre1, first, spread, pre2, second,
):
    lay_weights1(k1, w1)
    lay_weights2(k2, w2)
    lay_pick(pick)
    bias1 = jnp.concatenate([biases[0:1, :32]] * 8, axis=1)
    bias2 = jnp.concatenate([biases[1:2, :64]] * 4, axis=1)
    base_y, base_z = lax.axis_index("gy"), lax.axis_index("gz")
    size_y, size_z = lax.axis_size("gy"), lax.axis_size("gz")

    def inside(offset_y, offset_z, scale):
        row = base_y * (4 // scale) + offset_y
        col = base_z * (4 // scale) + offset_z
        ok_y = (row >= 0) & (row < size_y * (4 // scale))
        ok_z = (col >= 0) & (col < size_z * (4 // scale))
        return jnp.where(ok_y & ok_z, 1.0, 0.0)

    def lay(rows, target):
        rows = rows.astype(F32)
        pieces = []
        for one, two in PAIRS:
            a, b = 8 * (one + 3), 8 * (two + 3)
            pieces.append(jnp.concatenate([rows[a : a + 16], rows[b : b + 16]], axis=1))
        left[target] = jnp.concatenate(pieces, axis=0).astype(BF16)

    def lay_both(step, carry):
        lay(mid[step], step + 7)
        lay(mid[step + 4], step + 11)
        return carry

    def lay_ends(step, carry):
        lay(sided("gy", far[step + 1], near[step + 1])[0], step)
        lay(sided("gy", far[step], near[step])[1], step + 15)
        return carry

    lax.fori_loop(0, 4, lay_both, 0)
    lax.fori_loop(0, 7, lay_ends, 0)

    for part in range(2):
        block = left[part * 11 : part * 11 + 11].reshape(880, 256)
        out = dot(block, pick[...]).astype(BF16).reshape(11, 5, 16, 512)
        for step in range(11):
            row = part * 11 + step
            for px in range(4):
                at = (row % 2 * 4 + px) * 16
                for k in range(5):
                    field[row // 2, at : at + 16, k * 128 : k * 128 + 128] = out[
                        step, k, :, px * 128 : px * 128 + 128
                    ]
    for pair in range(11):
        turned[pair] = field[pair].T
    fields[...] = field[3:8, :, :256]
    first[:, :, 0:8] = jnp.zeros((10, 10, 8, 128), F32)
    first[:, :, 72:80] = jnp.zeros((10, 10, 8, 128), F32)

    def block1(step, carry):
        for part in range(2):
            stack = jnp.concatenate([turned[2 * step + part], turned[2 * step + part + 1]], axis=1)
            pre1[part] = dot(stack, w1[...])
        for part in range(2):
            yw = 2 * step + part
            for k, pair in enumerate(PAIRS):
                for h, zw in enumerate(pair):
                    at = k * 128 + h * 64
                    mean = pool1(exps(pre1[part, at : at + 64] + bias1))
                    pooled = rounded(jnp.log(mean) * 0.5)
                    first[yw, zw + 3, 8:72] = pooled * inside(yw - 3, zw, 1)
        return carry

    lax.fori_loop(0, 5, block1, 0)
    turned_own[...] = turned[3:8, :256]

    group1 = lane((32, 128)) // 32

    def frame(yi, carry):
        for zi in range(10):
            part = first[yi, zi, pl.ds(7, 32, stride=2), :]
            for px in range(1, 4):
                part = jnp.where(group1 == px, first[yi, zi, pl.ds(7 + px, 32, stride=2), :], part)
            spread[yi, zi] = part.astype(BF16)
        return carry

    lax.fori_loop(0, 10, frame, 0)
    patches1[...] = spread[2:8, 2:8]

    half = lane((16, 128)) < 64

    def block2(step, carry):
        for part in range(2):
            yp = 2 * step + part
            columns = []
            for zo in range(4):
                tiles = [spread[pl.ds(2 * yp + dy, 2), 2 * zo + pz] for dy in range(3) for pz in range(4)]
                columns.append(jnp.concatenate(tiles, axis=2)[:, None])
            block = jnp.concatenate(columns, axis=1).reshape(256, 1536)
            pre2[part] = dot(block, w2[...].reshape(1536, 256)).reshape(2, 4, 32, 256)
        for part in range(2):
            yp = 2 * step + part
            for zo in range(4):
                pre = pre2[part, :, zo] + bias2
                e = exps(pre)
                both = e[0] + e[1]
                total = both[:, :128] + both[:, 128:]
                total = total + roll(total, 64, 1)
                mean = total * 0.125
                ok = inside(yp - 1, zo - 1, 2)
                share = (0.125 * ok) / mean
                share = jnp.concatenate([share, share], axis=1)
                ratio2[pl.ds(2 * yp, 2), zo] = jnp.where(pre > 0, 1.0, SLOPE) * (e * share[None])
                second[part, zo] = rounded(jnp.log(mean) * 0.5) * ok
        for part in range(2):
            for zo in range(4):
                even = second[part, zo, pl.ds(0, 16, stride=2), :]
                odd = second[part, zo, pl.ds(1, 16, stride=2), :]
                hidden2[2 * step + part, zo] = jnp.where(half, even, odd).astype(BF16)
        return carry

    lax.fori_loop(0, 2, block2, 0)
    own = cot[...].astype(F32).T.astype(BF16)
    own_cot[...] = own
    side = odd("gz")
    to_far[:128] = hidden2[:, pl.ds(2 - 2 * side, 2)].reshape(128, 128)
    to_near[:128] = hidden2[:, pl.ds(2 * side, 2)].reshape(128, 128)
    to_far[128:144] = own
    to_near[128:144] = own


def lay_weights1(taps, out):
    group = lane((16, 128)) // 32
    zero = jnp.zeros((16, 128), F32)
    wide = []
    for k in range(9):
        pieces = [taps[3 * k + dz].astype(F32) for dz in range(3)] + [jnp.zeros((4, 32), F32)]
        rows = jnp.concatenate(pieces, axis=0)
        wide.append(jnp.concatenate([rows] * 4, axis=1))
    for py in range(4):
        for px in range(4):
            at = (py * 4 + px) * 16
            for qy in range(2):
                dy = py - qy
                sides = [
                    wide[(px - qx) * 3 + dy] if 0 <= dy < 3 and 0 <= px - qx < 3 else zero for qx in range(2)
                ]
                value = jnp.where(group == 0, sides[0], sides[1])
                shifted = jnp.where(group == 2, roll(sides[0], 4, 0), roll(sides[1], 4, 0))
                out[at : at + 16, qy * 128 : qy * 128 + 128] = jnp.where(group < 2, value, shifted).astype(BF16)


def lay_weights2(taps, out):
    zero = jnp.zeros((32, 64), F32)
    for dy in range(3):
        out[dy, 384:512, 0:128] = jnp.zeros((128, 128), BF16)
        out[dy, 0:128, 128:256] = jnp.zeros((128, 128), BF16)
        for dz in range(3):
            for px in range(4):
                sides = [taps[(px - qx) * 9 + dy * 3 + dz] if 0 <= px - qx < 3 else zero for qx in range(2)]
                tile = jnp.concatenate(sides, axis=1).astype(BF16)
                for qz in range(2):
                    at = (dz + qz) * 128 + px * 32
                    out[dy, at : at + 32, qz * 128 : qz * 128 + 128] = tile


def lay_weights3(taps, out):
    zero = jnp.zeros((64, 128), BF16)
    for tap in range(9):
        out[tap, 192:256, 0:128] = zero
        out[tap, 0:64, 128:256] = zero
        for dx in range(3):
            value = taps[dx * 9 + tap]
            out[tap, dx * 64 : dx * 64 + 64, 0:128] = value
            out[tap, dx * 64 + 64 : dx * 64 + 128, 128:256] = value


def run_forward(*operands):
    return pl.pallas_call(
        forward_kernel,
        name="forward",
        out_shape=(
            jax.ShapeDtypeStruct((144, 128), BF16),
            jax.ShapeDtypeStruct((144, 128), BF16),
            jax.ShapeDtypeStruct((4, 4, 16, 128), BF16),
            jax.ShapeDtypeStruct((16, 128), BF16),
            jax.ShapeDtypeStruct((8, 4, 32, 256), F32),
            jax.ShapeDtypeStruct((6, 6, 32, 128), BF16),
            jax.ShapeDtypeStruct((5, 256, 128), BF16),
            jax.ShapeDtypeStruct((5, 128, 256), BF16),
            jax.ShapeDtypeStruct((3, 512, 256), BF16),
            jax.ShapeDtypeStruct((256, 256), BF16),
        ),
        in_specs=[VMEM] * len(operands),
        out_specs=(VMEM,) * 10,
        cost_estimate=pl.CostEstimate(flops=5000000000, bytes_accessed=8000000, transcendentals=8000000),
        scratch_shapes=[
            pltpu.VMEM((256, 512), BF16),
            pltpu.VMEM((22, 80, 256), BF16),
            pltpu.VMEM((11, 128, 640), BF16),
            pltpu.VMEM((11, 640, 128), BF16),
            pltpu.VMEM((2, 640, 256), F32),
            pltpu.VMEM((10, 10, 80, 128), F32),
            pltpu.VMEM((10, 10, 32, 128), BF16),
            pltpu.VMEM((2, 2, 4, 32, 256), F32),
            pltpu.VMEM((2, 4, 32, 128), F32),
        ],
        compiler_params=pltpu.CompilerParams(vmem_limit_bytes=LIMIT),
    )(*operands)


def weave_kernel(far, near, hidden2, own_cot, to_far, to_near, lower, upper):
    lower[...], upper[...] = sided("gz", far[...], near[...])
    side = odd("gy")
    for target, first_row in ((to_far, 2 - 2 * side), (to_near, 2 * side)):
        for y in range(2):
            row, at = first_row + y, y * 128
            rows = pl.ds(pl.multiple_of(row * 32, 32), 32)
            target[at : at + 32] = lower[rows]
            target[at + 32 : at + 96] = hidden2[row].reshape(64, 128)
            target[at + 96 : at + 128] = upper[rows]
        target[256:272] = lower[128:144]
        target[272:288] = own_cot[...]
        target[288:304] = upper[128:144]


def run_weave(*operands):
    return pl.pallas_call(
        weave_kernel,
        name="weave",
        out_shape=(jax.ShapeDtypeStruct((304, 128), BF16),) * 2 + (jax.ShapeDtypeStruct((144, 128), BF16),) * 2,
        in_specs=[VMEM] * 4,
        out_specs=(VMEM,) * 4,
        compiler_params=pltpu.CompilerParams(vmem_limit_bytes=LIMIT),
    )(*operands)


def lay_patches2(rows, target):
    half = lane((16, 128)) < 64
    swapped = roll(rows.astype(F32), 64, 1)
    target[...] = jnp.concatenate(
        [jnp.where(half, down(swapped), swapped), jnp.where(half, swapped, up(swapped))], axis=1
    ).astype(BF16)


def pool3(pre, cot):
    e = exps(pre)
    total = e[0, 0] + e[0, 1] + e[1, 0] + e[1, 1]
    total = total[:, :128] + total[:, 128:]
    mean = total * 0.125
    share = cot.astype(F32) * (0.125 / mean)
    share = jnp.concatenate([share, share], axis=1)
    return mean, (jnp.where(pre > 0, 1.0, SLOPE) * (e * share)).astype(BF16)


def own_kernel(
    hidden2, own_cot, k3, biases, turned_own, w1, packed, shift3, w3, wide3, ratio1, patches2, pre3, turned
):
    groups = packed.shape[0]
    wide = 128 // groups
    bias1 = jnp.concatenate([biases[0:1, :32]] * 8, axis=1)
    for yw in range(4):
        stack = jnp.concatenate([turned_own[yw], turned_own[yw + 1]], axis=1)
        ratio1[yw] = dot(stack, w1[...])
    for yw in range(4):
        for at in range(0, 256, 64):
            pre = ratio1[yw, at : at + 64] + bias1
            e = exps(pre)
            share = 0.125 / pool1(e)
            share = jnp.concatenate([share, share], axis=1)
            ratio1[yw, at : at + 64] = jnp.where(pre > 0, 1.0, SLOPE) * (e * share)
    lay_weights3(k3, w3)
    wide3[...] = jnp.concatenate([biases[2:3]] * 2, axis=1)
    for y in range(4):
        for z in range(4):
            lay_patches2(hidden2[y, z], patches2.at[y, z])
    for tap in range(9):
        dy, dz = tap // 3, tap % 3
        block = patches2[dy : dy + 2, dz : dz + 2].reshape(64, 256)
        term = dot(block, w3[tap])
        pre3[...] = term + wide3[...] if tap == 0 else pre3[...] + term
    mean, delta = pool3(pre3[...].reshape(2, 2, 16, 256), own_cot[...])
    features = rounded(jnp.log(mean) * 0.5)
    own3 = delta.reshape(64, 256)
    bias3 = own3.astype(F32).sum(axis=0, keepdims=True)
    shift3[...] = bias3[:, :128] + bias3[:, 128:]
    low, high = [], []
    for tap in range(9):
        dy, dz = tap // 3, tap % 3
        block = patches2[dy : dy + 2, dz : dz + 2].reshape(64, 256)
        full = dot_tn(own3, block)
        one = full[:128]
        low_lanes, high_lanes = roll(full[128:, :128], 64, 1), roll(full[128:, 128:], 64, 1)
        tile0 = jnp.where(lane((128, 128)) < 64, low_lanes, high_lanes)
        tile1 = high_lanes
        low.append(one[:, :128] + tile0)
        high.append(one[:, 128:] + tile1)
    first_half = lane((128, 128)) < 64
    paired = []
    for m in range(5):
        other = roll(high[2 * m + 1], 64, 1) if 2 * m + 1 < 9 else jnp.zeros((128, 128), F32)
        paired.append(jnp.where(first_half, high[2 * m], other))
    kernel3 = [piece.reshape(groups, wide, 128) for piece in low + paired]

    turned[...] = jnp.concatenate([features, jnp.zeros((112, 128), F32)], axis=0).T
    feature_rows = turned[pl.ds(0, 16, stride=8), :]
    for c in range(1, 8):
        feature_rows = feature_rows + roll(turned[pl.ds(c, 16, stride=8), :], 16 * c, 1)
    feature_rows = feature_rows.reshape(groups, wide // 8, 128)
    fill = jnp.zeros((groups, packed.shape[1] - 14 * wide - wide // 8, 128), F32)
    packed[...] = jnp.concatenate(kernel3 + [feature_rows, fill], axis=1).astype(BF16)


def run_own(groups, *operands):
    wide = 128 // groups
    return pl.pallas_call(
        own_kernel,
        name="own",
        out_shape=(
            jax.ShapeDtypeStruct((groups, -(-(14 * wide + wide // 8) // 8) * 8, 128), BF16),
            jax.ShapeDtypeStruct((1, 128), F32),
            jax.ShapeDtypeStruct((9, 256, 256), BF16),
            jax.ShapeDtypeStruct((1, 256), F32),
            jax.ShapeDtypeStruct((4, 256, 256), F32),
        ),
        in_specs=[VMEM] * len(operands),
        out_specs=(VMEM,) * 5,
        scratch_shapes=[
            pltpu.VMEM((4, 4, 16, 256), BF16),
            pltpu.VMEM((64, 256), F32),
            pltpu.VMEM((128, 128), F32),
        ],
        compiler_params=pltpu.CompilerParams(vmem_limit_bytes=LIMIT),
        cost_estimate=pl.CostEstimate(flops=150000000, bytes_accessed=4000000, transcendentals=20000),
    )(*operands)


def backward_kernel(
    far, lower, middle, upper, near, own_cot, w3, bias3, w2, ratio2, patches1, ratio1, fields, packed3, shift3,
    packed, before, after, patches2, pre3, delta3, patch2, grad2, delta2, patch1, beside, grad1, delta1,
):
    before[...], after[...] = sided("gy", far[...], near[...])
    groups = packed.shape[0]
    half = lane((16, 128)) < 64

    def lay(y, source):
        for z in range(8):
            lay_patches2(source(z), patches2.at[y, z])

    for y in range(2):
        lay(y, lambda z: before[(y * 8 + z) * 16 : (y * 8 + z + 1) * 16])
        lay(y + 6, lambda z: after[(y * 8 + z) * 16 : (y * 8 + z + 1) * 16])

    def pick_middle(y, z):
        if z < 2:
            return lower[(y * 2 + z) * 16 : (y * 2 + z + 1) * 16]
        if z < 6:
            return middle[y, z - 2]
        return upper[(y * 2 + z - 6) * 16 : (y * 2 + z - 5) * 16]

    for y in range(4):
        lay(y + 2, functools.partial(pick_middle, y))

    for dy in range(3):
        blocks = [patches2[dy : dy + 6, dz : dz + 6].reshape(576, 256) for dz in range(3)]
        weights = w3[3 * dy : 3 * dy + 3].reshape(768, 256)
        term = dot(jnp.concatenate(blocks, axis=1), weights).reshape(6, 6, 16, 256)
        pre3[...] = term + bias3[...] if dy == 0 else pre3[...] + term

    for wy in range(3):
        for wz in range(3):
            pre = pre3[2 * wy : 2 * wy + 2, 2 * wz : 2 * wz + 2]
            if wy == 1:
                cot = own_cot[...] if wz == 1 else (lower if wz == 0 else upper)[128:144]
            else:
                cot = (before if wy == 0 else after)[256 + wz * 16 : 272 + wz * 16]
            delta3[2 * wy : 2 * wy + 2, 2 * wz : 2 * wz + 2] = pool3(pre, cot)[1]

    for dy in range(3):
        blocks = [delta3[2 - dy : 6 - dy, 2 - dz : 6 - dz].reshape(256, 256) for dz in range(3)]
        weights = jnp.concatenate([w3[3 * dy + dz] for dz in range(3)], axis=1)
        term = dot_nt(jnp.concatenate(blocks, axis=1), weights).reshape(4, 4, 16, 256)
        patch2[...] = term if dy == 0 else patch2[...] + term

    for y in range(4):
        for z in range(4):
            a, b = patch2[y, z, :, :128], patch2[y, z, :, 128:]
            x = rounded(jnp.where(half, b + up(a), a + down(b)))
            swapped = roll(x, 64, 1)
            grad2[y, z, pl.ds(0, 16, stride=2), :] = jnp.where(half, swapped, x)
            grad2[y, z, pl.ds(1, 16, stride=2), :] = jnp.where(half, x, swapped)

    for y in range(6):
        value = grad2[(y + 1) // 2]
        value = jnp.concatenate([value, value], axis=2)
        delta2[y] = (value * ratio2[y + 1]).astype(BF16)

    own2 = delta2[1:5, 1:3].reshape(256, 256)
    bias2 = own2.astype(F32).sum(axis=0, keepdims=True)
    bias2 = bias2[:, :128] + bias2[:, 128:]
    bias2 = bias2 + roll(bias2, 64, 1)
    taps = [None] * 27
    for dy in range(3):
        block = jnp.concatenate(
            [
                jnp.concatenate([patches1[dy : dy + 4, 2 * zo + pz] for pz in range(4)], axis=2)[:, None]
                for zo in range(2)
            ],
            axis=1,
        ).reshape(256, 512)
        full = dot_tn(block, own2)
        for dz in range(3):
            rows = full[dz * 128 : dz * 128 + 128, :128] + full[dz * 128 + 128 : dz * 128 + 256, 128:]
            for dx in range(3):
                taps[dx * 9 + dy * 3 + dz] = rows[dx * 32 : dx * 32 + 32] + roll(
                    rows[dx * 32 + 32 : dx * 32 + 64], 64, 1
                )
    def g1(columns, lanes, rows):
        blocks = [delta2[2 - dy : 6 - dy, columns, :, lanes].reshape(-1, lanes.stop - lanes.start) for dy in range(3)]
        weights = jnp.concatenate([w2[dy, rows, lanes] for dy in range(3)], axis=1)
        return dot_nt(jnp.concatenate(blocks, axis=1), weights)

    patch1[...] = g1(slice(1, 3), slice(0, 256), slice(0, 512)).reshape(4, 2, 32, 512)
    below = g1(slice(0, 1), slice(128, 256), slice(384, 512)).reshape(4, 32, 128)
    above = g1(slice(3, 4), slice(0, 128), slice(0, 128)).reshape(4, 32, 128)
    beside[0] = below
    beside[1] = above

    low_half = lane((32, 128)) < 64
    group = lane((32, 128)) // 32

    def widen(value, which):
        value = jnp.where(group == which, value, 0.0)
        value = value + roll(value, 32, 1)
        return value + roll(value, 64, 1)


    for y in range(4):
        def part(zo, pz):
            return patch1[y, zo, :, pz * 128 : pz * 128 + 128]

        sums = (
            beside[0, y] + part(0, 1), part(0, 2) + part(1, 0), part(0, 3) + part(1, 1), part(1, 2) + beside[1, y],
        )
        for z, value in enumerate(sums):
            value = rounded(value + roll(jnp.where(low_half, up(value), down(value)), 64, 1))
            grad1[y, z, pl.ds(0, 32, stride=2), :] = widen(value, 1)
            grad1[y, z, pl.ds(1, 32, stride=2), :] = widen(value, 2)
        value = grad1[y].reshape(256, 128)
        value = jnp.concatenate([value, value], axis=1)
        delta1[y] = (value * ratio1[y]).astype(BF16)

    bias1 = delta1[...].astype(F32).sum(axis=0).sum(axis=0, keepdims=True)
    bias1 = bias1[:, :128] + bias1[:, 128:]
    bias1 = bias1 + roll(bias1, 64, 1)
    bias1 = bias1 + roll(bias1, 32, 1)
    full = None
    for yw in range(4):
        term = dot(fields[yw : yw + 2].reshape(256, 256), delta1[yw])
        full = term if full is None else full + term
    full = full.reshape(4, 4, 16, 256)
    kernel1 = []
    group1 = lane((16, 128)) // 32
    for dy in range(3):
        rows = full[dy, :, :, :128] + full[dy + 1, :, :, 128:]
        pieces = []
        for dx in range(3):
            value = rows[dx] + roll(rows[dx + 1], 96, 1)
            value = value + roll(roll(value, 12, 0), 64, 1)
            pieces.append(roll(value, 32 * dx, 1) if dx else value)
        kernel1.append(jnp.where(group1 == 0, pieces[0], jnp.where(group1 == 1, pieces[1], pieces[2])))

    low_lane = lane((32, 128)) < 64
    kernel2 = [
        jnp.where(low_lane, taps[2 * m], roll(taps[2 * m + 1], 64, 1) if 2 * m + 1 < 27 else 0.0)
        for m in range(14)
    ]
    shifts = jnp.concatenate(
        [shift3[...], jnp.where(lane((1, 128)) < 64, bias2, bias1), jnp.zeros((14, 128), F32)], axis=0
    )
    shared = jnp.concatenate(kernel2 + kernel1 + [shifts], axis=0)
    rows = 512 // groups
    packed[:, :rows] = shared.reshape(groups, rows, 128).astype(BF16)
    packed[:, rows:] = packed3[...]


def run_backward(groups, *operands):
    return pl.pallas_call(
        backward_kernel,
        name="backward",
        out_shape=jax.ShapeDtypeStruct((groups, 512 // groups + operands[-2].shape[1], 128), BF16),
        in_specs=[VMEM] * len(operands),
        out_specs=VMEM,
        scratch_shapes=[
            pltpu.VMEM((304, 128), BF16),
            pltpu.VMEM((304, 128), BF16),
            pltpu.VMEM((8, 8, 16, 256), BF16),
            pltpu.VMEM((6, 6, 16, 256), F32),
            pltpu.VMEM((6, 6, 16, 256), BF16),
            pltpu.VMEM((4, 4, 16, 256), F32),
            pltpu.VMEM((4, 4, 32, 128), F32),
            pltpu.VMEM((6, 4, 32, 256), BF16),
            pltpu.VMEM((4, 2, 32, 512), F32),
            pltpu.VMEM((2, 4, 32, 128), F32),
            pltpu.VMEM((4, 4, 64, 128), F32),
            pltpu.VMEM((4, 256, 256), BF16),
        ],
        compiler_params=pltpu.CompilerParams(vmem_limit_bytes=LIMIT),
    )(*operands)


def sum_kernel(received, to_column, features):
    groups, rows = received.shape[0], to_column.shape[1]
    wide = 128 // groups
    own = received[:, rows : rows + wide // 8].astype(F32)
    for c in range(wide):
        features[c] = own[:, c // 8, (c % 8) * 16 : (c % 8) * 16 + 16].astype(BF16)
    total = received[:, :rows].astype(F32).sum(axis=0)
    to_column[...] = jnp.broadcast_to(total[None], to_column.shape).astype(BF16)


def run_sum(received, rows_y):
    groups = received.shape[0]
    wide = 128 // groups
    return pl.pallas_call(
        sum_kernel,
        name="sum",
        out_shape=(
            jax.ShapeDtypeStruct((rows_y, 512 // groups + 14 * wide, 128), BF16),
            jax.ShapeDtypeStruct((wide, groups, 16), BF16),
        ),
        in_specs=[VMEM],
        out_specs=(VMEM, VMEM),
        compiler_params=pltpu.CompilerParams(vmem_limit_bytes=LIMIT),
    )(received)


def share_kernel(column, to_all):
    total = column[:, : to_all.shape[1]].astype(F32).sum(axis=0)
    to_all[...] = jnp.broadcast_to(total[None], to_all.shape).astype(BF16)


def run_share(column, groups):
    return pl.pallas_call(
        share_kernel,
        name="share",
        out_shape=jax.ShapeDtypeStruct((groups, 512 // groups, 128), BF16),
        in_specs=[VMEM],
        out_specs=VMEM,
        compiler_params=pltpu.CompilerParams(vmem_limit_bytes=LIMIT),
    )(column)


def third_kernel(column, grad3):
    wide = grad3.shape[1]
    first = column.shape[1] - 14 * wide
    lines = column[:, first:].astype(F32).sum(axis=0)
    for tap in range(9):
        low = lines[tap * wide : tap * wide + wide]
        grad3[tap] = low[:, :64]
        grad3[9 + tap] = low[:, 64:]
        at = (9 + tap // 2) * wide
        grad3[18 + tap] = lines[at : at + wide][:, (tap % 2) * 64 : (tap % 2) * 64 + 64]


def run_third(column, wide):
    return pl.pallas_call(
        third_kernel,
        name="third",
        out_shape=jax.ShapeDtypeStruct((27, wide, 64), F32),
        in_specs=[VMEM],
        out_specs=VMEM,
        compiler_params=pltpu.CompilerParams(vmem_limit_bytes=LIMIT),
    )(column)


def unpack_kernel(shared, grad1, grad2, shift1, shift2, shift3):
    wide = shift3.shape[1]
    rows = shared[...].astype(F32).reshape(512, 128)
    for tap in range(27):
        at = (tap // 2) * 32
        grad2[tap] = rows[at : at + 32, (tap % 2) * 64 : (tap % 2) * 64 + 64]
    for dy in range(3):
        for dz in range(3):
            at = 448 + dy * 16 + dz * 4
            for dx in range(3):
                grad1[dx * 9 + dy * 3 + dz] = rows[at : at + 4, dx * 32 : dx * 32 + 32]
    biases = rows[496:504]
    shift1[...] = biases[1:2, 64:96]
    shift2[...] = biases[1:2, :64]
    place = lax.axis_index("gz")
    shift3[...] = roll(biases, lax.rem(128 - place * wide, 128), 1)[0:1, :wide]


def run_unpack(shared):
    wide = 128 // shared.shape[0]
    return pl.pallas_call(
        unpack_kernel,
        name="unpack",
        out_shape=(
            jax.ShapeDtypeStruct((27, 4, 32), F32),
            jax.ShapeDtypeStruct((27, 32, 64), F32),
            jax.ShapeDtypeStruct((1, 32), F32),
            jax.ShapeDtypeStruct((1, 64), F32),
            jax.ShapeDtypeStruct((1, wide), F32),
        ),
        in_specs=[VMEM],
        out_specs=(VMEM,) * 5,
        compiler_params=pltpu.CompilerParams(vmem_limit_bytes=LIMIT),
    )(shared)


def swap(to_far, to_near, axis):
    devices = lax.axis_size(axis)

    def pairs(first):
        forth = [(i, i + 1) for i in range(first, devices - 1, 2)]
        return forth + [(j, i) for i, j in forth]

    return lax.ppermute(to_far, axis, pairs(1)), lax.ppermute(to_near, axis, pairs(0))


def shards(universe, kernel1, bias1, kernel2, bias2, kernel3, bias3, cotangent):
    size_y, size_z = lax.axis_size("gy"), lax.axis_size("gz")
    wide = 128 // size_z

    tile = universe.transpose(1, 2, 0, 3).reshape(8, 32, 128)
    cot = lax.all_to_all(cotangent[:, 0].transpose(1, 0, 2), "gz", 0, 0, tiled=True).reshape(128, 16)
    far, near = swap(tile, tile, "gz")
    second = odd("gz") == 1
    lower, upper = jnp.where(second, near, far), jnp.where(second, far, near)
    strip = jnp.concatenate([lower[:, 4:], tile, upper[:, :28]], axis=1)
    strip, kernel1, kernel2, bias1, bias2, bias3 = lax.optimization_barrier(
        (strip, kernel1, kernel2, bias1, bias2, bias3)
    )
    far, near = swap(strip, strip, "gy")
    biases = jnp.stack([jnp.pad(bias1, (0, 96)), jnp.pad(bias2, (0, 64)), bias3])

    k1, k2 = kernel1.transpose(0, 2, 1).astype(F32), kernel2.transpose(0, 2, 1).astype(F32)
    k3 = kernel3.transpose(0, 2, 1)
    to_far, to_near, hidden2, own_cot, ratio2, patches1, turned_own, fields, w2, w1 = run_forward(
        near, strip, far, cot, k1, k2, biases
    )
    far, near = swap(to_far, to_near, "gz")
    to_far, to_near, lower, upper = run_weave(far, near, hidden2, own_cot)
    packed3, shift3, w3, wide3, ratio1 = run_own(size_z, hidden2, own_cot, k3, biases, turned_own, w1)
    far, near = swap(to_far, to_near, "gy")
    packed = run_backward(
        size_z,
        far, lower, hidden2, upper, near, own_cot, w3, wide3, w2, ratio2, patches1, ratio1, fields,
        packed3, shift3,
    )
    packed = lax.all_to_all(packed, "gz", 0, 0, tiled=True)
    column, features = run_sum(packed, size_y)
    column = lax.all_to_all(column, "gy", 0, 0, tiled=True)
    shared = lax.all_to_all(run_share(column, size_z), "gz", 0, 0, tiled=True)
    grad3 = run_third(column, wide)
    grad1, grad2, shift1, shift2, shift3 = run_unpack(shared)
    return (
        features[:, None], grad1.transpose(0, 2, 1), shift1[0], grad2.transpose(0, 2, 1), shift2[0], grad3, shift3[0]
    )


def solution(mesh):
    in_specs = (P(None, "gy", "gz", None), P(), P(), P(), P(), P(), P(), P("gz", "gy", None, None))
    out_specs = (P("gz", "gy", None, None), P(), P(), P(), P(), P(None, "gz", None), P("gz"))
    return jax.shard_map(shards, mesh=mesh, in_specs=in_specs, out_specs=out_specs, check_vma=False)
```

```python
import functools
import math

import jax
import jax.numpy as jnp
from jax import lax
from jax.experimental import pallas as pl
from jax.experimental.pallas import tpu as pltpu
from jax.sharding import PartitionSpec as P

F32 = jnp.float32
BF16 = jnp.bfloat16
SLOPE = 0.3
TWO_LOG2_E = 2.0 / math.log(2.0)
PAIRS = ((0, 1), (2, 3), (-3, -2), (4, 5), (-1, 6))
VMEM = pl.BlockSpec(memory_space=pltpu.VMEM)
LIMIT = 24 * 1024 * 1024


def dot(a, b):
    return jnp.dot(a, b, preferred_element_type=F32)


def dot_tn(a, b):
    return lax.dot_general(a, b, (((0,), (0,)), ((), ())), preferred_element_type=F32)


def dot_nt(a, b):
    return lax.dot_general(a, b, (((1,), (1,)), ((), ())), preferred_element_type=F32)


def lane(shape):
    return lax.broadcasted_iota(jnp.int32, shape, len(shape) - 1)


def exps(pre):
    scaled = pre * TWO_LOG2_E
    return jnp.exp2(jnp.maximum(scaled, SLOPE * scaled))


def pool1(e):
    total = e[:, :128] + e[:, 128:]
    total = total + roll(total, 64, 1)
    total = total + roll(total, 32, 1)
    return total * 0.125


def odd(axis):
    return lax.rem(lax.axis_index(axis), 2)


def sided(axis, far, near):
    flag = odd(axis).astype(F32)
    far, near = far.astype(F32), near.astype(F32)
    return (near * flag + far * (1.0 - flag)).astype(BF16), (far * flag + near * (1.0 - flag)).astype(BF16)


def rounded(value):
    return value.astype(BF16).astype(F32)


def roll(value, amount, axis):
    return pltpu.roll(value, amount, axis)


def down(value):
    rows = lax.broadcasted_iota(jnp.int32, value.shape, 0)
    return jnp.where(rows == 0, 0.0, roll(value, 1, 0))


def up(value):
    count = value.shape[0]
    rows = lax.broadcasted_iota(jnp.int32, value.shape, 0)
    return jnp.where(rows == count - 1, 0.0, roll(value, count - 1, 0))


def lay_pick(pick):
    for px in range(4):
        row = lax.broadcasted_iota(jnp.int32, (256, 128), 0)
        col = lax.broadcasted_iota(jnp.int32, (256, 128), 1)
        same = row // 128 == col // 64
        hit = (row % 128) == 2 * (col % 64) - 1 + px
        pick[:, px * 128 : px * 128 + 128] = jnp.where(same & hit, 1.0, 0.0).astype(BF16)


def forward_kernel(
    near, mid, far, cot, k1, k2, biases,
    to_far, to_near, hidden2, own_cot, ratio2, patches1, turned_own, fields, w2, w1,
    pick, left, field, turned, pre1, first, spread, pre2, second,
):
    lay_weights1(k1, w1)
    lay_weights2(k2, w2)
    lay_pick(pick)
    bias1 = jnp.concatenate([biases[0:1, :32]] * 8, axis=1)
    bias2 = jnp.concatenate([biases[1:2, :64]] * 4, axis=1)
    base_y, base_z = lax.axis_index("gy"), lax.axis_index("gz")
    size_y, size_z = lax.axis_size("gy"), lax.axis_size("gz")

    def inside(offset_y, offset_z, scale):
        row = base_y * (4 // scale) + offset_y
        col = base_z * (4 // scale) + offset_z
        ok_y = (row >= 0) & (row < size_y * (4 // scale))
        ok_z = (col >= 0) & (col < size_z * (4 // scale))
        return jnp.where(ok_y & ok_z, 1.0, 0.0)

    def lay(rows, target):
        rows = rows.astype(F32)
        pieces = []
        for one, two in PAIRS:
            a, b = 8 * (one + 3), 8 * (two + 3)
            pieces.append(jnp.concatenate([rows[a : a + 16], rows[b : b + 16]], axis=1))
        left[target] = jnp.concatenate(pieces, axis=0).astype(BF16)

    def lay_both(step, carry):
        lay(mid[step], step + 7)
        lay(mid[step + 4], step + 11)
        return carry

    def lay_ends(step, carry):
        lay(sided("gy", far[step + 1], near[step + 1])[0], step)
        lay(sided("gy", far[step], near[step])[1], step + 15)
        return carry

    lax.fori_loop(0, 4, lay_both, 0)
    lax.fori_loop(0, 7, lay_ends, 0)

    for part in range(2):
        block = left[part * 11 : part * 11 + 11].reshape(880, 256)
        out = dot(block, pick[...]).astype(BF16).reshape(11, 5, 16, 512)
        for step in range(11):
            row = part * 11 + step
            for px in range(4):
                at = (row % 2 * 4 + px) * 16
                for k in range(5):
                    field[row // 2, at : at + 16, k * 128 : k * 128 + 128] = out[
                        step, k, :, px * 128 : px * 128 + 128
                    ]
    for pair in range(11):
        turned[pair] = field[pair].T
    fields[...] = field[3:8, :, :256]
    first[:, :, 0:8] = jnp.zeros((10, 10, 8, 128), F32)
    first[:, :, 72:80] = jnp.zeros((10, 10, 8, 128), F32)

    def block1(step, carry):
        for part in range(2):
            stack = jnp.concatenate([turned[2 * step + part], turned[2 * step + part + 1]], axis=1)
            pre1[part] = dot(stack, w1[...])
        for part in range(2):
            yw = 2 * step + part
            for k, pair in enumerate(PAIRS):
                for h, zw in enumerate(pair):
                    at = k * 128 + h * 64
                    mean = pool1(exps(pre1[part, at : at + 64] + bias1))
                    pooled = rounded(jnp.log(mean) * 0.5)
                    first[yw, zw + 3, 8:72] = pooled * inside(yw - 3, zw, 1)
        return carry

    lax.fori_loop(0, 5, block1, 0)
    turned_own[...] = turned[3:8, :256]

    group1 = lane((32, 128)) // 32

    def frame(yi, carry):
        for zi in range(10):
            part = first[yi, zi, pl.ds(7, 32, stride=2), :]
            for px in range(1, 4):
                part = jnp.where(group1 == px, first[yi, zi, pl.ds(7 + px, 32, stride=2), :], part)
            spread[yi, zi] = part.astype(BF16)
        return carry

    lax.fori_loop(0, 10, frame, 0)
    patches1[...] = spread[2:8, 2:8]

    half = lane((16, 128)) < 64

    def block2(step, carry):
        for part in range(2):
            yp = 2 * step + part
            columns = []
            for zo in range(4):
                tiles = [spread[pl.ds(2 * yp + dy, 2), 2 * zo + pz] for dy in range(3) for pz in range(4)]
                columns.append(jnp.concatenate(tiles, axis=2)[:, None])
            block = jnp.concatenate(columns, axis=1).reshape(256, 1536)
            pre2[part] = dot(block, w2[...].reshape(1536, 256)).reshape(2, 4, 32, 256)
        for part in range(2):
            yp = 2 * step + part
            for zo in range(4):
                pre = pre2[part, :, zo] + bias2
                e = exps(pre)
                both = e[0] + e[1]
                total = both[:, :128] + both[:, 128:]
                total = total + roll(total, 64, 1)
                mean = total * 0.125
                ok = inside(yp - 1, zo - 1, 2)
                share = (0.125 * ok) / mean
                share = jnp.concatenate([share, share], axis=1)
                ratio2[pl.ds(2 * yp, 2), zo] = jnp.where(pre > 0, 1.0, SLOPE) * (e * share[None])
                second[part, zo] = rounded(jnp.log(mean) * 0.5) * ok
        for part in range(2):
            for zo in range(4):
                even = second[part, zo, pl.ds(0, 16, stride=2), :]
                odd = second[part, zo, pl.ds(1, 16, stride=2), :]
                hidden2[2 * step + part, zo] = jnp.where(half, even, odd).astype(BF16)
        return carry

    lax.fori_loop(0, 2, block2, 0)
    own = cot[...].astype(F32).T.astype(BF16)
    own_cot[...] = own
    side = odd("gz")
    to_far[:128] = hidden2[:, pl.ds(2 - 2 * side, 2)].reshape(128, 128)
    to_near[:128] = hidden2[:, pl.ds(2 * side, 2)].reshape(128, 128)
    to_far[128:144] = own
    to_near[128:144] = own


def lay_weights1(taps, out):
    group = lane((16, 128)) // 32
    zero = jnp.zeros((16, 128), F32)
    wide = []
    for k in range(9):
        pieces = [taps[3 * k + dz].astype(F32) for dz in range(3)] + [jnp.zeros((4, 32), F32)]
        rows = jnp.concatenate(pieces, axis=0)
        wide.append(jnp.concatenate([rows] * 4, axis=1))
    for py in range(4):
        for px in range(4):
            at = (py * 4 + px) * 16
            for qy in range(2):
                dy = py - qy
                sides = [
                    wide[(px - qx) * 3 + dy] if 0 <= dy < 3 and 0 <= px - qx < 3 else zero for qx in range(2)
                ]
                value = jnp.where(group == 0, sides[0], sides[1])
                shifted = jnp.where(group == 2, roll(sides[0], 4, 0), roll(sides[1], 4, 0))
                out[at : at + 16, qy * 128 : qy * 128 + 128] = jnp.where(group < 2, value, shifted).astype(BF16)


def lay_weights2(taps, out):
    zero = jnp.zeros((32, 64), F32)
    for dy in range(3):
        out[dy, 384:512, 0:128] = jnp.zeros((128, 128), BF16)
        out[dy, 0:128, 128:256] = jnp.zeros((128, 128), BF16)
        for dz in range(3):
            for px in range(4):
                sides = [taps[(px - qx) * 9 + dy * 3 + dz] if 0 <= px - qx < 3 else zero for qx in range(2)]
                tile = jnp.concatenate(sides, axis=1).astype(BF16)
                for qz in range(2):
                    at = (dz + qz) * 128 + px * 32
                    out[dy, at : at + 32, qz * 128 : qz * 128 + 128] = tile


def lay_weights3(taps, out):
    zero = jnp.zeros((64, 128), BF16)
    for tap in range(9):
        out[tap, 192:256, 0:128] = zero
        out[tap, 0:64, 128:256] = zero
        for dx in range(3):
            value = taps[dx * 9 + tap]
            out[tap, dx * 64 : dx * 64 + 64, 0:128] = value
            out[tap, dx * 64 + 64 : dx * 64 + 128, 128:256] = value


def run_forward(*operands):
    return pl.pallas_call(
        forward_kernel,
        name="forward",
        out_shape=(
            jax.ShapeDtypeStruct((144, 128), BF16),
            jax.ShapeDtypeStruct((144, 128), BF16),
            jax.ShapeDtypeStruct((4, 4, 16, 128), BF16),
            jax.ShapeDtypeStruct((16, 128), BF16),
            jax.ShapeDtypeStruct((8, 4, 32, 256), F32),
            jax.ShapeDtypeStruct((6, 6, 32, 128), BF16),
            jax.ShapeDtypeStruct((5, 256, 128), BF16),
            jax.ShapeDtypeStruct((5, 128, 256), BF16),
            jax.ShapeDtypeStruct((3, 512, 256), BF16),
            jax.ShapeDtypeStruct((256, 256), BF16),
        ),
        in_specs=[VMEM] * len(operands),
        out_specs=(VMEM,) * 10,
        cost_estimate=pl.CostEstimate(flops=5000000000, bytes_accessed=8000000, transcendentals=8000000),
        scratch_shapes=[
            pltpu.VMEM((256, 512), BF16),
            pltpu.VMEM((22, 80, 256), BF16),
            pltpu.VMEM((11, 128, 640), BF16),
            pltpu.VMEM((11, 640, 128), BF16),
            pltpu.VMEM((2, 640, 256), F32),
            pltpu.VMEM((10, 10, 80, 128), F32),
            pltpu.VMEM((10, 10, 32, 128), BF16),
            pltpu.VMEM((2, 2, 4, 32, 256), F32),
            pltpu.VMEM((2, 4, 32, 128), F32),
        ],
        compiler_params=pltpu.CompilerParams(vmem_limit_bytes=LIMIT),
    )(*operands)


def weave_kernel(far, near, hidden2, own_cot, to_far, to_near, lower, upper):
    lower[...], upper[...] = sided("gz", far[...], near[...])
    side = odd("gy")
    for target, first_row in ((to_far, 2 - 2 * side), (to_near, 2 * side)):
        for y in range(2):
            row, at = first_row + y, y * 128
            rows = pl.ds(pl.multiple_of(row * 32, 32), 32)
            target[at : at + 32] = lower[rows]
            target[at + 32 : at + 96] = hidden2[row].reshape(64, 128)
            target[at + 96 : at + 128] = upper[rows]
        target[256:272] = lower[128:144]
        target[272:288] = own_cot[...]
        target[288:304] = upper[128:144]


def run_weave(*operands):
    return pl.pallas_call(
        weave_kernel,
        name="weave",
        out_shape=(jax.ShapeDtypeStruct((304, 128), BF16),) * 2 + (jax.ShapeDtypeStruct((144, 128), BF16),) * 2,
        in_specs=[VMEM] * 4,
        out_specs=(VMEM,) * 4,
        compiler_params=pltpu.CompilerParams(vmem_limit_bytes=LIMIT),
    )(*operands)


def lay_patches2(rows, target):
    half = lane((16, 128)) < 64
    swapped = roll(rows.astype(F32), 64, 1)
    target[...] = jnp.concatenate(
        [jnp.where(half, down(swapped), swapped), jnp.where(half, swapped, up(swapped))], axis=1
    ).astype(BF16)


def pool3(pre, cot):
    e = exps(pre)
    total = e[0, 0] + e[0, 1] + e[1, 0] + e[1, 1]
    total = total[:, :128] + total[:, 128:]
    mean = total * 0.125
    share = cot.astype(F32) * (0.125 / mean)
    share = jnp.concatenate([share, share], axis=1)
    return mean, (jnp.where(pre > 0, 1.0, SLOPE) * (e * share)).astype(BF16)


def own_kernel(
    hidden2, own_cot, k3, biases, turned_own, w1, keep, send, shift3, w3, wide3, ratio1, patches2, pre3, turned
):
    groups = 2 * keep.shape[0]
    wide = 128 // groups
    bias1 = jnp.concatenate([biases[0:1, :32]] * 8, axis=1)
    for yw in range(4):
        stack = jnp.concatenate([turned_own[yw], turned_own[yw + 1]], axis=1)
        ratio1[yw] = dot(stack, w1[...])
    for yw in range(4):
        for at in range(0, 256, 64):
            pre = ratio1[yw, at : at + 64] + bias1
            e = exps(pre)
            share = 0.125 / pool1(e)
            share = jnp.concatenate([share, share], axis=1)
            ratio1[yw, at : at + 64] = jnp.where(pre > 0, 1.0, SLOPE) * (e * share)
    lay_weights3(k3, w3)
    wide3[...] = jnp.concatenate([biases[2:3]] * 2, axis=1)
    for y in range(4):
        for z in range(4):
            lay_patches2(hidden2[y, z], patches2.at[y, z])
    for tap in range(9):
        dy, dz = tap // 3, tap % 3
        block = patches2[dy : dy + 2, dz : dz + 2].reshape(64, 256)
        term = dot(block, w3[tap])
        pre3[...] = term + wide3[...] if tap == 0 else pre3[...] + term
    mean, delta = pool3(pre3[...].reshape(2, 2, 16, 256), own_cot[...])
    features = rounded(jnp.log(mean) * 0.5)
    own3 = delta.reshape(64, 256)
    bias3 = own3.astype(F32).sum(axis=0, keepdims=True)
    shift3[...] = bias3[:, :128] + bias3[:, 128:]
    low, high = [], []
    for tap in range(9):
        dy, dz = tap // 3, tap % 3
        block = patches2[dy : dy + 2, dz : dz + 2].reshape(64, 256)
        full = dot_tn(own3, block)
        one = full[:128]
        low_lanes, high_lanes = roll(full[128:, :128], 64, 1), roll(full[128:, 128:], 64, 1)
        tile0 = jnp.where(lane((128, 128)) < 64, low_lanes, high_lanes)
        tile1 = high_lanes
        low.append(one[:, :128] + tile0)
        high.append(one[:, 128:] + tile1)
    first_half = lane((128, 128)) < 64
    paired = []
    for m in range(5):
        other = roll(high[2 * m + 1], 64, 1) if 2 * m + 1 < 9 else jnp.zeros((128, 128), F32)
        paired.append(jnp.where(first_half, high[2 * m], other))
    kernel3 = [piece.reshape(groups, wide, 128) for piece in low + paired]

    turned[...] = jnp.concatenate([features, jnp.zeros((112, 128), F32)], axis=0).T
    feature_rows = turned[pl.ds(0, 16, stride=8), :]
    for c in range(1, 8):
        feature_rows = feature_rows + roll(turned[pl.ds(c, 16, stride=8), :], 16 * c, 1)
    feature_rows = feature_rows.reshape(groups, wide // 8, 128)
    flag = odd("gz").astype(F32)
    fill = jnp.zeros((groups, keep.shape[1] - 14 * wide - wide // 4, 128), F32)
    pieces = kernel3 + [feature_rows * (1.0 - flag), feature_rows * flag, fill]
    keep[...], send[...] = halves(jnp.concatenate(pieces, axis=1))


def halves(value):
    flag = odd("gz").astype(F32)
    pairs = value.reshape((value.shape[0] // 2, 2) + value.shape[1:])
    even, other = pairs[:, 0], pairs[:, 1]
    return (even * (1.0 - flag) + other * flag).astype(BF16), (even * flag + other * (1.0 - flag)).astype(BF16)


def run_own(groups, *operands):
    wide = 128 // groups
    return pl.pallas_call(
        own_kernel,
        name="own",
        out_shape=(
            jax.ShapeDtypeStruct((groups // 2, -(-(14 * wide + wide // 4) // 8) * 8, 128), BF16),
            jax.ShapeDtypeStruct((groups // 2, -(-(14 * wide + wide // 4) // 8) * 8, 128), BF16),
            jax.ShapeDtypeStruct((1, 128), F32),
            jax.ShapeDtypeStruct((9, 256, 256), BF16),
            jax.ShapeDtypeStruct((1, 256), F32),
            jax.ShapeDtypeStruct((4, 256, 256), F32),
        ),
        in_specs=[VMEM] * len(operands),
        out_specs=(VMEM,) * 6,
        scratch_shapes=[
            pltpu.VMEM((4, 4, 16, 256), BF16),
            pltpu.VMEM((64, 256), F32),
            pltpu.VMEM((128, 128), F32),
        ],
        compiler_params=pltpu.CompilerParams(vmem_limit_bytes=LIMIT),
        cost_estimate=pl.CostEstimate(flops=150000000, bytes_accessed=4000000, transcendentals=20000),
    )(*operands)


def backward_kernel(
    far, lower, middle, upper, near, own_cot, w3, bias3, w2, ratio2, patches1, ratio1, fields, keep3, send3, shift3,
    keep, send, before, after, patches2, pre3, delta3, patch2, grad2, delta2, patch1, beside, grad1, delta1,
):
    before[...], after[...] = sided("gy", far[...], near[...])
    groups = 2 * keep.shape[0]
    half = lane((16, 128)) < 64

    def lay(y, source):
        for z in range(8):
            lay_patches2(source(z), patches2.at[y, z])

    for y in range(2):
        lay(y, lambda z: before[(y * 8 + z) * 16 : (y * 8 + z + 1) * 16])
        lay(y + 6, lambda z: after[(y * 8 + z) * 16 : (y * 8 + z + 1) * 16])

    def pick_middle(y, z):
        if z < 2:
            return lower[(y * 2 + z) * 16 : (y * 2 + z + 1) * 16]
        if z < 6:
            return middle[y, z - 2]
        return upper[(y * 2 + z - 6) * 16 : (y * 2 + z - 5) * 16]

    for y in range(4):
        lay(y + 2, functools.partial(pick_middle, y))

    for dy in range(3):
        blocks = [patches2[dy : dy + 6, dz : dz + 6].reshape(576, 256) for dz in range(3)]
        weights = w3[3 * dy : 3 * dy + 3].reshape(768, 256)
        term = dot(jnp.concatenate(blocks, axis=1), weights).reshape(6, 6, 16, 256)
        pre3[...] = term + bias3[...] if dy == 0 else pre3[...] + term

    for wy in range(3):
        for wz in range(3):
            pre = pre3[2 * wy : 2 * wy + 2, 2 * wz : 2 * wz + 2]
            if wy == 1:
                cot = own_cot[...] if wz == 1 else (lower if wz == 0 else upper)[128:144]
            else:
                cot = (before if wy == 0 else after)[256 + wz * 16 : 272 + wz * 16]
            delta3[2 * wy : 2 * wy + 2, 2 * wz : 2 * wz + 2] = pool3(pre, cot)[1]

    for dy in range(3):
        blocks = [delta3[2 - dy : 6 - dy, 2 - dz : 6 - dz].reshape(256, 256) for dz in range(3)]
        weights = jnp.concatenate([w3[3 * dy + dz] for dz in range(3)], axis=1)
        term = dot_nt(jnp.concatenate(blocks, axis=1), weights).reshape(4, 4, 16, 256)
        patch2[...] = term if dy == 0 else patch2[...] + term

    for y in range(4):
        for z in range(4):
            a, b = patch2[y, z, :, :128], patch2[y, z, :, 128:]
            x = rounded(jnp.where(half, b + up(a), a + down(b)))
            swapped = roll(x, 64, 1)
            grad2[y, z, pl.ds(0, 16, stride=2), :] = jnp.where(half, swapped, x)
            grad2[y, z, pl.ds(1, 16, stride=2), :] = jnp.where(half, x, swapped)

    for y in range(6):
        value = grad2[(y + 1) // 2]
        value = jnp.concatenate([value, value], axis=2)
        delta2[y] = (value * ratio2[y + 1]).astype(BF16)

    own2 = delta2[1:5, 1:3].reshape(256, 256)
    bias2 = own2.astype(F32).sum(axis=0, keepdims=True)
    bias2 = bias2[:, :128] + bias2[:, 128:]
    bias2 = bias2 + roll(bias2, 64, 1)
    taps = [None] * 27
    for dy in range(3):
        block = jnp.concatenate(
            [
                jnp.concatenate([patches1[dy : dy + 4, 2 * zo + pz] for pz in range(4)], axis=2)[:, None]
                for zo in range(2)
            ],
            axis=1,
        ).reshape(256, 512)
        full = dot_tn(block, own2)
        for dz in range(3):
            rows = full[dz * 128 : dz * 128 + 128, :128] + full[dz * 128 + 128 : dz * 128 + 256, 128:]
            for dx in range(3):
                taps[dx * 9 + dy * 3 + dz] = rows[dx * 32 : dx * 32 + 32] + roll(
                    rows[dx * 32 + 32 : dx * 32 + 64], 64, 1
                )
    def g1(columns, lanes, rows):
        blocks = [delta2[2 - dy : 6 - dy, columns, :, lanes].reshape(-1, lanes.stop - lanes.start) for dy in range(3)]
        weights = jnp.concatenate([w2[dy, rows, lanes] for dy in range(3)], axis=1)
        return dot_nt(jnp.concatenate(blocks, axis=1), weights)

    patch1[...] = g1(slice(1, 3), slice(0, 256), slice(0, 512)).reshape(4, 2, 32, 512)
    below = g1(slice(0, 1), slice(128, 256), slice(384, 512)).reshape(4, 32, 128)
    above = g1(slice(3, 4), slice(0, 128), slice(0, 128)).reshape(4, 32, 128)
    beside[0] = below
    beside[1] = above

    low_half = lane((32, 128)) < 64
    group = lane((32, 128)) // 32

    def widen(value, which):
        value = jnp.where(group == which, value, 0.0)
        value = value + roll(value, 32, 1)
        return value + roll(value, 64, 1)


    for y in range(4):
        def part(zo, pz):
            return patch1[y, zo, :, pz * 128 : pz * 128 + 128]

        sums = (
            beside[0, y] + part(0, 1), part(0, 2) + part(1, 0), part(0, 3) + part(1, 1), part(1, 2) + beside[1, y],
        )
        for z, value in enumerate(sums):
            value = rounded(value + roll(jnp.where(low_half, up(value), down(value)), 64, 1))
            grad1[y, z, pl.ds(0, 32, stride=2), :] = widen(value, 1)
            grad1[y, z, pl.ds(1, 32, stride=2), :] = widen(value, 2)
        value = grad1[y].reshape(256, 128)
        value = jnp.concatenate([value, value], axis=1)
        delta1[y] = (value * ratio1[y]).astype(BF16)

    bias1 = delta1[...].astype(F32).sum(axis=0).sum(axis=0, keepdims=True)
    bias1 = bias1[:, :128] + bias1[:, 128:]
    bias1 = bias1 + roll(bias1, 64, 1)
    bias1 = bias1 + roll(bias1, 32, 1)
    full = None
    for yw in range(4):
        term = dot(fields[yw : yw + 2].reshape(256, 256), delta1[yw])
        full = term if full is None else full + term
    full = full.reshape(4, 4, 16, 256)
    kernel1 = []
    group1 = lane((16, 128)) // 32
    for dy in range(3):
        rows = full[dy, :, :, :128] + full[dy + 1, :, :, 128:]
        pieces = []
        for dx in range(3):
            value = rows[dx] + roll(rows[dx + 1], 96, 1)
            value = value + roll(roll(value, 12, 0), 64, 1)
            pieces.append(roll(value, 32 * dx, 1) if dx else value)
        kernel1.append(jnp.where(group1 == 0, pieces[0], jnp.where(group1 == 1, pieces[1], pieces[2])))

    low_lane = lane((32, 128)) < 64
    kernel2 = [
        jnp.where(low_lane, taps[2 * m], roll(taps[2 * m + 1], 64, 1) if 2 * m + 1 < 27 else 0.0)
        for m in range(14)
    ]
    shifts = jnp.concatenate(
        [shift3[...], jnp.where(lane((1, 128)) < 64, bias2, bias1), jnp.zeros((14, 128), F32)], axis=0
    )
    shared = jnp.concatenate(kernel2 + kernel1 + [shifts], axis=0)
    rows = 512 // groups
    keep[:, :rows], send[:, :rows] = halves(shared.reshape(groups, rows, 128))
    keep[:, rows:] = keep3[...]
    send[:, rows:] = send3[...]


def run_backward(groups, *operands):
    return pl.pallas_call(
        backward_kernel,
        name="backward",
        out_shape=(jax.ShapeDtypeStruct((groups // 2, 512 // groups + operands[-2].shape[1], 128), BF16),) * 2,
        in_specs=[VMEM] * len(operands),
        out_specs=(VMEM, VMEM),
        scratch_shapes=[
            pltpu.VMEM((304, 128), BF16),
            pltpu.VMEM((304, 128), BF16),
            pltpu.VMEM((8, 8, 16, 256), BF16),
            pltpu.VMEM((6, 6, 16, 256), F32),
            pltpu.VMEM((6, 6, 16, 256), BF16),
            pltpu.VMEM((4, 4, 16, 256), F32),
            pltpu.VMEM((4, 4, 32, 128), F32),
            pltpu.VMEM((6, 4, 32, 256), BF16),
            pltpu.VMEM((4, 2, 32, 512), F32),
            pltpu.VMEM((2, 4, 32, 128), F32),
            pltpu.VMEM((4, 4, 64, 128), F32),
            pltpu.VMEM((4, 256, 256), BF16),
        ],
        compiler_params=pltpu.CompilerParams(vmem_limit_bytes=LIMIT),
    )(*operands)


def pair_kernel(kept, received, total):
    total[...] = (kept[...].astype(F32) + received[...].astype(F32)).astype(BF16)


def run_pair(kept, received):
    return pl.pallas_call(
        pair_kernel,
        name="pair",
        out_shape=jax.ShapeDtypeStruct(kept.shape, BF16),
        in_specs=[VMEM] * 2,
        out_specs=VMEM,
        compiler_params=pltpu.CompilerParams(vmem_limit_bytes=LIMIT),
    )(kept, received)


def sum_kernel(received, to_column, features):
    half, rows = received.shape[0], to_column.shape[1]
    wide = 64 // half
    high = wide // 8
    own = received[:, rows : rows + 2 * high].astype(F32)
    for c in range(wide):
        for parity in range(2):
            line = own[:, parity * high + c // 8, (c % 8) * 16 : (c % 8) * 16 + 16]
            for j in range(half):
                features[c, 2 * j + parity : 2 * j + parity + 1] = line[j : j + 1]
    total = received[:, :rows].astype(F32).sum(axis=0)
    to_column[...] = jnp.broadcast_to(total[None], to_column.shape).astype(BF16)


def run_sum(received, rows_y):
    groups = 2 * received.shape[0]
    wide = 128 // groups
    return pl.pallas_call(
        sum_kernel,
        name="sum",
        out_shape=(
            jax.ShapeDtypeStruct((rows_y, 512 // groups + 14 * wide, 128), BF16),
            jax.ShapeDtypeStruct((wide, groups, 16), F32),
        ),
        in_specs=[VMEM],
        out_specs=(VMEM, VMEM),
        compiler_params=pltpu.CompilerParams(vmem_limit_bytes=LIMIT),
    )(received)


def share_kernel(column, to_all):
    total = column[:, : to_all.shape[1]].astype(F32).sum(axis=0)
    to_all[...] = jnp.broadcast_to(total[None], to_all.shape).astype(BF16)


def run_share(column, groups):
    return pl.pallas_call(
        share_kernel,
        name="share",
        out_shape=jax.ShapeDtypeStruct((groups, 512 // groups, 128), BF16),
        in_specs=[VMEM],
        out_specs=VMEM,
        compiler_params=pltpu.CompilerParams(vmem_limit_bytes=LIMIT),
    )(column)


def third_kernel(column, grad3):
    wide = grad3.shape[1]
    first = column.shape[1] - 14 * wide
    lines = column[:, first:].astype(F32).sum(axis=0)
    for tap in range(9):
        low = lines[tap * wide : tap * wide + wide]
        grad3[tap] = low[:, :64]
        grad3[9 + tap] = low[:, 64:]
        at = (9 + tap // 2) * wide
        grad3[18 + tap] = lines[at : at + wide][:, (tap % 2) * 64 : (tap % 2) * 64 + 64]


def run_third(column, wide):
    return pl.pallas_call(
        third_kernel,
        name="third",
        out_shape=jax.ShapeDtypeStruct((27, wide, 64), F32),
        in_specs=[VMEM],
        out_specs=VMEM,
        compiler_params=pltpu.CompilerParams(vmem_limit_bytes=LIMIT),
    )(column)


def unpack_kernel(shared, grad1, grad2, shift1, shift2, shift3):
    wide = shift3.shape[1]
    rows = shared[...].astype(F32).reshape(512, 128)
    for tap in range(27):
        at = (tap // 2) * 32
        grad2[tap] = rows[at : at + 32, (tap % 2) * 64 : (tap % 2) * 64 + 64]
    for dy in range(3):
        for dz in range(3):
            at = 448 + dy * 16 + dz * 4
            for dx in range(3):
                grad1[dx * 9 + dy * 3 + dz] = rows[at : at + 4, dx * 32 : dx * 32 + 32]
    biases = rows[496:504]
    shift1[...] = biases[1:2, 64:96]
    shift2[...] = biases[1:2, :64]
    place = lax.axis_index("gz")
    shift3[...] = roll(biases, lax.rem(128 - place * wide, 128), 1)[0:1, :wide]


def run_unpack(shared):
    wide = 128 // shared.shape[0]
    return pl.pallas_call(
        unpack_kernel,
        name="unpack",
        out_shape=(
            jax.ShapeDtypeStruct((27, 4, 32), F32),
            jax.ShapeDtypeStruct((27, 32, 64), F32),
            jax.ShapeDtypeStruct((1, 32), F32),
            jax.ShapeDtypeStruct((1, 64), F32),
            jax.ShapeDtypeStruct((1, wide), F32),
        ),
        in_specs=[VMEM],
        out_specs=(VMEM,) * 5,
        compiler_params=pltpu.CompilerParams(vmem_limit_bytes=LIMIT),
    )(shared)


def swap(to_far, to_near, axis):
    devices = lax.axis_size(axis)

    def pairs(first):
        forth = [(i, i + 1) for i in range(first, devices - 1, 2)]
        return forth + [(j, i) for i, j in forth]

    return lax.ppermute(to_far, axis, pairs(1)), lax.ppermute(to_near, axis, pairs(0))


def shards(universe, kernel1, bias1, kernel2, bias2, kernel3, bias3, cotangent):
    size_y, size_z = lax.axis_size("gy"), lax.axis_size("gz")
    wide = 128 // size_z

    tile = universe.transpose(1, 2, 0, 3).reshape(8, 32, 128)
    cot = lax.all_to_all(cotangent[:, 0].transpose(1, 0, 2), "gz", 0, 0, tiled=True).reshape(128, 16)
    far, near = swap(tile, tile, "gz")
    second = odd("gz") == 1
    lower, upper = jnp.where(second, near, far), jnp.where(second, far, near)
    strip = jnp.concatenate([lower[:, 4:], tile, upper[:, :28]], axis=1)
    strip, kernel1, kernel2, bias1, bias2, bias3 = lax.optimization_barrier(
        (strip, kernel1, kernel2, bias1, bias2, bias3)
    )
    far, near = swap(strip, strip, "gy")
    biases = jnp.stack([jnp.pad(bias1, (0, 96)), jnp.pad(bias2, (0, 64)), bias3])

    k1, k2 = kernel1.transpose(0, 2, 1).astype(F32), kernel2.transpose(0, 2, 1).astype(F32)
    k3 = kernel3.transpose(0, 2, 1)
    to_far, to_near, hidden2, own_cot, ratio2, patches1, turned_own, fields, w2, w1 = run_forward(
        near, strip, far, cot, k1, k2, biases
    )
    far, near = swap(to_far, to_near, "gz")
    to_far, to_near, lower, upper = run_weave(far, near, hidden2, own_cot)
    keep3, send3, shift3, w3, wide3, ratio1 = run_own(size_z, hidden2, own_cot, k3, biases, turned_own, w1)
    far, near = swap(to_far, to_near, "gy")
    keep, send = run_backward(
        size_z,
        far, lower, hidden2, upper, near, own_cot, w3, wide3, w2, ratio2, patches1, ratio1, fields,
        keep3, send3, shift3,
    )
    mates = [(i, i + 1 - 2 * (i % 2)) for i in range(size_z)]
    packed = run_pair(keep, lax.ppermute(send, "gz", mates))
    same = [list(range(parity, size_z, 2)) for parity in range(2)]
    packed = lax.all_to_all(packed, "gz", 0, 0, tiled=True, axis_index_groups=same)
    column, features = run_sum(packed, size_y)
    column = lax.all_to_all(column, "gy", 0, 0, tiled=True)
    shared = lax.all_to_all(run_share(column, size_z), "gz", 0, 0, tiled=True)
    grad3 = run_third(column, wide)
    grad1, grad2, shift1, shift2, shift3 = run_unpack(shared)
    return (
        features[:, None].astype(BF16), grad1.transpose(0, 2, 1), shift1[0], grad2.transpose(0, 2, 1), shift2[0], grad3, shift3[0]
    )


def solution(mesh):
    in_specs = (P(None, "gy", "gz", None), P(), P(), P(), P(), P(), P(), P("gz", "gy", None, None))
    out_specs = (P("gz", "gy", None, None), P(), P(), P(), P(), P(None, "gz", None), P("gz"))
    return jax.shard_map(shards, mesh=mesh, in_specs=in_specs, out_specs=out_specs, check_vma=False)
```

```python
import functools
import math

import jax
import jax.numpy as jnp
from jax import lax
from jax.experimental import pallas as pl
from jax.experimental.pallas import tpu as pltpu
from jax.sharding import PartitionSpec as P

F32 = jnp.float32
BF16 = jnp.bfloat16
SLOPE = 0.3
TWO_LOG2_E = 2.0 / math.log(2.0)
PAIRS = ((0, 1), (2, 3), (-3, -2), (4, 5), (-1, 6))
VMEM = pl.BlockSpec(memory_space=pltpu.VMEM)
LIMIT = 24 * 1024 * 1024


def dot(a, b):
    return jnp.dot(a, b, preferred_element_type=F32)


def dot_tn(a, b):
    return lax.dot_general(a, b, (((0,), (0,)), ((), ())), preferred_element_type=F32)


def dot_nt(a, b):
    return lax.dot_general(a, b, (((1,), (1,)), ((), ())), preferred_element_type=F32)


def lane(shape):
    return lax.broadcasted_iota(jnp.int32, shape, len(shape) - 1)


def exps(pre):
    scaled = pre * TWO_LOG2_E
    return jnp.exp2(jnp.maximum(scaled, SLOPE * scaled))


def pool1(e):
    total = e[:, :128] + e[:, 128:]
    total = total + roll(total, 64, 1)
    total = total + roll(total, 32, 1)
    return total * 0.125


def odd(axis):
    return lax.rem(lax.axis_index(axis), 2)


def sided(axis, far, near):
    flag = odd(axis).astype(F32)
    far, near = far.astype(F32), near.astype(F32)
    return (near * flag + far * (1.0 - flag)).astype(BF16), (far * flag + near * (1.0 - flag)).astype(BF16)


def rounded(value):
    return value.astype(BF16).astype(F32)


def roll(value, amount, axis):
    return pltpu.roll(value, amount, axis)


def down(value):
    rows = lax.broadcasted_iota(jnp.int32, value.shape, 0)
    return jnp.where(rows == 0, 0.0, roll(value, 1, 0))


def up(value):
    count = value.shape[0]
    rows = lax.broadcasted_iota(jnp.int32, value.shape, 0)
    return jnp.where(rows == count - 1, 0.0, roll(value, count - 1, 0))


def lay_pick(pick):
    for px in range(4):
        row = lax.broadcasted_iota(jnp.int32, (256, 128), 0)
        col = lax.broadcasted_iota(jnp.int32, (256, 128), 1)
        same = row // 128 == col // 64
        hit = (row % 128) == 2 * (col % 64) - 1 + px
        pick[:, px * 128 : px * 128 + 128] = jnp.where(same & hit, 1.0, 0.0).astype(BF16)


def lay_rows(rows, target):
    rows = rows.astype(F32)
    pieces = []
    for one, two in PAIRS:
        a, b = 8 * (one + 3), 8 * (two + 3)
        pieces.append(jnp.concatenate([rows[a : a + 16], rows[b : b + 16]], axis=1))
    target[...] = jnp.concatenate(pieces, axis=0).astype(BF16)


def select(block, pick):
    count = block.shape[0]
    out = dot(block.reshape(count * 80, 256), pick).astype(BF16).reshape(count, 5, 16, 512)
    return [
        jnp.concatenate(
            [
                jnp.concatenate([out[step, k, :, px * 128 : px * 128 + 128] for k in range(5)], axis=1)
                for px in range(4)
            ],
            axis=0,
        )
        for step in range(count)
    ]


def prepare_kernel(mid, k1, k2, w1, w2, pick, chosen, left):
    lay_weights1(k1, w1)
    lay_weights2(k2, w2)
    lay_pick(pick)
    for step in range(8):
        lay_rows(mid[step], left.at[step])
    for step, rows in enumerate(select(left[...], pick[...])):
        chosen[step] = rows


def run_prepare(*operands):
    return pl.pallas_call(
        prepare_kernel,
        name="prepare",
        out_shape=(
            jax.ShapeDtypeStruct((256, 256), BF16),
            jax.ShapeDtypeStruct((3, 512, 256), BF16),
            jax.ShapeDtypeStruct((256, 512), BF16),
            jax.ShapeDtypeStruct((8, 64, 640), BF16),
        ),
        in_specs=[VMEM] * 3,
        out_specs=(VMEM,) * 4,
        scratch_shapes=[pltpu.VMEM((8, 80, 256), BF16)],
        compiler_params=pltpu.CompilerParams(vmem_limit_bytes=LIMIT),
    )(*operands)


def forward_kernel(
    near, far, cot, w1, w2, pick, chosen, biases,
    to_far, to_near, hidden2, own_cot, ratio2, patches1, turned_own, fields,
    left, field, turned, pre1, first, spread, pre2, second,
):
    bias1 = jnp.concatenate([biases[0:1, :32]] * 8, axis=1)
    bias2 = jnp.concatenate([biases[1:2, :64]] * 4, axis=1)
    base_y, base_z = lax.axis_index("gy"), lax.axis_index("gz")
    size_y, size_z = lax.axis_size("gy"), lax.axis_size("gz")

    def inside(offset_y, offset_z, scale):
        row = base_y * (4 // scale) + offset_y
        col = base_z * (4 // scale) + offset_z
        ok_y = (row >= 0) & (row < size_y * (4 // scale))
        ok_z = (col >= 0) & (col < size_z * (4 // scale))
        return jnp.where(ok_y & ok_z, 1.0, 0.0)

    def lay_ends(step, carry):
        lay_rows(sided("gy", far[step + 1], near[step + 1])[0], left.at[step])
        lay_rows(sided("gy", far[step], near[step])[1], left.at[step + 7])
        return carry

    lax.fori_loop(0, 7, lay_ends, 0)
    for step in range(8):
        row = step + 7
        field[row // 2, row % 2 * 64 : row % 2 * 64 + 64] = chosen[step]
    for part in range(2):
        for step, rows in enumerate(select(left[7 * part : 7 * part + 7], pick[...])):
            row = step + 15 * part
            field[row // 2, row % 2 * 64 : row % 2 * 64 + 64] = rows
    for pair in range(11):
        turned[pair] = field[pair].T
    fields[...] = field[3:8, :, :256]
    first[:, :, 0:8] = jnp.zeros((10, 10, 8, 128), F32)
    first[:, :, 72:80] = jnp.zeros((10, 10, 8, 128), F32)

    def block1(step, carry):
        for part in range(2):
            stack = jnp.concatenate([turned[2 * step + part], turned[2 * step + part + 1]], axis=1)
            pre1[part] = dot(stack, w1[...])
        for part in range(2):
            yw = 2 * step + part
            for k, pair in enumerate(PAIRS):
                for h, zw in enumerate(pair):
                    at = k * 128 + h * 64
                    mean = pool1(exps(pre1[part, at : at + 64] + bias1))
                    pooled = rounded(jnp.log(mean) * 0.5)
                    first[yw, zw + 3, 8:72] = pooled * inside(yw - 3, zw, 1)
        return carry

    lax.fori_loop(0, 5, block1, 0)
    turned_own[...] = turned[3:8, :256]

    group1 = lane((32, 128)) // 32

    def frame(yi, carry):
        for zi in range(10):
            part = first[yi, zi, pl.ds(7, 32, stride=2), :]
            for px in range(1, 4):
                part = jnp.where(group1 == px, first[yi, zi, pl.ds(7 + px, 32, stride=2), :], part)
            spread[yi, zi] = part.astype(BF16)
        return carry

    lax.fori_loop(0, 10, frame, 0)
    patches1[...] = spread[2:8, 2:8]

    half = lane((16, 128)) < 64

    def block2(step, carry):
        for part in range(2):
            yp = 2 * step + part
            columns = []
            for zo in range(4):
                tiles = [spread[pl.ds(2 * yp + dy, 2), 2 * zo + pz] for dy in range(3) for pz in range(4)]
                columns.append(jnp.concatenate(tiles, axis=2)[:, None])
            block = jnp.concatenate(columns, axis=1).reshape(256, 1536)
            pre2[part] = dot(block, w2[...].reshape(1536, 256)).reshape(2, 4, 32, 256)
        for part in range(2):
            yp = 2 * step + part
            for zo in range(4):
                pre = pre2[part, :, zo] + bias2
                e = exps(pre)
                both = e[0] + e[1]
                total = both[:, :128] + both[:, 128:]
                total = total + roll(total, 64, 1)
                mean = total * 0.125
                ok = inside(yp - 1, zo - 1, 2)
                share = (0.125 * ok) / mean
                share = jnp.concatenate([share, share], axis=1)
                ratio2[pl.ds(2 * yp, 2), zo] = jnp.where(pre > 0, 1.0, SLOPE) * (e * share[None])
                second[part, zo] = rounded(jnp.log(mean) * 0.5) * ok
        for part in range(2):
            for zo in range(4):
                even = second[part, zo, pl.ds(0, 16, stride=2), :]
                odd = second[part, zo, pl.ds(1, 16, stride=2), :]
                hidden2[2 * step + part, zo] = jnp.where(half, even, odd).astype(BF16)
        return carry

    lax.fori_loop(0, 2, block2, 0)
    own = cot[...].astype(F32).T.astype(BF16)
    own_cot[...] = own
    side = odd("gz")
    to_far[:128] = hidden2[:, pl.ds(2 - 2 * side, 2)].reshape(128, 128)
    to_near[:128] = hidden2[:, pl.ds(2 * side, 2)].reshape(128, 128)
    to_far[128:144] = own
    to_near[128:144] = own


def lay_weights1(taps, out):
    group = lane((16, 128)) // 32
    zero = jnp.zeros((16, 128), F32)
    wide = []
    for k in range(9):
        pieces = [taps[3 * k + dz].astype(F32) for dz in range(3)] + [jnp.zeros((4, 32), F32)]
        rows = jnp.concatenate(pieces, axis=0)
        wide.append(jnp.concatenate([rows] * 4, axis=1))
    for py in range(4):
        for px in range(4):
            at = (py * 4 + px) * 16
            for qy in range(2):
                dy = py - qy
                sides = [
                    wide[(px - qx) * 3 + dy] if 0 <= dy < 3 and 0 <= px - qx < 3 else zero for qx in range(2)
                ]
                value = jnp.where(group == 0, sides[0], sides[1])
                shifted = jnp.where(group == 2, roll(sides[0], 4, 0), roll(sides[1], 4, 0))
                out[at : at + 16, qy * 128 : qy * 128 + 128] = jnp.where(group < 2, value, shifted).astype(BF16)


def lay_weights2(taps, out):
    zero = jnp.zeros((32, 64), F32)
    for dy in range(3):
        out[dy, 384:512, 0:128] = jnp.zeros((128, 128), BF16)
        out[dy, 0:128, 128:256] = jnp.zeros((128, 128), BF16)
        for dz in range(3):
            for px in range(4):
                sides = [taps[(px - qx) * 9 + dy * 3 + dz] if 0 <= px - qx < 3 else zero for qx in range(2)]
                tile = jnp.concatenate(sides, axis=1).astype(BF16)
                for qz in range(2):
                    at = (dz + qz) * 128 + px * 32
                    out[dy, at : at + 32, qz * 128 : qz * 128 + 128] = tile


def lay_weights3(taps, out):
    zero = jnp.zeros((64, 128), BF16)
    for tap in range(9):
        out[tap, 192:256, 0:128] = zero
        out[tap, 0:64, 128:256] = zero
        for dx in range(3):
            value = taps[dx * 9 + tap]
            out[tap, dx * 64 : dx * 64 + 64, 0:128] = value
            out[tap, dx * 64 + 64 : dx * 64 + 128, 128:256] = value


def run_forward(*operands):
    return pl.pallas_call(
        forward_kernel,
        name="forward",
        out_shape=(
            jax.ShapeDtypeStruct((144, 128), BF16),
            jax.ShapeDtypeStruct((144, 128), BF16),
            jax.ShapeDtypeStruct((4, 4, 16, 128), BF16),
            jax.ShapeDtypeStruct((16, 128), BF16),
            jax.ShapeDtypeStruct((8, 4, 32, 256), F32),
            jax.ShapeDtypeStruct((6, 6, 32, 128), BF16),
            jax.ShapeDtypeStruct((5, 256, 128), BF16),
            jax.ShapeDtypeStruct((5, 128, 256), BF16),
        ),
        in_specs=[VMEM] * len(operands),
        out_specs=(VMEM,) * 8,
        cost_estimate=pl.CostEstimate(flops=5000000000, bytes_accessed=8000000, transcendentals=8000000),
        scratch_shapes=[
            pltpu.VMEM((14, 80, 256), BF16),
            pltpu.VMEM((11, 128, 640), BF16),
            pltpu.VMEM((11, 640, 128), BF16),
            pltpu.VMEM((2, 640, 256), F32),
            pltpu.VMEM((10, 10, 80, 128), F32),
            pltpu.VMEM((10, 10, 32, 128), BF16),
            pltpu.VMEM((2, 2, 4, 32, 256), F32),
            pltpu.VMEM((2, 4, 32, 128), F32),
        ],
        compiler_params=pltpu.CompilerParams(vmem_limit_bytes=LIMIT),
    )(*operands)


def weave_kernel(far, near, hidden2, own_cot, to_far, to_near, lower, upper):
    lower[...], upper[...] = sided("gz", far[...], near[...])
    side = odd("gy")
    for target, first_row in ((to_far, 2 - 2 * side), (to_near, 2 * side)):
        for y in range(2):
            row, at = first_row + y, y * 128
            rows = pl.ds(pl.multiple_of(row * 32, 32), 32)
            target[at : at + 32] = lower[rows]
            target[at + 32 : at + 96] = hidden2[row].reshape(64, 128)
            target[at + 96 : at + 128] = upper[rows]
        target[256:272] = lower[128:144]
        target[272:288] = own_cot[...]
        target[288:304] = upper[128:144]


def run_weave(*operands):
    return pl.pallas_call(
        weave_kernel,
        name="weave",
        out_shape=(jax.ShapeDtypeStruct((304, 128), BF16),) * 2 + (jax.ShapeDtypeStruct((144, 128), BF16),) * 2,
        in_specs=[VMEM] * 4,
        out_specs=(VMEM,) * 4,
        compiler_params=pltpu.CompilerParams(vmem_limit_bytes=LIMIT),
    )(*operands)


def lay_patches2(rows, target):
    half = lane((16, 128)) < 64
    swapped = roll(rows.astype(F32), 64, 1)
    target[...] = jnp.concatenate(
        [jnp.where(half, down(swapped), swapped), jnp.where(half, swapped, up(swapped))], axis=1
    ).astype(BF16)


def pool3(pre, cot):
    e = exps(pre)
    total = e[0, 0] + e[0, 1] + e[1, 0] + e[1, 1]
    total = total[:, :128] + total[:, 128:]
    mean = total * 0.125
    share = cot.astype(F32) * (0.125 / mean)
    share = jnp.concatenate([share, share], axis=1)
    return mean, (jnp.where(pre > 0, 1.0, SLOPE) * (e * share)).astype(BF16)


def own_kernel(
    hidden2, own_cot, k3, biases, turned_own, w1, keep, send, shift3, w3, wide3, ratio1, patches2, pre3, turned
):
    groups = 2 * keep.shape[0]
    wide = 128 // groups
    bias1 = jnp.concatenate([biases[0:1, :32]] * 8, axis=1)
    for yw in range(4):
        stack = jnp.concatenate([turned_own[yw], turned_own[yw + 1]], axis=1)
        ratio1[yw] = dot(stack, w1[...])
    for yw in range(4):
        for at in range(0, 256, 64):
            pre = ratio1[yw, at : at + 64] + bias1
            e = exps(pre)
            share = 0.125 / pool1(e)
            share = jnp.concatenate([share, share], axis=1)
            ratio1[yw, at : at + 64] = jnp.where(pre > 0, 1.0, SLOPE) * (e * share)
    lay_weights3(k3, w3)
    wide3[...] = jnp.concatenate([biases[2:3]] * 2, axis=1)
    for y in range(4):
        for z in range(4):
            lay_patches2(hidden2[y, z], patches2.at[y, z])
    for tap in range(9):
        dy, dz = tap // 3, tap % 3
        block = patches2[dy : dy + 2, dz : dz + 2].reshape(64, 256)
        term = dot(block, w3[tap])
        pre3[...] = term + wide3[...] if tap == 0 else pre3[...] + term
    mean, delta = pool3(pre3[...].reshape(2, 2, 16, 256), own_cot[...])
    features = rounded(jnp.log(mean) * 0.5)
    own3 = delta.reshape(64, 256)
    bias3 = own3.astype(F32).sum(axis=0, keepdims=True)
    shift3[...] = bias3[:, :128] + bias3[:, 128:]
    low, high = [], []
    for tap in range(9):
        dy, dz = tap // 3, tap % 3
        block = patches2[dy : dy + 2, dz : dz + 2].reshape(64, 256)
        full = dot_tn(own3, block)
        one = full[:128]
        low_lanes, high_lanes = roll(full[128:, :128], 64, 1), roll(full[128:, 128:], 64, 1)
        tile0 = jnp.where(lane((128, 128)) < 64, low_lanes, high_lanes)
        tile1 = high_lanes
        low.append(one[:, :128] + tile0)
        high.append(one[:, 128:] + tile1)
    first_half = lane((128, 128)) < 64
    paired = []
    for m in range(5):
        other = roll(high[2 * m + 1], 64, 1) if 2 * m + 1 < 9 else jnp.zeros((128, 128), F32)
        paired.append(jnp.where(first_half, high[2 * m], other))
    kernel3 = [piece.reshape(groups, wide, 128) for piece in low + paired]

    turned[...] = jnp.concatenate([features, jnp.zeros((112, 128), F32)], axis=0).T
    feature_rows = turned[pl.ds(0, 16, stride=8), :]
    for c in range(1, 8):
        feature_rows = feature_rows + roll(turned[pl.ds(c, 16, stride=8), :], 16 * c, 1)
    feature_rows = feature_rows.reshape(groups, wide // 8, 128)
    flag = odd("gz").astype(F32)
    fill = jnp.zeros((groups, keep.shape[1] - 14 * wide - wide // 4, 128), F32)
    pieces = kernel3 + [feature_rows * (1.0 - flag), feature_rows * flag, fill]
    keep[...], send[...] = halves(jnp.concatenate(pieces, axis=1))


def halves(value):
    flag = odd("gz").astype(F32)
    pairs = value.reshape((value.shape[0] // 2, 2) + value.shape[1:])
    even, other = pairs[:, 0], pairs[:, 1]
    return (even * (1.0 - flag) + other * flag).astype(BF16), (even * flag + other * (1.0 - flag)).astype(BF16)


def run_own(groups, *operands):
    wide = 128 // groups
    return pl.pallas_call(
        own_kernel,
        name="own",
        out_shape=(
            jax.ShapeDtypeStruct((groups // 2, -(-(14 * wide + wide // 4) // 8) * 8, 128), BF16),
            jax.ShapeDtypeStruct((groups // 2, -(-(14 * wide + wide // 4) // 8) * 8, 128), BF16),
            jax.ShapeDtypeStruct((1, 128), F32),
            jax.ShapeDtypeStruct((9, 256, 256), BF16),
            jax.ShapeDtypeStruct((1, 256), F32),
            jax.ShapeDtypeStruct((4, 256, 256), F32),
        ),
        in_specs=[VMEM] * len(operands),
        out_specs=(VMEM,) * 6,
        scratch_shapes=[
            pltpu.VMEM((4, 4, 16, 256), BF16),
            pltpu.VMEM((64, 256), F32),
            pltpu.VMEM((128, 128), F32),
        ],
        compiler_params=pltpu.CompilerParams(vmem_limit_bytes=LIMIT),
        cost_estimate=pl.CostEstimate(flops=150000000, bytes_accessed=4000000, transcendentals=20000),
    )(*operands)


def backward_kernel(
    far, lower, middle, upper, near, own_cot, w3, bias3, w2, ratio2, patches1, ratio1, fields, keep3, send3, shift3,
    keep, send, before, after, patches2, pre3, delta3, patch2, grad2, delta2, patch1, beside, grad1, delta1,
):
    before[...], after[...] = sided("gy", far[...], near[...])
    groups = 2 * keep.shape[0]
    half = lane((16, 128)) < 64

    def lay(y, source):
        for z in range(8):
            lay_patches2(source(z), patches2.at[y, z])

    for y in range(2):
        lay(y, lambda z: before[(y * 8 + z) * 16 : (y * 8 + z + 1) * 16])
        lay(y + 6, lambda z: after[(y * 8 + z) * 16 : (y * 8 + z + 1) * 16])

    def pick_middle(y, z):
        if z < 2:
            return lower[(y * 2 + z) * 16 : (y * 2 + z + 1) * 16]
        if z < 6:
            return middle[y, z - 2]
        return upper[(y * 2 + z - 6) * 16 : (y * 2 + z - 5) * 16]

    for y in range(4):
        lay(y + 2, functools.partial(pick_middle, y))

    for dy in range(3):
        blocks = [patches2[dy : dy + 6, dz : dz + 6].reshape(576, 256) for dz in range(3)]
        weights = w3[3 * dy : 3 * dy + 3].reshape(768, 256)
        term = dot(jnp.concatenate(blocks, axis=1), weights).reshape(6, 6, 16, 256)
        pre3[...] = term + bias3[...] if dy == 0 else pre3[...] + term

    for wy in range(3):
        for wz in range(3):
            pre = pre3[2 * wy : 2 * wy + 2, 2 * wz : 2 * wz + 2]
            if wy == 1:
                cot = own_cot[...] if wz == 1 else (lower if wz == 0 else upper)[128:144]
            else:
                cot = (before if wy == 0 else after)[256 + wz * 16 : 272 + wz * 16]
            delta3[2 * wy : 2 * wy + 2, 2 * wz : 2 * wz + 2] = pool3(pre, cot)[1]

    for dy in range(3):
        blocks = [delta3[2 - dy : 6 - dy, 2 - dz : 6 - dz].reshape(256, 256) for dz in range(3)]
        weights = jnp.concatenate([w3[3 * dy + dz] for dz in range(3)], axis=1)
        term = dot_nt(jnp.concatenate(blocks, axis=1), weights).reshape(4, 4, 16, 256)
        patch2[...] = term if dy == 0 else patch2[...] + term

    for y in range(4):
        for z in range(4):
            a, b = patch2[y, z, :, :128], patch2[y, z, :, 128:]
            x = rounded(jnp.where(half, b + up(a), a + down(b)))
            swapped = roll(x, 64, 1)
            grad2[y, z, pl.ds(0, 16, stride=2), :] = jnp.where(half, swapped, x)
            grad2[y, z, pl.ds(1, 16, stride=2), :] = jnp.where(half, x, swapped)

    for y in range(6):
        value = grad2[(y + 1) // 2]
        value = jnp.concatenate([value, value], axis=2)
        delta2[y] = (value * ratio2[y + 1]).astype(BF16)

    own2 = delta2[1:5, 1:3].reshape(256, 256)
    bias2 = own2.astype(F32).sum(axis=0, keepdims=True)
    bias2 = bias2[:, :128] + bias2[:, 128:]
    bias2 = bias2 + roll(bias2, 64, 1)
    taps = [None] * 27
    for dy in range(3):
        block = jnp.concatenate(
            [
                jnp.concatenate([patches1[dy : dy + 4, 2 * zo + pz] for pz in range(4)], axis=2)[:, None]
                for zo in range(2)
            ],
            axis=1,
        ).reshape(256, 512)
        full = dot_tn(block, own2)
        for dz in range(3):
            rows = full[dz * 128 : dz * 128 + 128, :128] + full[dz * 128 + 128 : dz * 128 + 256, 128:]
            for dx in range(3):
                taps[dx * 9 + dy * 3 + dz] = rows[dx * 32 : dx * 32 + 32] + roll(
                    rows[dx * 32 + 32 : dx * 32 + 64], 64, 1
                )
    def g1(columns, lanes, rows):
        blocks = [delta2[2 - dy : 6 - dy, columns, :, lanes].reshape(-1, lanes.stop - lanes.start) for dy in range(3)]
        weights = jnp.concatenate([w2[dy, rows, lanes] for dy in range(3)], axis=1)
        return dot_nt(jnp.concatenate(blocks, axis=1), weights)

    patch1[...] = g1(slice(1, 3), slice(0, 256), slice(0, 512)).reshape(4, 2, 32, 512)
    below = g1(slice(0, 1), slice(128, 256), slice(384, 512)).reshape(4, 32, 128)
    above = g1(slice(3, 4), slice(0, 128), slice(0, 128)).reshape(4, 32, 128)
    beside[0] = below
    beside[1] = above

    low_half = lane((32, 128)) < 64
    group = lane((32, 128)) // 32

    def widen(value, which):
        value = jnp.where(group == which, value, 0.0)
        value = value + roll(value, 32, 1)
        return value + roll(value, 64, 1)


    for y in range(4):
        def part(zo, pz):
            return patch1[y, zo, :, pz * 128 : pz * 128 + 128]

        sums = (
            beside[0, y] + part(0, 1), part(0, 2) + part(1, 0), part(0, 3) + part(1, 1), part(1, 2) + beside[1, y],
        )
        for z, value in enumerate(sums):
            value = rounded(value + roll(jnp.where(low_half, up(value), down(value)), 64, 1))
            grad1[y, z, pl.ds(0, 32, stride=2), :] = widen(value, 1)
            grad1[y, z, pl.ds(1, 32, stride=2), :] = widen(value, 2)
        value = grad1[y].reshape(256, 128)
        value = jnp.concatenate([value, value], axis=1)
        delta1[y] = (value * ratio1[y]).astype(BF16)

    bias1 = delta1[...].astype(F32).sum(axis=0).sum(axis=0, keepdims=True)
    bias1 = bias1[:, :128] + bias1[:, 128:]
    bias1 = bias1 + roll(bias1, 64, 1)
    bias1 = bias1 + roll(bias1, 32, 1)
    full = None
    for yw in range(4):
        term = dot(fields[yw : yw + 2].reshape(256, 256), delta1[yw])
        full = term if full is None else full + term
    full = full.reshape(4, 4, 16, 256)
    kernel1 = []
    group1 = lane((16, 128)) // 32
    for dy in range(3):
        rows = full[dy, :, :, :128] + full[dy + 1, :, :, 128:]
        pieces = []
        for dx in range(3):
            value = rows[dx] + roll(rows[dx + 1], 96, 1)
            value = value + roll(roll(value, 12, 0), 64, 1)
            pieces.append(roll(value, 32 * dx, 1) if dx else value)
        kernel1.append(jnp.where(group1 == 0, pieces[0], jnp.where(group1 == 1, pieces[1], pieces[2])))

    low_lane = lane((32, 128)) < 64
    kernel2 = [
        jnp.where(low_lane, taps[2 * m], roll(taps[2 * m + 1], 64, 1) if 2 * m + 1 < 27 else 0.0)
        for m in range(14)
    ]
    shifts = jnp.concatenate(
        [shift3[...], jnp.where(lane((1, 128)) < 64, bias2, bias1), jnp.zeros((14, 128), F32)], axis=0
    )
    shared = jnp.concatenate(kernel2 + kernel1 + [shifts], axis=0)
    rows = 512 // groups
    keep[:, :rows], send[:, :rows] = halves(shared.reshape(groups, rows, 128))
    keep[:, rows:] = keep3[...]
    send[:, rows:] = send3[...]


def run_backward(groups, *operands):
    return pl.pallas_call(
        backward_kernel,
        name="backward",
        out_shape=(jax.ShapeDtypeStruct((groups // 2, 512 // groups + operands[-2].shape[1], 128), BF16),) * 2,
        in_specs=[VMEM] * len(operands),
        out_specs=(VMEM, VMEM),
        scratch_shapes=[
            pltpu.VMEM((304, 128), BF16),
            pltpu.VMEM((304, 128), BF16),
            pltpu.VMEM((8, 8, 16, 256), BF16),
            pltpu.VMEM((6, 6, 16, 256), F32),
            pltpu.VMEM((6, 6, 16, 256), BF16),
            pltpu.VMEM((4, 4, 16, 256), F32),
            pltpu.VMEM((4, 4, 32, 128), F32),
            pltpu.VMEM((6, 4, 32, 256), BF16),
            pltpu.VMEM((4, 2, 32, 512), F32),
            pltpu.VMEM((2, 4, 32, 128), F32),
            pltpu.VMEM((4, 4, 64, 128), F32),
            pltpu.VMEM((4, 256, 256), BF16),
        ],
        compiler_params=pltpu.CompilerParams(vmem_limit_bytes=LIMIT),
    )(*operands)


def pair_kernel(kept, received, total):
    total[...] = (kept[...].astype(F32) + received[...].astype(F32)).astype(BF16)


def run_pair(kept, received):
    return pl.pallas_call(
        pair_kernel,
        name="pair",
        out_shape=jax.ShapeDtypeStruct(kept.shape, BF16),
        in_specs=[VMEM] * 2,
        out_specs=VMEM,
        compiler_params=pltpu.CompilerParams(vmem_limit_bytes=LIMIT),
    )(kept, received)


def sum_kernel(received, to_column, features):
    half, rows = received.shape[0], to_column.shape[1]
    wide = 64 // half
    high = wide // 8
    own = received[:, rows : rows + 2 * high].astype(F32)
    for c in range(wide):
        for parity in range(2):
            line = own[:, parity * high + c // 8, (c % 8) * 16 : (c % 8) * 16 + 16]
            for j in range(half):
                features[c, 2 * j + parity : 2 * j + parity + 1] = line[j : j + 1]
    total = received[:, :rows].astype(F32).sum(axis=0)
    to_column[...] = jnp.broadcast_to(total[None], to_column.shape).astype(BF16)


def run_sum(received, rows_y):
    groups = 2 * received.shape[0]
    wide = 128 // groups
    return pl.pallas_call(
        sum_kernel,
        name="sum",
        out_shape=(
            jax.ShapeDtypeStruct((rows_y, 512 // groups + 14 * wide, 128), BF16),
            jax.ShapeDtypeStruct((wide, groups, 16), F32),
        ),
        in_specs=[VMEM],
        out_specs=(VMEM, VMEM),
        compiler_params=pltpu.CompilerParams(vmem_limit_bytes=LIMIT),
    )(received)


def share_kernel(column, to_all):
    total = column[:, : to_all.shape[1]].astype(F32).sum(axis=0)
    to_all[...] = jnp.broadcast_to(total[None], to_all.shape).astype(BF16)


def run_share(column, groups):
    return pl.pallas_call(
        share_kernel,
        name="share",
        out_shape=jax.ShapeDtypeStruct((groups, 512 // groups, 128), BF16),
        in_specs=[VMEM],
        out_specs=VMEM,
        compiler_params=pltpu.CompilerParams(vmem_limit_bytes=LIMIT),
    )(column)


def third_kernel(column, grad3):
    wide = grad3.shape[1]
    first = column.shape[1] - 14 * wide
    lines = column[:, first:].astype(F32).sum(axis=0)
    for tap in range(9):
        low = lines[tap * wide : tap * wide + wide]
        grad3[tap] = low[:, :64]
        grad3[9 + tap] = low[:, 64:]
        at = (9 + tap // 2) * wide
        grad3[18 + tap] = lines[at : at + wide][:, (tap % 2) * 64 : (tap % 2) * 64 + 64]


def run_third(column, wide):
    return pl.pallas_call(
        third_kernel,
        name="third",
        out_shape=jax.ShapeDtypeStruct((27, wide, 64), F32),
        in_specs=[VMEM],
        out_specs=VMEM,
        compiler_params=pltpu.CompilerParams(vmem_limit_bytes=LIMIT),
    )(column)


def unpack_kernel(shared, grad1, grad2, shift1, shift2, shift3):
    wide = shift3.shape[1]
    rows = shared[...].astype(F32).reshape(512, 128)
    for tap in range(27):
        at = (tap // 2) * 32
        grad2[tap] = rows[at : at + 32, (tap % 2) * 64 : (tap % 2) * 64 + 64]
    for dy in range(3):
        for dz in range(3):
            at = 448 + dy * 16 + dz * 4
            for dx in range(3):
                grad1[dx * 9 + dy * 3 + dz] = rows[at : at + 4, dx * 32 : dx * 32 + 32]
    biases = rows[496:504]
    shift1[...] = biases[1:2, 64:96]
    shift2[...] = biases[1:2, :64]
    place = lax.axis_index("gz")
    shift3[...] = roll(biases, lax.rem(128 - place * wide, 128), 1)[0:1, :wide]


def run_unpack(shared):
    wide = 128 // shared.shape[0]
    return pl.pallas_call(
        unpack_kernel,
        name="unpack",
        out_shape=(
            jax.ShapeDtypeStruct((27, 4, 32), F32),
            jax.ShapeDtypeStruct((27, 32, 64), F32),
            jax.ShapeDtypeStruct((1, 32), F32),
            jax.ShapeDtypeStruct((1, 64), F32),
            jax.ShapeDtypeStruct((1, wide), F32),
        ),
        in_specs=[VMEM],
        out_specs=(VMEM,) * 5,
        compiler_params=pltpu.CompilerParams(vmem_limit_bytes=LIMIT),
    )(shared)


def swap(to_far, to_near, axis):
    devices = lax.axis_size(axis)

    def pairs(first):
        forth = [(i, i + 1) for i in range(first, devices - 1, 2)]
        return forth + [(j, i) for i, j in forth]

    return lax.ppermute(to_far, axis, pairs(1)), lax.ppermute(to_near, axis, pairs(0))


def shards(universe, kernel1, bias1, kernel2, bias2, kernel3, bias3, cotangent):
    size_y, size_z = lax.axis_size("gy"), lax.axis_size("gz")
    wide = 128 // size_z

    tile = universe.transpose(1, 2, 0, 3).reshape(8, 32, 128)
    cot = lax.all_to_all(cotangent[:, 0].transpose(1, 0, 2), "gz", 0, 0, tiled=True).reshape(128, 16)
    far, near = swap(tile, tile, "gz")
    second = odd("gz") == 1
    lower, upper = jnp.where(second, near, far), jnp.where(second, far, near)
    strip = jnp.concatenate([lower[:, 4:], tile, upper[:, :28]], axis=1)
    strip, kernel1, kernel2, bias1, bias2, bias3 = lax.optimization_barrier(
        (strip, kernel1, kernel2, bias1, bias2, bias3)
    )
    far, near = swap(strip, strip, "gy")
    biases = jnp.stack([jnp.pad(bias1, (0, 96)), jnp.pad(bias2, (0, 64)), bias3])

    k1, k2 = kernel1.transpose(0, 2, 1).astype(F32), kernel2.transpose(0, 2, 1).astype(F32)
    k3 = kernel3.transpose(0, 2, 1)
    w1, w2, pick, chosen = run_prepare(strip, k1, k2)
    to_far, to_near, hidden2, own_cot, ratio2, patches1, turned_own, fields = run_forward(
        near, far, cot, w1, w2, pick, chosen, biases
    )
    far, near = swap(to_far, to_near, "gz")
    to_far, to_near, lower, upper = run_weave(far, near, hidden2, own_cot)
    keep3, send3, shift3, w3, wide3, ratio1 = run_own(size_z, hidden2, own_cot, k3, biases, turned_own, w1)
    far, near = swap(to_far, to_near, "gy")
    keep, send = run_backward(
        size_z,
        far, lower, hidden2, upper, near, own_cot, w3, wide3, w2, ratio2, patches1, ratio1, fields,
        keep3, send3, shift3,
    )
    mates = [(i, i + 1 - 2 * (i % 2)) for i in range(size_z)]
    packed = run_pair(keep, lax.ppermute(send, "gz", mates))
    same = [list(range(parity, size_z, 2)) for parity in range(2)]
    packed = lax.all_to_all(packed, "gz", 0, 0, tiled=True, axis_index_groups=same)
    column, features = run_sum(packed, size_y)
    column = lax.all_to_all(column, "gy", 0, 0, tiled=True)
    shared = lax.all_to_all(run_share(column, size_z), "gz", 0, 0, tiled=True)
    grad3 = run_third(column, wide)
    grad1, grad2, shift1, shift2, shift3 = run_unpack(shared)
    return (
        features[:, None].astype(BF16), grad1.transpose(0, 2, 1), shift1[0], grad2.transpose(0, 2, 1), shift2[0], grad3, shift3[0]
    )


def solution(mesh):
    in_specs = (P(None, "gy", "gz", None), P(), P(), P(), P(), P(), P(), P("gz", "gy", None, None))
    out_specs = (P("gz", "gy", None, None), P(), P(), P(), P(), P(None, "gz", None), P("gz"))
    return jax.shard_map(shards, mesh=mesh, in_specs=in_specs, out_specs=out_specs, check_vma=False)
```

```python
import functools
import math

import jax
import jax.numpy as jnp
from jax import lax
from jax.experimental import pallas as pl
from jax.experimental.pallas import tpu as pltpu
from jax.sharding import PartitionSpec as P

F32 = jnp.float32
BF16 = jnp.bfloat16
SLOPE = 0.3
TWO_LOG2_E = 2.0 / math.log(2.0)
PAIRS = ((0, 1), (2, 3), (-3, -2), (4, 5), (-1, 6))
VMEM = pl.BlockSpec(memory_space=pltpu.VMEM)
LIMIT = 24 * 1024 * 1024


def dot(a, b):
    return jnp.dot(a, b, preferred_element_type=F32)


def dot_tn(a, b):
    return lax.dot_general(a, b, (((0,), (0,)), ((), ())), preferred_element_type=F32)


def dot_nt(a, b):
    return lax.dot_general(a, b, (((1,), (1,)), ((), ())), preferred_element_type=F32)


def lane(shape):
    return lax.broadcasted_iota(jnp.int32, shape, len(shape) - 1)


def exps(pre):
    scaled = pre * TWO_LOG2_E
    return jnp.exp2(jnp.maximum(scaled, SLOPE * scaled))


def pool1(e):
    total = e[:, :128] + e[:, 128:]
    total = total + roll(total, 64, 1)
    total = total + roll(total, 32, 1)
    return total * 0.125


def odd(axis):
    return lax.rem(lax.axis_index(axis), 2)


def sided(axis, far, near):
    flag = odd(axis).astype(F32)
    far, near = far.astype(F32), near.astype(F32)
    return (near * flag + far * (1.0 - flag)).astype(BF16), (far * flag + near * (1.0 - flag)).astype(BF16)


def rounded(value):
    return value.astype(BF16).astype(F32)


def roll(value, amount, axis):
    return pltpu.roll(value, amount, axis)


def down(value):
    rows = lax.broadcasted_iota(jnp.int32, value.shape, 0)
    return jnp.where(rows == 0, 0.0, roll(value, 1, 0))


def up(value):
    count = value.shape[0]
    rows = lax.broadcasted_iota(jnp.int32, value.shape, 0)
    return jnp.where(rows == count - 1, 0.0, roll(value, count - 1, 0))


def lay_pick(pick):
    for px in range(4):
        row = lax.broadcasted_iota(jnp.int32, (256, 128), 0)
        col = lax.broadcasted_iota(jnp.int32, (256, 128), 1)
        same = row // 128 == col // 64
        hit = (row % 128) == 2 * (col % 64) - 1 + px
        pick[:, px * 128 : px * 128 + 128] = jnp.where(same & hit, 1.0, 0.0).astype(BF16)


def lay_rows(rows, target):
    rows = rows.astype(F32)
    pieces = []
    for one, two in PAIRS:
        a, b = 8 * (one + 3), 8 * (two + 3)
        pieces.append(jnp.concatenate([rows[a : a + 16], rows[b : b + 16]], axis=1))
    target[...] = jnp.concatenate(pieces, axis=0).astype(BF16)


def select(block, pick):
    count = block.shape[0]
    out = dot(block.reshape(count * 80, 256), pick).astype(BF16).reshape(count, 5, 16, 512)
    return [
        jnp.concatenate(
            [
                jnp.concatenate([out[step, k, :, px * 128 : px * 128 + 128] for k in range(5)], axis=1)
                for px in range(4)
            ],
            axis=0,
        )
        for step in range(count)
    ]


def prepare_kernel(mid, k1, k2, w1, w2, pick, chosen, left):
    lay_weights1(k1, w1)
    lay_weights2(k2, w2)
    lay_pick(pick)
    for step in range(8):
        lay_rows(mid[step], left.at[step])
    for step, rows in enumerate(select(left[...], pick[...])):
        chosen[step] = rows


def run_prepare(*operands):
    return pl.pallas_call(
        prepare_kernel,
        name="prepare",
        out_shape=(
            jax.ShapeDtypeStruct((256, 256), BF16),
            jax.ShapeDtypeStruct((3, 512, 256), BF16),
            jax.ShapeDtypeStruct((256, 512), BF16),
            jax.ShapeDtypeStruct((8, 64, 640), BF16),
        ),
        in_specs=[VMEM] * 3,
        out_specs=(VMEM,) * 4,
        scratch_shapes=[pltpu.VMEM((8, 80, 256), BF16)],
        compiler_params=pltpu.CompilerParams(vmem_limit_bytes=LIMIT),
    )(*operands)


def forward_kernel(
    near, far, cot, w1, w2, pick, chosen, biases,
    to_far, to_near, hidden2, own_cot, ratio2, patches1, turned_own, fields,
    left, field, turned, pre1, first, spread, pre2, second,
):
    bias1 = jnp.concatenate([biases[0:1, :32]] * 8, axis=1)
    bias2 = jnp.concatenate([biases[1:2, :64]] * 4, axis=1)
    base_y, base_z = lax.axis_index("gy"), lax.axis_index("gz")
    size_y, size_z = lax.axis_size("gy"), lax.axis_size("gz")

    def inside(offset_y, offset_z, scale):
        row = base_y * (4 // scale) + offset_y
        col = base_z * (4 // scale) + offset_z
        ok_y = (row >= 0) & (row < size_y * (4 // scale))
        ok_z = (col >= 0) & (col < size_z * (4 // scale))
        return jnp.where(ok_y & ok_z, 1.0, 0.0)

    def lay_ends(step, carry):
        lay_rows(sided("gy", far[step + 1], near[step + 1])[0], left.at[step])
        lay_rows(sided("gy", far[step], near[step])[1], left.at[step + 7])
        return carry

    lax.fori_loop(0, 7, lay_ends, 0)
    for step in range(8):
        row = step + 7
        field[row // 2, row % 2 * 64 : row % 2 * 64 + 64] = chosen[step]
    for part in range(2):
        for step, rows in enumerate(select(left[7 * part : 7 * part + 7], pick[...])):
            row = step + 15 * part
            field[row // 2, row % 2 * 64 : row % 2 * 64 + 64] = rows
    for pair in range(11):
        turned[pair] = field[pair].T
    fields[...] = field[3:8, :, :256]
    first[:, :, 0:8] = jnp.zeros((10, 10, 8, 128), F32)
    first[:, :, 72:80] = jnp.zeros((10, 10, 8, 128), F32)

    def block1(step, carry):
        for part in range(2):
            stack = jnp.concatenate([turned[2 * step + part], turned[2 * step + part + 1]], axis=1)
            pre1[part] = dot(stack, w1[...])
        for part in range(2):
            yw = 2 * step + part
            for k, pair in enumerate(PAIRS):
                for h, zw in enumerate(pair):
                    at = k * 128 + h * 64
                    mean = pool1(exps(pre1[part, at : at + 64] + bias1))
                    pooled = rounded(jnp.log(mean) * 0.5)
                    first[yw, zw + 3, 8:72] = pooled * inside(yw - 3, zw, 1)
        return carry

    lax.fori_loop(0, 5, block1, 0)
    turned_own[...] = turned[3:8, :256]

    group1 = lane((32, 128)) // 32

    def frame(yi, carry):
        for zi in range(10):
            part = first[yi, zi, pl.ds(7, 32, stride=2), :]
            for px in range(1, 4):
                part = jnp.where(group1 == px, first[yi, zi, pl.ds(7 + px, 32, stride=2), :], part)
            spread[yi, zi] = part.astype(BF16)
        return carry

    lax.fori_loop(0, 10, frame, 0)
    patches1[...] = spread[2:8, 2:8]

    half = lane((16, 128)) < 64

    def block2(step, carry):
        for part in range(2):
            yp = 2 * step + part
            columns = []
            for zo in range(4):
                tiles = [spread[pl.ds(2 * yp + dy, 2), 2 * zo + pz] for dy in range(3) for pz in range(4)]
                columns.append(jnp.concatenate(tiles, axis=2)[:, None])
            block = jnp.concatenate(columns, axis=1).reshape(256, 1536)
            pre2[part] = dot(block, w2[...].reshape(1536, 256)).reshape(2, 4, 32, 256)
        for part in range(2):
            yp = 2 * step + part
            for zo in range(4):
                pre = pre2[part, :, zo] + bias2
                e = exps(pre)
                both = e[0] + e[1]
                total = both[:, :128] + both[:, 128:]
                total = total + roll(total, 64, 1)
                mean = total * 0.125
                ok = inside(yp - 1, zo - 1, 2)
                share = (0.125 * ok) / mean
                share = jnp.concatenate([share, share], axis=1)
                ratio2[pl.ds(2 * yp, 2), zo] = jnp.where(pre > 0, 1.0, SLOPE) * (e * share[None])
                second[part, zo] = rounded(jnp.log(mean) * 0.5) * ok
        for part in range(2):
            for zo in range(4):
                even = second[part, zo, pl.ds(0, 16, stride=2), :]
                odd = second[part, zo, pl.ds(1, 16, stride=2), :]
                hidden2[2 * step + part, zo] = jnp.where(half, even, odd).astype(BF16)
        return carry

    lax.fori_loop(0, 2, block2, 0)
    own = cot[...].astype(F32).T.astype(BF16)
    own_cot[...] = own
    side = odd("gz")
    to_far[:128] = hidden2[:, pl.ds(2 - 2 * side, 2)].reshape(128, 128)
    to_near[:128] = hidden2[:, pl.ds(2 * side, 2)].reshape(128, 128)
    to_far[128:144] = own
    to_near[128:144] = own


def lay_weights1(taps, out):
    group = lane((16, 128)) // 32
    zero = jnp.zeros((16, 128), F32)
    wide = []
    for k in range(9):
        pieces = [taps[3 * k + dz].astype(F32) for dz in range(3)] + [jnp.zeros((4, 32), F32)]
        rows = jnp.concatenate(pieces, axis=0)
        wide.append(jnp.concatenate([rows] * 4, axis=1))
    for py in range(4):
        for px in range(4):
            at = (py * 4 + px) * 16
            for qy in range(2):
                dy = py - qy
                sides = [
                    wide[(px - qx) * 3 + dy] if 0 <= dy < 3 and 0 <= px - qx < 3 else zero for qx in range(2)
                ]
                value = jnp.where(group == 0, sides[0], sides[1])
                shifted = jnp.where(group == 2, roll(sides[0], 4, 0), roll(sides[1], 4, 0))
                out[at : at + 16, qy * 128 : qy * 128 + 128] = jnp.where(group < 2, value, shifted).astype(BF16)


def lay_weights2(taps, out):
    zero = jnp.zeros((32, 64), F32)
    for dy in range(3):
        out[dy, 384:512, 0:128] = jnp.zeros((128, 128), BF16)
        out[dy, 0:128, 128:256] = jnp.zeros((128, 128), BF16)
        for dz in range(3):
            for px in range(4):
                sides = [taps[(px - qx) * 9 + dy * 3 + dz] if 0 <= px - qx < 3 else zero for qx in range(2)]
                tile = jnp.concatenate(sides, axis=1).astype(BF16)
                for qz in range(2):
                    at = (dz + qz) * 128 + px * 32
                    out[dy, at : at + 32, qz * 128 : qz * 128 + 128] = tile


def lay_weights3(taps, out):
    zero = jnp.zeros((64, 128), BF16)
    for tap in range(9):
        out[tap, 192:256, 0:128] = zero
        out[tap, 0:64, 128:256] = zero
        for dx in range(3):
            value = taps[dx * 9 + tap]
            out[tap, dx * 64 : dx * 64 + 64, 0:128] = value
            out[tap, dx * 64 + 64 : dx * 64 + 128, 128:256] = value


def run_forward(*operands):
    return pl.pallas_call(
        forward_kernel,
        name="forward",
        out_shape=(
            jax.ShapeDtypeStruct((144, 128), BF16),
            jax.ShapeDtypeStruct((144, 128), BF16),
            jax.ShapeDtypeStruct((4, 4, 16, 128), BF16),
            jax.ShapeDtypeStruct((16, 128), BF16),
            jax.ShapeDtypeStruct((8, 4, 32, 256), F32),
            jax.ShapeDtypeStruct((6, 6, 32, 128), BF16),
            jax.ShapeDtypeStruct((5, 256, 128), BF16),
            jax.ShapeDtypeStruct((5, 128, 256), BF16),
        ),
        in_specs=[VMEM] * len(operands),
        out_specs=(VMEM,) * 8,
        cost_estimate=pl.CostEstimate(flops=5000000000, bytes_accessed=8000000, transcendentals=8000000),
        scratch_shapes=[
            pltpu.VMEM((14, 80, 256), BF16),
            pltpu.VMEM((11, 128, 640), BF16),
            pltpu.VMEM((11, 640, 128), BF16),
            pltpu.VMEM((2, 640, 256), F32),
            pltpu.VMEM((10, 10, 80, 128), F32),
            pltpu.VMEM((10, 10, 32, 128), BF16),
            pltpu.VMEM((2, 2, 4, 32, 256), F32),
            pltpu.VMEM((2, 4, 32, 128), F32),
        ],
        compiler_params=pltpu.CompilerParams(vmem_limit_bytes=LIMIT),
    )(*operands)


def weave_kernel(far, near, hidden2, own_cot, to_far, to_near, lower, upper):
    lower[...], upper[...] = sided("gz", far[...], near[...])
    side = odd("gy")
    for target, first_row in ((to_far, 2 - 2 * side), (to_near, 2 * side)):
        for y in range(2):
            row, at = first_row + y, y * 128
            rows = pl.ds(pl.multiple_of(row * 32, 32), 32)
            target[at : at + 32] = lower[rows]
            target[at + 32 : at + 96] = hidden2[row].reshape(64, 128)
            target[at + 96 : at + 128] = upper[rows]
        target[256:272] = lower[128:144]
        target[272:288] = own_cot[...]
        target[288:304] = upper[128:144]


def run_weave(*operands):
    return pl.pallas_call(
        weave_kernel,
        name="weave",
        out_shape=(jax.ShapeDtypeStruct((304, 128), BF16),) * 2 + (jax.ShapeDtypeStruct((144, 128), BF16),) * 2,
        in_specs=[VMEM] * 4,
        out_specs=(VMEM,) * 4,
        compiler_params=pltpu.CompilerParams(vmem_limit_bytes=LIMIT),
    )(*operands)


def lay_patches2(rows, target):
    half = lane((16, 128)) < 64
    swapped = roll(rows.astype(F32), 64, 1)
    target[...] = jnp.concatenate(
        [jnp.where(half, down(swapped), swapped), jnp.where(half, swapped, up(swapped))], axis=1
    ).astype(BF16)


def pool3(pre, cot):
    e = exps(pre)
    total = e[0, 0] + e[0, 1] + e[1, 0] + e[1, 1]
    total = total[:, :128] + total[:, 128:]
    mean = total * 0.125
    share = cot.astype(F32) * (0.125 / mean)
    share = jnp.concatenate([share, share], axis=1)
    return mean, (jnp.where(pre > 0, 1.0, SLOPE) * (e * share)).astype(BF16)


def own_kernel(
    hidden2, own_cot, k3, biases, turned_own, w1, keep, send, shift3, w3, wide3, ratio1, patches2, pre3, turned
):
    groups = 2 * keep.shape[0]
    wide = 128 // groups
    bias1 = jnp.concatenate([biases[0:1, :32]] * 8, axis=1)
    for yw in range(4):
        stack = jnp.concatenate([turned_own[yw], turned_own[yw + 1]], axis=1)
        ratio1[yw] = dot(stack, w1[...])
    for yw in range(4):
        for at in range(0, 256, 64):
            pre = ratio1[yw, at : at + 64] + bias1
            e = exps(pre)
            share = 0.125 / pool1(e)
            share = jnp.concatenate([share, share], axis=1)
            ratio1[yw, at : at + 64] = jnp.where(pre > 0, 1.0, SLOPE) * (e * share)
    lay_weights3(k3, w3)
    wide3[...] = jnp.concatenate([biases[2:3]] * 2, axis=1)
    for y in range(4):
        for z in range(4):
            lay_patches2(hidden2[y, z], patches2.at[y, z])
    for tap in range(9):
        dy, dz = tap // 3, tap % 3
        block = patches2[dy : dy + 2, dz : dz + 2].reshape(64, 256)
        term = dot(block, w3[tap])
        pre3[...] = term + wide3[...] if tap == 0 else pre3[...] + term
    mean, delta = pool3(pre3[...].reshape(2, 2, 16, 256), own_cot[...])
    features = rounded(jnp.log(mean) * 0.5)
    own3 = delta.reshape(64, 256)
    bias3 = own3.astype(F32).sum(axis=0, keepdims=True)
    shift3[...] = bias3[:, :128] + bias3[:, 128:]
    low, high = [], []
    for tap in range(9):
        dy, dz = tap // 3, tap % 3
        block = patches2[dy : dy + 2, dz : dz + 2].reshape(64, 256)
        full = dot_tn(own3, block)
        one = full[:128]
        low_lanes, high_lanes = roll(full[128:, :128], 64, 1), roll(full[128:, 128:], 64, 1)
        tile0 = jnp.where(lane((128, 128)) < 64, low_lanes, high_lanes)
        tile1 = high_lanes
        low.append(one[:, :128] + tile0)
        high.append(one[:, 128:] + tile1)
    first_half = lane((128, 128)) < 64
    paired = []
    for m in range(5):
        other = roll(high[2 * m + 1], 64, 1) if 2 * m + 1 < 9 else jnp.zeros((128, 128), F32)
        paired.append(jnp.where(first_half, high[2 * m], other))
    kernel3 = [piece.reshape(groups, wide, 128) for piece in low + paired]

    turned[...] = jnp.concatenate([features, jnp.zeros((112, 128), F32)], axis=0).T
    feature_rows = turned[pl.ds(0, 16, stride=8), :]
    for c in range(1, 8):
        feature_rows = feature_rows + roll(turned[pl.ds(c, 16, stride=8), :], 16 * c, 1)
    feature_rows = feature_rows.reshape(groups, wide // 8, 128)
    flag = odd("gz").astype(F32)
    fill = jnp.zeros((groups, keep.shape[1] - 14 * wide - wide // 4, 128), F32)
    pieces = kernel3 + [feature_rows * (1.0 - flag), feature_rows * flag, fill]
    keep[...], send[...] = halves(jnp.concatenate(pieces, axis=1))


def halves(value):
    flag = odd("gz").astype(F32)
    pairs = value.reshape((value.shape[0] // 2, 2) + value.shape[1:])
    even, other = pairs[:, 0], pairs[:, 1]
    return (even * (1.0 - flag) + other * flag).astype(BF16), (even * flag + other * (1.0 - flag)).astype(BF16)


def run_own(groups, *operands):
    wide = 128 // groups
    return pl.pallas_call(
        own_kernel,
        name="own",
        out_shape=(
            jax.ShapeDtypeStruct((groups // 2, -(-(14 * wide + wide // 4) // 8) * 8, 128), BF16),
            jax.ShapeDtypeStruct((groups // 2, -(-(14 * wide + wide // 4) // 8) * 8, 128), BF16),
            jax.ShapeDtypeStruct((1, 128), F32),
            jax.ShapeDtypeStruct((9, 256, 256), BF16),
            jax.ShapeDtypeStruct((1, 256), F32),
            jax.ShapeDtypeStruct((4, 256, 256), F32),
        ),
        in_specs=[VMEM] * len(operands),
        out_specs=(VMEM,) * 6,
        scratch_shapes=[
            pltpu.VMEM((4, 4, 16, 256), BF16),
            pltpu.VMEM((64, 256), F32),
            pltpu.VMEM((128, 128), F32),
        ],
        compiler_params=pltpu.CompilerParams(vmem_limit_bytes=LIMIT),
        cost_estimate=pl.CostEstimate(flops=150000000, bytes_accessed=4000000, transcendentals=20000),
    )(*operands)


def backward_kernel(
    far, lower, middle, upper, near, own_cot, w3, bias3, w2, ratio2, patches1, ratio1, fields, keep3, send3, shift3,
    keep, send, before, after, patches2, pre3, delta3, patch2, grad2, delta2, patch1, beside, grad1, delta1,
):
    before[...], after[...] = sided("gy", far[...], near[...])
    groups = 2 * keep.shape[0]
    half = lane((16, 128)) < 64

    def lay(y, source):
        for z in range(8):
            lay_patches2(source(z), patches2.at[y, z])

    for y in range(2):
        lay(y, lambda z: before[(y * 8 + z) * 16 : (y * 8 + z + 1) * 16])
        lay(y + 6, lambda z: after[(y * 8 + z) * 16 : (y * 8 + z + 1) * 16])

    def pick_middle(y, z):
        if z < 2:
            return lower[(y * 2 + z) * 16 : (y * 2 + z + 1) * 16]
        if z < 6:
            return middle[y, z - 2]
        return upper[(y * 2 + z - 6) * 16 : (y * 2 + z - 5) * 16]

    for y in range(4):
        lay(y + 2, functools.partial(pick_middle, y))

    for dy in range(3):
        blocks = [patches2[dy : dy + 6, dz : dz + 6].reshape(576, 256) for dz in range(3)]
        weights = w3[3 * dy : 3 * dy + 3].reshape(768, 256)
        term = dot(jnp.concatenate(blocks, axis=1), weights).reshape(6, 6, 16, 256)
        pre3[...] = term + bias3[...] if dy == 0 else pre3[...] + term

    for wy in range(3):
        for wz in range(3):
            pre = pre3[2 * wy : 2 * wy + 2, 2 * wz : 2 * wz + 2]
            if wy == 1:
                cot = own_cot[...] if wz == 1 else (lower if wz == 0 else upper)[128:144]
            else:
                cot = (before if wy == 0 else after)[256 + wz * 16 : 272 + wz * 16]
            delta3[2 * wy : 2 * wy + 2, 2 * wz : 2 * wz + 2] = pool3(pre, cot)[1]

    for dy in range(3):
        blocks = [delta3[2 - dy : 6 - dy, 2 - dz : 6 - dz].reshape(256, 256) for dz in range(3)]
        weights = jnp.concatenate([w3[3 * dy + dz] for dz in range(3)], axis=1)
        term = dot_nt(jnp.concatenate(blocks, axis=1), weights).reshape(4, 4, 16, 256)
        patch2[...] = term if dy == 0 else patch2[...] + term

    for y in range(4):
        for z in range(4):
            a, b = patch2[y, z, :, :128], patch2[y, z, :, 128:]
            x = rounded(jnp.where(half, b + up(a), a + down(b)))
            swapped = roll(x, 64, 1)
            grad2[y, z, pl.ds(0, 16, stride=2), :] = jnp.where(half, swapped, x)
            grad2[y, z, pl.ds(1, 16, stride=2), :] = jnp.where(half, x, swapped)

    for y in range(6):
        value = grad2[(y + 1) // 2]
        value = jnp.concatenate([value, value], axis=2)
        delta2[y] = (value * ratio2[y + 1]).astype(BF16)

    own2 = delta2[1:5, 1:3].reshape(256, 256)
    bias2 = own2.astype(F32).sum(axis=0, keepdims=True)
    bias2 = bias2[:, :128] + bias2[:, 128:]
    bias2 = bias2 + roll(bias2, 64, 1)
    taps = [None] * 27
    for dy in range(3):
        block = jnp.concatenate(
            [
                jnp.concatenate([patches1[dy : dy + 4, 2 * zo + pz] for pz in range(4)], axis=2)[:, None]
                for zo in range(2)
            ],
            axis=1,
        ).reshape(256, 512)
        full = dot_tn(block, own2)
        for dz in range(3):
            rows = full[dz * 128 : dz * 128 + 128, :128] + full[dz * 128 + 128 : dz * 128 + 256, 128:]
            for dx in range(3):
                taps[dx * 9 + dy * 3 + dz] = rows[dx * 32 : dx * 32 + 32] + roll(
                    rows[dx * 32 + 32 : dx * 32 + 64], 64, 1
                )
    def g1(columns, lanes, rows):
        blocks = [delta2[2 - dy : 6 - dy, columns, :, lanes].reshape(-1, lanes.stop - lanes.start) for dy in range(3)]
        weights = jnp.concatenate([w2[dy, rows, lanes] for dy in range(3)], axis=1)
        return dot_nt(jnp.concatenate(blocks, axis=1), weights)

    patch1[...] = g1(slice(1, 3), slice(0, 256), slice(0, 512)).reshape(4, 2, 32, 512)
    below = g1(slice(0, 1), slice(128, 256), slice(384, 512)).reshape(4, 32, 128)
    above = g1(slice(3, 4), slice(0, 128), slice(0, 128)).reshape(4, 32, 128)
    beside[0] = below
    beside[1] = above

    low_half = lane((32, 128)) < 64
    group = lane((32, 128)) // 32

    def widen(value, which):
        value = jnp.where(group == which, value, 0.0)
        value = value + roll(value, 32, 1)
        return value + roll(value, 64, 1)


    for y in range(4):
        def part(zo, pz):
            return patch1[y, zo, :, pz * 128 : pz * 128 + 128]

        sums = (
            beside[0, y] + part(0, 1), part(0, 2) + part(1, 0), part(0, 3) + part(1, 1), part(1, 2) + beside[1, y],
        )
        for z, value in enumerate(sums):
            value = rounded(value + roll(jnp.where(low_half, up(value), down(value)), 64, 1))
            grad1[y, z, pl.ds(0, 32, stride=2), :] = widen(value, 1)
            grad1[y, z, pl.ds(1, 32, stride=2), :] = widen(value, 2)
        value = grad1[y].reshape(256, 128)
        value = jnp.concatenate([value, value], axis=1)
        delta1[y] = (value * ratio1[y]).astype(BF16)

    bias1 = delta1[...].astype(F32).sum(axis=0).sum(axis=0, keepdims=True)
    bias1 = bias1[:, :128] + bias1[:, 128:]
    bias1 = bias1 + roll(bias1, 64, 1)
    bias1 = bias1 + roll(bias1, 32, 1)
    full = None
    for yw in range(4):
        term = dot(fields[yw : yw + 2].reshape(256, 256), delta1[yw])
        full = term if full is None else full + term
    full = full.reshape(4, 4, 16, 256)
    kernel1 = []
    group1 = lane((16, 128)) // 32
    for dy in range(3):
        rows = full[dy, :, :, :128] + full[dy + 1, :, :, 128:]
        pieces = []
        for dx in range(3):
            value = rows[dx] + roll(rows[dx + 1], 96, 1)
            value = value + roll(roll(value, 12, 0), 64, 1)
            pieces.append(roll(value, 32 * dx, 1) if dx else value)
        kernel1.append(jnp.where(group1 == 0, pieces[0], jnp.where(group1 == 1, pieces[1], pieces[2])))

    low_lane = lane((32, 128)) < 64
    kernel2 = [
        jnp.where(low_lane, taps[2 * m], roll(taps[2 * m + 1], 64, 1) if 2 * m + 1 < 27 else 0.0)
        for m in range(14)
    ]
    shifts = jnp.concatenate(
        [shift3[...], jnp.where(lane((1, 128)) < 64, bias2, bias1), jnp.zeros((14, 128), F32)], axis=0
    )
    shared = jnp.concatenate(kernel2 + kernel1 + [shifts], axis=0)
    rows = 512 // groups
    keep[:, :rows], send[:, :rows] = halves(shared.reshape(groups, rows, 128))
    keep[:, rows:] = keep3[...]
    send[:, rows:] = send3[...]


def run_backward(groups, *operands):
    return pl.pallas_call(
        backward_kernel,
        name="backward",
        out_shape=(jax.ShapeDtypeStruct((groups // 2, 512 // groups + operands[-2].shape[1], 128), BF16),) * 2,
        in_specs=[VMEM] * len(operands),
        out_specs=(VMEM, VMEM),
        scratch_shapes=[
            pltpu.VMEM((304, 128), BF16),
            pltpu.VMEM((304, 128), BF16),
            pltpu.VMEM((8, 8, 16, 256), BF16),
            pltpu.VMEM((6, 6, 16, 256), F32),
            pltpu.VMEM((6, 6, 16, 256), BF16),
            pltpu.VMEM((4, 4, 16, 256), F32),
            pltpu.VMEM((4, 4, 32, 128), F32),
            pltpu.VMEM((6, 4, 32, 256), BF16),
            pltpu.VMEM((4, 2, 32, 512), F32),
            pltpu.VMEM((2, 4, 32, 128), F32),
            pltpu.VMEM((4, 4, 64, 128), F32),
            pltpu.VMEM((4, 256, 256), BF16),
        ],
        compiler_params=pltpu.CompilerParams(vmem_limit_bytes=LIMIT),
    )(*operands)


def pair_kernel(kept, received, total):
    total[...] = (kept[...].astype(F32) + received[...].astype(F32)).astype(BF16)


def run_pair(kept, received):
    return pl.pallas_call(
        pair_kernel,
        name="pair",
        out_shape=jax.ShapeDtypeStruct(kept.shape, BF16),
        in_specs=[VMEM] * 2,
        out_specs=VMEM,
        compiler_params=pltpu.CompilerParams(vmem_limit_bytes=LIMIT),
    )(kept, received)


def sum_kernel(received, to_column, features):
    half, rows = received.shape[0], to_column.shape[1]
    wide = 64 // half
    high = wide // 8
    own = received[:, rows : rows + 2 * high].astype(F32)
    for c in range(wide):
        for parity in range(2):
            line = own[:, parity * high + c // 8, (c % 8) * 16 : (c % 8) * 16 + 16]
            for j in range(half):
                features[c, 2 * j + parity : 2 * j + parity + 1] = line[j : j + 1]
    total = received[:, :rows].astype(F32).sum(axis=0)
    to_column[...] = jnp.broadcast_to(total[None], to_column.shape).astype(BF16)


def run_sum(received, rows_y):
    groups = 2 * received.shape[0]
    wide = 128 // groups
    return pl.pallas_call(
        sum_kernel,
        name="sum",
        out_shape=(
            jax.ShapeDtypeStruct((rows_y, 512 // groups + 14 * wide, 128), BF16),
            jax.ShapeDtypeStruct((wide, groups, 16), F32),
        ),
        in_specs=[VMEM],
        out_specs=(VMEM, VMEM),
        compiler_params=pltpu.CompilerParams(vmem_limit_bytes=LIMIT),
    )(received)


def share_kernel(column, to_all):
    total = column[:, : to_all.shape[1]].astype(F32).sum(axis=0)
    to_all[...] = jnp.broadcast_to(total[None], to_all.shape).astype(BF16)


def run_share(column, groups):
    return pl.pallas_call(
        share_kernel,
        name="share",
        out_shape=jax.ShapeDtypeStruct((groups, 256 // groups, 128), BF16),
        in_specs=[VMEM],
        out_specs=VMEM,
        compiler_params=pltpu.CompilerParams(vmem_limit_bytes=LIMIT),
    )(column)


def third_kernel(column, grad3):
    wide = grad3.shape[1]
    first = column.shape[1] - 14 * wide
    lines = column[:, first:].astype(F32).sum(axis=0)
    for tap in range(9):
        low = lines[tap * wide : tap * wide + wide]
        grad3[tap] = low[:, :64]
        grad3[9 + tap] = low[:, 64:]
        at = (9 + tap // 2) * wide
        grad3[18 + tap] = lines[at : at + wide][:, (tap % 2) * 64 : (tap % 2) * 64 + 64]


def run_third(column, wide):
    return pl.pallas_call(
        third_kernel,
        name="third",
        out_shape=jax.ShapeDtypeStruct((27, wide, 64), F32),
        in_specs=[VMEM],
        out_specs=VMEM,
        compiler_params=pltpu.CompilerParams(vmem_limit_bytes=LIMIT),
    )(column)


def unpack_kernel(mine, other, grad1, grad2, shift1, shift2, shift3):
    wide = shift3.shape[1]
    even, uneven = sided("gz", mine[...], other[...])
    rows = jnp.concatenate([even.astype(F32)[:, None], uneven.astype(F32)[:, None]], axis=1).reshape(512, 128)
    for tap in range(27):
        at = (tap // 2) * 32
        grad2[tap] = rows[at : at + 32, (tap % 2) * 64 : (tap % 2) * 64 + 64]
    for dy in range(3):
        for dz in range(3):
            at = 448 + dy * 16 + dz * 4
            for dx in range(3):
                grad1[dx * 9 + dy * 3 + dz] = rows[at : at + 4, dx * 32 : dx * 32 + 32]
    biases = rows[496:504]
    shift1[...] = biases[1:2, 64:96]
    shift2[...] = biases[1:2, :64]
    place = lax.axis_index("gz")
    shift3[...] = roll(biases, lax.rem(128 - place * wide, 128), 1)[0:1, :wide]


def run_unpack(mine, other):
    wide = 64 // mine.shape[0]
    return pl.pallas_call(
        unpack_kernel,
        name="unpack",
        out_shape=(
            jax.ShapeDtypeStruct((27, 4, 32), F32),
            jax.ShapeDtypeStruct((27, 32, 64), F32),
            jax.ShapeDtypeStruct((1, 32), F32),
            jax.ShapeDtypeStruct((1, 64), F32),
            jax.ShapeDtypeStruct((1, wide), F32),
        ),
        in_specs=[VMEM] * 2,
        out_specs=(VMEM,) * 5,
        compiler_params=pltpu.CompilerParams(vmem_limit_bytes=LIMIT),
    )(mine, other)


def swap(to_far, to_near, axis):
    devices = lax.axis_size(axis)

    def pairs(first):
        forth = [(i, i + 1) for i in range(first, devices - 1, 2)]
        return forth + [(j, i) for i, j in forth]

    return lax.ppermute(to_far, axis, pairs(1)), lax.ppermute(to_near, axis, pairs(0))


def shards(universe, kernel1, bias1, kernel2, bias2, kernel3, bias3, cotangent):
    size_y, size_z = lax.axis_size("gy"), lax.axis_size("gz")
    wide = 128 // size_z

    tile = universe.transpose(1, 2, 0, 3).reshape(8, 32, 128)
    cot = lax.all_to_all(cotangent[:, 0].transpose(1, 0, 2), "gz", 0, 0, tiled=True).reshape(128, 16)
    far, near = swap(tile, tile, "gz")
    second = odd("gz") == 1
    lower, upper = jnp.where(second, near, far), jnp.where(second, far, near)
    strip = jnp.concatenate([lower[:, 4:], tile, upper[:, :28]], axis=1)
    strip, kernel1, kernel2, bias1, bias2, bias3 = lax.optimization_barrier(
        (strip, kernel1, kernel2, bias1, bias2, bias3)
    )
    far, near = swap(strip, strip, "gy")
    biases = jnp.stack([jnp.pad(bias1, (0, 96)), jnp.pad(bias2, (0, 64)), bias3])

    k1, k2 = kernel1.transpose(0, 2, 1).astype(F32), kernel2.transpose(0, 2, 1).astype(F32)
    k3 = kernel3.transpose(0, 2, 1)
    w1, w2, pick, chosen = run_prepare(strip, k1, k2)
    to_far, to_near, hidden2, own_cot, ratio2, patches1, turned_own, fields = run_forward(
        near, far, cot, w1, w2, pick, chosen, biases
    )
    far, near = swap(to_far, to_near, "gz")
    to_far, to_near, lower, upper = run_weave(far, near, hidden2, own_cot)
    keep3, send3, shift3, w3, wide3, ratio1 = run_own(size_z, hidden2, own_cot, k3, biases, turned_own, w1)
    far, near = swap(to_far, to_near, "gy")
    keep, send = run_backward(
        size_z,
        far, lower, hidden2, upper, near, own_cot, w3, wide3, w2, ratio2, patches1, ratio1, fields,
        keep3, send3, shift3,
    )
    mates = [(i, i + 1 - 2 * (i % 2)) for i in range(size_z)]
    packed = run_pair(keep, lax.ppermute(send, "gz", mates))
    same = [list(range(parity, size_z, 2)) for parity in range(2)]
    packed = lax.all_to_all(packed, "gz", 0, 0, tiled=True, axis_index_groups=same)
    column, features = run_sum(packed, size_y)
    column = lax.all_to_all(column, "gy", 0, 0, tiled=True)
    shared = run_share(column, size_z // 2)
    shared = lax.all_to_all(shared, "gz", 0, 0, tiled=True, axis_index_groups=same)
    other = lax.ppermute(shared, "gz", mates)
    grad3 = run_third(column, wide)
    grad1, grad2, shift1, shift2, shift3 = run_unpack(shared, other)
    return (
        features[:, None].astype(BF16), grad1.transpose(0, 2, 1), shift1[0], grad2.transpose(0, 2, 1), shift2[0], grad3, shift3[0]
    )


def solution(mesh):
    in_specs = (P(None, "gy", "gz", None), P(), P(), P(), P(), P(), P(), P("gz", "gy", None, None))
    out_specs = (P("gz", "gy", None, None), P(), P(), P(), P(), P(None, "gz", None), P("gz"))
    return jax.shard_map(shards, mesh=mesh, in_specs=in_specs, out_specs=out_specs, check_vma=False)
```
